32 devices in a mesh: seq: 16 (over z, y, x), mp: 2 (over core).
Axes of the slice: x: 2, y: 2, z: 4, core: 2. Of those that a mesh axis runs over, the one named last changes fastest.
Arguments:
- tokens: bfloat16 [1024, 2, 1024], P('seq'), may hold values from -6 to 6
- segments: int32 [2, 1024], replicated, may hold values from 0 to 3, as said below
- routed: int32 [2, 128], replicated, may hold values from 0 to 1023, as said below
- router: bfloat16 [1024], replicated, may hold values from -0.0625 to 0.0625
- dense_attn_gain: bfloat16 [1024], replicated, may hold values from 0.5 to 1.5
- dense_qkv: bfloat16 [1024, 3, 1024], P(None, None, 'mp'), may hold values from -0.1875 to 0.1875
- dense_out: bfloat16 [1024, 1024], P('mp'), may hold values from -3 to 3
- dense_mlp_gain: bfloat16 [1024], replicated, may hold values from 0.5 to 1.5
- dense_up: bfloat16 [1024, 4096], P(None, 'mp'), may hold values from -0.1875 to 0.1875
- dense_down: bfloat16 [4096, 1024], P('mp'), may hold values from -0.09375 to 0.09375
- routed_attn_gain: bfloat16 [1024], replicated, may hold values from 0.5 to 1.5
- routed_qkv: bfloat16 [1024, 3, 1024], P(None, None, 'mp'), may hold values from -0.1875 to 0.1875
- routed_out: bfloat16 [1024, 1024], P('mp'), may hold values from -3 to 3
- routed_mlp_gain: bfloat16 [1024], replicated, may hold values from 0.5 to 1.5
- routed_up: bfloat16 [1024, 4096], P(None, 'mp'), may hold values from -0.1875 to 0.1875
- routed_down: bfloat16 [4096, 1024], P('mp'), may hold values from -0.09375 to 0.09375
- cotangent: bfloat16 [1024, 2, 1024], P('seq'), may hold values from -6 to 6
Outputs:
- output: float32 [1024, 2, 1024], P('seq')
- grad_tokens: float32 [1024, 2, 1024], P('seq')
- grad_dense_attn_gain: float32 [1024], P('seq')
- grad_dense_qkv: float32 [1024, 3, 1024], P('seq', None, 'mp')
- grad_dense_out: float32 [1024, 1024], P('mp', 'seq')
- grad_dense_mlp_gain: float32 [1024], P('seq')
- grad_dense_up: float32 [1024, 4096], P('seq', 'mp')
- grad_dense_down: float32 [4096, 1024], P('mp', 'seq')
- grad_routed_attn_gain: float32 [1024], P('seq')
- grad_routed_qkv: float32 [1024, 3, 1024], P('seq', None, 'mp')
- grad_routed_out: float32 [1024, 1024], P('mp', 'seq')
- grad_routed_mlp_gain: float32 [1024], P('seq')
- grad_routed_up: float32 [1024, 4096], P('seq', 'mp')
- grad_routed_down: float32 [4096, 1024], P('mp', 'seq')
- grad_router: float32 [1024], P('seq')
The draws below stay inside these ranges and needn't reach their ends.
Inputs may be any that keep to these rules, and one draw needn't show every extreme that they name: `segments`: along each sequence the numbers start at 0 and never fall. One sequence of each draw, which one drawn from the seed, is a single document (all 0); every other holds exactly 4 documents. `routed`: each row lists 128 distinct positions of its sequence in increasing order. Of the 64 positions of a sequence on one index of seq at most 16 are listed, and exactly 16 on one index in every sequence.
All inputs are finite; a program needn't handle non-finite values.
Results may differ from the reference program's by a relative error of at most 0.024.
Values may be sent and summed in bfloat16 or wider, within the bound.
A program may use at most 192 MiB of HBM per device.

```python
import math
import jax
import jax.numpy as jnp
from jax import lax

D = 1024
HEADS = 16
HEAD_DIM = 64
FF = 4096
GROUP = 64
SEQS = 2
NDOC = 4
LENGTH = 1024


def draw_segments(key, part):
    key = jax.random.fold_in(key, 11)
    cut_key, pick_key = jax.random.split(key)

    def one_sequence(seq_key):
        shuffled = jax.random.permutation(seq_key, LENGTH - 1) + 1
        cut_points = shuffled[:NDOC - 1]
        places = jnp.arange(LENGTH, dtype=jnp.int32)
        return jnp.sum((places[:, None] >= cut_points[None, :]).astype(jnp.int32), axis=1)
    labels = jax.vmap(one_sequence)(jax.random.split(cut_key, SEQS))
    single = jax.random.randint(pick_key, (), 0, SEQS)
    others = (jnp.arange(SEQS) != single).astype(jnp.int32)
    return (labels * others[:, None]).astype(jnp.int32)


def draw_routed(key, part):
    key = jax.random.fold_in(key, 23)
    blocks = LENGTH // GROUP
    half_count = blocks // 2
    per_block = GROUP // 8

    def one_sequence(seq_key):
        shift_key, full_key, score_key = jax.random.split(seq_key, 3)
        shifts = jax.random.randint(shift_key, (half_count,), -per_block, per_block + 1)
        chosen = jax.random.randint(full_key, (), 0, blocks)
        forced = jnp.where(chosen < half_count, per_block, -per_block)
        shifts = jnp.where(jnp.arange(half_count) == chosen % half_count, forced, shifts)
        counts = jnp.concatenate([per_block + shifts, per_block - shifts])
        scores = jax.random.randint(score_key, (blocks, GROUP), 0, 1 << 20) * GROUP + jnp.arange(GROUP)[None, :]
        ranking = jnp.argsort(jnp.argsort(scores, axis=1), axis=1)
        chosen_cells = (ranking < counts[:, None]).reshape(-1)
        return jnp.nonzero(chosen_cells, size=LENGTH // 8)[0].astype(jnp.int32)
    return jax.vmap(one_sequence)(jax.random.split(key, SEQS))


def shard_levels(key, shape, cuts, least, largest):
    def one(dim, shards_of):
        heights = jax.random.uniform(jax.random.fold_in(jax.random.fold_in(key, 6), dim), (shards_of,), jnp.float32, least / len(cuts), largest / len(cuts))
        return jnp.repeat(jnp.exp(heights), shape[dim] // shards_of).reshape((-1,) + (1,) * (len(shape) - dim - 1))

    level = one(*cuts[0])
    for cut in cuts[1:]:
        level = level * one(*cut)
    return level


def scatter_about(key, shape, scale, bound, cuts=(), kind=jnp.bfloat16):
    values = scale * jax.random.normal(key, shape, jnp.float32)
    if cuts:
        values = values * shard_levels(key, shape, cuts, -0.22, 0.18)
    return jnp.clip(values, -bound, bound).astype(kind)


def setup_inputs(seed: int = 0) -> dict:
    streams_of = jax.random.split(jax.random.key(seed), 18)
    tokens = scatter_about(streams_of[0], (LENGTH, SEQS, D), 1.0, 6.0, ((0, 16),))
    segments = draw_segments(jax.random.fold_in(streams_of[17], 71), 0)
    routed = draw_routed(jax.random.fold_in(streams_of[17], 71), 0)
    router = scatter_about(streams_of[3], (D,), (8 * D) ** -0.5, 0.0625)
    dense_attn_gain = jnp.clip(1.0 + 0.1 * jax.random.normal(streams_of[4], (D,), jnp.float32), 0.5, 1.5).astype(jnp.bfloat16)
    dense_qkv = scatter_about(streams_of[5], (D, 3, HEADS * HEAD_DIM), D ** -0.5, 0.1875, ((2, 2),))
    dense_out = scatter_about(streams_of[6], (HEADS * HEAD_DIM, D), 4 ** -0.5, 3.0, ((0, 2),))
    dense_mlp_gain = jnp.clip(1.0 + 0.1 * jax.random.normal(streams_of[7], (D,), jnp.float32), 0.5, 1.5).astype(jnp.bfloat16)
    dense_up = scatter_about(streams_of[8], (D, FF), D ** -0.5, 0.1875, ((1, 2),))
    dense_down = scatter_about(streams_of[9], (FF, D), FF ** -0.5, 0.09375, ((0, 2),))
    routed_attn_gain = jnp.clip(1.0 + 0.1 * jax.random.normal(streams_of[10], (D,), jnp.float32), 0.5, 1.5).astype(jnp.bfloat16)
    routed_qkv = scatter_about(streams_of[11], (D, 3, HEADS * HEAD_DIM), D ** -0.5, 0.1875, ((2, 2),))
    routed_out = scatter_about(streams_of[12], (HEADS * HEAD_DIM, D), 4 ** -0.5, 3.0, ((0, 2),))
    routed_mlp_gain = jnp.clip(1.0 + 0.1 * jax.random.normal(streams_of[13], (D,), jnp.float32), 0.5, 1.5).astype(jnp.bfloat16)
    routed_up = scatter_about(streams_of[14], (D, FF), D ** -0.5, 0.1875, ((1, 2),))
    routed_down = scatter_about(streams_of[15], (FF, D), FF ** -0.5, 0.09375, ((0, 2),))
    cotangent = scatter_about(streams_of[16], (LENGTH, SEQS, D), 1.0, 6.0, ((0, 16),))
    return dict(tokens=tokens, segments=segments, routed=routed, router=router, dense_attn_gain=dense_attn_gain, dense_qkv=dense_qkv, dense_out=dense_out, dense_mlp_gain=dense_mlp_gain, dense_up=dense_up, dense_down=dense_down, routed_attn_gain=routed_attn_gain, routed_qkv=routed_qkv, routed_out=routed_out, routed_mlp_gain=routed_mlp_gain, routed_up=routed_up, routed_down=routed_down, cotangent=cotangent)


@jax.custom_vjp
def low(v):
    return lax.optimization_barrier(v.astype(jnp.bfloat16)).astype(jnp.float32)

@jax.custom_vjp
def low_back(v):
    return v

def low_keep(v):
    return (low(v), None)

def low_pass(kept, grad):
    return (grad,)

def back_keep(v):
    return (v, None)

def back_low(kept, grad):
    return (low(grad),)
low.defvjp(low_keep, low_pass)
low_back.defvjp(back_keep, back_low)
EPSILON = 1e-06
NEGATIVE = -1e+30
PRECISE = lax.Precision.HIGHEST

def rms_norm(hidden, gain):
    return hidden * lax.rsqrt(lax.optimization_barrier(jnp.mean(hidden * hidden, axis=-1, keepdims=True)) + EPSILON) * gain

def attend_block(query_block, place_block, label_block, key_heads, value_heads, key_places, key_labels):
    scores = low_back(jnp.einsum('qhe,khe->hqk', query_block, key_heads, precision=PRECISE) * HEAD_DIM ** (-0.5))
    allowed = (key_places[None, :] <= place_block[:, None]) & (key_labels[None, :] == label_block[:, None])
    scores = jnp.where(allowed[None], scores, NEGATIVE)
    highest = lax.optimization_barrier(jnp.max(scores, axis=-1, keepdims=True))
    weights = jnp.exp(scores - highest)
    totals = lax.optimization_barrier(jnp.sum(weights, axis=-1))
    mixed_heads = jnp.einsum('hqk,khe->qhe', low(weights), value_heads, precision=PRECISE)
    return mixed_heads / jnp.transpose(totals)[:, :, None]

def attend_sequence(operands):
    query_heads, key_heads, value_heads, places, labels = operands
    row_total = query_heads.shape[0]
    block_size = math.gcd(row_total, 256)
    blocks = row_total // block_size
    step_fn = jax.checkpoint(lambda pieces: attend_block(pieces[0], pieces[1], pieces[2], key_heads, value_heads, places, labels))
    mixed_heads = lax.map(step_fn, (query_heads.reshape(blocks, block_size, HEADS, HEAD_DIM), places.reshape(blocks, block_size), labels.reshape(blocks, block_size)))
    return mixed_heads.reshape(row_total, HEADS * HEAD_DIM)

def layer_block(hidden, places, labels, params):
    attn_gain, qkv_weight, out_weight, mlp_gain, up_weight, down_weight = params
    seq_count, row_total, _ = hidden.shape
    normed = low(rms_norm(hidden, attn_gain))
    projected = low(low_back(jnp.einsum('srd,dce->srce', normed, qkv_weight, precision=PRECISE)))
    split_heads = projected.reshape(seq_count, row_total, 3, HEADS, HEAD_DIM)
    mixed_rows = lax.map(attend_sequence, (split_heads[:, :, 0], split_heads[:, :, 1], split_heads[:, :, 2], places, labels))
    mixed_rows = low(low_back(mixed_rows))
    attention = low_back(jnp.einsum('srh,hd->srd', mixed_rows, out_weight, precision=PRECISE))
    middle = hidden + attention
    normed_mlp = low(rms_norm(middle, mlp_gain))
    before = low_back(jnp.einsum('srd,df->srf', normed_mlp, up_weight, precision=PRECISE))
    active = low(jax.nn.gelu(before, approximate=True))
    feed_out = low_back(jnp.einsum('srf,fd->srd', active, down_weight, precision=PRECISE))
    return (middle, attention, feed_out)

def forward(tokens, router, dense_params, routed_params, segments, routed):
    hidden = jnp.transpose(tokens, (1, 0, 2))
    places = jnp.broadcast_to(jnp.arange(LENGTH, dtype=jnp.int32)[None, :], segments.shape)
    middle, _, feed_out = layer_block(hidden, places, segments, dense_params)
    first_out = middle + feed_out
    picked = jnp.take_along_axis(first_out, routed[:, :, None], axis=1)
    labels = jnp.take_along_axis(segments, routed, axis=1)
    _, routed_attention, routed_feed = layer_block(low(low_back(picked)), routed, labels, routed_params)
    sent_rows = low(low_back(routed_attention + routed_feed))
    gate_value = jax.nn.sigmoid(jnp.einsum('scd,d->sc', picked, router, precision=PRECISE))
    update = gate_value[:, :, None] * sent_rows
    result = jax.vmap(lambda stream, where_at, addend: stream.at[where_at].add(addend))(first_out, routed, update)
    return jnp.transpose(result, (1, 0, 2))

def reference(tokens, segments, routed, router, dense_attn_gain, dense_qkv, dense_out, dense_mlp_gain, dense_up, dense_down, routed_attn_gain, routed_qkv, routed_out, routed_mlp_gain, routed_up, routed_down, cotangent):
    floats = tuple((operand.astype(jnp.float32) for operand in (tokens, router, dense_attn_gain, dense_qkv, dense_out, dense_mlp_gain, dense_up, dense_down, routed_attn_gain, routed_qkv, routed_out, routed_mlp_gain, routed_up, routed_down)))

    def whole_layer(*values):
        return forward(values[0], values[1], values[2:8], values[8:14], segments, routed)
    output, pullback = jax.vjp(whole_layer, *floats)
    gradients = pullback(cotangent.astype(jnp.float32))
    return (output, gradients[0], gradients[2], gradients[3], gradients[4], gradients[5], gradients[6], gradients[7], gradients[8], gradients[9], gradients[10], gradients[11], gradients[12], gradients[13], gradients[1])
```

```python
import math
import types

import jax
import jax.numpy as jnp
from jax import lax
from jax.experimental import pallas as pl
from jax.experimental.pallas import tpu as pltpu
from jax.sharding import PartitionSpec as P

HEAD_DIM = 64


EPSILON = 1e-06
NEGATIVE = -1e30
PRECISE = lax.Precision.HIGHEST


def rms_norm(hidden, gain):
    return hidden * lax.rsqrt(jnp.mean(hidden * hidden, axis=-1, keepdims=True) + EPSILON) * gain


def gelu_tanh(operand):
    return jax.nn.gelu(operand, approximate=True)


def model_sum(operand):
    return lax.psum(operand, "mp")


def block_loop(row_total, advance, carried):
    block_size = math.gcd(row_total, 512)
    return lax.fori_loop(
        0,
        row_total // block_size,
        lambda number, current: advance(current, number * block_size, block_size),
        carried,
    )


def key_mask(query_places, query_live, key_places, key_live, label_rows):
    query_labels = jnp.take_along_axis(label_rows, query_places, axis=0)
    key_labels = jnp.take_along_axis(label_rows, key_places, axis=0)
    allowed = jnp.transpose(key_places)[:, None, :] <= jnp.transpose(query_places)[:, :, None]
    allowed = allowed & (
        jnp.transpose(key_labels)[:, None, :] == jnp.transpose(query_labels)[:, :, None]
    )
    allowed = allowed & jnp.transpose(key_live)[:, None, :] & jnp.transpose(query_live)[:, :, None]
    return allowed[:, None]


def attend_forward(queries, key_rows, value_rows, own_places, own_live, row_info, label_rows):
    row_count, seq_count, head_count, head_size = queries.shape
    score_scale = head_size ** (-0.5)
    shape_rows = (seq_count, head_count, row_count)
    initial = (
        jnp.full(shape_rows, NEGATIVE, jnp.float32),
        jnp.zeros(shape_rows, jnp.float32),
        jnp.zeros(shape_rows + (head_size,), jnp.float32),
    )
    key_piece = lax.all_gather(key_rows, "seq", axis=0, tiled=True)
    value_piece = lax.all_gather(value_rows, "seq", axis=0, tiled=True)

    def advance(current, offset, block_size):
        highest, totals, summed = current
        key_block = lax.dynamic_slice_in_dim(key_piece, offset, block_size, 0).reshape(
            block_size, seq_count, head_count, head_size
        )
        value_block = lax.dynamic_slice_in_dim(value_piece, offset, block_size, 0).reshape(
            block_size, seq_count, head_count, head_size
        )
        key_places, key_live = row_info(offset, block_size)
        allowed = key_mask(own_places, own_live, key_places, key_live, label_rows)
        scores = (
            jnp.einsum("qshe,kshe->shqk", queries, key_block, preferred_element_type=jnp.float32)
            * score_scale
        )
        scores = jnp.where(allowed, scores, NEGATIVE)
        newest = jnp.maximum(highest, jnp.max(scores, axis=-1))
        weights = jnp.exp(scores - newest[..., None])
        factor = jnp.exp(highest - newest)
        totals = totals * factor + jnp.sum(weights, axis=-1)
        summed = summed * factor[..., None] + jnp.einsum(
            "shqk,kshe->shqe",
            weights.astype(jnp.bfloat16),
            value_block,
            preferred_element_type=jnp.float32,
        )
        return (newest, totals, summed)

    highest, totals, summed = block_loop(key_piece.shape[0], advance, initial)
    mixed_rows = jnp.transpose(summed / totals[..., None], (2, 0, 1, 3)).reshape(
        row_count, seq_count, head_count * head_size
    )
    return (mixed_rows, highest + jnp.log(totals), None)


def attend_backward(
    queries,
    key_rows,
    value_rows,
    grad_mixed,
    mixed_rows,
    log_sum,
    own_places,
    own_live,
    row_info,
    label_rows,
):
    row_count, seq_count, head_count, head_size = queries.shape
    score_scale = head_size ** (-0.5)
    grad_heads = grad_mixed.reshape(row_count, seq_count, head_count, head_size)
    offsets = jnp.sum(
        grad_heads.astype(jnp.float32)
        * mixed_rows.reshape(row_count, seq_count, head_count, head_size),
        axis=-1,
    )
    offsets_rows = jnp.transpose(offsets, (1, 2, 0))
    key_piece = lax.all_gather(key_rows, "seq", axis=0, tiled=True)
    value_piece = lax.all_gather(value_rows, "seq", axis=0, tiled=True)

    def advance(current, offset, block_size):
        key_block = lax.dynamic_slice_in_dim(key_piece, offset, block_size, 0).reshape(
            block_size, seq_count, head_count, head_size
        )
        value_block = lax.dynamic_slice_in_dim(value_piece, offset, block_size, 0).reshape(
            block_size, seq_count, head_count, head_size
        )
        key_places, key_live = row_info(offset, block_size)
        allowed = key_mask(own_places, own_live, key_places, key_live, label_rows)
        scores = (
            jnp.einsum("qshe,kshe->shqk", queries, key_block, preferred_element_type=jnp.float32)
            * score_scale
        )
        scores = jnp.where(allowed, scores, NEGATIVE)
        chances = jnp.exp(scores - log_sum[..., None])
        pushes = jnp.einsum(
            "qshe,kshe->shqk", grad_heads, value_block, preferred_element_type=jnp.float32
        )
        slopes = (chances * (pushes - offsets_rows[..., None])).astype(jnp.bfloat16)
        return current + jnp.einsum(
            "shqk,kshe->qshe", slopes, key_block, preferred_element_type=jnp.float32
        )

    grad_queries = block_loop(key_piece.shape[0], advance, jnp.zeros(queries.shape, jnp.float32))
    log_all, offsets_all = (
        lax.all_gather(jnp.transpose(log_sum, (2, 0, 1)), "seq", axis=0, tiled=True),
        lax.all_gather(offsets, "seq", axis=0, tiled=True),
    )
    own_keys = key_rows.reshape(row_count, seq_count, head_count, head_size)
    own_values = value_rows.reshape(row_count, seq_count, head_count, head_size)
    zero_rows = jnp.zeros(queries.shape, jnp.float32)
    query_flat = queries.reshape(row_count, seq_count, head_count * head_size)
    query_piece = lax.all_gather(query_flat, "seq", axis=0, tiled=True)
    grad_piece = lax.all_gather(grad_mixed, "seq", axis=0, tiled=True)

    def advance(current, offset, block_size):
        key_sum, value_sum = current
        query_block = lax.dynamic_slice_in_dim(query_piece, offset, block_size, 0).reshape(
            block_size, seq_count, head_count, head_size
        )
        grad_block = lax.dynamic_slice_in_dim(grad_piece, offset, block_size, 0).reshape(
            block_size, seq_count, head_count, head_size
        )
        block_log = jnp.transpose(
            lax.dynamic_slice_in_dim(log_all, offset, block_size, 0), (1, 2, 0)
        )
        block_offsets = jnp.transpose(
            lax.dynamic_slice_in_dim(offsets_all, offset, block_size, 0), (1, 2, 0)
        )
        query_places, query_live = row_info(offset, block_size)
        allowed = key_mask(query_places, query_live, own_places, own_live, label_rows)
        scores = (
            jnp.einsum("qshe,kshe->shqk", query_block, own_keys, preferred_element_type=jnp.float32)
            * score_scale
        )
        scores = jnp.where(allowed, scores, NEGATIVE)
        chances = jnp.exp(scores - block_log[..., None])
        pushes = jnp.einsum(
            "qshe,kshe->shqk", grad_block, own_values, preferred_element_type=jnp.float32
        )
        slopes = (chances * (pushes - block_offsets[..., None])).astype(jnp.bfloat16)
        key_sum = key_sum + jnp.einsum(
            "shqk,qshe->kshe", slopes, query_block, preferred_element_type=jnp.float32
        )
        value_sum = value_sum + jnp.einsum(
            "shqk,qshe->kshe",
            chances.astype(jnp.bfloat16),
            grad_block,
            preferred_element_type=jnp.float32,
        )
        return (key_sum, value_sum)

    key_sum, value_sum = block_loop(query_piece.shape[0], advance, (zero_rows, zero_rows))
    flat_shape = (row_count, seq_count, head_count * head_size)
    return (
        (grad_queries * score_scale).reshape(flat_shape),
        (key_sum * score_scale).reshape(flat_shape),
        value_sum.reshape(flat_shape),
    )


def block_forward(hidden, params, row_info, label_rows):
    attn_gain, qkv_weight, out_weight, mlp_gain, up_weight, down_weight = params
    row_count, seq_count, _ = hidden.shape
    head_width = qkv_weight.shape[2]
    head_count = head_width // HEAD_DIM
    own_places, own_live = row_info(lax.axis_index("seq") * row_count, row_count)
    normed = rms_norm(hidden, attn_gain.astype(jnp.float32)).astype(jnp.bfloat16)
    projected = jnp.einsum(
        "rsd,dce->rsce", normed, qkv_weight, preferred_element_type=jnp.float32
    ).astype(jnp.bfloat16)
    queries = projected[:, :, 0].reshape(row_count, seq_count, head_count, HEAD_DIM)
    key_rows = projected[:, :, 1]
    value_rows = projected[:, :, 2]
    mixed_rows, log_sum, kept_rows = attend_forward(
        queries, key_rows, value_rows, own_places, own_live, row_info, label_rows
    )
    mixed_low = mixed_rows.astype(jnp.bfloat16)
    attention = model_sum(
        jnp.einsum("rsh,hd->rsd", mixed_low, out_weight, preferred_element_type=jnp.float32)
    )
    middle = hidden + attention
    normed_mlp = rms_norm(middle, mlp_gain.astype(jnp.float32)).astype(jnp.bfloat16)
    before = jnp.einsum("rsd,df->rsf", normed_mlp, up_weight, preferred_element_type=jnp.float32)
    active = gelu_tanh(before).astype(jnp.bfloat16)
    feed_out = model_sum(
        jnp.einsum("rsf,fd->rsd", active, down_weight, preferred_element_type=jnp.float32)
    )
    stored = (
        hidden,
        normed,
        queries,
        key_rows,
        value_rows,
        mixed_rows,
        log_sum,
        mixed_low,
        middle,
        normed_mlp,
        before,
        active,
        own_places,
        own_live,
        kept_rows,
    )
    return (attention, middle, feed_out, stored)


def block_backward(incoming, stored, params, row_info, label_rows):
    attn_gain, qkv_weight, out_weight, mlp_gain, up_weight, down_weight = params
    (
        hidden,
        normed,
        queries,
        key_rows,
        value_rows,
        mixed_rows,
        log_sum,
        mixed_low,
        middle,
        normed_mlp,
        before,
        active,
        own_places,
        own_live,
        kept_rows,
    ) = stored
    incoming_low = incoming.astype(jnp.bfloat16)
    grad_down = jnp.einsum("rsf,rsd->fd", active, incoming_low, preferred_element_type=jnp.float32)
    grad_active = jnp.einsum(
        "rsd,fd->rsf", incoming_low, down_weight, preferred_element_type=jnp.float32
    )
    _, gelu_pull = jax.vjp(gelu_tanh, before)
    grad_before = gelu_pull(grad_active)[0].astype(jnp.bfloat16)
    grad_up = jnp.einsum("rsd,rsf->df", normed_mlp, grad_before, preferred_element_type=jnp.float32)
    grad_normed_mlp = model_sum(
        jnp.einsum("rsf,df->rsd", grad_before, up_weight, preferred_element_type=jnp.float32)
    )
    _, mlp_pull = jax.vjp(rms_norm, middle, mlp_gain.astype(jnp.float32))
    grad_middle, grad_mlp_gain = mlp_pull(grad_normed_mlp)
    along_low = (incoming + grad_middle).astype(jnp.bfloat16)
    grad_out = jnp.einsum("rsh,rsd->hd", mixed_low, along_low, preferred_element_type=jnp.float32)
    grad_mixed = jnp.einsum(
        "rsd,hd->rsh", along_low, out_weight, preferred_element_type=jnp.float32
    ).astype(jnp.bfloat16)
    grad_queries, grad_keys, grad_values = attend_backward(
        queries,
        key_rows,
        value_rows,
        grad_mixed,
        mixed_rows,
        log_sum,
        own_places,
        own_live,
        row_info,
        label_rows,
    )
    grad_projected = jnp.stack((grad_queries, grad_keys, grad_values), axis=2).astype(jnp.bfloat16)
    grad_qkv = jnp.einsum(
        "rsd,rsce->dce", normed, grad_projected, preferred_element_type=jnp.float32
    )
    grad_normed = model_sum(
        jnp.einsum("rsce,dce->rsd", grad_projected, qkv_weight, preferred_element_type=jnp.float32)
    )
    _, attn_pull = jax.vjp(rms_norm, hidden, attn_gain.astype(jnp.float32))
    grad_hidden, grad_attn_gain = attn_pull(grad_normed)
    return (
        grad_middle + grad_hidden,
        (grad_attn_gain, grad_qkv, grad_out, grad_mlp_gain, grad_up, grad_down),
    )


def on_device(
    tokens,
    segments,
    routed,
    router,
    dense_attn_gain,
    dense_qkv,
    dense_out,
    dense_mlp_gain,
    dense_up,
    dense_down,
    routed_attn_gain,
    routed_qkv,
    routed_out,
    routed_mlp_gain,
    routed_up,
    routed_down,
    cotangent,
):
    group_rows, seq_count, _ = tokens.shape
    devices = lax.axis_size("seq")
    my_index = lax.axis_index("seq")
    capacity = routed.shape[1]
    most_rows = group_rows // 4
    label_rows = jnp.transpose(segments)
    route_rows = jnp.transpose(routed)
    local_ids = jnp.arange(group_rows, dtype=jnp.int32)
    bounds = jnp.arange(devices + 1, dtype=jnp.int32) * group_rows
    starts = jnp.sum((routed[None, :, :] < bounds[:, None, None]).astype(jnp.int32), axis=2)
    first_rank = starts[my_index]
    routed_here = starts[my_index + 1] - first_rank
    dense_params = (dense_attn_gain, dense_qkv, dense_out, dense_mlp_gain, dense_up, dense_down)
    routed_params = (
        routed_attn_gain,
        routed_qkv,
        routed_out,
        routed_mlp_gain,
        routed_up,
        routed_down,
    )

    def dense_info(first_row, row_total):
        places = first_row + jnp.broadcast_to(
            jnp.arange(row_total, dtype=jnp.int32)[:, None], (row_total, seq_count)
        )
        return (places, jnp.ones((row_total, seq_count), jnp.bool_))

    slot_rows = jnp.arange(most_rows, dtype=jnp.int32)
    is_live = slot_rows[:, None] < routed_here[None, :]
    hold_places = (
        jnp.take_along_axis(
            route_rows, jnp.clip(first_rank[None, :] + slot_rows[:, None], 0, capacity - 1), axis=0
        )
        - my_index * group_rows
    )
    hold_table = (
        (jnp.transpose(hold_places)[:, :, None] == local_ids[None, None, :])
        & jnp.transpose(is_live)[:, :, None]
    ).astype(jnp.bfloat16)

    def select_rows(rows_in):
        return jnp.einsum(
            "smc,csd->msd", hold_table, rows_in, preferred_element_type=jnp.float32
        ).astype(jnp.bfloat16)

    def restore_rows(rows_in):
        return jnp.einsum("smc,msd->csd", hold_table, rows_in, preferred_element_type=jnp.float32)

    def routed_info(first_row, row_total):
        number = first_row + jnp.arange(row_total, dtype=jnp.int32)
        source = number // most_rows
        within = number % most_rows
        base = jnp.take(starts, source, axis=0)
        filled = jnp.take(starts, source + 1, axis=0) - base
        rank_rows = jnp.clip(base + within[:, None], 0, capacity - 1)
        return (jnp.take_along_axis(route_rows, rank_rows, axis=0), within[:, None] < filled)

    hidden = tokens.astype(jnp.float32)
    _, middle, feed_out, dense_stored = block_forward(hidden, dense_params, dense_info, label_rows)
    first_out = middle + feed_out
    lifted = select_rows(first_out.astype(jnp.bfloat16))
    routed_attention, _, routed_feed, routed_stored = block_forward(
        lifted.astype(jnp.float32), routed_params, routed_info, label_rows
    )
    sent_rows = (routed_attention + routed_feed).astype(jnp.bfloat16)
    returned = restore_rows(sent_rows)
    router_float = router.astype(jnp.float32)
    gate_value = jax.nn.sigmoid(jnp.einsum("csd,d->cs", first_out, router_float, precision=PRECISE))
    output = first_out + gate_value[:, :, None] * returned
    grad_output = cotangent.astype(jnp.float32)
    grad_sent = select_rows((gate_value[:, :, None] * grad_output).astype(jnp.bfloat16))
    grad_logit = jnp.sum(grad_output * returned, axis=-1) * gate_value * (1.0 - gate_value)
    grad_router = jnp.einsum("cs,csd->d", grad_logit, first_out, precision=PRECISE)
    grad_first = grad_output + grad_logit[:, :, None] * router_float
    routed_branch, routed_grads = block_backward(
        grad_sent.astype(jnp.float32), routed_stored, routed_params, routed_info, label_rows
    )
    grad_first = grad_first + restore_rows(routed_branch.astype(jnp.bfloat16))
    dense_branch, dense_grads = block_backward(
        grad_first, dense_stored, dense_params, dense_info, label_rows
    )
    grad_tokens = grad_first + dense_branch
    summed_all = (
        lax.psum_scatter(dense_grads[0], "seq", scatter_dimension=0, tiled=True),
        lax.psum_scatter(dense_grads[1], "seq", scatter_dimension=0, tiled=True),
        lax.psum_scatter(dense_grads[2], "seq", scatter_dimension=1, tiled=True),
        lax.psum_scatter(dense_grads[3], "seq", scatter_dimension=0, tiled=True),
        lax.psum_scatter(dense_grads[4], "seq", scatter_dimension=0, tiled=True),
        lax.psum_scatter(dense_grads[5], "seq", scatter_dimension=1, tiled=True),
        lax.psum_scatter(routed_grads[0], "seq", scatter_dimension=0, tiled=True),
        lax.psum_scatter(routed_grads[1], "seq", scatter_dimension=0, tiled=True),
        lax.psum_scatter(routed_grads[2], "seq", scatter_dimension=1, tiled=True),
        lax.psum_scatter(routed_grads[3], "seq", scatter_dimension=0, tiled=True),
        lax.psum_scatter(routed_grads[4], "seq", scatter_dimension=0, tiled=True),
        lax.psum_scatter(routed_grads[5], "seq", scatter_dimension=1, tiled=True),
        lax.psum_scatter(grad_router, "seq", scatter_dimension=0, tiled=True),
    )
    dense_sums = tuple(summed_all[0:6])
    routed_sums = tuple(summed_all[6:13])
    return (output, grad_tokens) + tuple(dense_sums) + tuple(routed_sums)


BF = jnp.bfloat16
LIMIT = 63 * 1024 * 1024
F32 = jnp.float32
MESH = pl.DeviceIdType.MESH
COLS = ((0, 1536), (1536, 512), (2048, 2048), (4096, 2048))


def dot(a, b):
    return lax.dot_general(a, b, (((1,), (0,)), ((), ())), preferred_element_type=F32)


def dot_t(a, b):
    return lax.dot_general(a, b, (((1,), (1,)), ((), ())), preferred_element_type=F32)


def dot_l(a, b):
    return lax.dot_general(a, b, (((0,), (0,)), ((), ())), preferred_element_type=F32)


def swap_halves(tile):
    return pltpu.roll(tile, 64, 1)


def low_lanes(rows):
    return lax.broadcasted_iota(jnp.int32, (rows, 128), 1) < 64


def inverse_rms(rows):
    return lax.rsqrt(jnp.mean(rows * rows, axis=1, keepdims=True) + EPSILON)


def norm_back(grad, rows, gain):
    inverse = inverse_rms(rows)
    unit = rows * inverse
    pulled = grad * gain
    grad_rows = inverse * (pulled - unit * jnp.mean(pulled * unit, axis=1, keepdims=True))
    return grad_rows, jnp.sum(grad * unit, axis=0, keepdims=True)


class Env:
    def __init__(self, refs, sems, seq_size):
        self.b = refs
        self.sems = sems
        self.count = 0
        self.sends = []
        self.flying = {}
        self.stores = {}
        self.stored = 0
        self.barrier_done = False
        self.n = seq_size
        self.s = lax.axis_index("seq")
        self.c = lax.axis_index("mp")
        self.q = lax.rem(self.s, 4)
        self.z = lax.div(self.s, 4)

    def sem(self):
        self.count += 1
        return self.sems.at[self.count - 1]

    def greet(self):
        barrier = pltpu.get_barrier_semaphore()

        def signal(step, _):
            other = lax.rem(self.s + step, self.n)
            pl.semaphore_signal(barrier, inc=1, device_id=(other, self.c), device_id_type=MESH)
            return 0

        lax.fori_loop(1, self.n, signal, 0)
        pl.semaphore_signal(barrier, inc=1, device_id=(self.s, 1 - self.c), device_id_type=MESH)

    def meet(self):
        if not self.barrier_done:
            pl.semaphore_wait(pltpu.get_barrier_semaphore(), self.n)
            self.barrier_done = True

    def remote(self, src, dst, send, recv, seq, core):
        return pltpu.make_async_remote_copy(
            src_ref=src,
            dst_ref=dst,
            send_sem=send,
            recv_sem=recv,
            device_id=(seq, core),
            device_id_type=MESH,
        )

    def exchange(self, send_ref, recv_ref):
        self.meet()
        send, recv = self.sem(), self.sem()
        n = self.n

        def start(step, _):
            other = lax.rem(self.s + step, n)
            self.remote(
                send_ref.at[other], recv_ref.at[self.s], send, recv, other, self.c
            ).start()
            return 0

        lax.fori_loop(1, n, start, 0)
        recv_ref[pl.ds(self.s, 1)] = send_ref[pl.ds(self.s, 1)]
        whole = self.remote(
            send_ref.at[pl.ds(0, n - 1)],
            recv_ref.at[pl.ds(0, n - 1)],
            send,
            recv,
            lax.rem(self.s + 1, n),
            self.c,
        )
        self.sends.append(whole)
        return whole.wait_recv

    def core_sum(self, layer, half, chunk, sink):
        self.meet()
        send_ref, recv_ref = layer.b.ps.at[half], layer.b.pr.at[half]
        copies = []
        for number in range(4):
            earlier = self.flying.pop((layer.packed, half, number), None)
            if earlier is not None:
                earlier.wait_send()
            send_ref[number] = chunk(number).astype(BF)
            copy = self.remote(
                send_ref.at[number], recv_ref.at[number], self.sem(), self.sem(), self.s, 1 - self.c
            )
            copy.start()
            copies.append(copy)
            self.flying[(layer.packed, half, number)] = copy
        for number, copy in enumerate(copies):
            copy.wait_recv()
            sink(number, send_ref[number].astype(F32) + recv_ref[number].astype(F32))

    def plane_send(self, pieces, recv_piece, wait_piece):
        self.meet()
        send, recv = self.sem(), self.sem()
        for step in range(1, 4):
            other = lax.rem(self.q + step, 4)
            self.remote(
                pieces(other), recv_piece, send, recv, self.z * 4 + other, self.c
            ).start()
        whole = self.remote(wait_piece, wait_piece, send, recv, self.z * 4 + lax.rem(self.q + 1, 4), self.c)
        self.sends.append(whole)
        return whole.wait_recv

    def line_send(self, pieces, recv_piece, wait_piece):
        self.meet()
        send, recv = self.sem(), self.sem()
        for step in range(1, 4):
            other = lax.rem(self.z + step, 4)
            self.remote(
                pieces(other), recv_piece(step), send, recv, other * 4 + self.q, self.c
            ).start()
        whole = self.remote(wait_piece, wait_piece, send, recv, lax.rem(self.z + 1, 4) * 4 + self.q, self.c)
        self.sends.append(whole)
        return whole.wait_recv

    def drain(self):
        for copy in self.sends + list(self.flying.values()):
            copy.wait_send()
        for copy in self.stores.values():
            copy.wait()


class Layer:
    def __init__(self, packed, per, n):
        self.per = per
        self.n = n
        self.rows = 2 * per
        self.packed = packed
        self.value_rows = per // 2 if self.packed else per
        self.message = per + self.value_rows
        self.total = n * per
        self.block = 256
        self.gains = (0, 1) if packed else (2, 3)

    def attach(self, env, refs, sources, weights, results):
        self.b = refs
        self.held = weights
        self.results = results
        self.right_waits, self.left_waits, self.line_waits = {}, {}, {}
        self.loads = {}
        for number, (source, weight) in enumerate(zip(sources, weights, strict=True)):
            copy = pltpu.make_async_copy(source, weight, env.sem())
            copy.start()
            self.loads[number] = copy

    def weight(self, number):
        if number in self.loads:
            self.loads.pop(number).wait()
        return self.held[number]

    def buffers(self):
        r, t, n = self.rows, self.total, self.n
        vr, m = self.value_rows, self.message
        table = dict(
            normed=((r, 1024), BF),
            s1=((n, m, 128), BF),
            r1=((n, m, 128), BF),
            qa=((t, 128), BF),
            kb=((t, 128), BF),
            va=((t, 128), BF),
            mixp=((t, 128), F32),
            lse=((t, 128), F32),
            s2=((n, vr, 128), BF),
            r2=((n, vr, 128), BF),
            mixl=((r, 512), BF),
            mid=((r, 1024), F32),
            nm=((r, 1024), BF),
            gp=((r, 2048), BF),
            act=((r, 2048), BF),
            e=((r, 1024), F32),
            el=((r, 1024), BF),
            gb=((r, 2048), BF),
            gm=((r, 1024), F32),
            al=((r, 1024), BF),
            s6=((n, vr, 128), BF),
            r6=((n, vr, 128), BF),
            gx=((t, 128), BF),
            dk=((t, 128), F32),
            dv=((t, 128), F32),
            s7=((n, m, 128), BF),
            r7=((n, m, 128), BF),
            dp=((r, 1536), BF),
            acc=((r, 1024), F32),
            ps=((2, 4, r, 256), BF),
            pr=((2, 4, r, 256), BF),
            fg=((4, r, 6144), BF),
            ds=((4, r, 1024), BF),
            dg=((4, r, 1024), BF),
            sb=((4, 64, 6144), BF),
            rb=((3, 64, 6144), BF),
        )
        if not self.packed:
            table.update(
                x=((r, 1024), BF),
                same=((t, t), F32),
                lab=((t, 128), BF),
                hot=((2, self.per, 64), BF),
                labs=((r, 128), F32),
            )
        return table

    def gain(self, env, which):
        row = self.gains[which]
        return env.b.vecs[row : row + 1, :]

    def pack(self, tile):
        if not self.packed:
            return tile
        half = self.per // 2
        return jnp.where(low_lanes(half), tile[:half], swap_halves(tile[half:]))

    def send_pairs(self, store, tile_of):
        for seq in range(2):
            for j in range(4):
                tile = tile_of(seq, j)
                store(8 * seq + 2 * j, self.pack(tile))
                store(8 * seq + 2 * j + 1, self.pack(swap_halves(tile)))

    def join_pairs(self, tile_a, tile_b):
        vr = self.value_rows
        low = low_lanes(vr)
        first = jnp.where(low, tile_a, swap_halves(tile_b))
        if not self.packed:
            return [first]
        return [first, jnp.where(low, swap_halves(tile_a), tile_b)]

    def project(self, env):
        hidden = self.b.x[...].astype(F32)
        normed = (hidden * inverse_rms(hidden) * self.gain(env, 0)).astype(BF)
        self.b.normed[...] = normed
        weight = self.weight(QKV)
        queries, keys, values = (dot(normed, weight[part]) for part in range(3))
        send = self.b.s1
        per = self.per
        low = low_lanes(per)
        for seq in range(2):
            rows = slice(seq * per, (seq + 1) * per)
            for j in range(4):
                cols = slice(128 * j, 128 * j + 128)
                qt, kt, vt = queries[rows, cols], keys[rows, cols], values[rows, cols]
                pair = 8 * seq + 2 * j
                send[pair, 0:per] = jnp.where(low, qt, swap_halves(kt)).astype(BF)
                send[pair + 1, 0:per] = jnp.where(low, swap_halves(qt), kt).astype(BF)
                va, vb = vt, swap_halves(vt)
                if self.packed:
                    va, vb = self.pack(va), self.pack(vb)
                else:
                    labels = self.b.labs[rows, :]
                    va, vb = jnp.where(low, va, labels), jnp.where(low, vb, labels)
                send[pair, per:] = va.astype(BF)
                send[pair + 1, per:] = vb.astype(BF)
        self.wait1 = env.exchange(send, self.b.r1)

    def unpack(self, env):
        recv = self.b.r1
        qa, kb, va = self.b.qa, self.b.kb, self.b.va
        per, vr = self.per, self.value_rows
        low, low_v = low_lanes(per), low_lanes(vr)
        zero = jnp.zeros((per, 128), F32)
        zero_v = jnp.zeros((vr, 128), F32)
        for i in range(self.n):
            both = recv[i, 0:per].astype(F32)
            qa[i * per : (i + 1) * per] = jnp.where(low, both * 0.125, zero).astype(BF)
            kb[i * per : (i + 1) * per] = swap_halves(both).astype(BF)
            tile = recv[i, per:].astype(F32)
            va[i * per : i * per + vr] = jnp.where(low_v, tile, zero_v).astype(BF)
            if self.packed:
                va[i * per + vr : (i + 1) * per] = jnp.where(low_v, swap_halves(tile), zero_v).astype(BF)
            else:
                self.b.lab[i * per : (i + 1) * per] = jnp.where(low_v, zero_v, tile).astype(BF)
        if not self.packed:
            labels = self.b.lab[...]
            self.b.same[...] = dot_t(labels, labels)

    def allowed(self, env, start, stop):
        size = stop - start
        rows = lax.broadcasted_iota(jnp.int32, (size, stop), 0) + start
        keys = lax.broadcasted_iota(jnp.int32, (size, stop), 1)
        ok = keys <= rows
        if self.packed:
            segments = env.b.segments[pl.ds(lax.div(env.s, 8), 1), :]
            row = (lax.broadcasted_iota(jnp.int32, (size, 1), 0) + start).astype(F32)
            opening = jnp.zeros((size, 1), F32)
            for label in range(1, 4):
                edge = jnp.sum((segments < label).astype(F32), axis=1, keepdims=True)
                opening = jnp.where(row >= edge, jnp.maximum(opening, edge), opening)
            return ok & (keys >= opening.astype(jnp.int32))
        return ok & (self.b.same[start:stop, 0:stop] > 0.5)

    def attend(self, env):
        self.wait1()
        self.unpack(env)
        qa, kb, va = self.b.qa, self.b.kb, self.b.va
        mixp, lse = self.b.mixp, self.b.lse
        for start in range(0, self.total, self.block):
            stop = start + self.block
            scores = dot_t(qa[start:stop], kb[0:stop])
            scores = jnp.where(self.allowed(env, start, stop), scores, NEGATIVE)
            highest = jnp.max(scores, axis=1, keepdims=True)
            weights = jnp.exp(scores - highest)
            totals = jnp.sum(weights, axis=1, keepdims=True)
            mixp[start:stop] = dot(weights.astype(BF), va[0:stop]) / totals
            lse[start:stop] = jnp.broadcast_to(highest + jnp.log(totals), (self.block, 128))
        send = self.b.s2
        for i in range(self.n):
            send[i] = self.pack(mixp[i * self.per : (i + 1) * self.per]).astype(BF)
        self.wait2 = env.exchange(send, self.b.r2)

    def gather_heads(self, recv, row0, put):
        per, vr = self.per, self.value_rows
        for seq in range(2):
            for j in range(4):
                pair = 8 * seq + 2 * j
                tiles = self.join_pairs(
                    recv[pair, row0:].astype(F32), recv[pair + 1, row0:].astype(F32)
                )
                for number, tile in enumerate(tiles):
                    begin = seq * per + number * vr
                    put(slice(begin, begin + vr), slice(128 * j, 128 * j + 128), tile)

    def feed(self, env, finish):
        self.wait2()
        mixl = self.b.mixl

        def put(rows, cols, tile):
            mixl[rows, cols] = tile.astype(BF)

        self.gather_heads(self.b.r2, 0, put)
        out = self.weight(OUT)
        mid = self.b.mid
        hidden = self.b.x
        mixed = mixl[...]

        def sink(number, value):
            cols = slice(256 * number, 256 * number + 256)
            mid[:, cols] = value + hidden[:, cols].astype(F32)

        env.core_sum(
            self,
            0,
            lambda number: dot(mixed, out[:, 256 * number : 256 * number + 256]),
            sink,
        )
        middle = mid[...]
        normed = (middle * inverse_rms(middle) * self.gain(env, 1)).astype(BF)
        self.b.nm[...] = normed
        up = self.weight(UP)
        act, slope = self.b.act, self.b.gp
        for number in range(4):
            cols = slice(512 * number, 512 * number + 512)
            before = dot(normed, up[:, cols])
            square = before * before
            bent = jnp.tanh(0.7978845608028654 * before * (1.0 + 0.044715 * square))
            half = 0.5 * (1.0 + bent)
            act[:, cols] = (before * half).astype(BF)
            slope[:, cols] = (
                half
                + 0.5 * before * (1.0 - bent * bent) * (0.7978845608028654 + 0.1070322243 * square)
            ).astype(BF)
        down = self.weight(DOWN)
        env.core_sum(
            self,
            1,
            lambda number: dot(act[...], down[:, 256 * number : 256 * number + 256]),
            finish,
        )

    def back_feed(self, env):
        grad_low = self.b.e[...].astype(BF)
        self.b.el[...] = grad_low
        down, up, out = self.weight(DOWN), self.weight(UP), self.weight(OUT)
        gb, slope = self.b.gb, self.b.gp
        for number in range(4):
            cols = slice(512 * number, 512 * number + 512)
            grad = dot_t(grad_low, down[cols, :])
            gb[:, cols] = (grad * slope[:, cols].astype(F32)).astype(BF)
        acc = self.b.acc

        def sink(number, value):
            acc[:, 256 * number : 256 * number + 256] = value

        env.core_sum(
            self,
            0,
            lambda number: dot_t(gb[...], up[256 * number : 256 * number + 256, :]),
            sink,
        )
        grad_mid, grad_gain = norm_back(acc[...], self.b.mid[...], self.gain(env, 1))
        row = self.gains[1]
        env.b.vg[row : row + 1, :] = grad_gain
        self.b.gm[...] = grad_mid
        along = (self.b.e[...] + grad_mid).astype(BF)
        self.b.al[...] = along
        grad_mixed = dot_t(along, out[...])
        send = self.b.s6
        per = self.per

        def store(pair, tile):
            send[pair] = tile.astype(BF)

        self.send_pairs(
            store,
            lambda seq, j: grad_mixed[seq * per : (seq + 1) * per, 128 * j : 128 * j + 128],
        )
        self.wait6 = env.exchange(send, self.b.r6)

    def back_attend(self, env):
        self.wait6()
        recv, gx = self.b.r6, self.b.gx
        per, vr = self.per, self.value_rows
        low_v = low_lanes(vr)
        zero_v = jnp.zeros((vr, 128), F32)
        for i in range(self.n):
            tile = recv[i].astype(F32)
            gx[i * per : i * per + vr] = jnp.where(low_v, tile, zero_v).astype(BF)
            if self.packed:
                gx[i * per + vr : (i + 1) * per] = jnp.where(low_v, swap_halves(tile), zero_v).astype(BF)
        qa, kb, va = self.b.qa, self.b.kb, self.b.va
        mixp, lse = self.b.mixp, self.b.lse
        dk, dv = self.b.dk, self.b.dv
        dk[...] = jnp.zeros_like(dk)
        dv[...] = jnp.zeros_like(dv)
        dq = {}
        for start in range(0, self.total, self.block):
            stop = start + self.block
            query, grad = qa[start:stop], gx[start:stop]
            scores = dot_t(query, kb[0:stop])
            scores = jnp.where(self.allowed(env, start, stop), scores, NEGATIVE)
            probs = jnp.exp(scores - lse[start:stop, 0:1])
            offsets = jnp.sum(grad.astype(F32) * mixp[start:stop], axis=1, keepdims=True)
            slopes = (probs * (dot_t(grad, va[0:stop]) - offsets)).astype(BF)
            mixp[start:stop] = dot(slopes, kb[0:stop])
            dk[0:stop] += dot_l(slopes, query)
            dv[0:stop] += dot_l(probs.astype(BF), grad)
        send = self.b.s7
        low = low_lanes(per)
        for i in range(self.n):
            rows = slice(i * per, (i + 1) * per)
            send[i, 0:per] = jnp.where(low, mixp[rows] * 0.125, swap_halves(dk[rows])).astype(BF)
            send[i, per:] = self.pack(dv[rows]).astype(BF)
        self.wait7 = env.exchange(send, self.b.r7)

    def back_project(self, env, finish):
        self.wait7()
        recv, dp = self.b.r7, self.b.dp
        per = self.per
        low = low_lanes(per)
        for seq in range(2):
            rows = slice(seq * per, (seq + 1) * per)
            for j in range(4):
                pair = 8 * seq + 2 * j
                one, two = recv[pair, 0:per].astype(F32), recv[pair + 1, 0:per].astype(F32)
                dp[rows, 128 * j : 128 * j + 128] = jnp.where(low, one, swap_halves(two)).astype(BF)
                dp[rows, 512 + 128 * j : 640 + 128 * j] = jnp.where(low, swap_halves(one), two).astype(BF)

        def put(rows, cols, tile):
            dp[rows, 1024 + cols.start : 1024 + cols.stop] = tile.astype(BF)

        self.gather_heads(recv, per, put)
        weight = self.weight(QKV)
        acc = self.b.acc

        def chunk(number):
            rows = slice(256 * number, 256 * number + 256)
            total = dot_t(dp[:, 0:512], weight[0, rows, :])
            total += dot_t(dp[:, 512:1024], weight[1, rows, :])
            return total + dot_t(dp[:, 1024:1536], weight[2, rows, :])

        def sink(number, value):
            acc[:, 256 * number : 256 * number + 256] = value

        env.core_sum(self, 1, chunk, sink)
        grad_hidden, grad_gain = norm_back(
            acc[...], self.b.x[...].astype(F32), self.gain(env, 0)
        )
        row = self.gains[0]
        env.b.vg[row : row + 1, :] = grad_gain
        finish(self.b.gm[...] + grad_hidden)

    def parts(self, env, which):
        b = self.b
        left = (b.normed, b.al, b.nm, b.el)[which]
        right = (b.dp, b.mixl, b.gb, b.act)[which]
        return left, right

    def share(self, env, which):
        self.share_right(env, which)
        self.share_left(env, which)

    def share_right(self, env, which):
        begin, size = COLS[which]
        _, right = self.parts(env, which)
        fg = self.b.fg
        cols = pl.ds(begin, size)
        fg[pl.ds(env.q, 1), :, begin : begin + size] = right[...][None]
        mine = fg.at[env.q, :, cols]
        self.right_waits[which] = env.plane_send(
            lambda other: mine, mine, fg.at[pl.ds(0, 3), :, cols]
        )

    def share_left(self, env, which):
        left, _ = self.parts(env, which)
        ds, dg = self.b.ds, self.b.dg
        low = low_lanes(self.rows)
        begin = 256 * which
        for a in range(2):
            tiles = [
                left[:, 128 * (2 * z + a) : 128 * (2 * z + a) + 128].astype(F32) for z in range(4)
            ]
            for two in range(2):
                even, odd = tiles[2 * two], tiles[2 * two + 1]
                at = begin + 128 * two
                ds[2 * a, :, at : at + 128] = jnp.where(low, even, swap_halves(odd)).astype(BF)
                ds[2 * a + 1, :, at : at + 128] = jnp.where(low, swap_halves(even), odd).astype(BF)
        cols = pl.ds(begin, 256)
        dg[pl.ds(env.q, 1), :, begin : begin + 256] = ds[pl.ds(env.q, 1), :, begin : begin + 256]
        self.left_waits[which] = env.plane_send(
            lambda other: ds.at[other, :, cols],
            dg.at[env.q, :, cols],
            dg.at[pl.ds(0, 3), :, cols],
        )

    def multiply(self, env, which):
        self.right_waits[which]()
        self.left_waits[which]()
        begin, size = COLS[which]
        fg, dg, sb, rb = self.b.fg, self.b.dg, self.b.sb, self.b.rb
        rows = 4 * self.rows
        left = dg[:, :, 256 * which : 256 * which + 256].reshape(rows, 256)
        for at in range(begin, begin + size, 512):
            right = fg[:, :, at : at + 512].reshape(rows, 512)
            product = dot_l(left, right)
            for z in range(4):
                sb[z, :, at : at + 512] = product[64 * z : 64 * z + 64].astype(BF)
        cols = pl.ds(begin, size)
        self.line_waits[which] = env.line_send(
            lambda other: sb.at[other, :, cols],
            lambda step: rb.at[step - 1, :, cols],
            rb.at[:, :, cols],
        )

    def collect(self, env, which):
        self.line_waits[which]()
        begin, size = COLS[which]
        sb, rb = self.b.sb, self.b.rb
        result = self.results[which]
        for at in range(0, size, 512):
            cols = slice(begin + at, begin + at + 512)
            slot = env.stored % 4
            env.stored += 1
            if slot in env.stores:
                env.stores.pop(slot).wait()
            total = sb[pl.ds(env.z, 1), :, cols].astype(F32)
            for step in range(1, 4):
                total = total + rb[step - 1 : step, :, cols].astype(F32)
            stage = env.b.stage
            stage[slot] = total[0]
            target = result.at[at // 512] if which == 0 else result.at[:, pl.ds(at, 512)]
            copy = pltpu.make_async_copy(stage.at[slot], target, env.sem())
            copy.start()
            env.stores[slot] = copy


def pick_rows(env, dense, routed):
    hot, labs, first = routed.b.hot, routed.b.labs, env.b.output
    group, slots = dense.per, routed.per
    base = env.s * group
    for seq in range(2):
        listed = env.b.routed[seq : seq + 1, :]
        places = listed.shape[1]
        place = lax.broadcasted_iota(jnp.int32, (group, places), 0) + base
        here = (place == listed).astype(F32).astype(BF)
        before = jnp.sum((listed < base).astype(F32), axis=1, keepdims=True).astype(jnp.int32)
        number = lax.broadcasted_iota(jnp.int32, (slots, places), 1) - before
        slot = lax.broadcasted_iota(jnp.int32, (slots, places), 0)
        mine = (number == slot).astype(F32).astype(BF)
        table = dot_t(mine, here).astype(BF)
        hot[seq] = table
        segments = env.b.segments[seq : seq + 1, :]
        row = (lax.broadcasted_iota(jnp.int32, (group, 1), 0) + base).astype(F32)
        label = jnp.zeros((group, 1), F32)
        for number in range(1, 4):
            edge = jnp.sum((segments < number).astype(F32), axis=1, keepdims=True)
            label = label + (row >= edge).astype(F32)
        lane = lax.broadcasted_iota(jnp.int32, (group, 128), 1)
        one_hot = (lane == label.astype(jnp.int32) + 64).astype(F32).astype(BF)
        labs[seq * slots : (seq + 1) * slots, :] = dot(table, one_hot)
        rows = first[seq * group : (seq + 1) * group, :].astype(BF)
        routed.b.x[seq * slots : (seq + 1) * slots, :] = dot(table, rows).astype(BF)


def restore(env, dense, routed, sent, seq):
    slots = routed.per
    return dot_l(routed.b.hot[seq], sent[seq * slots : (seq + 1) * slots])


def gate_rows(env, dense, routed):
    group, slots = dense.per, routed.per
    sent = routed.b.acc[...].astype(BF)
    router = env.b.vecs[4:5, :]
    grad_router = jnp.zeros((1, 1024), F32)
    for seq in range(2):
        rows = slice(seq * group, (seq + 1) * group)
        first = env.b.output[rows, :]
        returned = restore(env, dense, routed, sent, seq)
        gate = jax.nn.sigmoid(jnp.sum(first * router, axis=1, keepdims=True))
        env.b.output[rows, :] = first + gate * returned
        grad = env.b.cotangent[rows, :].astype(F32)
        low = (gate * grad).astype(BF)
        routed.b.e[seq * slots : (seq + 1) * slots, :] = dot(routed.b.hot[seq], low)
        logit = jnp.sum(grad * returned, axis=1, keepdims=True) * gate * (1.0 - gate)
        grad_router = grad_router + jnp.sum(logit * first, axis=0, keepdims=True)
        dense.b.e[rows, :] = grad + logit * router
    env.b.vg[4:5, :] = grad_router


def share_vectors(env):
    vg, sv, rv = env.b.vg, env.b.sv, env.b.rv
    for number in range(env.n):
        tile = vg[:, 128 * (number // 2) : 128 * (number // 2) + 128]
        sv[number] = swap_halves(tile) if number % 2 else tile
    return env.exchange(sv, rv)


def sum_vectors(env, wait):
    wait()
    total = env.b.rv[0]
    for number in range(1, env.n):
        total = total + env.b.rv[number]
    env.b.gvec[...] = total


QKV, OUT, UP, DOWN = range(4)
SHAPES = ((3, 1024, 512), (512, 1024), (1024, 2048), (2048, 1024))
GRADS = ((3, 64, 512), (64, 512), (64, 2048), (64, 2048))


def whole_step(env, dense, routed):
    env.greet()
    env.b.vg[...] = jnp.zeros_like(env.b.vg)
    dense.project(env)
    dense.attend(env)
    mid_d, first = dense.b.mid, env.b.output

    def finish_dense(number, value):
        cols = slice(256 * number, 256 * number + 256)
        first[:, cols] = mid_d[:, cols] + value

    dense.feed(env, finish_dense)
    pick_rows(env, dense, routed)
    routed.project(env)
    routed.attend(env)
    mid_r, x_r, sent = routed.b.mid, routed.b.x, routed.b.acc

    def finish_routed(number, value):
        cols = slice(256 * number, 256 * number + 256)
        sent[:, cols] = mid_r[:, cols] - x_r[:, cols].astype(F32) + value

    routed.feed(env, finish_routed)
    gate_rows(env, dense, routed)
    routed.back_feed(env)
    for which in (3, 2, 1):
        routed.share(env, which)
    routed.back_attend(env)
    for which in (3, 2, 1):
        routed.multiply(env, which)

    def finish_back(branch):
        low = branch.astype(BF)
        for seq in range(2):
            rows = slice(seq * dense.per, (seq + 1) * dense.per)
            dense.b.e[rows, :] += restore(env, dense, routed, low, seq)

    routed.back_project(env, finish_back)
    routed.share(env, 0)
    dense.back_feed(env)
    for which in (3, 2, 1):
        dense.share(env, which)
    routed.multiply(env, 0)
    dense.back_attend(env)
    for which in (3, 2, 1):
        dense.multiply(env, which)

    def finish_tokens(branch):
        env.b.grad_tokens[...] = dense.b.e[...] + branch

    dense.back_project(env, finish_tokens)
    dense.share(env, 0)
    wait = share_vectors(env)
    for which in (3, 2, 1, 0):
        routed.collect(env, which)
    dense.multiply(env, 0)
    for which in (3, 2, 1, 0):
        dense.collect(env, which)
    sum_vectors(env, wait)
    env.drain()


def fused(group, tokens, cotangent, segments, routed_places, vecs, weights):
    n = lax.axis_size("seq")
    rows = 2 * group
    dense, routed = Layer(True, group, n), Layer(False, group // 4, n)
    wide = ((rows, 1024), F32)
    common = dict(
        stage=((4, 64, 512), F32),
        vg=((8, 1024), F32),
        sv=((n, 8, 128), F32),
        rv=((n, 8, 128), F32),
    )
    groups = (dense.buffers(), routed.buffers(), common)
    scratch = [spec for table in groups for spec in table.values()]

    def kernel(*refs):
        refs = list(refs)

        def take(count):
            taken = refs[:count]
            del refs[:count]
            return taken

        x, cotangent_ref, segments_ref, routed_ref, vecs_ref = take(5)
        sources = take(8)
        output, grad_tokens, gvec = take(3)
        results = take(8)
        held = take(8)
        dense_refs, routed_refs, common_refs = (
            types.SimpleNamespace(**dict(zip(table, take(len(table)), strict=True))) for table in groups
        )
        dense_refs.x = x
        common_refs.cotangent = cotangent_ref
        common_refs.segments = segments_ref
        common_refs.routed = routed_ref
        common_refs.vecs = vecs_ref
        common_refs.output = output
        common_refs.grad_tokens = grad_tokens
        common_refs.gvec = gvec
        env = Env(common_refs, refs[0], n)
        dense.attach(env, dense_refs, sources[:4], held[:4], results[:4])
        routed.attach(env, routed_refs, sources[4:], held[4:], results[4:])
        whole_step(env, dense, routed)

    vmem = pl.BlockSpec(memory_space=pltpu.VMEM)
    hbm = pl.BlockSpec(memory_space=pl.ANY)
    outs = [wide, wide, ((8, 128), F32)] + [(shape, F32) for shape in GRADS * 2]
    results = pl.pallas_call(
        kernel,
        out_shape=[jax.ShapeDtypeStruct(*spec) for spec in outs],
        in_specs=[vmem] * 5 + [hbm] * 8,
        out_specs=[vmem] * 3 + [hbm] * 8,
        scratch_shapes=[pltpu.VMEM(shape, BF) for shape in SHAPES * 2]
        + [pltpu.VMEM(*spec) for spec in scratch]
        + [pltpu.SemaphoreType.DMA((192,))],
        compiler_params=pltpu.CompilerParams(
            collective_id=0, has_side_effects=True, vmem_limit_bytes=LIMIT
        ),
    )(tokens, cotangent, segments, routed_places, vecs, *weights)
    return results[0], results[1], results[2], results[3:7], results[7:]


def on_device_fused(
    tokens,
    segments,
    routed,
    router,
    dense_attn_gain,
    dense_qkv,
    dense_out,
    dense_mlp_gain,
    dense_up,
    dense_down,
    routed_attn_gain,
    routed_qkv,
    routed_out,
    routed_mlp_gain,
    routed_up,
    routed_down,
    cotangent,
):
    group, seqs, width = tokens.shape
    zeros = jnp.zeros_like(router)
    vecs = jnp.stack(
        (dense_attn_gain, dense_mlp_gain, routed_attn_gain, routed_mlp_gain, router, zeros, zeros, zeros)
    ).astype(F32)

    def rows_of(array):
        return jnp.transpose(array, (1, 0, 2)).reshape(seqs * group, width)

    output, grad_tokens, gvec, dense_grads, routed_grads = fused(
        group,
        rows_of(tokens),
        rows_of(cotangent),
        segments,
        routed,
        vecs,
        (
            jnp.transpose(dense_qkv, (1, 0, 2)),
            dense_out,
            dense_up,
            dense_down,
            jnp.transpose(routed_qkv, (1, 0, 2)),
            routed_out,
            routed_up,
            routed_down,
        ),
    )

    def back(array):
        return jnp.transpose(array.reshape(seqs, group, width), (1, 0, 2))

    def vector(row):
        return gvec[row, 0:64]

    def weights_of(grads, first, second):
        return (
            vector(first),
            jnp.transpose(grads[QKV], (1, 0, 2)),
            jnp.transpose(grads[OUT]),
            vector(second),
            grads[UP],
            jnp.transpose(grads[DOWN]),
        )

    return (
        (back(output), back(grad_tokens))
        + weights_of(dense_grads, 0, 1)
        + weights_of(routed_grads, 2, 3)
        + (vector(4),)
    )


def solution(mesh):
    in_specs = (
        P("seq", None, None),
        P(),
        P(),
        P(),
        P(),
        P(None, None, "mp"),
        P("mp", None),
        P(),
        P(None, "mp"),
        P("mp", None),
        P(),
        P(None, None, "mp"),
        P("mp", None),
        P(),
        P(None, "mp"),
        P("mp", None),
        P("seq", None, None),
    )
    out_specs = (
        P("seq", None, None),
        P("seq", None, None),
        P("seq"),
        P("seq", None, "mp"),
        P("mp", "seq"),
        P("seq"),
        P("seq", "mp"),
        P("mp", "seq"),
        P("seq"),
        P("seq", None, "mp"),
        P("mp", "seq"),
        P("seq"),
        P("seq", "mp"),
        P("mp", "seq"),
        P("seq"),
    )
    seq_size = mesh.shape["seq"]
    pairs = 2 * (16 // mesh.shape["mp"])
    body = on_device_fused if seq_size == pairs else on_device

    return jax.shard_map(
        body, mesh=mesh, in_specs=in_specs, out_specs=out_specs, check_vma=False
    )
```

```python
import math
import types

import jax
import jax.numpy as jnp
from jax import lax
from jax.experimental import pallas as pl
from jax.experimental.pallas import tpu as pltpu
from jax.sharding import PartitionSpec as P

HEAD_DIM = 64


EPSILON = 1e-06
NEGATIVE = -1e30
PRECISE = lax.Precision.HIGHEST


def rms_norm(hidden, gain):
    return hidden * lax.rsqrt(jnp.mean(hidden * hidden, axis=-1, keepdims=True) + EPSILON) * gain


def gelu_tanh(operand):
    return jax.nn.gelu(operand, approximate=True)


def model_sum(operand):
    return lax.psum(operand, "mp")


def block_loop(row_total, advance, carried):
    block_size = math.gcd(row_total, 512)
    return lax.fori_loop(
        0,
        row_total // block_size,
        lambda number, current: advance(current, number * block_size, block_size),
        carried,
    )


def key_mask(query_places, query_live, key_places, key_live, label_rows):
    query_labels = jnp.take_along_axis(label_rows, query_places, axis=0)
    key_labels = jnp.take_along_axis(label_rows, key_places, axis=0)
    allowed = jnp.transpose(key_places)[:, None, :] <= jnp.transpose(query_places)[:, :, None]
    allowed = allowed & (
        jnp.transpose(key_labels)[:, None, :] == jnp.transpose(query_labels)[:, :, None]
    )
    allowed = allowed & jnp.transpose(key_live)[:, None, :] & jnp.transpose(query_live)[:, :, None]
    return allowed[:, None]


def attend_forward(queries, key_rows, value_rows, own_places, own_live, row_info, label_rows):
    row_count, seq_count, head_count, head_size = queries.shape
    score_scale = head_size ** (-0.5)
    shape_rows = (seq_count, head_count, row_count)
    initial = (
        jnp.full(shape_rows, NEGATIVE, jnp.float32),
        jnp.zeros(shape_rows, jnp.float32),
        jnp.zeros(shape_rows + (head_size,), jnp.float32),
    )
    key_piece = lax.all_gather(key_rows, "seq", axis=0, tiled=True)
    value_piece = lax.all_gather(value_rows, "seq", axis=0, tiled=True)

    def advance(current, offset, block_size):
        highest, totals, summed = current
        key_block = lax.dynamic_slice_in_dim(key_piece, offset, block_size, 0).reshape(
            block_size, seq_count, head_count, head_size
        )
        value_block = lax.dynamic_slice_in_dim(value_piece, offset, block_size, 0).reshape(
            block_size, seq_count, head_count, head_size
        )
        key_places, key_live = row_info(offset, block_size)
        allowed = key_mask(own_places, own_live, key_places, key_live, label_rows)
        scores = (
            jnp.einsum("qshe,kshe->shqk", queries, key_block, preferred_element_type=jnp.float32)
            * score_scale
        )
        scores = jnp.where(allowed, scores, NEGATIVE)
        newest = jnp.maximum(highest, jnp.max(scores, axis=-1))
        weights = jnp.exp(scores - newest[..., None])
        factor = jnp.exp(highest - newest)
        totals = totals * factor + jnp.sum(weights, axis=-1)
        summed = summed * factor[..., None] + jnp.einsum(
            "shqk,kshe->shqe",
            weights.astype(jnp.bfloat16),
            value_block,
            preferred_element_type=jnp.float32,
        )
        return (newest, totals, summed)

    highest, totals, summed = block_loop(key_piece.shape[0], advance, initial)
    mixed_rows = jnp.transpose(summed / totals[..., None], (2, 0, 1, 3)).reshape(
        row_count, seq_count, head_count * head_size
    )
    return (mixed_rows, highest + jnp.log(totals), None)


def attend_backward(
    queries,
    key_rows,
    value_rows,
    grad_mixed,
    mixed_rows,
    log_sum,
    own_places,
    own_live,
    row_info,
    label_rows,
):
    row_count, seq_count, head_count, head_size = queries.shape
    score_scale = head_size ** (-0.5)
    grad_heads = grad_mixed.reshape(row_count, seq_count, head_count, head_size)
    offsets = jnp.sum(
        grad_heads.astype(jnp.float32)
        * mixed_rows.reshape(row_count, seq_count, head_count, head_size),
        axis=-1,
    )
    offsets_rows = jnp.transpose(offsets, (1, 2, 0))
    key_piece = lax.all_gather(key_rows, "seq", axis=0, tiled=True)
    value_piece = lax.all_gather(value_rows, "seq", axis=0, tiled=True)

    def advance(current, offset, block_size):
        key_block = lax.dynamic_slice_in_dim(key_piece, offset, block_size, 0).reshape(
            block_size, seq_count, head_count, head_size
        )
        value_block = lax.dynamic_slice_in_dim(value_piece, offset, block_size, 0).reshape(
            block_size, seq_count, head_count, head_size
        )
        key_places, key_live = row_info(offset, block_size)
        allowed = key_mask(own_places, own_live, key_places, key_live, label_rows)
        scores = (
            jnp.einsum("qshe,kshe->shqk", queries, key_block, preferred_element_type=jnp.float32)
            * score_scale
        )
        scores = jnp.where(allowed, scores, NEGATIVE)
        chances = jnp.exp(scores - log_sum[..., None])
        pushes = jnp.einsum(
            "qshe,kshe->shqk", grad_heads, value_block, preferred_element_type=jnp.float32
        )
        slopes = (chances * (pushes - offsets_rows[..., None])).astype(jnp.bfloat16)
        return current + jnp.einsum(
            "shqk,kshe->qshe", slopes, key_block, preferred_element_type=jnp.float32
        )

    grad_queries = block_loop(key_piece.shape[0], advance, jnp.zeros(queries.shape, jnp.float32))
    log_all, offsets_all = (
        lax.all_gather(jnp.transpose(log_sum, (2, 0, 1)), "seq", axis=0, tiled=True),
        lax.all_gather(offsets, "seq", axis=0, tiled=True),
    )
    own_keys = key_rows.reshape(row_count, seq_count, head_count, head_size)
    own_values = value_rows.reshape(row_count, seq_count, head_count, head_size)
    zero_rows = jnp.zeros(queries.shape, jnp.float32)
    query_flat = queries.reshape(row_count, seq_count, head_count * head_size)
    query_piece = lax.all_gather(query_flat, "seq", axis=0, tiled=True)
    grad_piece = lax.all_gather(grad_mixed, "seq", axis=0, tiled=True)

    def advance(current, offset, block_size):
        key_sum, value_sum = current
        query_block = lax.dynamic_slice_in_dim(query_piece, offset, block_size, 0).reshape(
            block_size, seq_count, head_count, head_size
        )
        grad_block = lax.dynamic_slice_in_dim(grad_piece, offset, block_size, 0).reshape(
            block_size, seq_count, head_count, head_size
        )
        block_log = jnp.transpose(
            lax.dynamic_slice_in_dim(log_all, offset, block_size, 0), (1, 2, 0)
        )
        block_offsets = jnp.transpose(
            lax.dynamic_slice_in_dim(offsets_all, offset, block_size, 0), (1, 2, 0)
        )
        query_places, query_live = row_info(offset, block_size)
        allowed = key_mask(query_places, query_live, own_places, own_live, label_rows)
        scores = (
            jnp.einsum("qshe,kshe->shqk", query_block, own_keys, preferred_element_type=jnp.float32)
            * score_scale
        )
        scores = jnp.where(allowed, scores, NEGATIVE)
        chances = jnp.exp(scores - block_log[..., None])
        pushes = jnp.einsum(
            "qshe,kshe->shqk", grad_block, own_values, preferred_element_type=jnp.float32
        )
        slopes = (chances * (pushes - block_offsets[..., None])).astype(jnp.bfloat16)
        key_sum = key_sum + jnp.einsum(
            "shqk,qshe->kshe", slopes, query_block, preferred_element_type=jnp.float32
        )
        value_sum = value_sum + jnp.einsum(
            "shqk,qshe->kshe",
            chances.astype(jnp.bfloat16),
            grad_block,
            preferred_element_type=jnp.float32,
        )
        return (key_sum, value_sum)

    key_sum, value_sum = block_loop(query_piece.shape[0], advance, (zero_rows, zero_rows))
    flat_shape = (row_count, seq_count, head_count * head_size)
    return (
        (grad_queries * score_scale).reshape(flat_shape),
        (key_sum * score_scale).reshape(flat_shape),
        value_sum.reshape(flat_shape),
    )


def block_forward(hidden, params, row_info, label_rows):
    attn_gain, qkv_weight, out_weight, mlp_gain, up_weight, down_weight = params
    row_count, seq_count, _ = hidden.shape
    head_width = qkv_weight.shape[2]
    head_count = head_width // HEAD_DIM
    own_places, own_live = row_info(lax.axis_index("seq") * row_count, row_count)
    normed = rms_norm(hidden, attn_gain.astype(jnp.float32)).astype(jnp.bfloat16)
    projected = jnp.einsum(
        "rsd,dce->rsce", normed, qkv_weight, preferred_element_type=jnp.float32
    ).astype(jnp.bfloat16)
    queries = projected[:, :, 0].reshape(row_count, seq_count, head_count, HEAD_DIM)
    key_rows = projected[:, :, 1]
    value_rows = projected[:, :, 2]
    mixed_rows, log_sum, kept_rows = attend_forward(
        queries, key_rows, value_rows, own_places, own_live, row_info, label_rows
    )
    mixed_low = mixed_rows.astype(jnp.bfloat16)
    attention = model_sum(
        jnp.einsum("rsh,hd->rsd", mixed_low, out_weight, preferred_element_type=jnp.float32)
    )
    middle = hidden + attention
    normed_mlp = rms_norm(middle, mlp_gain.astype(jnp.float32)).astype(jnp.bfloat16)
    before = jnp.einsum("rsd,df->rsf", normed_mlp, up_weight, preferred_element_type=jnp.float32)
    active = gelu_tanh(before).astype(jnp.bfloat16)
    feed_out = model_sum(
        jnp.einsum("rsf,fd->rsd", active, down_weight, preferred_element_type=jnp.float32)
    )
    stored = (
        hidden,
        normed,
        queries,
        key_rows,
        value_rows,
        mixed_rows,
        log_sum,
        mixed_low,
        middle,
        normed_mlp,
        before,
        active,
        own_places,
        own_live,
        kept_rows,
    )
    return (attention, middle, feed_out, stored)


def block_backward(incoming, stored, params, row_info, label_rows):
    attn_gain, qkv_weight, out_weight, mlp_gain, up_weight, down_weight = params
    (
        hidden,
        normed,
        queries,
        key_rows,
        value_rows,
        mixed_rows,
        log_sum,
        mixed_low,
        middle,
        normed_mlp,
        before,
        active,
        own_places,
        own_live,
        kept_rows,
    ) = stored
    incoming_low = incoming.astype(jnp.bfloat16)
    grad_down = jnp.einsum("rsf,rsd->fd", active, incoming_low, preferred_element_type=jnp.float32)
    grad_active = jnp.einsum(
        "rsd,fd->rsf", incoming_low, down_weight, preferred_element_type=jnp.float32
    )
    _, gelu_pull = jax.vjp(gelu_tanh, before)
    grad_before = gelu_pull(grad_active)[0].astype(jnp.bfloat16)
    grad_up = jnp.einsum("rsd,rsf->df", normed_mlp, grad_before, preferred_element_type=jnp.float32)
    grad_normed_mlp = model_sum(
        jnp.einsum("rsf,df->rsd", grad_before, up_weight, preferred_element_type=jnp.float32)
    )
    _, mlp_pull = jax.vjp(rms_norm, middle, mlp_gain.astype(jnp.float32))
    grad_middle, grad_mlp_gain = mlp_pull(grad_normed_mlp)
    along_low = (incoming + grad_middle).astype(jnp.bfloat16)
    grad_out = jnp.einsum("rsh,rsd->hd", mixed_low, along_low, preferred_element_type=jnp.float32)
    grad_mixed = jnp.einsum(
        "rsd,hd->rsh", along_low, out_weight, preferred_element_type=jnp.float32
    ).astype(jnp.bfloat16)
    grad_queries, grad_keys, grad_values = attend_backward(
        queries,
        key_rows,
        value_rows,
        grad_mixed,
        mixed_rows,
        log_sum,
        own_places,
        own_live,
        row_info,
        label_rows,
    )
    grad_projected = jnp.stack((grad_queries, grad_keys, grad_values), axis=2).astype(jnp.bfloat16)
    grad_qkv = jnp.einsum(
        "rsd,rsce->dce", normed, grad_projected, preferred_element_type=jnp.float32
    )
    grad_normed = model_sum(
        jnp.einsum("rsce,dce->rsd", grad_projected, qkv_weight, preferred_element_type=jnp.float32)
    )
    _, attn_pull = jax.vjp(rms_norm, hidden, attn_gain.astype(jnp.float32))
    grad_hidden, grad_attn_gain = attn_pull(grad_normed)
    return (
        grad_middle + grad_hidden,
        (grad_attn_gain, grad_qkv, grad_out, grad_mlp_gain, grad_up, grad_down),
    )


def on_device(
    tokens,
    segments,
    routed,
    router,
    dense_attn_gain,
    dense_qkv,
    dense_out,
    dense_mlp_gain,
    dense_up,
    dense_down,
    routed_attn_gain,
    routed_qkv,
    routed_out,
    routed_mlp_gain,
    routed_up,
    routed_down,
    cotangent,
):
    group_rows, seq_count, _ = tokens.shape
    devices = lax.axis_size("seq")
    my_index = lax.axis_index("seq")
    capacity = routed.shape[1]
    most_rows = group_rows // 4
    label_rows = jnp.transpose(segments)
    route_rows = jnp.transpose(routed)
    local_ids = jnp.arange(group_rows, dtype=jnp.int32)
    bounds = jnp.arange(devices + 1, dtype=jnp.int32) * group_rows
    starts = jnp.sum((routed[None, :, :] < bounds[:, None, None]).astype(jnp.int32), axis=2)
    first_rank = starts[my_index]
    routed_here = starts[my_index + 1] - first_rank
    dense_params = (dense_attn_gain, dense_qkv, dense_out, dense_mlp_gain, dense_up, dense_down)
    routed_params = (
        routed_attn_gain,
        routed_qkv,
        routed_out,
        routed_mlp_gain,
        routed_up,
        routed_down,
    )

    def dense_info(first_row, row_total):
        places = first_row + jnp.broadcast_to(
            jnp.arange(row_total, dtype=jnp.int32)[:, None], (row_total, seq_count)
        )
        return (places, jnp.ones((row_total, seq_count), jnp.bool_))

    slot_rows = jnp.arange(most_rows, dtype=jnp.int32)
    is_live = slot_rows[:, None] < routed_here[None, :]
    hold_places = (
        jnp.take_along_axis(
            route_rows, jnp.clip(first_rank[None, :] + slot_rows[:, None], 0, capacity - 1), axis=0
        )
        - my_index * group_rows
    )
    hold_table = (
        (jnp.transpose(hold_places)[:, :, None] == local_ids[None, None, :])
        & jnp.transpose(is_live)[:, :, None]
    ).astype(jnp.bfloat16)

    def select_rows(rows_in):
        return jnp.einsum(
            "smc,csd->msd", hold_table, rows_in, preferred_element_type=jnp.float32
        ).astype(jnp.bfloat16)

    def restore_rows(rows_in):
        return jnp.einsum("smc,msd->csd", hold_table, rows_in, preferred_element_type=jnp.float32)

    def routed_info(first_row, row_total):
        number = first_row + jnp.arange(row_total, dtype=jnp.int32)
        source = number // most_rows
        within = number % most_rows
        base = jnp.take(starts, source, axis=0)
        filled = jnp.take(starts, source + 1, axis=0) - base
        rank_rows = jnp.clip(base + within[:, None], 0, capacity - 1)
        return (jnp.take_along_axis(route_rows, rank_rows, axis=0), within[:, None] < filled)

    hidden = tokens.astype(jnp.float32)
    _, middle, feed_out, dense_stored = block_forward(hidden, dense_params, dense_info, label_rows)
    first_out = middle + feed_out
    lifted = select_rows(first_out.astype(jnp.bfloat16))
    routed_attention, _, routed_feed, routed_stored = block_forward(
        lifted.astype(jnp.float32), routed_params, routed_info, label_rows
    )
    sent_rows = (routed_attention + routed_feed).astype(jnp.bfloat16)
    returned = restore_rows(sent_rows)
    router_float = router.astype(jnp.float32)
    gate_value = jax.nn.sigmoid(jnp.einsum("csd,d->cs", first_out, router_float, precision=PRECISE))
    output = first_out + gate_value[:, :, None] * returned
    grad_output = cotangent.astype(jnp.float32)
    grad_sent = select_rows((gate_value[:, :, None] * grad_output).astype(jnp.bfloat16))
    grad_logit = jnp.sum(grad_output * returned, axis=-1) * gate_value * (1.0 - gate_value)
    grad_router = jnp.einsum("cs,csd->d", grad_logit, first_out, precision=PRECISE)
    grad_first = grad_output + grad_logit[:, :, None] * router_float
    routed_branch, routed_grads = block_backward(
        grad_sent.astype(jnp.float32), routed_stored, routed_params, routed_info, label_rows
    )
    grad_first = grad_first + restore_rows(routed_branch.astype(jnp.bfloat16))
    dense_branch, dense_grads = block_backward(
        grad_first, dense_stored, dense_params, dense_info, label_rows
    )
    grad_tokens = grad_first + dense_branch
    summed_all = (
        lax.psum_scatter(dense_grads[0], "seq", scatter_dimension=0, tiled=True),
        lax.psum_scatter(dense_grads[1], "seq", scatter_dimension=0, tiled=True),
        lax.psum_scatter(dense_grads[2], "seq", scatter_dimension=1, tiled=True),
        lax.psum_scatter(dense_grads[3], "seq", scatter_dimension=0, tiled=True),
        lax.psum_scatter(dense_grads[4], "seq", scatter_dimension=0, tiled=True),
        lax.psum_scatter(dense_grads[5], "seq", scatter_dimension=1, tiled=True),
        lax.psum_scatter(routed_grads[0], "seq", scatter_dimension=0, tiled=True),
        lax.psum_scatter(routed_grads[1], "seq", scatter_dimension=0, tiled=True),
        lax.psum_scatter(routed_grads[2], "seq", scatter_dimension=1, tiled=True),
        lax.psum_scatter(routed_grads[3], "seq", scatter_dimension=0, tiled=True),
        lax.psum_scatter(routed_grads[4], "seq", scatter_dimension=0, tiled=True),
        lax.psum_scatter(routed_grads[5], "seq", scatter_dimension=1, tiled=True),
        lax.psum_scatter(grad_router, "seq", scatter_dimension=0, tiled=True),
    )
    dense_sums = tuple(summed_all[0:6])
    routed_sums = tuple(summed_all[6:13])
    return (output, grad_tokens) + tuple(dense_sums) + tuple(routed_sums)


BF = jnp.bfloat16
LIMIT = 63 * 1024 * 1024
F32 = jnp.float32
MESH = pl.DeviceIdType.MESH
WIDTHS = (384, 128, 512, 512)
BEGINS = (0, 384, 512, 1024)
SIZES = (1536, 512, 2048, 2048)
COLS = (None, (0, 512), (512, 2048), (2560, 2048))


def dot(a, b):
    return lax.dot_general(a, b, (((1,), (0,)), ((), ())), preferred_element_type=F32)


def dot_t(a, b):
    return lax.dot_general(a, b, (((1,), (1,)), ((), ())), preferred_element_type=F32)


def dot_l(a, b):
    return lax.dot_general(a, b, (((0,), (0,)), ((), ())), preferred_element_type=F32)


def swap_halves(tile):
    return pltpu.roll(tile, 64, 1)


def low_lanes(rows):
    return lax.broadcasted_iota(jnp.int32, (rows, 128), 1) < 64


def inverse_rms(rows):
    return lax.rsqrt(jnp.mean(rows * rows, axis=1, keepdims=True) + EPSILON)


def norm_back(grad, rows, gain):
    inverse = inverse_rms(rows)
    unit = rows * inverse
    pulled = grad * gain
    grad_rows = inverse * (pulled - unit * jnp.mean(pulled * unit, axis=1, keepdims=True))
    return grad_rows, jnp.sum(grad * unit, axis=0, keepdims=True)


class Env:
    def __init__(self, refs, sems, seq_size):
        self.b = refs
        self.sems = sems
        self.count = 0
        self.sends = []
        self.flying = {}
        self.stores = {}
        self.stored = 0
        self.barrier_done = False
        self.n = seq_size
        self.s = lax.axis_index("seq")
        self.c = lax.axis_index("mp")
        self.q = lax.rem(self.s, 4)
        self.z = lax.div(self.s, 4)
        high = lax.div(self.z, 2)
        self.near = self.z + 1 - 2 * lax.rem(self.z, 2)
        self.across = 2 - high
        self.far = 3 - 3 * high
        self.middle = lax.rem(self.z + high, 2) == 1

    def sem(self):
        self.count += 1
        return self.sems.at[self.count - 1]

    def vector(self, number):
        return self.b.vectors[number][...].astype(F32).reshape(1, 1024)

    def greet(self):
        barrier = pltpu.get_barrier_semaphore()

        def signal(step, _):
            other = lax.rem(self.s + step, self.n)
            pl.semaphore_signal(barrier, inc=1, device_id=(other, self.c), device_id_type=MESH)
            return 0

        lax.fori_loop(1, self.n, signal, 0)
        pl.semaphore_signal(barrier, inc=1, device_id=(self.s, 1 - self.c), device_id_type=MESH)

    def meet(self):
        if not self.barrier_done:
            pl.semaphore_wait(pltpu.get_barrier_semaphore(), self.n)
            self.barrier_done = True

    def remote(self, src, dst, send, recv, seq, core):
        return pltpu.make_async_remote_copy(
            src_ref=src,
            dst_ref=dst,
            send_sem=send,
            recv_sem=recv,
            device_id=(seq, core),
            device_id_type=MESH,
        )

    def exchange(self, send_ref, recv_ref):
        self.meet()
        send, recv = self.sem(), self.sem()
        n = self.n

        def start(step, _):
            other = lax.rem(self.s + step, n)
            self.remote(
                send_ref.at[other], recv_ref.at[self.s], send, recv, other, self.c
            ).start()
            return 0

        lax.fori_loop(1, n, start, 0)
        recv_ref[pl.ds(self.s, 1)] = send_ref[pl.ds(self.s, 1)]
        whole = self.remote(
            send_ref.at[pl.ds(0, n - 1)],
            recv_ref.at[pl.ds(0, n - 1)],
            send,
            recv,
            lax.rem(self.s + 1, n),
            self.c,
        )
        self.sends.append(whole)
        return whole.wait_recv

    def core_sum(self, layer, half, chunk, sink):
        self.meet()
        send_ref, recv_ref = layer.b.ps.at[half], layer.b.pr.at[half]
        copies = []
        for number in range(4):
            earlier = self.flying.pop((layer.packed, half, number), None)
            if earlier is not None:
                earlier.wait_send()
            send_ref[number] = chunk(number).astype(BF)
            copy = self.remote(
                send_ref.at[number], recv_ref.at[number], self.sem(), self.sem(), self.s, 1 - self.c
            )
            copy.start()
            copies.append(copy)
            self.flying[(layer.packed, half, number)] = copy
        for number, copy in enumerate(copies):
            copy.wait_recv()
            sink(number, send_ref[number].astype(F32) + recv_ref[number].astype(F32))

    def plane_send(self, pieces, recv_piece, wait_piece):
        self.meet()
        send, recv = self.sem(), self.sem()
        for step in range(1, 4):
            other = lax.rem(self.q + step, 4)
            self.remote(
                pieces(other), recv_piece, send, recv, self.z * 4 + other, self.c
            ).start()
        whole = self.remote(wait_piece, wait_piece, send, recv, self.z * 4 + lax.rem(self.q + 1, 4), self.c)
        self.sends.append(whole)
        return whole.wait_recv

    def line_send(self, pieces, recv_piece, wait_piece):
        self.meet()
        send, recv = self.sem(), self.sem()
        for step in range(1, 4):
            other = lax.rem(self.z + step, 4)
            self.remote(
                pieces(other), recv_piece(step), send, recv, other * 4 + self.q, self.c
            ).start()
        whole = self.remote(wait_piece, wait_piece, send, recv, lax.rem(self.z + 1, 4) * 4 + self.q, self.c)
        self.sends.append(whole)
        return whole.wait_recv

    def line_reduce(self, blocks, slots):
        self.meet()
        receive = [self.sem() for _ in range(4)]
        send = [self.sem() for _ in range(3)]

        def copy(block, slot, way, z):
            return self.remote(
                blocks.at[block], slots.at[slot], send[way], receive[slot], z * 4 + self.q, self.c
            )

        copy(self.near, 0, 0, self.near).start()

        @pl.when(self.middle)
        def _():
            copy(self.across, 1, 1, self.across).start()

        @pl.when(jnp.logical_not(self.middle))
        def _():
            copy(self.far, 3, 2, self.near).start()
            copy(self.across, 2, 1, self.across).start()

        self.sends += [copy(0, 0, way, self.near) for way in range(3)]

        def arrived():
            copy(0, 3, 0, self.near).wait_recv()

        def pass_on():
            copy(self.far, 1, 2, self.far).start()

        def finish():
            copy(0, 0, 0, self.near).wait_recv()
            copy(0, 1, 0, self.near).wait_recv()

            @pl.when(self.middle)
            def _():
                copy(0, 2, 0, self.near).wait_recv()

        return arrived, pass_on, finish

    def store(self, result, which, at, fill):
        slot = self.stored % 4
        self.stored += 1
        if slot in self.stores:
            self.stores.pop(slot).wait()
        stage = self.b.stage.at[slot]
        fill(stage)
        target = result.at[at // 512] if which == 0 else result.at[:, pl.ds(at, 512)]
        copy = pltpu.make_async_copy(stage, target, self.sem())
        copy.start()
        self.stores[slot] = copy

    def drain(self):
        for copy in self.sends + list(self.flying.values()):
            copy.wait_send()
        for copy in self.stores.values():
            copy.wait()


class Layer:
    def __init__(self, packed, per, n):
        self.per = per
        self.n = n
        self.rows = 2 * per
        self.packed = packed
        self.value_rows = per // 2 if self.packed else per
        self.message = per + self.value_rows
        self.total = n * per
        self.block = 256
        self.gains = (0, 1) if packed else (2, 3)

    def attach(self, env, refs, sources, weights, results):
        self.b = refs
        self.sources = sources
        self.held = weights
        self.results = results
        self.right_waits, self.left_waits, self.line_waits = {}, {}, {}
        self.loads = {}

    def load(self, env, number):
        copy = pltpu.make_async_copy(self.sources[number], self.held[number], env.sem())
        copy.start()
        self.loads[number] = copy

    def weight(self, number):
        if number in self.loads:
            self.loads.pop(number).wait()
        return self.held[number]

    def buffers(self):
        r, t, n = self.rows, self.total, self.n
        vr, m = self.value_rows, self.message
        table = dict(
            x=((r, 1024), BF),
            normed=((r, 1024), BF),
            s1=((n, m, 128), BF),
            r1=((n, m, 128), BF),
            qa=((t, 128), BF),
            kb=((t, 128), BF),
            va=((t, 128), BF),
            mixp=((t, 128), F32),
            lse=((t, 128), F32),
            s2=((n, vr, 128), BF),
            r2=((n, vr, 128), BF),
            mixl=((r, 512), BF),
            mid=((r, 1024), F32),
            nm=((r, 1024), BF),
            gp=((r, 2048), BF),
            act=((r, 2048), BF),
            e=((r, 1024), F32),
            el=((r, 1024), BF),
            gb=((r, 2048), BF),
            gm=((r, 1024), F32),
            al=((r, 1024), BF),
            s6=((n, vr, 128), BF),
            r6=((n, vr, 128), BF),
            gx=((t, 128), BF),
            dk=((t, 128), F32),
            dv=((t, 128), F32),
            s7=((n, m, 128), BF),
            r7=((n, m, 128), BF),
            dp=((r, 1536), BF),
            acc=((r, 1024), F32),
            ps=((2, 4, r, 256), BF),
            pr=((2, 4, r, 256), BF),
        )
        if self.packed:
            table.update(
                ng=((4, 4, self.per, 1024), BF),
                x7=((t, 256), BF),
                s9=((n, m, 128), BF),
                r9=((n, m, 128), BF),
                fg=((4, r, 4608), BF),
                ds=((4, r, 768), BF),
                dg=((4, r, 768), BF),
                sb=((4, 64, 4608), BF),
                rb=((4, 64, 4608), BF),
            )
        else:
            table.update(
                fg=((4, 4, r, 1536), BF),
                dg=((4, 4, r, 1024), BF),
                sb=((4, 64, 1536), BF),
                rb=((4, 64, 1536), BF),
                same=((t, t), F32),
                lab=((t, 128), BF),
                hot=((2, self.per, 64), BF),
                labs=((r, 128), F32),
            )
        return table

    def gain(self, env, which):
        return env.vector(self.gains[which])

    def pack(self, tile):
        if not self.packed:
            return tile
        half = self.per // 2
        return jnp.where(low_lanes(half), tile[:half], swap_halves(tile[half:]))

    def send_pairs(self, store, tile_of):
        for seq in range(2):
            for j in range(4):
                tile = tile_of(seq, j)
                store(8 * seq + 2 * j, self.pack(tile))
                store(8 * seq + 2 * j + 1, self.pack(swap_halves(tile)))

    def join_pairs(self, tile_a, tile_b):
        vr = self.value_rows
        low = low_lanes(vr)
        first = jnp.where(low, tile_a, swap_halves(tile_b))
        if not self.packed:
            return [first]
        return [first, jnp.where(low, swap_halves(tile_a), tile_b)]

    def project(self, env, then=None):
        hidden = self.b.x[...].astype(F32)
        normed = (hidden * inverse_rms(hidden) * self.gain(env, 0)).astype(BF)
        self.b.normed[...] = normed
        weight = self.weight(QKV)
        if then is not None:
            then()
        queries, keys, values = (dot(normed, weight[part]) for part in range(3))
        send = self.b.s1
        per = self.per
        low = low_lanes(per)
        for seq in range(2):
            rows = slice(seq * per, (seq + 1) * per)
            for j in range(4):
                cols = slice(128 * j, 128 * j + 128)
                qt, kt, vt = queries[rows, cols], keys[rows, cols], values[rows, cols]
                pair = 8 * seq + 2 * j
                send[pair, 0:per] = jnp.where(low, qt, swap_halves(kt)).astype(BF)
                send[pair + 1, 0:per] = jnp.where(low, swap_halves(qt), kt).astype(BF)
                va, vb = vt, swap_halves(vt)
                if self.packed:
                    va, vb = self.pack(va), self.pack(vb)
                else:
                    labels = self.b.labs[rows, :]
                    va, vb = jnp.where(low, va, labels), jnp.where(low, vb, labels)
                send[pair, per:] = va.astype(BF)
                send[pair + 1, per:] = vb.astype(BF)
        self.wait1 = env.exchange(send, self.b.r1)

    def unpack(self, env):
        recv = self.b.r1
        qa, kb, va = self.b.qa, self.b.kb, self.b.va
        per, vr = self.per, self.value_rows
        low, low_v = low_lanes(per), low_lanes(vr)
        zero = jnp.zeros((per, 128), F32)
        zero_v = jnp.zeros((vr, 128), F32)
        for i in range(self.n):
            both = recv[i, 0:per].astype(F32)
            qa[i * per : (i + 1) * per] = jnp.where(low, both * 0.125, zero).astype(BF)
            kb[i * per : (i + 1) * per] = swap_halves(both).astype(BF)
            tile = recv[i, per:].astype(F32)
            va[i * per : i * per + vr] = jnp.where(low_v, tile, zero_v).astype(BF)
            if self.packed:
                va[i * per + vr : (i + 1) * per] = jnp.where(low_v, swap_halves(tile), zero_v).astype(BF)
            else:
                self.b.lab[i * per : (i + 1) * per] = jnp.where(low_v, zero_v, tile).astype(BF)
        if not self.packed:
            labels = self.b.lab[...]
            self.b.same[...] = dot_t(labels, labels)

    def allowed(self, env, start, stop):
        size = stop - start
        rows = lax.broadcasted_iota(jnp.int32, (size, stop), 0) + start
        keys = lax.broadcasted_iota(jnp.int32, (size, stop), 1)
        ok = keys <= rows
        if self.packed:
            segments = env.b.segments[pl.ds(lax.div(env.s, 8), 1), :]
            row = (lax.broadcasted_iota(jnp.int32, (size, 1), 0) + start).astype(F32)
            opening = jnp.zeros((size, 1), F32)
            for label in range(1, 4):
                edge = jnp.sum((segments < label).astype(F32), axis=1, keepdims=True)
                opening = jnp.where(row >= edge, jnp.maximum(opening, edge), opening)
            return ok & (keys >= opening.astype(jnp.int32))
        return ok & (self.b.same[start:stop, 0:stop] > 0.5)

    def attend(self, env):
        self.wait1()
        self.unpack(env)
        qa, kb, va = self.b.qa, self.b.kb, self.b.va
        mixp, lse = self.b.mixp, self.b.lse
        for start in range(0, self.total, self.block):
            stop = start + self.block
            scores = dot_t(qa[start:stop], kb[0:stop])
            scores = jnp.where(self.allowed(env, start, stop), scores, NEGATIVE)
            highest = jnp.max(scores, axis=1, keepdims=True)
            weights = jnp.exp(scores - highest)
            totals = jnp.sum(weights, axis=1, keepdims=True)
            mixp[start:stop] = dot(weights.astype(BF), va[0:stop]) / totals
            lse[start:stop] = jnp.broadcast_to(highest + jnp.log(totals), (self.block, 128))
        send = self.b.s2
        for i in range(self.n):
            send[i] = self.pack(mixp[i * self.per : (i + 1) * self.per]).astype(BF)
        self.wait2 = env.exchange(send, self.b.r2)

    def gather_heads(self, recv, row0, put):
        per, vr = self.per, self.value_rows
        for seq in range(2):
            for j in range(4):
                pair = 8 * seq + 2 * j
                tiles = self.join_pairs(
                    recv[pair, row0:].astype(F32), recv[pair + 1, row0:].astype(F32)
                )
                for number, tile in enumerate(tiles):
                    begin = seq * per + number * vr
                    put(slice(begin, begin + vr), slice(128 * j, 128 * j + 128), tile)

    def feed(self, env, finish):
        self.wait2()
        mixl = self.b.mixl

        def put(rows, cols, tile):
            mixl[rows, cols] = tile.astype(BF)

        self.gather_heads(self.b.r2, 0, put)
        out = self.weight(OUT)
        mid = self.b.mid
        hidden = self.b.x
        mixed = mixl[...]

        def sink(number, value):
            cols = slice(256 * number, 256 * number + 256)
            mid[:, cols] = value + hidden[:, cols].astype(F32)

        env.core_sum(
            self,
            0,
            lambda number: dot(mixed, out[:, 256 * number : 256 * number + 256]),
            sink,
        )
        middle = mid[...]
        normed = (middle * inverse_rms(middle) * self.gain(env, 1)).astype(BF)
        self.b.nm[...] = normed
        up = self.weight(UP)
        act, slope = self.b.act, self.b.gp
        for number in range(4):
            cols = slice(512 * number, 512 * number + 512)
            before = dot(normed, up[:, cols])
            square = before * before
            bent = jnp.tanh(0.7978845608028654 * before * (1.0 + 0.044715 * square))
            half = 0.5 * (1.0 + bent)
            act[:, cols] = (before * half).astype(BF)
            slope[:, cols] = (
                half
                + 0.5 * before * (1.0 - bent * bent) * (0.7978845608028654 + 0.1070322243 * square)
            ).astype(BF)
        down = self.weight(DOWN)
        env.core_sum(
            self,
            1,
            lambda number: dot(act[...], down[:, 256 * number : 256 * number + 256]),
            finish,
        )

    def back_feed(self, env):
        grad_low = self.b.e[...].astype(BF)
        self.b.el[...] = grad_low
        down, up, out = self.weight(DOWN), self.weight(UP), self.weight(OUT)
        gb, slope = self.b.gb, self.b.gp
        for number in range(4):
            cols = slice(512 * number, 512 * number + 512)
            grad = dot_t(grad_low, down[cols, :])
            gb[:, cols] = (grad * slope[:, cols].astype(F32)).astype(BF)
        acc = self.b.acc

        def sink(number, value):
            acc[:, 256 * number : 256 * number + 256] = value

        env.core_sum(
            self,
            0,
            lambda number: dot_t(gb[...], up[256 * number : 256 * number + 256, :]),
            sink,
        )
        grad_mid, grad_gain = norm_back(acc[...], self.b.mid[...], self.gain(env, 1))
        row = self.gains[1]
        env.b.vg[row : row + 1, :] = grad_gain
        self.b.gm[...] = grad_mid
        along = (self.b.e[...] + grad_mid).astype(BF)
        self.b.al[...] = along
        grad_mixed = dot_t(along, out[...])
        send = self.b.s6
        per = self.per

        def store(pair, tile):
            send[pair] = tile.astype(BF)

        self.send_pairs(
            store,
            lambda seq, j: grad_mixed[seq * per : (seq + 1) * per, 128 * j : 128 * j + 128],
        )
        self.wait6 = env.exchange(send, self.b.r6)

    def back_attend(self, env):
        self.wait6()
        recv, gx = self.b.r6, self.b.gx
        per, vr = self.per, self.value_rows
        low_v = low_lanes(vr)
        zero_v = jnp.zeros((vr, 128), F32)
        for i in range(self.n):
            tile = recv[i].astype(F32)
            gx[i * per : i * per + vr] = jnp.where(low_v, tile, zero_v).astype(BF)
            if self.packed:
                gx[i * per + vr : (i + 1) * per] = jnp.where(low_v, swap_halves(tile), zero_v).astype(BF)
        qa, kb, va = self.b.qa, self.b.kb, self.b.va
        mixp, lse = self.b.mixp, self.b.lse
        dk, dv = self.b.dk, self.b.dv
        dk[...] = jnp.zeros_like(dk)
        dv[...] = jnp.zeros_like(dv)
        dq = {}
        for start in range(0, self.total, self.block):
            stop = start + self.block
            query, grad = qa[start:stop], gx[start:stop]
            scores = dot_t(query, kb[0:stop])
            scores = jnp.where(self.allowed(env, start, stop), scores, NEGATIVE)
            probs = jnp.exp(scores - lse[start:stop, 0:1])
            offsets = jnp.sum(grad.astype(F32) * mixp[start:stop], axis=1, keepdims=True)
            slopes = (probs * (dot_t(grad, va[0:stop]) - offsets)).astype(BF)
            mixp[start:stop] = dot(slopes, kb[0:stop])
            dk[0:stop] += dot_l(slopes, query)
            dv[0:stop] += dot_l(probs.astype(BF), grad)
        send = self.b.s7
        low = low_lanes(per)
        for i in range(self.n):
            rows = slice(i * per, (i + 1) * per)
            send[i, 0:per] = jnp.where(low, mixp[rows] * 0.125, swap_halves(dk[rows])).astype(BF)
            send[i, per:] = self.pack(dv[rows]).astype(BF)
            if self.packed:
                self.b.x7[rows, 0:128] = send[i, 0:per]
                self.b.x7[rows, 128:256] = dv[rows].astype(BF)
        self.wait7 = env.exchange(send, self.b.r7)

    def back_project(self, env, finish, then=None):
        self.wait7()
        recv, dp = self.b.r7, self.b.dp
        per = self.per
        low = low_lanes(per)
        for seq in range(2):
            rows = slice(seq * per, (seq + 1) * per)
            for j in range(4):
                pair = 8 * seq + 2 * j
                one, two = recv[pair, 0:per].astype(F32), recv[pair + 1, 0:per].astype(F32)
                dp[rows, 128 * j : 128 * j + 128] = jnp.where(low, one, swap_halves(two)).astype(BF)
                dp[rows, 512 + 128 * j : 640 + 128 * j] = jnp.where(low, swap_halves(one), two).astype(BF)

        def put(rows, cols, tile):
            dp[rows, 1024 + cols.start : 1024 + cols.stop] = tile.astype(BF)

        self.gather_heads(recv, per, put)
        if then is not None:
            then()
        weight = self.weight(QKV)
        acc = self.b.acc

        def chunk(number):
            rows = slice(256 * number, 256 * number + 256)
            total = dot_t(dp[:, 0:512], weight[0, rows, :])
            total += dot_t(dp[:, 512:1024], weight[1, rows, :])
            return total + dot_t(dp[:, 1024:1536], weight[2, rows, :])

        def sink(number, value):
            acc[:, 256 * number : 256 * number + 256] = value

        env.core_sum(self, 1, chunk, sink)
        grad_hidden, grad_gain = norm_back(
            acc[...], self.b.x[...].astype(F32), self.gain(env, 0)
        )
        row = self.gains[0]
        env.b.vg[row : row + 1, :] = grad_gain
        finish(self.b.gm[...] + grad_hidden)

    def parts(self, env, which):
        b = self.b
        left = (b.normed, b.al, b.nm, b.el)[which]
        right = (b.dp, b.mixl, b.gb, b.act)[which]
        return left, right

    def share_right(self, env, which, begin=0, size=None):
        at, full = COLS[which]
        size = full if size is None else size
        _, right = self.parts(env, which)
        fg = self.b.fg
        cols = pl.ds(at + begin, size)
        fg[pl.ds(env.q, 1), :, cols] = right[:, begin : begin + size][None]
        mine = fg.at[env.q, :, cols]
        self.right_waits.setdefault(which, []).append(
            env.plane_send(lambda other: mine, mine, fg.at[pl.ds(0, 3), :, cols])
        )

    def share_left(self, env, which):
        left, _ = self.parts(env, which)
        ds, dg = self.b.ds, self.b.dg
        low = low_lanes(self.rows)
        begin = 256 * (which - 1)
        for a in range(2):
            tiles = [
                left[:, 128 * (2 * z + a) : 128 * (2 * z + a) + 128].astype(F32) for z in range(4)
            ]
            for two in range(2):
                even, odd = tiles[2 * two], tiles[2 * two + 1]
                at = begin + 128 * two
                ds[2 * a, :, at : at + 128] = jnp.where(low, even, swap_halves(odd)).astype(BF)
                ds[2 * a + 1, :, at : at + 128] = jnp.where(low, swap_halves(even), odd).astype(BF)
        cols = pl.ds(begin, 256)
        dg[pl.ds(env.q, 1), :, begin : begin + 256] = ds[pl.ds(env.q, 1), :, begin : begin + 256]
        self.left_waits[which] = env.plane_send(
            lambda other: ds.at[other, :, cols],
            dg.at[env.q, :, cols],
            dg.at[pl.ds(0, 3), :, cols],
        )

    def multiply(self, env, which):
        for wait in self.right_waits[which]:
            wait()
        self.left_waits[which]()
        begin, size = COLS[which]
        fg, dg, sb, rb = self.b.fg, self.b.dg, self.b.sb, self.b.rb
        rows = 4 * self.rows
        left = dg[:, :, 256 * (which - 1) : 256 * which].reshape(rows, 256)
        for at in range(begin, begin + size, 512):
            right = fg[:, :, at : at + 512].reshape(rows, 512)
            product = dot_l(left, right)
            for z in range(4):
                sb[z, :, at : at + 512] = product[64 * z : 64 * z + 64].astype(BF)
        self.line_waits[which] = env.line_reduce(sb.at[:, :, pl.ds(begin, size)], rb.at[:, :, pl.ds(begin, size)])

    def relay(self, env, which):
        begin, size = COLS[which]
        sb, rb = self.b.sb, self.b.rb
        arrived, pass_on, _ = self.line_waits[which]

        @pl.when(env.middle)
        def _():
            arrived()
            for at in range(begin, begin + size, 512):
                cols = slice(at, at + 512)
                far = pl.ds(env.far, 1)
                total = sb[far, :, cols].astype(F32) + rb[3:4, :, cols].astype(F32)
                sb[far, :, cols] = total.astype(BF)
            pass_on()

    def collect(self, env, which):
        self.line_waits[which][2]()
        begin, size = COLS[which]
        sb, rb = self.b.sb, self.b.rb
        for at in range(0, size, 512):
            cols = slice(begin + at, begin + at + 512)

            def fill(stage):
                total = sb[pl.ds(env.z, 1), :, cols].astype(F32)
                for slot in range(2):
                    total = total + rb[slot : slot + 1, :, cols].astype(F32)
                stage[...] = total[0]

                @pl.when(env.middle)
                def _():
                    stage[...] += rb[2, :, cols].astype(F32)

            env.store(self.results[which], which, at, fill)

    def gather_line(self, env):
        normed, ng, per = self.b.normed, self.b.ng, self.per
        cols = pl.ds(pl.multiple_of(512 * env.c, 512), 512)

        def rows(z):
            return pl.ds(pl.multiple_of(lax.div(z, 2) * per, per), per)

        ng[pl.ds(env.z, 1), pl.ds(env.q, 1), :, cols] = normed[rows(env.z), cols][None, None]
        self.gather_wait = env.line_send(
            lambda other: normed.at[rows(other), cols],
            lambda step: ng.at[env.z, env.q, :, cols],
            ng.at[pl.ds(0, 3), 0, :, cols],
        )

    def gather_plane(self, env):
        self.gather_wait()
        ng = self.b.ng
        cols = pl.ds(pl.multiple_of(512 * env.c, 512), 512)
        mine = ng.at[:, env.q, :, cols]
        self.gather_wait = env.plane_send(lambda other: mine, mine, ng.at[:, pl.ds(0, 3), :, cols])

    def gather_core(self, env):
        self.gather_wait()
        cols = pl.ds(pl.multiple_of(512 * env.c, 512), 512)
        mine = self.b.ng.at[:, :, :, cols]
        copy = env.remote(mine, mine, env.sem(), env.sem(), env.s, 1 - env.c)
        copy.start()
        env.sends.append(copy)
        self.gather_wait = copy.wait_recv

    def head_gradient(self, env):
        self.gather_wait()
        per, total = self.per, self.total
        product = dot_l(self.b.x7[...], self.b.ng[...].reshape(total, 1024))
        turned = jnp.transpose(product)
        send = self.b.s9
        for i in range(self.n):
            rows = slice(i * 64, i * 64 + 64)
            send[i, 0:per] = turned[rows, 0:128].astype(BF)
            send[i, per:] = self.pack(turned[rows, 128:256]).astype(BF)
        self.wait9 = env.exchange(send, self.b.r9)

    def head_collect(self, env):
        self.wait9()
        recv, per, vr = self.b.r9, self.per, self.value_rows
        low = low_lanes(per)

        def both(pair, rows):
            return recv[pair, rows].astype(F32) + recv[pair + 8, rows].astype(F32)

        for part in range(3):

            def fill(stage):
                for j in range(4):
                    cols = slice(128 * j, 128 * j + 128)
                    rows = slice(0, per) if part < 2 else slice(per, per + vr)
                    one, two = both(2 * j, rows), both(2 * j + 1, rows)
                    if part == 0:
                        stage[:, cols] = jnp.where(low, one, swap_halves(two))
                    elif part == 1:
                        stage[:, cols] = jnp.where(low, swap_halves(one), two)
                    else:
                        first, second = self.join_pairs(one, two)
                        stage[0:vr, cols] = first
                        stage[vr:, cols] = second

            env.store(self.results[QKV], QKV, 512 * part, fill)

    def spread_right(self, env, which):
        _, right = self.parts(env, which)
        fg, width = self.b.fg, WIDTHS[which]
        cols = pl.ds(BEGINS[which], width)

        def quarter(number):
            return pl.ds(pl.multiple_of(number * width, 128), width)

        fg[pl.ds(env.z, 1), pl.ds(env.q, 1), :, cols] = right[:, quarter(env.q)][None, None]
        self.right_waits[which] = env.plane_send(
            lambda other: right.at[:, quarter(other)],
            fg.at[env.z, env.q, :, cols],
            fg.at[env.z, pl.ds(0, 3), :, cols],
        )

    def spread_right_on(self, env, which):
        self.right_waits[which]()
        fg = self.b.fg
        cols = pl.ds(BEGINS[which], WIDTHS[which])
        mine = fg.at[env.z, :, :, cols]
        self.right_waits[which] = env.line_send(
            lambda other: mine, lambda step: mine, fg.at[pl.ds(0, 3), :, :, cols]
        )

    def spread_left(self, env, which):
        left, _ = self.parts(env, which)
        dg = self.b.dg
        cols = pl.ds(256 * which, 256)

        def quarter(number):
            return pl.ds(pl.multiple_of(number * 256, 256), 256)

        dg[pl.ds(env.z, 1), pl.ds(env.q, 1), :, cols] = left[:, quarter(env.z)][None, None]
        self.left_waits[which] = env.line_send(
            lambda other: left.at[:, quarter(other)],
            lambda step: dg.at[env.z, env.q, :, cols],
            dg.at[pl.ds(0, 3), env.q, :, cols],
        )

    def spread_left_on(self, env, which):
        self.left_waits[which]()
        dg = self.b.dg
        cols = pl.ds(256 * which, 256)
        mine = dg.at[:, env.q, :, cols]
        self.left_waits[which] = env.plane_send(
            lambda other: mine, mine, dg.at[:, pl.ds(0, 3), :, cols]
        )

    def spread_multiply(self, env, which):
        self.right_waits[which]()
        self.left_waits[which]()
        fg, dg, sb, rb = self.b.fg, self.b.dg, self.b.sb, self.b.rb
        width = WIDTHS[which]
        cols = pl.ds(BEGINS[which], width)
        rows = 16 * self.rows
        product = dot_l(
            dg[:, :, :, 256 * which : 256 * which + 256].reshape(rows, 256),
            fg[:, :, :, cols].reshape(rows, width),
        ).astype(BF)
        for number in range(4):
            sb[number, :, cols] = product[64 * number : 64 * number + 64]
        rb[pl.ds(env.q, 1), :, cols] = sb[pl.ds(env.q, 1), :, cols]
        self.line_waits[which] = env.plane_send(
            lambda other: sb.at[other, :, cols],
            rb.at[env.q, :, cols],
            rb.at[pl.ds(0, 3), :, cols],
        )

    def spread_collect(self, env, which):
        self.line_waits[which]()
        rb, begin, width = self.b.rb, BEGINS[which], WIDTHS[which]
        for at in range(0, SIZES[which], 512):

            def fill(stage):
                for inner in range(0, 512, 128):
                    source, offset = divmod(at + inner, width)
                    stage[:, inner : inner + 128] = rb[
                        source, :, begin + offset : begin + offset + 128
                    ].astype(F32)

            env.store(self.results[which], which, at, fill)


def pick_rows(env, dense, routed):
    hot, labs, first = routed.b.hot, routed.b.labs, env.b.first
    group, slots = dense.per, routed.per
    base = env.s * group
    for seq in range(2):
        listed = env.b.routed[seq : seq + 1, :]
        places = listed.shape[1]
        place = lax.broadcasted_iota(jnp.int32, (group, places), 0) + base
        here = (place == listed).astype(F32).astype(BF)
        before = jnp.sum((listed < base).astype(F32), axis=1, keepdims=True).astype(jnp.int32)
        number = lax.broadcasted_iota(jnp.int32, (slots, places), 1) - before
        slot = lax.broadcasted_iota(jnp.int32, (slots, places), 0)
        mine = (number == slot).astype(F32).astype(BF)
        table = dot_t(mine, here).astype(BF)
        hot[seq] = table
        segments = env.b.segments[seq : seq + 1, :]
        row = (lax.broadcasted_iota(jnp.int32, (group, 1), 0) + base).astype(F32)
        label = jnp.zeros((group, 1), F32)
        for number in range(1, 4):
            edge = jnp.sum((segments < number).astype(F32), axis=1, keepdims=True)
            label = label + (row >= edge).astype(F32)
        lane = lax.broadcasted_iota(jnp.int32, (group, 128), 1)
        one_hot = (lane == label.astype(jnp.int32) + 64).astype(F32).astype(BF)
        labs[seq * slots : (seq + 1) * slots, :] = dot(table, one_hot)
        rows = first[seq * group : (seq + 1) * group, :].astype(BF)
        routed.b.x[seq * slots : (seq + 1) * slots, :] = dot(table, rows).astype(BF)


def restore(env, dense, routed, sent, seq):
    slots = routed.per
    return dot_l(routed.b.hot[seq], sent[seq * slots : (seq + 1) * slots])


def gate_rows(env, dense, routed):
    group, slots = dense.per, routed.per
    sent = routed.b.acc[...].astype(BF)
    router = env.vector(4)
    grad_router = jnp.zeros((1, 1024), F32)
    for seq in range(2):
        rows = slice(seq * group, (seq + 1) * group)
        first = env.b.first[rows, :]
        returned = restore(env, dense, routed, sent, seq)
        gate = jax.nn.sigmoid(jnp.sum(first * router, axis=1, keepdims=True))
        env.b.output[rows, :] = first + gate * returned
        grad = env.b.cotangent[:, seq, :].astype(F32)
        low = (gate * grad).astype(BF)
        routed.b.e[seq * slots : (seq + 1) * slots, :] = dot(routed.b.hot[seq], low)
        logit = jnp.sum(grad * returned, axis=1, keepdims=True) * gate * (1.0 - gate)
        grad_router = grad_router + jnp.sum(logit * first, axis=0, keepdims=True)
        dense.b.e[rows, :] = grad + logit * router
    env.b.vg[4:5, :] = grad_router


def share_vectors(env):
    vg, sv, rv = env.b.vg, env.b.sv, env.b.rv
    for number in range(env.n):
        tile = vg[:, 128 * (number // 2) : 128 * (number // 2) + 128]
        sv[number] = swap_halves(tile) if number % 2 else tile
    return env.exchange(sv, rv)


def sum_vectors(env, wait):
    wait()
    total = env.b.rv[0]
    for number in range(1, env.n):
        total = total + env.b.rv[number]
    env.b.gvec[...] = total


QKV, OUT, UP, DOWN = range(4)
SHAPES = ((3, 1024, 512), (512, 1024), (1024, 2048), (2048, 1024))
GRADS = ((3, 64, 512), (64, 512), (64, 2048), (64, 2048))


def whole_step(env, dense, routed):
    env.greet()
    dense.load(env, QKV)
    for seq in range(2):
        dense.b.x[seq * dense.per : (seq + 1) * dense.per, :] = env.b.tokens[:, seq, :]
    env.b.vg[...] = jnp.zeros_like(env.b.vg)

    dense.project(env)
    for number in (OUT, UP, DOWN):
        dense.load(env, number)
    dense.gather_line(env)
    dense.attend(env)
    for number in range(4):
        routed.load(env, number)
    dense.gather_plane(env)
    mid_d, first = dense.b.mid, env.b.first

    def finish_dense(number, value):
        cols = slice(256 * number, 256 * number + 256)
        first[:, cols] = mid_d[:, cols] + value

    dense.feed(env, finish_dense)
    pick_rows(env, dense, routed)
    routed.project(env)
    dense.gather_core(env)
    dense.share_left(env, UP)
    dense.share_right(env, OUT)
    routed.attend(env)
    dense.share_right(env, DOWN, 0, 1024)
    mid_r, x_r, sent = routed.b.mid, routed.b.x, routed.b.acc

    def finish_routed(number, value):
        cols = slice(256 * number, 256 * number + 256)
        sent[:, cols] = mid_r[:, cols] - x_r[:, cols].astype(F32) + value

    routed.feed(env, finish_routed)
    routed.spread_right(env, DOWN)
    routed.spread_right(env, OUT)
    routed.spread_left(env, QKV)
    routed.spread_left(env, UP)
    gate_rows(env, dense, routed)
    routed.back_feed(env)
    routed.spread_right(env, UP)
    routed.spread_left(env, DOWN)
    routed.spread_left(env, OUT)
    routed.spread_right_on(env, OUT)
    routed.back_attend(env)
    routed.spread_right_on(env, DOWN)
    dense.share_right(env, DOWN, 1024, 1024)

    def finish_back(branch):
        low = branch.astype(BF)
        for seq in range(2):
            rows = slice(seq * dense.per, (seq + 1) * dense.per)
            dense.b.e[rows, :] += restore(env, dense, routed, low, seq)

    routed.back_project(env, finish_back, lambda: routed.spread_right(env, QKV))
    dense.back_feed(env)
    routed.spread_right_on(env, UP)
    dense.share_left(env, DOWN)
    dense.share_left(env, OUT)
    dense.share_right(env, UP, 0, 1024)
    routed.spread_left_on(env, DOWN)
    routed.spread_left_on(env, OUT)
    dense.back_attend(env)
    dense.multiply(env, DOWN)
    dense.head_gradient(env)
    dense.multiply(env, OUT)
    dense.share_right(env, UP, 1024, 1024)
    routed.spread_right_on(env, QKV)
    routed.spread_left_on(env, UP)
    routed.spread_left_on(env, QKV)

    def finish_tokens(branch):
        env.b.grad_tokens[...] = dense.b.e[...] + branch

    dense.back_project(env, finish_tokens)
    wait = share_vectors(env)
    dense.multiply(env, UP)
    dense.relay(env, DOWN)
    dense.relay(env, OUT)
    for which in (DOWN, OUT, UP, QKV):
        routed.spread_multiply(env, which)
    dense.relay(env, UP)
    dense.head_collect(env)
    for which in (DOWN, OUT, UP, QKV):
        routed.spread_collect(env, which)
    for which in (DOWN, OUT, UP):
        dense.collect(env, which)
    sum_vectors(env, wait)
    env.drain()


def fused(group, tokens, cotangent, segments, routed_places, vectors, weights):
    n = lax.axis_size("seq")
    rows = 2 * group
    dense, routed = Layer(True, group, n), Layer(False, group // 4, n)
    wide = ((rows, 1024), F32)
    common = dict(
        stage=((4, 64, 512), F32),
        first=wide,
        vg=((8, 1024), F32),
        sv=((n, 8, 128), F32),
        rv=((n, 8, 128), F32),
    )
    groups = (dense.buffers(), routed.buffers(), common)
    scratch = [spec for table in groups for spec in table.values()]

    def kernel(*refs):
        refs = list(refs)

        def take(count):
            taken = refs[:count]
            del refs[:count]
            return taken

        inputs = take(4)
        vector_refs = take(5)
        sources = take(8)
        outputs = take(3)
        results = take(8)
        held = take(8)
        dense_refs, routed_refs, common_refs = (
            types.SimpleNamespace(**dict(zip(table, take(len(table)), strict=True))) for table in groups
        )
        b = common_refs
        b.tokens, b.cotangent, b.segments, b.routed = inputs
        b.output, b.grad_tokens, b.gvec = outputs
        b.vectors = vector_refs
        env = Env(b, refs[0], n)
        dense.attach(env, dense_refs, sources[:4], held[:4], results[:4])
        routed.attach(env, routed_refs, sources[4:], held[4:], results[4:])
        whole_step(env, dense, routed)

    vmem = pl.BlockSpec(memory_space=pltpu.VMEM)
    hbm = pl.BlockSpec(memory_space=pl.ANY)
    outs = [wide, wide, ((8, 128), F32)] + [(shape, F32) for shape in GRADS * 2]
    return pl.pallas_call(
        kernel,
        out_shape=[jax.ShapeDtypeStruct(*spec) for spec in outs],
        in_specs=[vmem] * 9 + [hbm] * 8,
        out_specs=[vmem] * 3 + [hbm] * 8,
        scratch_shapes=[pltpu.VMEM(shape, BF) for shape in SHAPES * 2]
        + [pltpu.VMEM(*spec) for spec in scratch]
        + [pltpu.SemaphoreType.DMA((256,))],
        compiler_params=pltpu.CompilerParams(
            collective_id=0, has_side_effects=True, vmem_limit_bytes=LIMIT
        ),
    )(tokens, cotangent, segments, routed_places, *vectors, *weights)


def place_results(group, parts):
    def kernel(*refs):
        output, grad_tokens, gvec = refs[:3]
        grads, outs, held = refs[3:11], refs[11:26], refs[26:34]
        sems = refs[34]
        loads = [
            pltpu.make_async_copy(source, target, sems.at[0, number])
            for number, (source, target) in enumerate(zip(grads, held, strict=True))
        ]
        for copy in loads:
            copy.start()
        for source, target in ((output, outs[0]), (grad_tokens, outs[1])):
            for seq in range(2):
                target[:, seq, :] = source[seq * group : (seq + 1) * group, :]
        for number in range(5):
            outs[2 + number][...] = gvec[number, 0:64]
        stores = []
        for number, copy in enumerate(loads):
            copy.wait()
            stores.append(pltpu.make_async_copy(held[number], outs[7 + number], sems.at[1, number]))
            stores[-1].start()
        for copy in stores:
            copy.wait()

    vmem = pl.BlockSpec(memory_space=pltpu.VMEM)
    hbm = pl.BlockSpec(memory_space=pl.ANY)
    shapes = [(group, 2, 1024)] * 2 + [(64,)] * 5 + list(GRADS * 2)
    return pl.pallas_call(
        kernel,
        out_shape=[jax.ShapeDtypeStruct(shape, F32) for shape in shapes],
        in_specs=[vmem] * 3 + [hbm] * 8,
        out_specs=[vmem] * 7 + [hbm] * 8,
        scratch_shapes=[pltpu.VMEM(shape, F32) for shape in GRADS * 2]
        + [pltpu.SemaphoreType.DMA((2, 8))],
        compiler_params=pltpu.CompilerParams(vmem_limit_bytes=LIMIT),
    )(*parts)


def on_device_fused(
    tokens,
    segments,
    routed,
    router,
    dense_attn_gain,
    dense_qkv,
    dense_out,
    dense_mlp_gain,
    dense_up,
    dense_down,
    routed_attn_gain,
    routed_qkv,
    routed_out,
    routed_mlp_gain,
    routed_up,
    routed_down,
    cotangent,
):
    group = tokens.shape[0]
    parts = fused(
        group,
        tokens,
        cotangent,
        segments,
        routed,
        (dense_attn_gain, dense_mlp_gain, routed_attn_gain, routed_mlp_gain, router),
        (
            jnp.transpose(dense_qkv, (1, 0, 2)),
            dense_out,
            dense_up,
            dense_down,
            jnp.transpose(routed_qkv, (1, 0, 2)),
            routed_out,
            routed_up,
            routed_down,
        ),
    )
    placed = place_results(group, parts)
    vectors = placed[2:7]

    def weights_of(grads, first, second):
        return (
            vectors[first],
            jnp.transpose(grads[QKV], (1, 0, 2)),
            jnp.transpose(grads[OUT]),
            vectors[second],
            grads[UP],
            jnp.transpose(grads[DOWN]),
        )

    return (
        tuple(placed[:2])
        + weights_of(placed[7:11], 0, 1)
        + weights_of(placed[11:], 2, 3)
        + (vectors[4],)
    )


def solution(mesh):
    in_specs = (
        P("seq", None, None),
        P(),
        P(),
        P(),
        P(),
        P(None, None, "mp"),
        P("mp", None),
        P(),
        P(None, "mp"),
        P("mp", None),
        P(),
        P(None, None, "mp"),
        P("mp", None),
        P(),
        P(None, "mp"),
        P("mp", None),
        P("seq", None, None),
    )
    out_specs = (
        P("seq", None, None),
        P("seq", None, None),
        P("seq"),
        P("seq", None, "mp"),
        P("mp", "seq"),
        P("seq"),
        P("seq", "mp"),
        P("mp", "seq"),
        P("seq"),
        P("seq", None, "mp"),
        P("mp", "seq"),
        P("seq"),
        P("seq", "mp"),
        P("mp", "seq"),
        P("seq"),
    )
    seq_size = mesh.shape["seq"]
    pairs = 2 * (16 // mesh.shape["mp"])
    body = on_device_fused if seq_size == pairs else on_device

    return jax.shard_map(
        body, mesh=mesh, in_specs=in_specs, out_specs=out_specs, check_vma=False
    )
```

```python
import math
import types

import jax
import jax.numpy as jnp
from jax import lax
from jax.experimental import pallas as pl
from jax.experimental.pallas import tpu as pltpu
from jax.sharding import PartitionSpec as P

HEAD_DIM = 64


EPSILON = 1e-06
NEGATIVE = -1e30
PRECISE = lax.Precision.HIGHEST


def rms_norm(hidden, gain):
    return hidden * lax.rsqrt(jnp.mean(hidden * hidden, axis=-1, keepdims=True) + EPSILON) * gain


def gelu_tanh(operand):
    return jax.nn.gelu(operand, approximate=True)


def model_sum(operand):
    return lax.psum(operand, "mp")


def block_loop(row_total, advance, carried):
    block_size = math.gcd(row_total, 512)
    return lax.fori_loop(
        0,
        row_total // block_size,
        lambda number, current: advance(current, number * block_size, block_size),
        carried,
    )


def key_mask(query_places, query_live, key_places, key_live, label_rows):
    query_labels = jnp.take_along_axis(label_rows, query_places, axis=0)
    key_labels = jnp.take_along_axis(label_rows, key_places, axis=0)
    allowed = jnp.transpose(key_places)[:, None, :] <= jnp.transpose(query_places)[:, :, None]
    allowed = allowed & (
        jnp.transpose(key_labels)[:, None, :] == jnp.transpose(query_labels)[:, :, None]
    )
    allowed = allowed & jnp.transpose(key_live)[:, None, :] & jnp.transpose(query_live)[:, :, None]
    return allowed[:, None]


def attend_forward(queries, key_rows, value_rows, own_places, own_live, row_info, label_rows):
    row_count, seq_count, head_count, head_size = queries.shape
    score_scale = head_size ** (-0.5)
    shape_rows = (seq_count, head_count, row_count)
    initial = (
        jnp.full(shape_rows, NEGATIVE, jnp.float32),
        jnp.zeros(shape_rows, jnp.float32),
        jnp.zeros(shape_rows + (head_size,), jnp.float32),
    )
    key_piece = lax.all_gather(key_rows, "seq", axis=0, tiled=True)
    value_piece = lax.all_gather(value_rows, "seq", axis=0, tiled=True)

    def advance(current, offset, block_size):
        highest, totals, summed = current
        key_block = lax.dynamic_slice_in_dim(key_piece, offset, block_size, 0).reshape(
            block_size, seq_count, head_count, head_size
        )
        value_block = lax.dynamic_slice_in_dim(value_piece, offset, block_size, 0).reshape(
            block_size, seq_count, head_count, head_size
        )
        key_places, key_live = row_info(offset, block_size)
        allowed = key_mask(own_places, own_live, key_places, key_live, label_rows)
        scores = (
            jnp.einsum("qshe,kshe->shqk", queries, key_block, preferred_element_type=jnp.float32)
            * score_scale
        )
        scores = jnp.where(allowed, scores, NEGATIVE)
        newest = jnp.maximum(highest, jnp.max(scores, axis=-1))
        weights = jnp.exp(scores - newest[..., None])
        factor = jnp.exp(highest - newest)
        totals = totals * factor + jnp.sum(weights, axis=-1)
        summed = summed * factor[..., None] + jnp.einsum(
            "shqk,kshe->shqe",
            weights.astype(jnp.bfloat16),
            value_block,
            preferred_element_type=jnp.float32,
        )
        return (newest, totals, summed)

    highest, totals, summed = block_loop(key_piece.shape[0], advance, initial)
    mixed_rows = jnp.transpose(summed / totals[..., None], (2, 0, 1, 3)).reshape(
        row_count, seq_count, head_count * head_size
    )
    return (mixed_rows, highest + jnp.log(totals), None)


def attend_backward(
    queries,
    key_rows,
    value_rows,
    grad_mixed,
    mixed_rows,
    log_sum,
    own_places,
    own_live,
    row_info,
    label_rows,
):
    row_count, seq_count, head_count, head_size = queries.shape
    score_scale = head_size ** (-0.5)
    grad_heads = grad_mixed.reshape(row_count, seq_count, head_count, head_size)
    offsets = jnp.sum(
        grad_heads.astype(jnp.float32)
        * mixed_rows.reshape(row_count, seq_count, head_count, head_size),
        axis=-1,
    )
    offsets_rows = jnp.transpose(offsets, (1, 2, 0))
    key_piece = lax.all_gather(key_rows, "seq", axis=0, tiled=True)
    value_piece = lax.all_gather(value_rows, "seq", axis=0, tiled=True)

    def advance(current, offset, block_size):
        key_block = lax.dynamic_slice_in_dim(key_piece, offset, block_size, 0).reshape(
            block_size, seq_count, head_count, head_size
        )
        value_block = lax.dynamic_slice_in_dim(value_piece, offset, block_size, 0).reshape(
            block_size, seq_count, head_count, head_size
        )
        key_places, key_live = row_info(offset, block_size)
        allowed = key_mask(own_places, own_live, key_places, key_live, label_rows)
        scores = (
            jnp.einsum("qshe,kshe->shqk", queries, key_block, preferred_element_type=jnp.float32)
            * score_scale
        )
        scores = jnp.where(allowed, scores, NEGATIVE)
        chances = jnp.exp(scores - log_sum[..., None])
        pushes = jnp.einsum(
            "qshe,kshe->shqk", grad_heads, value_block, preferred_element_type=jnp.float32
        )
        slopes = (chances * (pushes - offsets_rows[..., None])).astype(jnp.bfloat16)
        return current + jnp.einsum(
            "shqk,kshe->qshe", slopes, key_block, preferred_element_type=jnp.float32
        )

    grad_queries = block_loop(key_piece.shape[0], advance, jnp.zeros(queries.shape, jnp.float32))
    log_all, offsets_all = (
        lax.all_gather(jnp.transpose(log_sum, (2, 0, 1)), "seq", axis=0, tiled=True),
        lax.all_gather(offsets, "seq", axis=0, tiled=True),
    )
    own_keys = key_rows.reshape(row_count, seq_count, head_count, head_size)
    own_values = value_rows.reshape(row_count, seq_count, head_count, head_size)
    zero_rows = jnp.zeros(queries.shape, jnp.float32)
    query_flat = queries.reshape(row_count, seq_count, head_count * head_size)
    query_piece = lax.all_gather(query_flat, "seq", axis=0, tiled=True)
    grad_piece = lax.all_gather(grad_mixed, "seq", axis=0, tiled=True)

    def advance(current, offset, block_size):
        key_sum, value_sum = current
        query_block = lax.dynamic_slice_in_dim(query_piece, offset, block_size, 0).reshape(
            block_size, seq_count, head_count, head_size
        )
        grad_block = lax.dynamic_slice_in_dim(grad_piece, offset, block_size, 0).reshape(
            block_size, seq_count, head_count, head_size
        )
        block_log = jnp.transpose(
            lax.dynamic_slice_in_dim(log_all, offset, block_size, 0), (1, 2, 0)
        )
        block_offsets = jnp.transpose(
            lax.dynamic_slice_in_dim(offsets_all, offset, block_size, 0), (1, 2, 0)
        )
        query_places, query_live = row_info(offset, block_size)
        allowed = key_mask(query_places, query_live, own_places, own_live, label_rows)
        scores = (
            jnp.einsum("qshe,kshe->shqk", query_block, own_keys, preferred_element_type=jnp.float32)
            * score_scale
        )
        scores = jnp.where(allowed, scores, NEGATIVE)
        chances = jnp.exp(scores - block_log[..., None])
        pushes = jnp.einsum(
            "qshe,kshe->shqk", grad_block, own_values, preferred_element_type=jnp.float32
        )
        slopes = (chances * (pushes - block_offsets[..., None])).astype(jnp.bfloat16)
        key_sum = key_sum + jnp.einsum(
            "shqk,qshe->kshe", slopes, query_block, preferred_element_type=jnp.float32
        )
        value_sum = value_sum + jnp.einsum(
            "shqk,qshe->kshe",
            chances.astype(jnp.bfloat16),
            grad_block,
            preferred_element_type=jnp.float32,
        )
        return (key_sum, value_sum)

    key_sum, value_sum = block_loop(query_piece.shape[0], advance, (zero_rows, zero_rows))
    flat_shape = (row_count, seq_count, head_count * head_size)
    return (
        (grad_queries * score_scale).reshape(flat_shape),
        (key_sum * score_scale).reshape(flat_shape),
        value_sum.reshape(flat_shape),
    )


def block_forward(hidden, params, row_info, label_rows):
    attn_gain, qkv_weight, out_weight, mlp_gain, up_weight, down_weight = params
    row_count, seq_count, _ = hidden.shape
    head_width = qkv_weight.shape[2]
    head_count = head_width // HEAD_DIM
    own_places, own_live = row_info(lax.axis_index("seq") * row_count, row_count)
    normed = rms_norm(hidden, attn_gain.astype(jnp.float32)).astype(jnp.bfloat16)
    projected = jnp.einsum(
        "rsd,dce->rsce", normed, qkv_weight, preferred_element_type=jnp.float32
    ).astype(jnp.bfloat16)
    queries = projected[:, :, 0].reshape(row_count, seq_count, head_count, HEAD_DIM)
    key_rows = projected[:, :, 1]
    value_rows = projected[:, :, 2]
    mixed_rows, log_sum, kept_rows = attend_forward(
        queries, key_rows, value_rows, own_places, own_live, row_info, label_rows
    )
    mixed_low = mixed_rows.astype(jnp.bfloat16)
    attention = model_sum(
        jnp.einsum("rsh,hd->rsd", mixed_low, out_weight, preferred_element_type=jnp.float32)
    )
    middle = hidden + attention
    normed_mlp = rms_norm(middle, mlp_gain.astype(jnp.float32)).astype(jnp.bfloat16)
    before = jnp.einsum("rsd,df->rsf", normed_mlp, up_weight, preferred_element_type=jnp.float32)
    active = gelu_tanh(before).astype(jnp.bfloat16)
    feed_out = model_sum(
        jnp.einsum("rsf,fd->rsd", active, down_weight, preferred_element_type=jnp.float32)
    )
    stored = (
        hidden,
        normed,
        queries,
        key_rows,
        value_rows,
        mixed_rows,
        log_sum,
        mixed_low,
        middle,
        normed_mlp,
        before,
        active,
        own_places,
        own_live,
        kept_rows,
    )
    return (attention, middle, feed_out, stored)


def block_backward(incoming, stored, params, row_info, label_rows):
    attn_gain, qkv_weight, out_weight, mlp_gain, up_weight, down_weight = params
    (
        hidden,
        normed,
        queries,
        key_rows,
        value_rows,
        mixed_rows,
        log_sum,
        mixed_low,
        middle,
        normed_mlp,
        before,
        active,
        own_places,
        own_live,
        kept_rows,
    ) = stored
    incoming_low = incoming.astype(jnp.bfloat16)
    grad_down = jnp.einsum("rsf,rsd->fd", active, incoming_low, preferred_element_type=jnp.float32)
    grad_active = jnp.einsum(
        "rsd,fd->rsf", incoming_low, down_weight, preferred_element_type=jnp.float32
    )
    _, gelu_pull = jax.vjp(gelu_tanh, before)
    grad_before = gelu_pull(grad_active)[0].astype(jnp.bfloat16)
    grad_up = jnp.einsum("rsd,rsf->df", normed_mlp, grad_before, preferred_element_type=jnp.float32)
    grad_normed_mlp = model_sum(
        jnp.einsum("rsf,df->rsd", grad_before, up_weight, preferred_element_type=jnp.float32)
    )
    _, mlp_pull = jax.vjp(rms_norm, middle, mlp_gain.astype(jnp.float32))
    grad_middle, grad_mlp_gain = mlp_pull(grad_normed_mlp)
    along_low = (incoming + grad_middle).astype(jnp.bfloat16)
    grad_out = jnp.einsum("rsh,rsd->hd", mixed_low, along_low, preferred_element_type=jnp.float32)
    grad_mixed = jnp.einsum(
        "rsd,hd->rsh", along_low, out_weight, preferred_element_type=jnp.float32
    ).astype(jnp.bfloat16)
    grad_queries, grad_keys, grad_values = attend_backward(
        queries,
        key_rows,
        value_rows,
        grad_mixed,
        mixed_rows,
        log_sum,
        own_places,
        own_live,
        row_info,
        label_rows,
    )
    grad_projected = jnp.stack((grad_queries, grad_keys, grad_values), axis=2).astype(jnp.bfloat16)
    grad_qkv = jnp.einsum(
        "rsd,rsce->dce", normed, grad_projected, preferred_element_type=jnp.float32
    )
    grad_normed = model_sum(
        jnp.einsum("rsce,dce->rsd", grad_projected, qkv_weight, preferred_element_type=jnp.float32)
    )
    _, attn_pull = jax.vjp(rms_norm, hidden, attn_gain.astype(jnp.float32))
    grad_hidden, grad_attn_gain = attn_pull(grad_normed)
    return (
        grad_middle + grad_hidden,
        (grad_attn_gain, grad_qkv, grad_out, grad_mlp_gain, grad_up, grad_down),
    )


def on_device(
    tokens,
    segments,
    routed,
    router,
    dense_attn_gain,
    dense_qkv,
    dense_out,
    dense_mlp_gain,
    dense_up,
    dense_down,
    routed_attn_gain,
    routed_qkv,
    routed_out,
    routed_mlp_gain,
    routed_up,
    routed_down,
    cotangent,
):
    group_rows, seq_count, _ = tokens.shape
    devices = lax.axis_size("seq")
    my_index = lax.axis_index("seq")
    capacity = routed.shape[1]
    most_rows = group_rows // 4
    label_rows = jnp.transpose(segments)
    route_rows = jnp.transpose(routed)
    local_ids = jnp.arange(group_rows, dtype=jnp.int32)
    bounds = jnp.arange(devices + 1, dtype=jnp.int32) * group_rows
    starts = jnp.sum((routed[None, :, :] < bounds[:, None, None]).astype(jnp.int32), axis=2)
    first_rank = starts[my_index]
    routed_here = starts[my_index + 1] - first_rank
    dense_params = (dense_attn_gain, dense_qkv, dense_out, dense_mlp_gain, dense_up, dense_down)
    routed_params = (
        routed_attn_gain,
        routed_qkv,
        routed_out,
        routed_mlp_gain,
        routed_up,
        routed_down,
    )

    def dense_info(first_row, row_total):
        places = first_row + jnp.broadcast_to(
            jnp.arange(row_total, dtype=jnp.int32)[:, None], (row_total, seq_count)
        )
        return (places, jnp.ones((row_total, seq_count), jnp.bool_))

    slot_rows = jnp.arange(most_rows, dtype=jnp.int32)
    is_live = slot_rows[:, None] < routed_here[None, :]
    hold_places = (
        jnp.take_along_axis(
            route_rows, jnp.clip(first_rank[None, :] + slot_rows[:, None], 0, capacity - 1), axis=0
        )
        - my_index * group_rows
    )
    hold_table = (
        (jnp.transpose(hold_places)[:, :, None] == local_ids[None, None, :])
        & jnp.transpose(is_live)[:, :, None]
    ).astype(jnp.bfloat16)

    def select_rows(rows_in):
        return jnp.einsum(
            "smc,csd->msd", hold_table, rows_in, preferred_element_type=jnp.float32
        ).astype(jnp.bfloat16)

    def restore_rows(rows_in):
        return jnp.einsum("smc,msd->csd", hold_table, rows_in, preferred_element_type=jnp.float32)

    def routed_info(first_row, row_total):
        number = first_row + jnp.arange(row_total, dtype=jnp.int32)
        source = number // most_rows
        within = number % most_rows
        base = jnp.take(starts, source, axis=0)
        filled = jnp.take(starts, source + 1, axis=0) - base
        rank_rows = jnp.clip(base + within[:, None], 0, capacity - 1)
        return (jnp.take_along_axis(route_rows, rank_rows, axis=0), within[:, None] < filled)

    hidden = tokens.astype(jnp.float32)
    _, middle, feed_out, dense_stored = block_forward(hidden, dense_params, dense_info, label_rows)
    first_out = middle + feed_out
    lifted = select_rows(first_out.astype(jnp.bfloat16))
    routed_attention, _, routed_feed, routed_stored = block_forward(
        lifted.astype(jnp.float32), routed_params, routed_info, label_rows
    )
    sent_rows = (routed_attention + routed_feed).astype(jnp.bfloat16)
    returned = restore_rows(sent_rows)
    router_float = router.astype(jnp.float32)
    gate_value = jax.nn.sigmoid(jnp.einsum("csd,d->cs", first_out, router_float, precision=PRECISE))
    output = first_out + gate_value[:, :, None] * returned
    grad_output = cotangent.astype(jnp.float32)
    grad_sent = select_rows((gate_value[:, :, None] * grad_output).astype(jnp.bfloat16))
    grad_logit = jnp.sum(grad_output * returned, axis=-1) * gate_value * (1.0 - gate_value)
    grad_router = jnp.einsum("cs,csd->d", grad_logit, first_out, precision=PRECISE)
    grad_first = grad_output + grad_logit[:, :, None] * router_float
    routed_branch, routed_grads = block_backward(
        grad_sent.astype(jnp.float32), routed_stored, routed_params, routed_info, label_rows
    )
    grad_first = grad_first + restore_rows(routed_branch.astype(jnp.bfloat16))
    dense_branch, dense_grads = block_backward(
        grad_first, dense_stored, dense_params, dense_info, label_rows
    )
    grad_tokens = grad_first + dense_branch
    summed_all = (
        lax.psum_scatter(dense_grads[0], "seq", scatter_dimension=0, tiled=True),
        lax.psum_scatter(dense_grads[1], "seq", scatter_dimension=0, tiled=True),
        lax.psum_scatter(dense_grads[2], "seq", scatter_dimension=1, tiled=True),
        lax.psum_scatter(dense_grads[3], "seq", scatter_dimension=0, tiled=True),
        lax.psum_scatter(dense_grads[4], "seq", scatter_dimension=0, tiled=True),
        lax.psum_scatter(dense_grads[5], "seq", scatter_dimension=1, tiled=True),
        lax.psum_scatter(routed_grads[0], "seq", scatter_dimension=0, tiled=True),
        lax.psum_scatter(routed_grads[1], "seq", scatter_dimension=0, tiled=True),
        lax.psum_scatter(routed_grads[2], "seq", scatter_dimension=1, tiled=True),
        lax.psum_scatter(routed_grads[3], "seq", scatter_dimension=0, tiled=True),
        lax.psum_scatter(routed_grads[4], "seq", scatter_dimension=0, tiled=True),
        lax.psum_scatter(routed_grads[5], "seq", scatter_dimension=1, tiled=True),
        lax.psum_scatter(grad_router, "seq", scatter_dimension=0, tiled=True),
    )
    dense_sums = tuple(summed_all[0:6])
    routed_sums = tuple(summed_all[6:13])
    return (output, grad_tokens) + tuple(dense_sums) + tuple(routed_sums)


BF = jnp.bfloat16
LIMIT = 63 * 1024 * 1024
F32 = jnp.float32
MESH = pl.DeviceIdType.MESH
PIECE = 1024
WIDTHS = (384, 128, 512, 512)
BEGINS = (0, 384, 512, 1024)
SIZES = (1536, 512, 2048, 2048)
COLS = (None, (0, 512), (512, 2048), None)


def dot(a, b):
    return lax.dot_general(a, b, (((1,), (0,)), ((), ())), preferred_element_type=F32)


def dot_t(a, b):
    return lax.dot_general(a, b, (((1,), (1,)), ((), ())), preferred_element_type=F32)


def dot_l(a, b):
    return lax.dot_general(a, b, (((0,), (0,)), ((), ())), preferred_element_type=F32)


def swap_halves(tile):
    return pltpu.roll(tile, 64, 1)


def low_lanes(rows):
    return lax.broadcasted_iota(jnp.int32, (rows, 128), 1) < 64


def inverse_rms(rows):
    return lax.rsqrt(jnp.mean(rows * rows, axis=1, keepdims=True) + EPSILON)


def norm_back(grad, rows, gain):
    inverse = inverse_rms(rows)
    unit = rows * inverse
    pulled = grad * gain
    grad_rows = inverse * (pulled - unit * jnp.mean(pulled * unit, axis=1, keepdims=True))
    return grad_rows, jnp.sum(grad * unit, axis=0, keepdims=True)


class Env:
    def __init__(self, refs, sems, seq_size):
        self.b = refs
        self.sems = sems
        self.count = 0
        self.sends = []
        self.middle_sends = []
        self.flying = {}
        self.stores = {}
        self.stored = 0
        self.barrier_done = False
        self.n = seq_size
        self.s = lax.axis_index("seq")
        self.c = lax.axis_index("mp")
        self.q = lax.rem(self.s, 4)
        self.z = lax.div(self.s, 4)
        high = lax.div(self.z, 2)
        self.near = self.z + 1 - 2 * lax.rem(self.z, 2)
        self.across = 2 - high
        self.far = 3 - 3 * high
        self.middle = lax.rem(self.z + high, 2) == 1

    def sem(self):
        self.count += 1
        return self.sems.at[self.count - 1]

    def vector(self, number):
        return self.b.vectors[number][...].astype(F32).reshape(1, 1024)

    def greet(self):
        barrier = pltpu.get_barrier_semaphore()

        def signal(step, _):
            other = lax.rem(self.s + step, self.n)
            pl.semaphore_signal(barrier, inc=1, device_id=(other, self.c), device_id_type=MESH)
            return 0

        lax.fori_loop(1, self.n, signal, 0)
        pl.semaphore_signal(barrier, inc=1, device_id=(self.s, 1 - self.c), device_id_type=MESH)

    def meet(self):
        if not self.barrier_done:
            pl.semaphore_wait(pltpu.get_barrier_semaphore(), self.n)
            self.barrier_done = True

    def remote(self, src, dst, send, recv, seq, core):
        return pltpu.make_async_remote_copy(
            src_ref=src,
            dst_ref=dst,
            send_sem=send,
            recv_sem=recv,
            device_id=(seq, core),
            device_id_type=MESH,
        )

    def exchange(self, send_ref, recv_ref):
        self.meet()
        send, recv = self.sem(), self.sem()
        n = self.n

        def start(step, _):
            other = lax.rem(self.s + step, n)
            self.remote(
                send_ref.at[other], recv_ref.at[self.s], send, recv, other, self.c
            ).start()
            return 0

        lax.fori_loop(1, n, start, 0)
        recv_ref[pl.ds(self.s, 1)] = send_ref[pl.ds(self.s, 1)]
        whole = self.remote(
            send_ref.at[pl.ds(0, n - 1)],
            recv_ref.at[pl.ds(0, n - 1)],
            send,
            recv,
            lax.rem(self.s + 1, n),
            self.c,
        )
        self.sends.append(whole)
        return whole.wait_recv

    def core_sum(self, layer, half, chunk, sink):
        self.meet()
        send_ref, recv_ref = layer.b.ps.at[half], layer.b.pr.at[half]
        copies = []
        for number in range(4):
            earlier = self.flying.pop((layer.packed, half, number), None)
            if earlier is not None:
                earlier.wait_send()
            send_ref[number] = chunk(number).astype(BF)
            copy = self.remote(
                send_ref.at[number], recv_ref.at[number], self.sem(), self.sem(), self.s, 1 - self.c
            )
            copy.start()
            copies.append(copy)
            self.flying[(layer.packed, half, number)] = copy
        for number, copy in enumerate(copies):
            copy.wait_recv()
            sink(number, send_ref[number].astype(F32) + recv_ref[number].astype(F32))

    def plane_send(self, pieces, recv_piece, wait_piece):
        self.meet()
        send, recv = self.sem(), self.sem()
        for step in range(1, 4):
            other = lax.rem(self.q + step, 4)
            self.remote(
                pieces(other), recv_piece, send, recv, self.z * 4 + other, self.c
            ).start()
        whole = self.remote(wait_piece, wait_piece, send, recv, self.z * 4 + lax.rem(self.q + 1, 4), self.c)
        self.sends.append(whole)
        return whole.wait_recv

    def line_send(self, pieces, recv_piece, wait_piece):
        self.meet()
        send, recv = self.sem(), self.sem()
        for step in range(1, 4):
            other = lax.rem(self.z + step, 4)
            self.remote(
                pieces(other), recv_piece(step), send, recv, other * 4 + self.q, self.c
            ).start()
        whole = self.remote(wait_piece, wait_piece, send, recv, lax.rem(self.z + 1, 4) * 4 + self.q, self.c)
        self.sends.append(whole)
        return whole.wait_recv

    def line_reduce(self, blocks, slots):
        self.meet()
        receive = [self.sem() for _ in range(4)]
        send = [self.sem() for _ in range(3)]

        def copy(block, slot, way, z):
            return self.remote(
                blocks.at[block], slots.at[slot], send[way], receive[slot], z * 4 + self.q, self.c
            )

        @pl.when(jnp.logical_not(self.middle))
        def _():
            copy(self.far, 3, 2, self.near).start()
            copy(self.across, 2, 1, self.near).start()

        copy(self.near, 0, 0, self.near).start()

        self.sends += [copy(0, 0, way, self.near) for way in range(3)]

        def arrived(slot):
            copy(0, slot, 0, self.near).wait_recv()

        def pass_on(slot):
            block = (self.across, self.far)[slot - 2]
            copy(block, 1, slot - 1, block).start()

        def finish():
            for slot in range(2):
                copy(0, slot, 0, self.near).wait_recv()

        return arrived, pass_on, finish

    def line_gather(self, ref):
        self.meet()
        receive = [self.sem() for _ in range(3)]
        send = [self.sem() for _ in range(5)]

        def copy(piece, way, slot, z):
            return self.remote(
                ref.at[piece], ref.at[piece], send[way], receive[slot], z * 4 + self.q, self.c
            )

        copy(self.z, 0, 0, self.near).start()

        @pl.when(self.middle)
        def _():
            copy(self.z, 1, 1, self.across).start()

        def second():
            @pl.when(self.middle)
            def _():
                copy(0, 0, 0, self.near).wait_recv()
                copy(self.near, 2, 2, self.across).start()
                copy(0, 0, 1, self.near).wait_recv()
                copy(self.across, 3, 1, self.near).start()

        def third():
            @pl.when(self.middle)
            def _():
                copy(0, 0, 2, self.near).wait_recv()
                copy(self.far, 4, 2, self.near).start()

        self.sends.append(copy(0, 0, 0, self.near))
        self.middle_sends += [copy(0, way, 0, self.near) for way in range(1, 5)]

        def finish():
            @pl.when(jnp.logical_not(self.middle))
            def _():
                for slot in range(3):
                    copy(0, 0, slot, self.near).wait_recv()

        return second, third, finish

    def store(self, result, which, at, fill):
        slot = self.stored % 4
        self.stored += 1
        if slot in self.stores:
            self.stores.pop(slot).wait()
        stage = self.b.stage.at[slot]
        fill(stage)
        target = result.at[at // 512] if which == 0 else result.at[:, pl.ds(at, 512)]
        copy = pltpu.make_async_copy(stage, target, self.sem())
        copy.start()
        self.stores[slot] = copy

    def drain(self):
        for copy in self.sends + list(self.flying.values()):
            copy.wait_send()
        for copy in self.stores.values():
            copy.wait()

        @pl.when(self.middle)
        def _():
            for copy in self.middle_sends:
                copy.wait_send()


class Layer:
    def __init__(self, packed, per, n):
        self.per = per
        self.n = n
        self.rows = 2 * per
        self.packed = packed
        self.value_rows = per // 2 if self.packed else per
        self.message = per + self.value_rows
        self.total = n * per
        self.block = 256
        self.gains = (0, 1) if packed else (2, 3)

    def attach(self, env, refs, sources, weights, results):
        self.b = refs
        self.sources = sources
        self.held = weights
        self.results = results
        self.right_waits, self.left_waits, self.line_waits, self.hops = {}, {}, {}, {}
        self.loads = {}

    def load(self, env, number):
        copy = pltpu.make_async_copy(self.sources[number], self.held[number], env.sem())
        copy.start()
        self.loads[number] = copy

    def weight(self, number):
        if number in self.loads:
            self.loads.pop(number).wait()
        return self.held[number]

    def buffers(self):
        r, t, n = self.rows, self.total, self.n
        vr, m = self.value_rows, self.message
        table = dict(
            x=((r, 1024), BF),
            normed=((r, 1024), BF),
            s1=((n, m, 128), BF),
            r1=((n, m, 128), BF),
            qa=((t, 128), BF),
            kb=((t, 128), BF),
            va=((t, 128), BF),
            mixp=((t, 128), F32),
            lse=((t, 128), F32),
            s2=((n, vr, 128), BF),
            r2=((n, vr, 128), BF),
            mixl=((r, 512), BF),
            mid=((r, 1024), F32),
            nm=((r, 1024), BF),
            gp=((r, 2048), BF),
            act=((r, 2048), BF),
            e=((r, 1024), F32),
            el=((r, 1024), BF),
            gb=((r, 2048), BF),
            gm=((r, 1024), F32),
            al=((r, 1024), BF),
            s6=((n, vr, 128), BF),
            r6=((n, vr, 128), BF),
            gx=((t, 128), BF),
            dk=((t, 128), F32),
            dv=((t, 128), F32),
            s7=((n, m, 128), BF),
            r7=((n, m, 128), BF),
            dp=((r, 1536), BF),
            acc=((r, 1024), F32),
            ps=((2, 4, r, 256), BF),
            pr=((2, 4, r, 256), BF),
        )
        if self.packed:
            table.update(
                ng=((4, 4, self.per, 1024), BF),
                x7=((t, 256), BF),
                s9=((n, m, 128), BF),
                r9=((n, m, 128), BF),
                fg=((4, r, 2560), BF),
                ds=((4, r, 512), BF),
                dg=((4, r, 512), BF),
                sb=((4, 64, 2560), BF),
                rb=((4, 64, 2560), BF),
                ul=((4, r, 1024), BF),
                ur=((4, r, 512), BF),
                us=((4, 256, 512), BF),
                ub=((4, 256, 512), BF),
                ux=((4, 64, 512), BF),
                uy=((4, 64, 512), BF),
            )
        else:
            table.update(
                fg=((4, 4, r, 1536), BF),
                dg=((4, 4, r, 1024), BF),
                sb=((4, 64, 1536), BF),
                rb=((4, 64, 1536), BF),
                same=((t, t), F32),
                lab=((t, 128), BF),
                hot=((2, self.per, 64), BF),
                labs=((r, 128), F32),
            )
        return table

    def gain(self, env, which):
        return env.vector(self.gains[which])

    def pack(self, tile):
        if not self.packed:
            return tile
        half = self.per // 2
        return jnp.where(low_lanes(half), tile[:half], swap_halves(tile[half:]))

    def send_pairs(self, store, tile_of):
        for seq in range(2):
            for j in range(4):
                tile = tile_of(seq, j)
                store(8 * seq + 2 * j, self.pack(tile))
                store(8 * seq + 2 * j + 1, self.pack(swap_halves(tile)))

    def join_pairs(self, tile_a, tile_b):
        vr = self.value_rows
        low = low_lanes(vr)
        first = jnp.where(low, tile_a, swap_halves(tile_b))
        if not self.packed:
            return [first]
        return [first, jnp.where(low, swap_halves(tile_a), tile_b)]

    def project(self, env, then=None):
        hidden = self.b.x[...].astype(F32)
        normed = (hidden * inverse_rms(hidden) * self.gain(env, 0)).astype(BF)
        self.b.normed[...] = normed
        weight = self.weight(QKV)
        if then is not None:
            then()
        queries, keys, values = (dot(normed, weight[part]) for part in range(3))
        send = self.b.s1
        per = self.per
        low = low_lanes(per)
        for seq in range(2):
            rows = slice(seq * per, (seq + 1) * per)
            for j in range(4):
                cols = slice(128 * j, 128 * j + 128)
                qt, kt, vt = queries[rows, cols], keys[rows, cols], values[rows, cols]
                pair = 8 * seq + 2 * j
                send[pair, 0:per] = jnp.where(low, qt, swap_halves(kt)).astype(BF)
                send[pair + 1, 0:per] = jnp.where(low, swap_halves(qt), kt).astype(BF)
                va, vb = vt, swap_halves(vt)
                if self.packed:
                    va, vb = self.pack(va), self.pack(vb)
                else:
                    labels = self.b.labs[rows, :]
                    va, vb = jnp.where(low, va, labels), jnp.where(low, vb, labels)
                send[pair, per:] = va.astype(BF)
                send[pair + 1, per:] = vb.astype(BF)
        self.wait1 = env.exchange(send, self.b.r1)

    def unpack(self, env):
        recv = self.b.r1
        qa, kb, va = self.b.qa, self.b.kb, self.b.va
        per, vr = self.per, self.value_rows
        low, low_v = low_lanes(per), low_lanes(vr)
        zero = jnp.zeros((per, 128), F32)
        zero_v = jnp.zeros((vr, 128), F32)
        for i in range(self.n):
            both = recv[i, 0:per].astype(F32)
            qa[i * per : (i + 1) * per] = jnp.where(low, both * 0.125, zero).astype(BF)
            kb[i * per : (i + 1) * per] = swap_halves(both).astype(BF)
            tile = recv[i, per:].astype(F32)
            va[i * per : i * per + vr] = jnp.where(low_v, tile, zero_v).astype(BF)
            if self.packed:
                va[i * per + vr : (i + 1) * per] = jnp.where(low_v, swap_halves(tile), zero_v).astype(BF)
            else:
                self.b.lab[i * per : (i + 1) * per] = jnp.where(low_v, zero_v, tile).astype(BF)
        if not self.packed:
            labels = self.b.lab[...]
            self.b.same[...] = dot_t(labels, labels)

    def allowed(self, env, start, stop):
        size = stop - start
        rows = lax.broadcasted_iota(jnp.int32, (size, stop), 0) + start
        keys = lax.broadcasted_iota(jnp.int32, (size, stop), 1)
        ok = keys <= rows
        if self.packed:
            segments = env.b.segments[pl.ds(lax.div(env.s, 8), 1), :]
            row = (lax.broadcasted_iota(jnp.int32, (size, 1), 0) + start).astype(F32)
            opening = jnp.zeros((size, 1), F32)
            for label in range(1, 4):
                edge = jnp.sum((segments < label).astype(F32), axis=1, keepdims=True)
                opening = jnp.where(row >= edge, jnp.maximum(opening, edge), opening)
            return ok & (keys >= opening.astype(jnp.int32))
        return ok & (self.b.same[start:stop, 0:stop] > 0.5)

    def attend(self, env):
        self.wait1()
        self.unpack(env)
        qa, kb, va = self.b.qa, self.b.kb, self.b.va
        mixp, lse = self.b.mixp, self.b.lse
        for start in range(0, self.total, self.block):
            stop = start + self.block
            scores = dot_t(qa[start:stop], kb[0:stop])
            scores = jnp.where(self.allowed(env, start, stop), scores, NEGATIVE)
            highest = jnp.max(scores, axis=1, keepdims=True)
            weights = jnp.exp(scores - highest)
            totals = jnp.sum(weights, axis=1, keepdims=True)
            mixp[start:stop] = dot(weights.astype(BF), va[0:stop]) / totals
            lse[start:stop] = jnp.broadcast_to(highest + jnp.log(totals), (self.block, 128))
        send = self.b.s2
        for i in range(self.n):
            send[i] = self.pack(mixp[i * self.per : (i + 1) * self.per]).astype(BF)
        self.wait2 = env.exchange(send, self.b.r2)

    def gather_heads(self, recv, row0, put):
        per, vr = self.per, self.value_rows
        for seq in range(2):
            for j in range(4):
                pair = 8 * seq + 2 * j
                tiles = self.join_pairs(
                    recv[pair, row0:].astype(F32), recv[pair + 1, row0:].astype(F32)
                )
                for number, tile in enumerate(tiles):
                    begin = seq * per + number * vr
                    put(slice(begin, begin + vr), slice(128 * j, 128 * j + 128), tile)

    def feed(self, env, finish, then=None):
        self.wait2()
        mixl = self.b.mixl

        def put(rows, cols, tile):
            mixl[rows, cols] = tile.astype(BF)

        self.gather_heads(self.b.r2, 0, put)
        out = self.weight(OUT)
        mid = self.b.mid
        hidden = self.b.x
        mixed = mixl[...]

        def sink(number, value):
            cols = slice(256 * number, 256 * number + 256)
            mid[:, cols] = value + hidden[:, cols].astype(F32)

        env.core_sum(
            self,
            0,
            lambda number: dot(mixed, out[:, 256 * number : 256 * number + 256]),
            sink,
        )
        middle = mid[...]
        normed = (middle * inverse_rms(middle) * self.gain(env, 1)).astype(BF)
        self.b.nm[...] = normed
        up = self.weight(UP)
        act, slope = self.b.act, self.b.gp
        for number in range(4):
            cols = slice(512 * number, 512 * number + 512)
            before = dot(normed, up[:, cols])
            square = before * before
            bent = jnp.tanh(0.7978845608028654 * before * (1.0 + 0.044715 * square))
            half = 0.5 * (1.0 + bent)
            act[:, cols] = (before * half).astype(BF)
            slope[:, cols] = (
                half
                + 0.5 * before * (1.0 - bent * bent) * (0.7978845608028654 + 0.1070322243 * square)
            ).astype(BF)
        if then is not None:
            then()
        down = self.weight(DOWN)
        env.core_sum(
            self,
            1,
            lambda number: dot(act[...], down[:, 256 * number : 256 * number + 256]),
            finish,
        )

    def round_incoming(self):
        self.b.el[...] = self.b.e[...].astype(BF)

    def back_feed(self, env):
        grad_low = self.b.el[...]
        down, up, out = self.weight(DOWN), self.weight(UP), self.weight(OUT)
        gb, slope = self.b.gb, self.b.gp
        for number in range(4):
            cols = slice(512 * number, 512 * number + 512)
            grad = dot_t(grad_low, down[cols, :])
            gb[:, cols] = (grad * slope[:, cols].astype(F32)).astype(BF)
        acc = self.b.acc

        def sink(number, value):
            acc[:, 256 * number : 256 * number + 256] = value

        env.core_sum(
            self,
            0,
            lambda number: dot_t(gb[...], up[256 * number : 256 * number + 256, :]),
            sink,
        )
        grad_mid, grad_gain = norm_back(acc[...], self.b.mid[...], self.gain(env, 1))
        row = self.gains[1]
        env.b.vg[row : row + 1, :] = grad_gain
        self.b.gm[...] = grad_mid
        along = (self.b.e[...] + grad_mid).astype(BF)
        self.b.al[...] = along
        grad_mixed = dot_t(along, out[...])
        send = self.b.s6
        per = self.per

        def store(pair, tile):
            send[pair] = tile.astype(BF)

        self.send_pairs(
            store,
            lambda seq, j: grad_mixed[seq * per : (seq + 1) * per, 128 * j : 128 * j + 128],
        )
        self.wait6 = env.exchange(send, self.b.r6)

    def back_attend(self, env):
        self.wait6()
        recv, gx = self.b.r6, self.b.gx
        per, vr = self.per, self.value_rows
        low_v = low_lanes(vr)
        zero_v = jnp.zeros((vr, 128), F32)
        for i in range(self.n):
            tile = recv[i].astype(F32)
            gx[i * per : i * per + vr] = jnp.where(low_v, tile, zero_v).astype(BF)
            if self.packed:
                gx[i * per + vr : (i + 1) * per] = jnp.where(low_v, swap_halves(tile), zero_v).astype(BF)
        qa, kb, va = self.b.qa, self.b.kb, self.b.va
        mixp, lse = self.b.mixp, self.b.lse
        dk, dv = self.b.dk, self.b.dv
        dk[...] = jnp.zeros_like(dk)
        dv[...] = jnp.zeros_like(dv)
        dq = {}
        for start in range(0, self.total, self.block):
            stop = start + self.block
            query, grad = qa[start:stop], gx[start:stop]
            scores = dot_t(query, kb[0:stop])
            scores = jnp.where(self.allowed(env, start, stop), scores, NEGATIVE)
            probs = jnp.exp(scores - lse[start:stop, 0:1])
            offsets = jnp.sum(grad.astype(F32) * mixp[start:stop], axis=1, keepdims=True)
            slopes = (probs * (dot_t(grad, va[0:stop]) - offsets)).astype(BF)
            mixp[start:stop] = dot(slopes, kb[0:stop])
            dk[0:stop] += dot_l(slopes, query)
            dv[0:stop] += dot_l(probs.astype(BF), grad)
        send = self.b.s7
        low = low_lanes(per)
        for i in range(self.n):
            rows = slice(i * per, (i + 1) * per)
            send[i, 0:per] = jnp.where(low, mixp[rows] * 0.125, swap_halves(dk[rows])).astype(BF)
            send[i, per:] = self.pack(dv[rows]).astype(BF)
            if self.packed:
                self.b.x7[rows, 0:128] = send[i, 0:per]
                self.b.x7[rows, 128:256] = dv[rows].astype(BF)
        self.wait7 = env.exchange(send, self.b.r7)

    def back_project(self, env, finish, then=None):
        self.wait7()
        recv, dp = self.b.r7, self.b.dp
        per = self.per
        low = low_lanes(per)
        for seq in range(2):
            rows = slice(seq * per, (seq + 1) * per)
            for j in range(4):
                pair = 8 * seq + 2 * j
                one, two = recv[pair, 0:per].astype(F32), recv[pair + 1, 0:per].astype(F32)
                dp[rows, 128 * j : 128 * j + 128] = jnp.where(low, one, swap_halves(two)).astype(BF)
                dp[rows, 512 + 128 * j : 640 + 128 * j] = jnp.where(low, swap_halves(one), two).astype(BF)

        def put(rows, cols, tile):
            dp[rows, 1024 + cols.start : 1024 + cols.stop] = tile.astype(BF)

        self.gather_heads(recv, per, put)
        if then is not None:
            then()
        weight = self.weight(QKV)
        acc = self.b.acc

        def chunk(number):
            rows = slice(256 * number, 256 * number + 256)
            total = dot_t(dp[:, 0:512], weight[0, rows, :])
            total += dot_t(dp[:, 512:1024], weight[1, rows, :])
            return total + dot_t(dp[:, 1024:1536], weight[2, rows, :])

        def sink(number, value):
            acc[:, 256 * number : 256 * number + 256] = value

        env.core_sum(self, 1, chunk, sink)
        grad_hidden, grad_gain = norm_back(
            acc[...], self.b.x[...].astype(F32), self.gain(env, 0)
        )
        row = self.gains[0]
        env.b.vg[row : row + 1, :] = grad_gain
        finish(self.b.gm[...] + grad_hidden)

    def parts(self, env, which):
        b = self.b
        left = (b.normed, b.al, b.nm, b.el)[which]
        right = (b.dp, b.mixl, b.gb, b.act)[which]
        return left, right

    def share_right(self, env, which, begin=0, size=None):
        at, full = COLS[which]
        size = full if size is None else size
        _, right = self.parts(env, which)
        fg = self.b.fg
        cols = pl.ds(at + begin, size)
        fg[pl.ds(env.q, 1), :, cols] = right[:, begin : begin + size][None]
        mine = fg.at[env.q, :, cols]
        self.right_waits.setdefault(which, []).append(
            env.plane_send(lambda other: mine, mine, fg.at[pl.ds(0, 3), :, cols])
        )

    def share_left(self, env, which):
        left, _ = self.parts(env, which)
        ds, dg = self.b.ds, self.b.dg
        low = low_lanes(self.rows)
        begin = 256 * (which - 1)
        for a in range(2):
            tiles = [
                left[:, 128 * (2 * z + a) : 128 * (2 * z + a) + 128].astype(F32) for z in range(4)
            ]
            for two in range(2):
                even, odd = tiles[2 * two], tiles[2 * two + 1]
                at = begin + 128 * two
                ds[2 * a, :, at : at + 128] = jnp.where(low, even, swap_halves(odd)).astype(BF)
                ds[2 * a + 1, :, at : at + 128] = jnp.where(low, swap_halves(even), odd).astype(BF)
        cols = pl.ds(begin, 256)
        dg[pl.ds(env.q, 1), :, begin : begin + 256] = ds[pl.ds(env.q, 1), :, begin : begin + 256]
        self.left_waits[which] = env.plane_send(
            lambda other: ds.at[other, :, cols],
            dg.at[env.q, :, cols],
            dg.at[pl.ds(0, 3), :, cols],
        )

    def multiply(self, env, which, first=0, last=None):
        if which in self.right_waits:
            for wait in self.right_waits.pop(which):
                wait()
            self.left_waits[which]()
        begin, size = COLS[which]
        last = size if last is None else last
        fg, dg, sb, rb = self.b.fg, self.b.dg, self.b.sb, self.b.rb
        rows = 4 * self.rows
        left = dg[:, :, 256 * (which - 1) : 256 * which].reshape(rows, 256)
        for at in range(begin + first, begin + last, 512):
            right = fg[:, :, at : at + 512].reshape(rows, 512)
            product = dot_l(left, right)
            for z in range(4):
                sb[z, :, at : at + 512] = product[64 * z : 64 * z + 64].astype(BF)
            if (at + 512 - begin) % PIECE == 0 or at + 512 == begin + last:
                low = begin + (at - begin) // PIECE * PIECE
                cols = pl.ds(low, at + 512 - low)
                steps = env.line_reduce(sb.at[:, :, cols], rb.at[:, :, cols])
                self.line_waits.setdefault(which, []).append((low, at + 512, steps))

    def relay(self, env, which, pieces=None):
        sb, rb = self.b.sb, self.b.rb
        for low, high, (arrived, pass_on, _) in self.line_waits[which][pieces or slice(None)]:

            @pl.when(env.middle)
            def _():
                for slot, block in ((3, env.far), (2, env.across)):
                    arrived(slot)
                    for at in range(low, high, 512):
                        cols = slice(at, at + 512)
                        total = sb[pl.ds(block, 1), :, cols].astype(F32)
                        total = total + rb[slot : slot + 1, :, cols].astype(F32)
                        sb[pl.ds(block, 1), :, cols] = total.astype(BF)
                    pass_on(slot)

    def collect(self, env, which):
        begin, _ = COLS[which]
        sb, rb = self.b.sb, self.b.rb
        for low, high, (_, _, finish) in self.line_waits[which]:
            finish()
            for at in range(low, high, 512):
                cols = slice(at, at + 512)

                def fill(stage):
                    total = sb[pl.ds(env.z, 1), :, cols].astype(F32)
                    for slot in range(2):
                        total = total + rb[slot : slot + 1, :, cols].astype(F32)
                    stage[...] = total[0]

                env.store(self.results[which], which, at - begin, fill)

    def quarter_left(self, env):
        ul, left = self.b.ul, self.b.el
        cols = pl.ds(pl.multiple_of(512 * env.c, 512), 512)
        ul[pl.ds(env.q, 1), :, cols] = left[:, cols][None]
        self.quarter_wait = env.plane_send(
            lambda other: left.at[:, cols], ul.at[env.q, :, cols], ul.at[pl.ds(0, 3), :, cols]
        )

    def quarter_core(self, env):
        self.quarter_wait()
        mine = self.b.ul.at[:, :, pl.ds(pl.multiple_of(512 * env.c, 512), 512)]
        copy = env.remote(mine, mine, env.sem(), env.sem(), env.s, 1 - env.c)
        copy.start()
        env.sends.append(copy)
        self.quarter_wait = copy.wait_recv

    def quarter_right(self, env):
        right, ur = self.b.act, self.b.ur

        def quarter(number):
            return pl.ds(pl.multiple_of(number * 512, 512), 512)

        ur[pl.ds(env.q, 1)] = right[:, quarter(env.q)][None]
        self.quarter_columns = env.plane_send(
            lambda other: right.at[:, quarter(other)], ur.at[env.q], ur.at[pl.ds(0, 3)]
        )

    def quarter_multiply(self, env):
        self.quarter_wait()
        self.quarter_columns()
        ul, ur, us, ub = self.b.ul, self.b.ur, self.b.us, self.b.ub
        rows = 4 * self.rows
        left = ul[...].reshape(rows, 1024)
        self.quarter_steps = []
        for at in range(0, 512, 256):
            product = dot_l(left, ur[:, :, at : at + 256].reshape(rows, 256))
            for z in range(4):
                us[z, :, at : at + 256] = product[256 * z : 256 * z + 256].astype(BF)
            cols = pl.ds(at, 256)
            self.quarter_steps.append(env.line_reduce(us.at[:, :, cols], ub.at[:, :, cols]))

    def quarter_relay(self, env):
        us, ub = self.b.us, self.b.ub
        for number, (arrived, pass_on, _) in enumerate(self.quarter_steps):
            cols = slice(256 * number, 256 * number + 256)

            @pl.when(env.middle)
            def _():
                for slot, block in ((3, env.far), (2, env.across)):
                    arrived(slot)
                    total = us[pl.ds(block, 1), :, cols].astype(F32)
                    total = total + ub[slot : slot + 1, :, cols].astype(F32)
                    us[pl.ds(block, 1), :, cols] = total.astype(BF)
                    pass_on(slot)

    def quarter_share(self, env):
        us, ub, ux, uy = self.b.us, self.b.ub, self.b.ux, self.b.uy
        for number, (_, _, finish) in enumerate(self.quarter_steps):
            finish()
            cols = slice(256 * number, 256 * number + 256)
            total = us[pl.ds(env.z, 1), :, cols].astype(F32)
            for slot in range(2):
                total = total + ub[slot : slot + 1, :, cols].astype(F32)
            for q in range(4):
                ux[q, :, cols] = total[0, 64 * q : 64 * q + 64].astype(BF)
        uy[pl.ds(env.q, 1)] = ux[pl.ds(env.q, 1)]
        self.quarter_back = env.plane_send(
            lambda other: ux.at[other], uy.at[env.q], uy.at[pl.ds(0, 3)]
        )

    def quarter_collect(self, env):
        self.quarter_back()
        for q in range(4):

            def fill(stage):
                stage[...] = self.b.uy[q].astype(F32)

            env.store(self.results[DOWN], DOWN, 512 * q, fill)

    def gather_line(self, env):
        normed, ng, per = self.b.normed, self.b.ng, self.per
        cols = pl.ds(pl.multiple_of(512 * env.c, 512), 512)

        def rows(z):
            return pl.ds(pl.multiple_of(lax.div(z, 2) * per, per), per)

        ng[pl.ds(env.z, 1), pl.ds(env.q, 1), :, cols] = normed[rows(env.z), cols][None, None]
        self.gather_wait = env.line_send(
            lambda other: normed.at[rows(other), cols],
            lambda step: ng.at[env.z, env.q, :, cols],
            ng.at[pl.ds(0, 3), 0, :, cols],
        )

    def gather_plane(self, env):
        self.gather_wait()
        ng = self.b.ng
        cols = pl.ds(pl.multiple_of(512 * env.c, 512), 512)
        mine = ng.at[:, env.q, :, cols]
        self.gather_wait = env.plane_send(lambda other: mine, mine, ng.at[:, pl.ds(0, 3), :, cols])

    def gather_core(self, env):
        self.gather_wait()
        cols = pl.ds(pl.multiple_of(512 * env.c, 512), 512)
        mine = self.b.ng.at[:, :, :, cols]
        copy = env.remote(mine, mine, env.sem(), env.sem(), env.s, 1 - env.c)
        copy.start()
        env.sends.append(copy)
        self.gather_wait = copy.wait_recv

    def head_gradient(self, env):
        self.gather_wait()
        per, total = self.per, self.total
        product = dot_l(self.b.x7[...], self.b.ng[...].reshape(total, 1024))
        turned = jnp.transpose(product)
        send = self.b.s9
        for i in range(self.n):
            rows = slice(i * 64, i * 64 + 64)
            send[i, 0:per] = turned[rows, 0:128].astype(BF)
            send[i, per:] = self.pack(turned[rows, 128:256]).astype(BF)
        self.wait9 = env.exchange(send, self.b.r9)

    def head_collect(self, env):
        self.wait9()
        recv, per, vr = self.b.r9, self.per, self.value_rows
        low = low_lanes(per)

        def both(pair, rows):
            return recv[pair, rows].astype(F32) + recv[pair + 8, rows].astype(F32)

        for part in range(3):

            def fill(stage):
                for j in range(4):
                    cols = slice(128 * j, 128 * j + 128)
                    rows = slice(0, per) if part < 2 else slice(per, per + vr)
                    one, two = both(2 * j, rows), both(2 * j + 1, rows)
                    if part == 0:
                        stage[:, cols] = jnp.where(low, one, swap_halves(two))
                    elif part == 1:
                        stage[:, cols] = jnp.where(low, swap_halves(one), two)
                    else:
                        first, second = self.join_pairs(one, two)
                        stage[0:vr, cols] = first
                        stage[vr:, cols] = second

            env.store(self.results[QKV], QKV, 512 * part, fill)

    def spread_right(self, env, which):
        _, right = self.parts(env, which)
        fg, width = self.b.fg, WIDTHS[which]
        cols = pl.ds(BEGINS[which], width)

        def quarter(number):
            return pl.ds(pl.multiple_of(number * width, 128), width)

        fg[pl.ds(env.z, 1), pl.ds(env.q, 1), :, cols] = right[:, quarter(env.q)][None, None]
        self.right_waits[which] = env.plane_send(
            lambda other: right.at[:, quarter(other)],
            fg.at[env.z, env.q, :, cols],
            fg.at[env.z, pl.ds(0, 3), :, cols],
        )

    def spread_right_on(self, env, which):
        self.right_waits[which]()
        fg = self.b.fg
        cols = pl.ds(BEGINS[which], WIDTHS[which])
        self.hops[which] = env.line_gather(fg.at[:, :, :, cols])

    def spread_hop(self, env, which, number):
        self.hops[which][number]()

    def spread_left(self, env, which):
        left, _ = self.parts(env, which)
        dg = self.b.dg
        cols = pl.ds(256 * which, 256)

        def quarter(number):
            return pl.ds(pl.multiple_of(number * 256, 256), 256)

        dg[pl.ds(env.z, 1), pl.ds(env.q, 1), :, cols] = left[:, quarter(env.z)][None, None]
        self.left_waits[which] = env.line_send(
            lambda other: left.at[:, quarter(other)],
            lambda step: dg.at[env.z, env.q, :, cols],
            dg.at[pl.ds(0, 3), env.q, :, cols],
        )

    def spread_left_on(self, env, which):
        self.left_waits[which]()
        dg = self.b.dg
        cols = pl.ds(256 * which, 256)
        mine = dg.at[:, env.q, :, cols]
        self.left_waits[which] = env.plane_send(
            lambda other: mine, mine, dg.at[:, pl.ds(0, 3), :, cols]
        )

    def spread_multiply(self, env, which):
        self.hops[which][2]()
        self.left_waits[which]()
        fg, dg, sb, rb = self.b.fg, self.b.dg, self.b.sb, self.b.rb
        width = WIDTHS[which]
        cols = pl.ds(BEGINS[which], width)
        rows = 16 * self.rows
        product = dot_l(
            dg[:, :, :, 256 * which : 256 * which + 256].reshape(rows, 256),
            fg[:, :, :, cols].reshape(rows, width),
        ).astype(BF)
        for number in range(4):
            sb[number, :, cols] = product[64 * number : 64 * number + 64]
        rb[pl.ds(env.q, 1), :, cols] = sb[pl.ds(env.q, 1), :, cols]
        self.line_waits[which] = env.plane_send(
            lambda other: sb.at[other, :, cols],
            rb.at[env.q, :, cols],
            rb.at[pl.ds(0, 3), :, cols],
        )

    def spread_collect(self, env, which):
        self.line_waits[which]()
        rb, begin, width = self.b.rb, BEGINS[which], WIDTHS[which]
        for at in range(0, SIZES[which], 512):

            def fill(stage):
                for inner in range(0, 512, 128):
                    source, offset = divmod(at + inner, width)
                    stage[:, inner : inner + 128] = rb[
                        source, :, begin + offset : begin + offset + 128
                    ].astype(F32)

            env.store(self.results[which], which, at, fill)


def pick_rows(env, dense, routed):
    hot, labs, first = routed.b.hot, routed.b.labs, env.b.first
    group, slots = dense.per, routed.per
    base = env.s * group
    for seq in range(2):
        listed = env.b.routed[seq : seq + 1, :]
        places = listed.shape[1]
        place = lax.broadcasted_iota(jnp.int32, (group, places), 0) + base
        here = (place == listed).astype(F32).astype(BF)
        before = jnp.sum((listed < base).astype(F32), axis=1, keepdims=True).astype(jnp.int32)
        number = lax.broadcasted_iota(jnp.int32, (slots, places), 1) - before
        slot = lax.broadcasted_iota(jnp.int32, (slots, places), 0)
        mine = (number == slot).astype(F32).astype(BF)
        table = dot_t(mine, here).astype(BF)
        hot[seq] = table
        segments = env.b.segments[seq : seq + 1, :]
        row = (lax.broadcasted_iota(jnp.int32, (group, 1), 0) + base).astype(F32)
        label = jnp.zeros((group, 1), F32)
        for number in range(1, 4):
            edge = jnp.sum((segments < number).astype(F32), axis=1, keepdims=True)
            label = label + (row >= edge).astype(F32)
        lane = lax.broadcasted_iota(jnp.int32, (group, 128), 1)
        one_hot = (lane == label.astype(jnp.int32) + 64).astype(F32).astype(BF)
        labs[seq * slots : (seq + 1) * slots, :] = dot(table, one_hot)
        rows = first[seq * group : (seq + 1) * group, :].astype(BF)
        routed.b.x[seq * slots : (seq + 1) * slots, :] = dot(table, rows).astype(BF)


def restore(env, dense, routed, sent, seq):
    slots = routed.per
    return dot_l(routed.b.hot[seq], sent[seq * slots : (seq + 1) * slots])


def gate_rows(env, dense, routed):
    group, slots = dense.per, routed.per
    sent = routed.b.acc[...].astype(BF)
    router = env.vector(4)
    grad_router = jnp.zeros((1, 1024), F32)
    for seq in range(2):
        rows = slice(seq * group, (seq + 1) * group)
        first = env.b.first[rows, :]
        returned = restore(env, dense, routed, sent, seq)
        gate = jax.nn.sigmoid(jnp.sum(first * router, axis=1, keepdims=True))
        env.b.output[rows, :] = first + gate * returned
        grad = env.b.cotangent[:, seq, :].astype(F32)
        low = (gate * grad).astype(BF)
        routed.b.e[seq * slots : (seq + 1) * slots, :] = dot(routed.b.hot[seq], low)
        logit = jnp.sum(grad * returned, axis=1, keepdims=True) * gate * (1.0 - gate)
        grad_router = grad_router + jnp.sum(logit * first, axis=0, keepdims=True)
        dense.b.e[rows, :] = grad + logit * router
    env.b.vg[4:5, :] = grad_router


def share_vectors(env):
    vg, sv, rv = env.b.vg, env.b.sv, env.b.rv
    for number in range(env.n):
        tile = vg[:, 128 * (number // 2) : 128 * (number // 2) + 128]
        sv[number] = swap_halves(tile) if number % 2 else tile
    return env.exchange(sv, rv)


def sum_vectors(env, wait):
    wait()
    total = env.b.rv[0]
    for number in range(1, env.n):
        total = total + env.b.rv[number]
    env.b.gvec[...] = total


QKV, OUT, UP, DOWN = range(4)
SHAPES = ((3, 1024, 512), (512, 1024), (1024, 2048), (2048, 1024))
GRADS = ((3, 64, 512), (64, 512), (64, 2048), (64, 2048))


def whole_step(env, dense, routed):
    env.greet()
    dense.load(env, QKV)
    for seq in range(2):
        dense.b.x[seq * dense.per : (seq + 1) * dense.per, :] = env.b.tokens[:, seq, :]
    env.b.vg[...] = jnp.zeros_like(env.b.vg)

    dense.project(env)
    for number in (OUT, UP, DOWN):
        dense.load(env, number)
    dense.gather_line(env)
    dense.attend(env)
    for number in range(4):
        routed.load(env, number)
    dense.gather_plane(env)
    mid_d, first = dense.b.mid, env.b.first

    def finish_dense(number, value):
        cols = slice(256 * number, 256 * number + 256)
        first[:, cols] = mid_d[:, cols] + value

    dense.feed(env, finish_dense)
    pick_rows(env, dense, routed)
    routed.project(env)
    dense.gather_core(env)
    dense.share_left(env, UP)
    dense.share_right(env, OUT)
    routed.attend(env)
    mid_r, x_r, sent = routed.b.mid, routed.b.x, routed.b.acc

    def finish_routed(number, value):
        cols = slice(256 * number, 256 * number + 256)
        sent[:, cols] = mid_r[:, cols] - x_r[:, cols].astype(F32) + value

    def spread_early():
        routed.spread_right(env, DOWN)
        routed.spread_right(env, OUT)

    routed.feed(env, finish_routed, spread_early)
    dense.quarter_right(env)
    routed.spread_left(env, QKV)
    routed.spread_left(env, UP)
    gate_rows(env, dense, routed)
    routed.round_incoming()
    routed.back_feed(env)
    routed.spread_right_on(env, DOWN)
    routed.spread_right_on(env, OUT)
    routed.spread_right(env, UP)
    routed.spread_left(env, DOWN)
    routed.spread_left(env, OUT)
    routed.back_attend(env)
    routed.spread_hop(env, DOWN, 0)
    routed.spread_hop(env, OUT, 0)
    routed.spread_right_on(env, UP)

    def finish_back(branch):
        low = branch.astype(BF)
        for seq in range(2):
            rows = slice(seq * dense.per, (seq + 1) * dense.per)
            dense.b.e[rows, :] += restore(env, dense, routed, low, seq)

    routed.back_project(env, finish_back, lambda: routed.spread_right(env, QKV))
    dense.round_incoming()
    dense.quarter_left(env)
    dense.back_feed(env)
    routed.spread_hop(env, DOWN, 1)
    routed.spread_hop(env, OUT, 1)
    routed.spread_hop(env, UP, 0)
    routed.spread_right_on(env, QKV)
    dense.share_left(env, OUT)
    dense.share_right(env, UP, 0, 1024)
    dense.quarter_core(env)
    dense.back_attend(env)
    routed.spread_hop(env, UP, 1)
    routed.spread_hop(env, QKV, 0)
    dense.quarter_multiply(env)
    dense.head_gradient(env)
    dense.multiply(env, OUT)
    dense.share_right(env, UP, 1024, 1024)
    routed.spread_left_on(env, DOWN)
    routed.spread_left_on(env, OUT)
    routed.spread_left_on(env, UP)
    routed.spread_left_on(env, QKV)

    def finish_tokens(branch):
        env.b.grad_tokens[...] = dense.b.e[...] + branch

    dense.back_project(env, finish_tokens)
    routed.spread_hop(env, QKV, 1)
    wait = share_vectors(env)
    dense.quarter_relay(env)
    dense.relay(env, OUT)
    dense.multiply(env, UP)
    for which in (DOWN, OUT, UP):
        routed.spread_multiply(env, which)
    dense.relay(env, UP)
    routed.spread_multiply(env, QKV)
    dense.quarter_share(env)
    dense.head_collect(env)
    for which in (DOWN, OUT, UP, QKV):
        routed.spread_collect(env, which)
    for which in (OUT, UP):
        dense.collect(env, which)
    sum_vectors(env, wait)
    dense.quarter_collect(env)
    env.drain()


def fused(group, tokens, cotangent, segments, routed_places, vectors, weights):
    n = lax.axis_size("seq")
    rows = 2 * group
    dense, routed = Layer(True, group, n), Layer(False, group // 4, n)
    wide = ((rows, 1024), F32)
    common = dict(
        stage=((4, 64, 512), F32),
        first=wide,
        vg=((8, 1024), F32),
        sv=((n, 8, 128), F32),
        rv=((n, 8, 128), F32),
    )
    groups = (dense.buffers(), routed.buffers(), common)
    scratch = [spec for table in groups for spec in table.values()]

    def kernel(*refs):
        refs = list(refs)

        def take(count):
            taken = refs[:count]
            del refs[:count]
            return taken

        inputs = take(4)
        vector_refs = take(5)
        sources = take(8)
        outputs = take(3)
        results = take(8)
        held = take(8)
        dense_refs, routed_refs, common_refs = (
            types.SimpleNamespace(**dict(zip(table, take(len(table)), strict=True))) for table in groups
        )
        b = common_refs
        b.tokens, b.cotangent, b.segments, b.routed = inputs
        b.output, b.grad_tokens, b.gvec = outputs
        b.vectors = vector_refs
        env = Env(b, refs[0], n)
        dense.attach(env, dense_refs, sources[:4], held[:4], results[:4])
        routed.attach(env, routed_refs, sources[4:], held[4:], results[4:])
        whole_step(env, dense, routed)

    vmem = pl.BlockSpec(memory_space=pltpu.VMEM)
    hbm = pl.BlockSpec(memory_space=pl.ANY)
    outs = [wide, wide, ((8, 128), F32)] + [(shape, F32) for shape in GRADS * 2]
    return pl.pallas_call(
        kernel,
        out_shape=[jax.ShapeDtypeStruct(*spec) for spec in outs],
        in_specs=[vmem] * 9 + [hbm] * 8,
        out_specs=[vmem] * 3 + [hbm] * 8,
        scratch_shapes=[pltpu.VMEM(shape, BF) for shape in SHAPES * 2]
        + [pltpu.VMEM(*spec) for spec in scratch]
        + [pltpu.SemaphoreType.DMA((384,))],
        compiler_params=pltpu.CompilerParams(
            collective_id=0, has_side_effects=True, vmem_limit_bytes=LIMIT
        ),
    )(tokens, cotangent, segments, routed_places, *vectors, *weights)


def place_results(group, parts):
    def kernel(*refs):
        output, grad_tokens, gvec = refs[:3]
        grads, outs, held = refs[3:11], refs[11:26], refs[26:34]
        sems = refs[34]
        loads = [
            pltpu.make_async_copy(source, target, sems.at[0, number])
            for number, (source, target) in enumerate(zip(grads, held, strict=True))
        ]
        for copy in loads:
            copy.start()
        for source, target in ((output, outs[0]), (grad_tokens, outs[1])):
            for seq in range(2):
                target[:, seq, :] = source[seq * group : (seq + 1) * group, :]
        for number in range(5):
            outs[2 + number][...] = gvec[number, 0:64]
        stores = []
        for number, copy in enumerate(loads):
            copy.wait()
            stores.append(pltpu.make_async_copy(held[number], outs[7 + number], sems.at[1, number]))
            stores[-1].start()
        for copy in stores:
            copy.wait()

    vmem = pl.BlockSpec(memory_space=pltpu.VMEM)
    hbm = pl.BlockSpec(memory_space=pl.ANY)
    shapes = [(group, 2, 1024)] * 2 + [(64,)] * 5 + list(GRADS * 2)
    return pl.pallas_call(
        kernel,
        out_shape=[jax.ShapeDtypeStruct(shape, F32) for shape in shapes],
        in_specs=[vmem] * 3 + [hbm] * 8,
        out_specs=[vmem] * 7 + [hbm] * 8,
        scratch_shapes=[pltpu.VMEM(shape, F32) for shape in GRADS * 2]
        + [pltpu.SemaphoreType.DMA((2, 8))],
        compiler_params=pltpu.CompilerParams(vmem_limit_bytes=LIMIT),
    )(*parts)


def on_device_fused(
    tokens,
    segments,
    routed,
    router,
    dense_attn_gain,
    dense_qkv,
    dense_out,
    dense_mlp_gain,
    dense_up,
    dense_down,
    routed_attn_gain,
    routed_qkv,
    routed_out,
    routed_mlp_gain,
    routed_up,
    routed_down,
    cotangent,
):
    group = tokens.shape[0]
    parts = fused(
        group,
        tokens,
        cotangent,
        segments,
        routed,
        (dense_attn_gain, dense_mlp_gain, routed_attn_gain, routed_mlp_gain, router),
        (
            jnp.transpose(dense_qkv, (1, 0, 2)),
            dense_out,
            dense_up,
            dense_down,
            jnp.transpose(routed_qkv, (1, 0, 2)),
            routed_out,
            routed_up,
            routed_down,
        ),
    )
    placed = place_results(group, parts)
    vectors = placed[2:7]

    def weights_of(grads, first, second):
        return (
            vectors[first],
            jnp.transpose(grads[QKV], (1, 0, 2)),
            jnp.transpose(grads[OUT]),
            vectors[second],
            grads[UP],
            jnp.transpose(grads[DOWN]),
        )

    return (
        tuple(placed[:2])
        + weights_of(placed[7:11], 0, 1)
        + weights_of(placed[11:], 2, 3)
        + (vectors[4],)
    )


def solution(mesh):
    in_specs = (
        P("seq", None, None),
        P(),
        P(),
        P(),
        P(),
        P(None, None, "mp"),
        P("mp", None),
        P(),
        P(None, "mp"),
        P("mp", None),
        P(),
        P(None, None, "mp"),
        P("mp", None),
        P(),
        P(None, "mp"),
        P("mp", None),
        P("seq", None, None),
    )
    out_specs = (
        P("seq", None, None),
        P("seq", None, None),
        P("seq"),
        P("seq", None, "mp"),
        P("mp", "seq"),
        P("seq"),
        P("seq", "mp"),
        P("mp", "seq"),
        P("seq"),
        P("seq", None, "mp"),
        P("mp", "seq"),
        P("seq"),
        P("seq", "mp"),
        P("mp", "seq"),
        P("seq"),
    )
    seq_size = mesh.shape["seq"]
    pairs = 2 * (16 // mesh.shape["mp"])
    body = on_device_fused if seq_size == pairs else on_device

    return jax.shard_map(
        body, mesh=mesh, in_specs=in_specs, out_specs=out_specs, check_vma=False
    )
```

```python
import math
import types

import jax
import jax.numpy as jnp
from jax import lax
from jax.experimental import pallas as pl
from jax.experimental.pallas import tpu as pltpu
from jax.sharding import PartitionSpec as P

HEAD_DIM = 64


EPSILON = 1e-06
NEGATIVE = -1e30
PRECISE = lax.Precision.HIGHEST


def rms_norm(hidden, gain):
    return hidden * lax.rsqrt(jnp.mean(hidden * hidden, axis=-1, keepdims=True) + EPSILON) * gain


def gelu_tanh(operand):
    return jax.nn.gelu(operand, approximate=True)


def model_sum(operand):
    return lax.psum(operand, "mp")


def block_loop(row_total, advance, carried):
    block_size = math.gcd(row_total, 512)
    return lax.fori_loop(
        0,
        row_total // block_size,
        lambda number, current: advance(current, number * block_size, block_size),
        carried,
    )


def key_mask(query_places, query_live, key_places, key_live, label_rows):
    query_labels = jnp.take_along_axis(label_rows, query_places, axis=0)
    key_labels = jnp.take_along_axis(label_rows, key_places, axis=0)
    allowed = jnp.transpose(key_places)[:, None, :] <= jnp.transpose(query_places)[:, :, None]
    allowed = allowed & (
        jnp.transpose(key_labels)[:, None, :] == jnp.transpose(query_labels)[:, :, None]
    )
    allowed = allowed & jnp.transpose(key_live)[:, None, :] & jnp.transpose(query_live)[:, :, None]
    return allowed[:, None]


def attend_forward(queries, key_rows, value_rows, own_places, own_live, row_info, label_rows):
    row_count, seq_count, head_count, head_size = queries.shape
    score_scale = head_size ** (-0.5)
    shape_rows = (seq_count, head_count, row_count)
    initial = (
        jnp.full(shape_rows, NEGATIVE, jnp.float32),
        jnp.zeros(shape_rows, jnp.float32),
        jnp.zeros(shape_rows + (head_size,), jnp.float32),
    )
    key_piece = lax.all_gather(key_rows, "seq", axis=0, tiled=True)
    value_piece = lax.all_gather(value_rows, "seq", axis=0, tiled=True)

    def advance(current, offset, block_size):
        highest, totals, summed = current
        key_block = lax.dynamic_slice_in_dim(key_piece, offset, block_size, 0).reshape(
            block_size, seq_count, head_count, head_size
        )
        value_block = lax.dynamic_slice_in_dim(value_piece, offset, block_size, 0).reshape(
            block_size, seq_count, head_count, head_size
        )
        key_places, key_live = row_info(offset, block_size)
        allowed = key_mask(own_places, own_live, key_places, key_live, label_rows)
        scores = (
            jnp.einsum("qshe,kshe->shqk", queries, key_block, preferred_element_type=jnp.float32)
            * score_scale
        )
        scores = jnp.where(allowed, scores, NEGATIVE)
        newest = jnp.maximum(highest, jnp.max(scores, axis=-1))
        weights = jnp.exp(scores - newest[..., None])
        factor = jnp.exp(highest - newest)
        totals = totals * factor + jnp.sum(weights, axis=-1)
        summed = summed * factor[..., None] + jnp.einsum(
            "shqk,kshe->shqe",
            weights.astype(jnp.bfloat16),
            value_block,
            preferred_element_type=jnp.float32,
        )
        return (newest, totals, summed)

    highest, totals, summed = block_loop(key_piece.shape[0], advance, initial)
    mixed_rows = jnp.transpose(summed / totals[..., None], (2, 0, 1, 3)).reshape(
        row_count, seq_count, head_count * head_size
    )
    return (mixed_rows, highest + jnp.log(totals), None)


def attend_backward(
    queries,
    key_rows,
    value_rows,
    grad_mixed,
    mixed_rows,
    log_sum,
    own_places,
    own_live,
    row_info,
    label_rows,
):
    row_count, seq_count, head_count, head_size = queries.shape
    score_scale = head_size ** (-0.5)
    grad_heads = grad_mixed.reshape(row_count, seq_count, head_count, head_size)
    offsets = jnp.sum(
        grad_heads.astype(jnp.float32)
        * mixed_rows.reshape(row_count, seq_count, head_count, head_size),
        axis=-1,
    )
    offsets_rows = jnp.transpose(offsets, (1, 2, 0))
    key_piece = lax.all_gather(key_rows, "seq", axis=0, tiled=True)
    value_piece = lax.all_gather(value_rows, "seq", axis=0, tiled=True)

    def advance(current, offset, block_size):
        key_block = lax.dynamic_slice_in_dim(key_piece, offset, block_size, 0).reshape(
            block_size, seq_count, head_count, head_size
        )
        value_block = lax.dynamic_slice_in_dim(value_piece, offset, block_size, 0).reshape(
            block_size, seq_count, head_count, head_size
        )
        key_places, key_live = row_info(offset, block_size)
        allowed = key_mask(own_places, own_live, key_places, key_live, label_rows)
        scores = (
            jnp.einsum("qshe,kshe->shqk", queries, key_block, preferred_element_type=jnp.float32)
            * score_scale
        )
        scores = jnp.where(allowed, scores, NEGATIVE)
        chances = jnp.exp(scores - log_sum[..., None])
        pushes = jnp.einsum(
            "qshe,kshe->shqk", grad_heads, value_block, preferred_element_type=jnp.float32
        )
        slopes = (chances * (pushes - offsets_rows[..., None])).astype(jnp.bfloat16)
        return current + jnp.einsum(
            "shqk,kshe->qshe", slopes, key_block, preferred_element_type=jnp.float32
        )

    grad_queries = block_loop(key_piece.shape[0], advance, jnp.zeros(queries.shape, jnp.float32))
    log_all, offsets_all = (
        lax.all_gather(jnp.transpose(log_sum, (2, 0, 1)), "seq", axis=0, tiled=True),
        lax.all_gather(offsets, "seq", axis=0, tiled=True),
    )
    own_keys = key_rows.reshape(row_count, seq_count, head_count, head_size)
    own_values = value_rows.reshape(row_count, seq_count, head_count, head_size)
    zero_rows = jnp.zeros(queries.shape, jnp.float32)
    query_flat = queries.reshape(row_count, seq_count, head_count * head_size)
    query_piece = lax.all_gather(query_flat, "seq", axis=0, tiled=True)
    grad_piece = lax.all_gather(grad_mixed, "seq", axis=0, tiled=True)

    def advance(current, offset, block_size):
        key_sum, value_sum = current
        query_block = lax.dynamic_slice_in_dim(query_piece, offset, block_size, 0).reshape(
            block_size, seq_count, head_count, head_size
        )
        grad_block = lax.dynamic_slice_in_dim(grad_piece, offset, block_size, 0).reshape(
            block_size, seq_count, head_count, head_size
        )
        block_log = jnp.transpose(
            lax.dynamic_slice_in_dim(log_all, offset, block_size, 0), (1, 2, 0)
        )
        block_offsets = jnp.transpose(
            lax.dynamic_slice_in_dim(offsets_all, offset, block_size, 0), (1, 2, 0)
        )
        query_places, query_live = row_info(offset, block_size)
        allowed = key_mask(query_places, query_live, own_places, own_live, label_rows)
        scores = (
            jnp.einsum("qshe,kshe->shqk", query_block, own_keys, preferred_element_type=jnp.float32)
            * score_scale
        )
        scores = jnp.where(allowed, scores, NEGATIVE)
        chances = jnp.exp(scores - block_log[..., None])
        pushes = jnp.einsum(
            "qshe,kshe->shqk", grad_block, own_values, preferred_element_type=jnp.float32
        )
        slopes = (chances * (pushes - block_offsets[..., None])).astype(jnp.bfloat16)
        key_sum = key_sum + jnp.einsum(
            "shqk,qshe->kshe", slopes, query_block, preferred_element_type=jnp.float32
        )
        value_sum = value_sum + jnp.einsum(
            "shqk,qshe->kshe",
            chances.astype(jnp.bfloat16),
            grad_block,
            preferred_element_type=jnp.float32,
        )
        return (key_sum, value_sum)

    key_sum, value_sum = block_loop(query_piece.shape[0], advance, (zero_rows, zero_rows))
    flat_shape = (row_count, seq_count, head_count * head_size)
    return (
        (grad_queries * score_scale).reshape(flat_shape),
        (key_sum * score_scale).reshape(flat_shape),
        value_sum.reshape(flat_shape),
    )


def block_forward(hidden, params, row_info, label_rows):
    attn_gain, qkv_weight, out_weight, mlp_gain, up_weight, down_weight = params
    row_count, seq_count, _ = hidden.shape
    head_width = qkv_weight.shape[2]
    head_count = head_width // HEAD_DIM
    own_places, own_live = row_info(lax.axis_index("seq") * row_count, row_count)
    normed = rms_norm(hidden, attn_gain.astype(jnp.float32)).astype(jnp.bfloat16)
    projected = jnp.einsum(
        "rsd,dce->rsce", normed, qkv_weight, preferred_element_type=jnp.float32
    ).astype(jnp.bfloat16)
    queries = projected[:, :, 0].reshape(row_count, seq_count, head_count, HEAD_DIM)
    key_rows = projected[:, :, 1]
    value_rows = projected[:, :, 2]
    mixed_rows, log_sum, kept_rows = attend_forward(
        queries, key_rows, value_rows, own_places, own_live, row_info, label_rows
    )
    mixed_low = mixed_rows.astype(jnp.bfloat16)
    attention = model_sum(
        jnp.einsum("rsh,hd->rsd", mixed_low, out_weight, preferred_element_type=jnp.float32)
    )
    middle = hidden + attention
    normed_mlp = rms_norm(middle, mlp_gain.astype(jnp.float32)).astype(jnp.bfloat16)
    before = jnp.einsum("rsd,df->rsf", normed_mlp, up_weight, preferred_element_type=jnp.float32)
    active = gelu_tanh(before).astype(jnp.bfloat16)
    feed_out = model_sum(
        jnp.einsum("rsf,fd->rsd", active, down_weight, preferred_element_type=jnp.float32)
    )
    stored = (
        hidden,
        normed,
        queries,
        key_rows,
        value_rows,
        mixed_rows,
        log_sum,
        mixed_low,
        middle,
        normed_mlp,
        before,
        active,
        own_places,
        own_live,
        kept_rows,
    )
    return (attention, middle, feed_out, stored)


def block_backward(incoming, stored, params, row_info, label_rows):
    attn_gain, qkv_weight, out_weight, mlp_gain, up_weight, down_weight = params
    (
        hidden,
        normed,
        queries,
        key_rows,
        value_rows,
        mixed_rows,
        log_sum,
        mixed_low,
        middle,
        normed_mlp,
        before,
        active,
        own_places,
        own_live,
        kept_rows,
    ) = stored
    incoming_low = incoming.astype(jnp.bfloat16)
    grad_down = jnp.einsum("rsf,rsd->fd", active, incoming_low, preferred_element_type=jnp.float32)
    grad_active = jnp.einsum(
        "rsd,fd->rsf", incoming_low, down_weight, preferred_element_type=jnp.float32
    )
    _, gelu_pull = jax.vjp(gelu_tanh, before)
    grad_before = gelu_pull(grad_active)[0].astype(jnp.bfloat16)
    grad_up = jnp.einsum("rsd,rsf->df", normed_mlp, grad_before, preferred_element_type=jnp.float32)
    grad_normed_mlp = model_sum(
        jnp.einsum("rsf,df->rsd", grad_before, up_weight, preferred_element_type=jnp.float32)
    )
    _, mlp_pull = jax.vjp(rms_norm, middle, mlp_gain.astype(jnp.float32))
    grad_middle, grad_mlp_gain = mlp_pull(grad_normed_mlp)
    along_low = (incoming + grad_middle).astype(jnp.bfloat16)
    grad_out = jnp.einsum("rsh,rsd->hd", mixed_low, along_low, preferred_element_type=jnp.float32)
    grad_mixed = jnp.einsum(
        "rsd,hd->rsh", along_low, out_weight, preferred_element_type=jnp.float32
    ).astype(jnp.bfloat16)
    grad_queries, grad_keys, grad_values = attend_backward(
        queries,
        key_rows,
        value_rows,
        grad_mixed,
        mixed_rows,
        log_sum,
        own_places,
        own_live,
        row_info,
        label_rows,
    )
    grad_projected = jnp.stack((grad_queries, grad_keys, grad_values), axis=2).astype(jnp.bfloat16)
    grad_qkv = jnp.einsum(
        "rsd,rsce->dce", normed, grad_projected, preferred_element_type=jnp.float32
    )
    grad_normed = model_sum(
        jnp.einsum("rsce,dce->rsd", grad_projected, qkv_weight, preferred_element_type=jnp.float32)
    )
    _, attn_pull = jax.vjp(rms_norm, hidden, attn_gain.astype(jnp.float32))
    grad_hidden, grad_attn_gain = attn_pull(grad_normed)
    return (
        grad_middle + grad_hidden,
        (grad_attn_gain, grad_qkv, grad_out, grad_mlp_gain, grad_up, grad_down),
    )


def on_device(
    tokens,
    segments,
    routed,
    router,
    dense_attn_gain,
    dense_qkv,
    dense_out,
    dense_mlp_gain,
    dense_up,
    dense_down,
    routed_attn_gain,
    routed_qkv,
    routed_out,
    routed_mlp_gain,
    routed_up,
    routed_down,
    cotangent,
):
    group_rows, seq_count, _ = tokens.shape
    devices = lax.axis_size("seq")
    my_index = lax.axis_index("seq")
    capacity = routed.shape[1]
    most_rows = group_rows // 4
    label_rows = jnp.transpose(segments)
    route_rows = jnp.transpose(routed)
    local_ids = jnp.arange(group_rows, dtype=jnp.int32)
    bounds = jnp.arange(devices + 1, dtype=jnp.int32) * group_rows
    starts = jnp.sum((routed[None, :, :] < bounds[:, None, None]).astype(jnp.int32), axis=2)
    first_rank = starts[my_index]
    routed_here = starts[my_index + 1] - first_rank
    dense_params = (dense_attn_gain, dense_qkv, dense_out, dense_mlp_gain, dense_up, dense_down)
    routed_params = (
        routed_attn_gain,
        routed_qkv,
        routed_out,
        routed_mlp_gain,
        routed_up,
        routed_down,
    )

    def dense_info(first_row, row_total):
        places = first_row + jnp.broadcast_to(
            jnp.arange(row_total, dtype=jnp.int32)[:, None], (row_total, seq_count)
        )
        return (places, jnp.ones((row_total, seq_count), jnp.bool_))

    slot_rows = jnp.arange(most_rows, dtype=jnp.int32)
    is_live = slot_rows[:, None] < routed_here[None, :]
    hold_places = (
        jnp.take_along_axis(
            route_rows, jnp.clip(first_rank[None, :] + slot_rows[:, None], 0, capacity - 1), axis=0
        )
        - my_index * group_rows
    )
    hold_table = (
        (jnp.transpose(hold_places)[:, :, None] == local_ids[None, None, :])
        & jnp.transpose(is_live)[:, :, None]
    ).astype(jnp.bfloat16)

    def select_rows(rows_in):
        return jnp.einsum(
            "smc,csd->msd", hold_table, rows_in, preferred_element_type=jnp.float32
        ).astype(jnp.bfloat16)

    def restore_rows(rows_in):
        return jnp.einsum("smc,msd->csd", hold_table, rows_in, preferred_element_type=jnp.float32)

    def routed_info(first_row, row_total):
        number = first_row + jnp.arange(row_total, dtype=jnp.int32)
        source = number // most_rows
        within = number % most_rows
        base = jnp.take(starts, source, axis=0)
        filled = jnp.take(starts, source + 1, axis=0) - base
        rank_rows = jnp.clip(base + within[:, None], 0, capacity - 1)
        return (jnp.take_along_axis(route_rows, rank_rows, axis=0), within[:, None] < filled)

    hidden = tokens.astype(jnp.float32)
    _, middle, feed_out, dense_stored = block_forward(hidden, dense_params, dense_info, label_rows)
    first_out = middle + feed_out
    lifted = select_rows(first_out.astype(jnp.bfloat16))
    routed_attention, _, routed_feed, routed_stored = block_forward(
        lifted.astype(jnp.float32), routed_params, routed_info, label_rows
    )
    sent_rows = (routed_attention + routed_feed).astype(jnp.bfloat16)
    returned = restore_rows(sent_rows)
    router_float = router.astype(jnp.float32)
    gate_value = jax.nn.sigmoid(jnp.einsum("csd,d->cs", first_out, router_float, precision=PRECISE))
    output = first_out + gate_value[:, :, None] * returned
    grad_output = cotangent.astype(jnp.float32)
    grad_sent = select_rows((gate_value[:, :, None] * grad_output).astype(jnp.bfloat16))
    grad_logit = jnp.sum(grad_output * returned, axis=-1) * gate_value * (1.0 - gate_value)
    grad_router = jnp.einsum("cs,csd->d", grad_logit, first_out, precision=PRECISE)
    grad_first = grad_output + grad_logit[:, :, None] * router_float
    routed_branch, routed_grads = block_backward(
        grad_sent.astype(jnp.float32), routed_stored, routed_params, routed_info, label_rows
    )
    grad_first = grad_first + restore_rows(routed_branch.astype(jnp.bfloat16))
    dense_branch, dense_grads = block_backward(
        grad_first, dense_stored, dense_params, dense_info, label_rows
    )
    grad_tokens = grad_first + dense_branch
    summed_all = (
        lax.psum_scatter(dense_grads[0], "seq", scatter_dimension=0, tiled=True),
        lax.psum_scatter(dense_grads[1], "seq", scatter_dimension=0, tiled=True),
        lax.psum_scatter(dense_grads[2], "seq", scatter_dimension=1, tiled=True),
        lax.psum_scatter(dense_grads[3], "seq", scatter_dimension=0, tiled=True),
        lax.psum_scatter(dense_grads[4], "seq", scatter_dimension=0, tiled=True),
        lax.psum_scatter(dense_grads[5], "seq", scatter_dimension=1, tiled=True),
        lax.psum_scatter(routed_grads[0], "seq", scatter_dimension=0, tiled=True),
        lax.psum_scatter(routed_grads[1], "seq", scatter_dimension=0, tiled=True),
        lax.psum_scatter(routed_grads[2], "seq", scatter_dimension=1, tiled=True),
        lax.psum_scatter(routed_grads[3], "seq", scatter_dimension=0, tiled=True),
        lax.psum_scatter(routed_grads[4], "seq", scatter_dimension=0, tiled=True),
        lax.psum_scatter(routed_grads[5], "seq", scatter_dimension=1, tiled=True),
        lax.psum_scatter(grad_router, "seq", scatter_dimension=0, tiled=True),
    )
    dense_sums = tuple(summed_all[0:6])
    routed_sums = tuple(summed_all[6:13])
    return (output, grad_tokens) + tuple(dense_sums) + tuple(routed_sums)


BF = jnp.bfloat16
LIMIT = 63 * 1024 * 1024
F32 = jnp.float32
MESH = pl.DeviceIdType.MESH
PIECE = 1024
WIDTHS = (384, 128, 512, 512)
BEGINS = (0, 384, 512, 1024)
SIZES = (1536, 512, 2048, 2048)
COLS = (None, (0, 512), (512, 2048), None)


def dot(a, b):
    return lax.dot_general(a, b, (((1,), (0,)), ((), ())), preferred_element_type=F32)


def dot_t(a, b):
    return lax.dot_general(a, b, (((1,), (1,)), ((), ())), preferred_element_type=F32)


def dot_l(a, b):
    return lax.dot_general(a, b, (((0,), (0,)), ((), ())), preferred_element_type=F32)


def swap_halves(tile):
    return pltpu.roll(tile, 64, 1)


def low_lanes(rows):
    return lax.broadcasted_iota(jnp.int32, (rows, 128), 1) < 64


def inverse_rms(rows):
    return lax.rsqrt(jnp.mean(rows * rows, axis=1, keepdims=True) + EPSILON)


def norm_back(grad, rows, gain):
    inverse = inverse_rms(rows)
    unit = rows * inverse
    pulled = grad * gain
    grad_rows = inverse * (pulled - unit * jnp.mean(pulled * unit, axis=1, keepdims=True))
    return grad_rows, jnp.sum(grad * unit, axis=0, keepdims=True)


class Env:
    def __init__(self, refs, sems, seq_size):
        self.b = refs
        self.sems = sems
        self.count = 0
        self.sends = []
        self.middle_sends = []
        self.flying = {}
        self.stores = {}
        self.stored = 0
        self.barrier_done = False
        self.n = seq_size
        self.s = lax.axis_index("seq")
        self.c = lax.axis_index("mp")
        self.q = lax.rem(self.s, 4)
        self.z = lax.div(self.s, 4)
        high = lax.div(self.z, 2)
        self.near = self.z + 1 - 2 * lax.rem(self.z, 2)
        self.across = 2 - high
        self.far = 3 - 3 * high
        self.middle = lax.rem(self.z + high, 2) == 1

    def sem(self):
        self.count += 1
        return self.sems.at[self.count - 1]

    def vector(self, number):
        return self.b.vectors[number][...].astype(F32).reshape(1, 1024)

    def greet(self):
        barrier = pltpu.get_barrier_semaphore()

        def signal(step, _):
            other = lax.rem(self.s + step, self.n)
            pl.semaphore_signal(barrier, inc=1, device_id=(other, self.c), device_id_type=MESH)
            return 0

        lax.fori_loop(1, self.n, signal, 0)
        pl.semaphore_signal(barrier, inc=1, device_id=(self.s, 1 - self.c), device_id_type=MESH)

    def meet(self):
        if not self.barrier_done:
            pl.semaphore_wait(pltpu.get_barrier_semaphore(), self.n)
            self.barrier_done = True

    def remote(self, src, dst, send, recv, seq, core):
        return pltpu.make_async_remote_copy(
            src_ref=src,
            dst_ref=dst,
            send_sem=send,
            recv_sem=recv,
            device_id=(seq, core),
            device_id_type=MESH,
        )

    def exchange(self, send_ref, recv_ref):
        self.meet()
        send, recv = self.sem(), self.sem()
        n = self.n

        def start(step, _):
            other = lax.rem(self.s + step, n)
            self.remote(
                send_ref.at[other], recv_ref.at[self.s], send, recv, other, self.c
            ).start()
            return 0

        lax.fori_loop(1, n, start, 0)
        recv_ref[pl.ds(self.s, 1)] = send_ref[pl.ds(self.s, 1)]
        whole = self.remote(
            send_ref.at[pl.ds(0, n - 1)],
            recv_ref.at[pl.ds(0, n - 1)],
            send,
            recv,
            lax.rem(self.s + 1, n),
            self.c,
        )
        self.sends.append(whole)
        return whole.wait_recv

    def core_sum(self, layer, half, chunk, sink):
        self.meet()
        send_ref, recv_ref = layer.b.ps.at[half], layer.b.pr.at[half]
        copies = []
        for number in range(4):
            earlier = self.flying.pop((layer.packed, half, number), None)
            if earlier is not None:
                earlier.wait_send()
            send_ref[number] = chunk(number).astype(BF)
            copy = self.remote(
                send_ref.at[number], recv_ref.at[number], self.sem(), self.sem(), self.s, 1 - self.c
            )
            copy.start()
            copies.append(copy)
            self.flying[(layer.packed, half, number)] = copy
        for number, copy in enumerate(copies):
            copy.wait_recv()
            sink(number, send_ref[number].astype(F32) + recv_ref[number].astype(F32))

    def plane_send(self, pieces, recv_piece, wait_piece):
        self.meet()
        send, recv = self.sem(), self.sem()
        for step in range(1, 4):
            other = lax.rem(self.q + step, 4)
            self.remote(
                pieces(other), recv_piece, send, recv, self.z * 4 + other, self.c
            ).start()
        whole = self.remote(wait_piece, wait_piece, send, recv, self.z * 4 + lax.rem(self.q + 1, 4), self.c)
        self.sends.append(whole)
        return whole.wait_recv

    def line_send(self, pieces, recv_piece, wait_piece):
        self.meet()
        send, recv = self.sem(), self.sem()
        for step in range(1, 4):
            other = lax.rem(self.z + step, 4)
            self.remote(
                pieces(other), recv_piece(step), send, recv, other * 4 + self.q, self.c
            ).start()
        whole = self.remote(wait_piece, wait_piece, send, recv, lax.rem(self.z + 1, 4) * 4 + self.q, self.c)
        self.sends.append(whole)
        return whole.wait_recv

    def line_reduce(self, blocks, slots):
        self.meet()
        receive = [self.sem() for _ in range(4)]
        send = [self.sem() for _ in range(3)]

        def copy(block, slot, way, z):
            return self.remote(
                blocks.at[block], slots.at[slot], send[way], receive[slot], z * 4 + self.q, self.c
            )

        @pl.when(jnp.logical_not(self.middle))
        def _():
            copy(self.far, 3, 2, self.near).start()
            copy(self.across, 2, 1, self.near).start()

        copy(self.near, 0, 0, self.near).start()

        self.sends += [copy(0, 0, way, self.near) for way in range(3)]

        def arrived(slot):
            copy(0, slot, 0, self.near).wait_recv()

        def pass_on(slot):
            block = (self.across, self.far)[slot - 2]
            copy(block, 1, slot - 1, block).start()

        def finish():
            for slot in range(2):
                copy(0, slot, 0, self.near).wait_recv()

        return arrived, pass_on, finish

    def line_gather(self, ref):
        self.meet()
        receive = [self.sem() for _ in range(3)]
        send = [self.sem() for _ in range(5)]

        def copy(piece, way, slot, z):
            return self.remote(
                ref.at[piece], ref.at[piece], send[way], receive[slot], z * 4 + self.q, self.c
            )

        copy(self.z, 0, 0, self.near).start()

        @pl.when(self.middle)
        def _():
            copy(self.z, 1, 1, self.across).start()

        def second():
            @pl.when(self.middle)
            def _():
                copy(0, 0, 0, self.near).wait_recv()
                copy(self.near, 2, 2, self.across).start()
                copy(0, 0, 1, self.near).wait_recv()
                copy(self.across, 3, 1, self.near).start()

        def third():
            @pl.when(self.middle)
            def _():
                copy(0, 0, 2, self.near).wait_recv()
                copy(self.far, 4, 2, self.near).start()

        self.sends.append(copy(0, 0, 0, self.near))
        self.middle_sends += [copy(0, way, 0, self.near) for way in range(1, 5)]

        def finish():
            @pl.when(jnp.logical_not(self.middle))
            def _():
                for slot in range(3):
                    copy(0, 0, slot, self.near).wait_recv()

        return second, third, finish

    def store(self, result, which, at, fill):
        slot = self.stored % 4
        self.stored += 1
        if slot in self.stores:
            self.stores.pop(slot).wait()
        stage = self.b.stage.at[slot]
        fill(stage)
        target = result.at[at // 512] if which == 0 else result.at[:, pl.ds(at, 512)]
        copy = pltpu.make_async_copy(stage, target, self.sem())
        copy.start()
        self.stores[slot] = copy

    def drain(self):
        for copy in self.sends + list(self.flying.values()):
            copy.wait_send()
        for copy in self.stores.values():
            copy.wait()

        @pl.when(self.middle)
        def _():
            for copy in self.middle_sends:
                copy.wait_send()


class Layer:
    def __init__(self, packed, per, n):
        self.per = per
        self.n = n
        self.rows = 2 * per
        self.packed = packed
        self.value_rows = per // 2 if self.packed else per
        self.message = per + self.value_rows
        self.total = n * per
        self.block = 256
        self.gains = (0, 1) if packed else (2, 3)

    def attach(self, env, refs, sources, weights, results):
        self.b = refs
        self.sources = sources
        self.held = weights
        self.results = results
        self.right_waits, self.left_waits, self.line_waits, self.hops = {}, {}, {}, {}
        self.loads = {}

    def load(self, env, number):
        copy = pltpu.make_async_copy(self.sources[number], self.held[number], env.sem())
        copy.start()
        self.loads[number] = copy

    def weight(self, number):
        if number in self.loads:
            self.loads.pop(number).wait()
        return self.held[number]

    def buffers(self):
        r, t, n = self.rows, self.total, self.n
        vr, m = self.value_rows, self.message
        table = dict(
            x=((r, 1024), BF),
            normed=((r, 1024), BF),
            s1=((n, m, 128), BF),
            r1=((n, m, 128), BF),
            qa=((t, 128), BF),
            kb=((t, 128), BF),
            va=((t, 128), BF),
            mixp=((t, 128), F32),
            lse=((t, 128), F32),
            s2=((n, vr, 128), BF),
            r2=((n, vr, 128), BF),
            mixl=((r, 512), BF),
            mid=((r, 1024), F32),
            nm=((r, 1024), BF),
            gp=((r, 2048), BF),
            act=((r, 2048), BF),
            e=((r, 1024), F32),
            el=((r, 1024), BF),
            gb=((r, 2048), BF),
            gm=((r, 1024), F32),
            al=((r, 1024), BF),
            s6=((n, vr, 128), BF),
            r6=((n, vr, 128), BF),
            gx=((t, 128), BF),
            dk=((t, 128), F32),
            dv=((t, 128), F32),
            s7=((n, m, 128), BF),
            r7=((n, m, 128), BF),
            dp=((r, 1536), BF),
            acc=((r, 1024), F32),
            ps=((2, 4, r, 256), BF),
            pr=((2, 4, r, 256), BF),
        )
        if self.packed:
            table.update(
                ng=((4, 4, self.per, 1024), BF),
                x7=((t, 256), BF),
                s9=((n, m, 128), BF),
                r9=((n, m, 128), BF),
                fg=((4, r, 2560), BF),
                ds=((4, r, 512), BF),
                dg=((4, r, 512), BF),
                sb=((4, 64, 2560), BF),
                rb=((4, 64, 2560), BF),
                ul=((4, r, 1024), BF),
                ur=((4, r, 512), BF),
                us=((4, 256, 512), BF),
                ub=((4, 256, 512), BF),
                ux=((4, 64, 512), BF),
                uy=((4, 64, 512), BF),
            )
        else:
            table.update(
                fg=((4, 4, r, 1536), BF),
                dg=((4, 4, r, 1024), BF),
                sb=((4, 64, 1536), BF),
                rb=((4, 64, 1536), BF),
                same=((t, t), F32),
                lab=((t, 128), BF),
                hot=((2, self.per, 64), BF),
                labs=((r, 128), F32),
            )
        return table

    def gain(self, env, which):
        return env.vector(self.gains[which])

    def pack(self, tile):
        if not self.packed:
            return tile
        half = self.per // 2
        return jnp.where(low_lanes(half), tile[:half], swap_halves(tile[half:]))

    def send_pairs(self, store, tile_of):
        for seq in range(2):
            for j in range(4):
                tile = tile_of(seq, j)
                store(8 * seq + 2 * j, self.pack(tile))
                store(8 * seq + 2 * j + 1, self.pack(swap_halves(tile)))

    def join_pairs(self, tile_a, tile_b):
        vr = self.value_rows
        low = low_lanes(vr)
        first = jnp.where(low, tile_a, swap_halves(tile_b))
        if not self.packed:
            return [first]
        return [first, jnp.where(low, swap_halves(tile_a), tile_b)]

    def project(self, env, then=None):
        hidden = self.b.x[...].astype(F32)
        normed = (hidden * inverse_rms(hidden) * self.gain(env, 0)).astype(BF)
        self.b.normed[...] = normed
        weight = self.weight(QKV)
        if then is not None:
            then()
        queries, keys, values = (dot(normed, weight[part]) for part in range(3))
        send = self.b.s1
        per = self.per
        low = low_lanes(per)
        for seq in range(2):
            rows = slice(seq * per, (seq + 1) * per)
            for j in range(4):
                cols = slice(128 * j, 128 * j + 128)
                qt, kt, vt = queries[rows, cols], keys[rows, cols], values[rows, cols]
                pair = 8 * seq + 2 * j
                send[pair, 0:per] = jnp.where(low, qt, swap_halves(kt)).astype(BF)
                send[pair + 1, 0:per] = jnp.where(low, swap_halves(qt), kt).astype(BF)
                va, vb = vt, swap_halves(vt)
                if self.packed:
                    va, vb = self.pack(va), self.pack(vb)
                else:
                    labels = self.b.labs[rows, :]
                    va, vb = jnp.where(low, va, labels), jnp.where(low, vb, labels)
                send[pair, per:] = va.astype(BF)
                send[pair + 1, per:] = vb.astype(BF)
        self.wait1 = env.exchange(send, self.b.r1)

    def unpack(self, env):
        recv = self.b.r1
        qa, kb, va = self.b.qa, self.b.kb, self.b.va
        per, vr = self.per, self.value_rows
        low, low_v = low_lanes(per), low_lanes(vr)
        zero = jnp.zeros((per, 128), F32)
        zero_v = jnp.zeros((vr, 128), F32)
        for i in range(self.n):
            both = recv[i, 0:per].astype(F32)
            qa[i * per : (i + 1) * per] = jnp.where(low, both * 0.125, zero).astype(BF)
            kb[i * per : (i + 1) * per] = swap_halves(both).astype(BF)
            tile = recv[i, per:].astype(F32)
            va[i * per : i * per + vr] = jnp.where(low_v, tile, zero_v).astype(BF)
            if self.packed:
                va[i * per + vr : (i + 1) * per] = jnp.where(low_v, swap_halves(tile), zero_v).astype(BF)
            else:
                self.b.lab[i * per : (i + 1) * per] = jnp.where(low_v, zero_v, tile).astype(BF)
        if not self.packed:
            labels = self.b.lab[...]
            self.b.same[...] = dot_t(labels, labels)

    def allowed(self, env, start, stop):
        size = stop - start
        rows = lax.broadcasted_iota(jnp.int32, (size, stop), 0) + start
        keys = lax.broadcasted_iota(jnp.int32, (size, stop), 1)
        ok = keys <= rows
        if self.packed:
            segments = env.b.segments[pl.ds(lax.div(env.s, 8), 1), :]
            row = (lax.broadcasted_iota(jnp.int32, (size, 1), 0) + start).astype(F32)
            opening = jnp.zeros((size, 1), F32)
            for label in range(1, 4):
                edge = jnp.sum((segments < label).astype(F32), axis=1, keepdims=True)
                opening = jnp.where(row >= edge, jnp.maximum(opening, edge), opening)
            return ok & (keys >= opening.astype(jnp.int32))
        return ok & (self.b.same[start:stop, 0:stop] > 0.5)

    def attend(self, env):
        self.wait1()
        self.unpack(env)
        qa, kb, va = self.b.qa, self.b.kb, self.b.va
        mixp, lse = self.b.mixp, self.b.lse
        for start in range(0, self.total, self.block):
            stop = start + self.block
            scores = dot_t(qa[start:stop], kb[0:stop])
            scores = jnp.where(self.allowed(env, start, stop), scores, NEGATIVE)
            highest = jnp.max(scores, axis=1, keepdims=True)
            weights = jnp.exp(scores - highest)
            totals = jnp.sum(weights, axis=1, keepdims=True)
            mixp[start:stop] = dot(weights.astype(BF), va[0:stop]) / totals
            lse[start:stop] = jnp.broadcast_to(highest + jnp.log(totals), (self.block, 128))
        send = self.b.s2
        for i in range(self.n):
            send[i] = self.pack(mixp[i * self.per : (i + 1) * self.per]).astype(BF)
        self.wait2 = env.exchange(send, self.b.r2)

    def gather_heads(self, recv, row0, put):
        per, vr = self.per, self.value_rows
        for seq in range(2):
            for j in range(4):
                pair = 8 * seq + 2 * j
                tiles = self.join_pairs(
                    recv[pair, row0:].astype(F32), recv[pair + 1, row0:].astype(F32)
                )
                for number, tile in enumerate(tiles):
                    begin = seq * per + number * vr
                    put(slice(begin, begin + vr), slice(128 * j, 128 * j + 128), tile)

    def feed(self, env, finish, then=None):
        self.wait2()
        mixl = self.b.mixl

        def put(rows, cols, tile):
            mixl[rows, cols] = tile.astype(BF)

        self.gather_heads(self.b.r2, 0, put)
        out = self.weight(OUT)
        mid = self.b.mid
        hidden = self.b.x
        mixed = mixl[...]

        def sink(number, value):
            cols = slice(256 * number, 256 * number + 256)
            mid[:, cols] = value + hidden[:, cols].astype(F32)

        env.core_sum(
            self,
            0,
            lambda number: dot(mixed, out[:, 256 * number : 256 * number + 256]),
            sink,
        )
        middle = mid[...]
        normed = (middle * inverse_rms(middle) * self.gain(env, 1)).astype(BF)
        self.b.nm[...] = normed
        up = self.weight(UP)
        act, slope = self.b.act, self.b.gp
        for number in range(4):
            cols = slice(512 * number, 512 * number + 512)
            before = dot(normed, up[:, cols])
            square = before * before
            bent = jnp.tanh(0.7978845608028654 * before * (1.0 + 0.044715 * square))
            half = 0.5 * (1.0 + bent)
            act[:, cols] = (before * half).astype(BF)
            slope[:, cols] = (
                half
                + 0.5 * before * (1.0 - bent * bent) * (0.7978845608028654 + 0.1070322243 * square)
            ).astype(BF)
        if then is not None:
            then()
        down = self.weight(DOWN)
        env.core_sum(
            self,
            1,
            lambda number: dot(act[...], down[:, 256 * number : 256 * number + 256]),
            finish,
        )

    def round_incoming(self):
        self.b.el[...] = self.b.e[...].astype(BF)

    def back_feed(self, env):
        grad_low = self.b.el[...]
        down, up, out = self.weight(DOWN), self.weight(UP), self.weight(OUT)
        gb, slope = self.b.gb, self.b.gp
        for number in range(4):
            cols = slice(512 * number, 512 * number + 512)
            grad = dot_t(grad_low, down[cols, :])
            gb[:, cols] = (grad * slope[:, cols].astype(F32)).astype(BF)
        acc = self.b.acc

        def sink(number, value):
            acc[:, 256 * number : 256 * number + 256] = value

        env.core_sum(
            self,
            0,
            lambda number: dot_t(gb[...], up[256 * number : 256 * number + 256, :]),
            sink,
        )
        grad_mid, grad_gain = norm_back(acc[...], self.b.mid[...], self.gain(env, 1))
        row = self.gains[1]
        env.b.vg[row : row + 1, :] = grad_gain
        self.b.gm[...] = grad_mid
        along = (self.b.e[...] + grad_mid).astype(BF)
        self.b.al[...] = along
        grad_mixed = dot_t(along, out[...])
        send = self.b.s6
        per = self.per

        def store(pair, tile):
            send[pair] = tile.astype(BF)

        self.send_pairs(
            store,
            lambda seq, j: grad_mixed[seq * per : (seq + 1) * per, 128 * j : 128 * j + 128],
        )
        self.wait6 = env.exchange(send, self.b.r6)

    def back_attend(self, env):
        self.wait6()
        recv, gx = self.b.r6, self.b.gx
        per, vr = self.per, self.value_rows
        low_v = low_lanes(vr)
        zero_v = jnp.zeros((vr, 128), F32)
        for i in range(self.n):
            tile = recv[i].astype(F32)
            gx[i * per : i * per + vr] = jnp.where(low_v, tile, zero_v).astype(BF)
            if self.packed:
                gx[i * per + vr : (i + 1) * per] = jnp.where(low_v, swap_halves(tile), zero_v).astype(BF)
        qa, kb, va = self.b.qa, self.b.kb, self.b.va
        mixp, lse = self.b.mixp, self.b.lse
        dk, dv = self.b.dk, self.b.dv
        dk[...] = jnp.zeros_like(dk)
        dv[...] = jnp.zeros_like(dv)
        dq = {}
        for start in range(0, self.total, self.block):
            stop = start + self.block
            query, grad = qa[start:stop], gx[start:stop]
            scores = dot_t(query, kb[0:stop])
            scores = jnp.where(self.allowed(env, start, stop), scores, NEGATIVE)
            probs = jnp.exp(scores - lse[start:stop, 0:1])
            offsets = jnp.sum(grad.astype(F32) * mixp[start:stop], axis=1, keepdims=True)
            slopes = (probs * (dot_t(grad, va[0:stop]) - offsets)).astype(BF)
            mixp[start:stop] = dot(slopes, kb[0:stop])
            dk[0:stop] += dot_l(slopes, query)
            dv[0:stop] += dot_l(probs.astype(BF), grad)
        send = self.b.s7
        low = low_lanes(per)
        for i in range(self.n):
            rows = slice(i * per, (i + 1) * per)
            send[i, 0:per] = jnp.where(low, mixp[rows] * 0.125, swap_halves(dk[rows])).astype(BF)
            send[i, per:] = self.pack(dv[rows]).astype(BF)
            if self.packed:
                self.b.x7[rows, 0:128] = send[i, 0:per]
                self.b.x7[rows, 128:256] = dv[rows].astype(BF)
        self.wait7 = env.exchange(send, self.b.r7)

    def back_project(self, env, finish, then=None):
        self.wait7()
        recv, dp = self.b.r7, self.b.dp
        per = self.per
        low = low_lanes(per)
        for seq in range(2):
            rows = slice(seq * per, (seq + 1) * per)
            for j in range(4):
                pair = 8 * seq + 2 * j
                one, two = recv[pair, 0:per].astype(F32), recv[pair + 1, 0:per].astype(F32)
                dp[rows, 128 * j : 128 * j + 128] = jnp.where(low, one, swap_halves(two)).astype(BF)
                dp[rows, 512 + 128 * j : 640 + 128 * j] = jnp.where(low, swap_halves(one), two).astype(BF)

        def put(rows, cols, tile):
            dp[rows, 1024 + cols.start : 1024 + cols.stop] = tile.astype(BF)

        self.gather_heads(recv, per, put)
        if then is not None:
            then()
        weight = self.weight(QKV)
        acc = self.b.acc

        def chunk(number):
            rows = slice(256 * number, 256 * number + 256)
            total = dot_t(dp[:, 0:512], weight[0, rows, :])
            total += dot_t(dp[:, 512:1024], weight[1, rows, :])
            return total + dot_t(dp[:, 1024:1536], weight[2, rows, :])

        def sink(number, value):
            acc[:, 256 * number : 256 * number + 256] = value

        env.core_sum(self, 1, chunk, sink)
        grad_hidden, grad_gain = norm_back(
            acc[...], self.b.x[...].astype(F32), self.gain(env, 0)
        )
        row = self.gains[0]
        env.b.vg[row : row + 1, :] = grad_gain
        finish(self.b.gm[...] + grad_hidden)

    def parts(self, env, which):
        b = self.b
        left = (b.normed, b.al, b.nm, b.el)[which]
        right = (b.dp, b.mixl, b.gb, b.act)[which]
        return left, right

    def share_right(self, env, which, begin=0, size=None):
        at, full = COLS[which]
        size = full if size is None else size
        _, right = self.parts(env, which)
        fg = self.b.fg
        cols = pl.ds(at + begin, size)
        fg[pl.ds(env.q, 1), :, cols] = right[:, begin : begin + size][None]
        mine = fg.at[env.q, :, cols]
        self.right_waits.setdefault(which, []).append(
            env.plane_send(lambda other: mine, mine, fg.at[pl.ds(0, 3), :, cols])
        )

    def share_left(self, env, which):
        left, _ = self.parts(env, which)
        ds, dg = self.b.ds, self.b.dg
        low = low_lanes(self.rows)
        begin = 256 * (which - 1)
        for a in range(2):
            tiles = [
                left[:, 128 * (2 * z + a) : 128 * (2 * z + a) + 128].astype(F32) for z in range(4)
            ]
            for two in range(2):
                even, odd = tiles[2 * two], tiles[2 * two + 1]
                at = begin + 128 * two
                ds[2 * a, :, at : at + 128] = jnp.where(low, even, swap_halves(odd)).astype(BF)
                ds[2 * a + 1, :, at : at + 128] = jnp.where(low, swap_halves(even), odd).astype(BF)
        cols = pl.ds(begin, 256)
        dg[pl.ds(env.q, 1), :, begin : begin + 256] = ds[pl.ds(env.q, 1), :, begin : begin + 256]
        self.left_waits[which] = env.plane_send(
            lambda other: ds.at[other, :, cols],
            dg.at[env.q, :, cols],
            dg.at[pl.ds(0, 3), :, cols],
        )

    def multiply(self, env, which, first=0, last=None):
        if first == 0:
            self.left_waits[which]()
        self.right_waits[which].pop(0)()
        if last is None:
            for wait in self.right_waits.pop(which):
                wait()
        begin, size = COLS[which]
        last = size if last is None else last
        fg, dg, sb, rb = self.b.fg, self.b.dg, self.b.sb, self.b.rb
        rows = 4 * self.rows
        left = dg[:, :, 256 * (which - 1) : 256 * which].reshape(rows, 256)
        for at in range(begin + first, begin + last, 512):
            right = fg[:, :, at : at + 512].reshape(rows, 512)
            product = dot_l(left, right)
            for z in range(4):
                sb[z, :, at : at + 512] = product[64 * z : 64 * z + 64].astype(BF)
            if (at + 512 - begin) % PIECE == 0 or at + 512 == begin + last:
                low = begin + (at - begin) // PIECE * PIECE
                cols = pl.ds(low, at + 512 - low)
                steps = env.line_reduce(sb.at[:, :, cols], rb.at[:, :, cols])
                self.line_waits.setdefault(which, []).append((low, at + 512, steps))

    def relay(self, env, which, pieces=None):
        sb, rb = self.b.sb, self.b.rb
        for low, high, (arrived, pass_on, _) in self.line_waits[which][pieces or slice(None)]:

            @pl.when(env.middle)
            def _():
                for slot, block in ((3, env.far), (2, env.across)):
                    arrived(slot)
                    for at in range(low, high, 512):
                        cols = slice(at, at + 512)
                        total = sb[pl.ds(block, 1), :, cols].astype(F32)
                        total = total + rb[slot : slot + 1, :, cols].astype(F32)
                        sb[pl.ds(block, 1), :, cols] = total.astype(BF)
                    pass_on(slot)

    def collect(self, env, which):
        begin, _ = COLS[which]
        sb, rb = self.b.sb, self.b.rb
        for low, high, (_, _, finish) in self.line_waits[which]:
            finish()
            for at in range(low, high, 512):
                cols = slice(at, at + 512)

                def fill(stage):
                    total = sb[pl.ds(env.z, 1), :, cols].astype(F32)
                    for slot in range(2):
                        total = total + rb[slot : slot + 1, :, cols].astype(F32)
                    stage[...] = total[0]

                env.store(self.results[which], which, at - begin, fill)

    def quarter_left(self, env):
        ul, left = self.b.ul, self.b.el
        cols = pl.ds(pl.multiple_of(512 * env.c, 512), 512)
        ul[pl.ds(env.q, 1), :, cols] = left[:, cols][None]
        self.quarter_wait = env.plane_send(
            lambda other: left.at[:, cols], ul.at[env.q, :, cols], ul.at[pl.ds(0, 3), :, cols]
        )

    def quarter_core(self, env):
        self.quarter_wait()
        mine = self.b.ul.at[:, :, pl.ds(pl.multiple_of(512 * env.c, 512), 512)]
        copy = env.remote(mine, mine, env.sem(), env.sem(), env.s, 1 - env.c)
        copy.start()
        env.sends.append(copy)
        self.quarter_wait = copy.wait_recv

    def quarter_right(self, env):
        right, ur = self.b.act, self.b.ur

        def quarter(number):
            return pl.ds(pl.multiple_of(number * 512, 512), 512)

        ur[pl.ds(env.q, 1)] = right[:, quarter(env.q)][None]
        self.quarter_columns = env.plane_send(
            lambda other: right.at[:, quarter(other)], ur.at[env.q], ur.at[pl.ds(0, 3)]
        )

    def quarter_multiply(self, env):
        self.quarter_wait()
        self.quarter_columns()
        ul, ur, us, ub = self.b.ul, self.b.ur, self.b.us, self.b.ub
        rows = 4 * self.rows
        left = ul[...].reshape(rows, 1024)
        self.quarter_steps = []
        for at in range(0, 512, 256):
            product = dot_l(left, ur[:, :, at : at + 256].reshape(rows, 256))
            for z in range(4):
                us[z, :, at : at + 256] = product[256 * z : 256 * z + 256].astype(BF)
            cols = pl.ds(at, 256)
            self.quarter_steps.append(env.line_reduce(us.at[:, :, cols], ub.at[:, :, cols]))

    def quarter_relay(self, env):
        us, ub = self.b.us, self.b.ub
        for number, (arrived, pass_on, _) in enumerate(self.quarter_steps):
            cols = slice(256 * number, 256 * number + 256)

            @pl.when(env.middle)
            def _():
                for slot, block in ((3, env.far), (2, env.across)):
                    arrived(slot)
                    total = us[pl.ds(block, 1), :, cols].astype(F32)
                    total = total + ub[slot : slot + 1, :, cols].astype(F32)
                    us[pl.ds(block, 1), :, cols] = total.astype(BF)
                    pass_on(slot)

    def quarter_share(self, env):
        us, ub, ux, uy = self.b.us, self.b.ub, self.b.ux, self.b.uy
        for number, (_, _, finish) in enumerate(self.quarter_steps):
            finish()
            cols = slice(256 * number, 256 * number + 256)
            total = us[pl.ds(env.z, 1), :, cols].astype(F32)
            for slot in range(2):
                total = total + ub[slot : slot + 1, :, cols].astype(F32)
            for q in range(4):
                ux[q, :, cols] = total[0, 64 * q : 64 * q + 64].astype(BF)
        uy[pl.ds(env.q, 1)] = ux[pl.ds(env.q, 1)]
        self.quarter_back = env.plane_send(
            lambda other: ux.at[other], uy.at[env.q], uy.at[pl.ds(0, 3)]
        )

    def quarter_collect(self, env):
        self.quarter_back()
        for q in range(4):

            def fill(stage):
                stage[...] = self.b.uy[q].astype(F32)

            env.store(self.results[DOWN], DOWN, 512 * q, fill)

    def gather_line(self, env):
        normed, ng, per = self.b.normed, self.b.ng, self.per
        cols = pl.ds(pl.multiple_of(512 * env.c, 512), 512)

        def rows(z):
            return pl.ds(pl.multiple_of(lax.div(z, 2) * per, per), per)

        ng[pl.ds(env.z, 1), pl.ds(env.q, 1), :, cols] = normed[rows(env.z), cols][None, None]
        self.gather_wait = env.line_send(
            lambda other: normed.at[rows(other), cols],
            lambda step: ng.at[env.z, env.q, :, cols],
            ng.at[pl.ds(0, 3), 0, :, cols],
        )

    def gather_plane(self, env):
        self.gather_wait()
        ng = self.b.ng
        cols = pl.ds(pl.multiple_of(512 * env.c, 512), 512)
        mine = ng.at[:, env.q, :, cols]
        self.gather_wait = env.plane_send(lambda other: mine, mine, ng.at[:, pl.ds(0, 3), :, cols])

    def gather_core(self, env):
        self.gather_wait()
        cols = pl.ds(pl.multiple_of(512 * env.c, 512), 512)
        mine = self.b.ng.at[:, :, :, cols]
        copy = env.remote(mine, mine, env.sem(), env.sem(), env.s, 1 - env.c)
        copy.start()
        env.sends.append(copy)
        self.gather_wait = copy.wait_recv

    def head_gradient(self, env):
        self.gather_wait()
        per, total = self.per, self.total
        product = dot_l(self.b.x7[...], self.b.ng[...].reshape(total, 1024))
        turned = jnp.transpose(product)
        send = self.b.s9
        for i in range(self.n):
            rows = slice(i * 64, i * 64 + 64)
            send[i, 0:per] = turned[rows, 0:128].astype(BF)
            send[i, per:] = self.pack(turned[rows, 128:256]).astype(BF)
        self.wait9 = env.exchange(send, self.b.r9)

    def head_collect(self, env):
        self.wait9()
        recv, per, vr = self.b.r9, self.per, self.value_rows
        low = low_lanes(per)

        def both(pair, rows):
            return recv[pair, rows].astype(F32) + recv[pair + 8, rows].astype(F32)

        for part in range(3):

            def fill(stage):
                for j in range(4):
                    cols = slice(128 * j, 128 * j + 128)
                    rows = slice(0, per) if part < 2 else slice(per, per + vr)
                    one, two = both(2 * j, rows), both(2 * j + 1, rows)
                    if part == 0:
                        stage[:, cols] = jnp.where(low, one, swap_halves(two))
                    elif part == 1:
                        stage[:, cols] = jnp.where(low, swap_halves(one), two)
                    else:
                        first, second = self.join_pairs(one, two)
                        stage[0:vr, cols] = first
                        stage[vr:, cols] = second

            env.store(self.results[QKV], QKV, 512 * part, fill)

    def spread_right(self, env, which):
        _, right = self.parts(env, which)
        fg, width = self.b.fg, WIDTHS[which]
        cols = pl.ds(BEGINS[which], width)

        def quarter(number):
            return pl.ds(pl.multiple_of(number * width, 128), width)

        fg[pl.ds(env.z, 1), pl.ds(env.q, 1), :, cols] = right[:, quarter(env.q)][None, None]
        self.right_waits[which] = env.plane_send(
            lambda other: right.at[:, quarter(other)],
            fg.at[env.z, env.q, :, cols],
            fg.at[env.z, pl.ds(0, 3), :, cols],
        )

    def spread_right_on(self, env, which):
        self.right_waits[which]()
        fg = self.b.fg
        cols = pl.ds(BEGINS[which], WIDTHS[which])
        self.hops[which] = env.line_gather(fg.at[:, :, :, cols])

    def spread_hop(self, env, which, number):
        self.hops[which][number]()

    def spread_left(self, env, which):
        left, _ = self.parts(env, which)
        dg = self.b.dg

        def quarter(number):
            return pl.ds(pl.multiple_of(number * 256 + 128 * env.c, 128), 128)

        cols = self.core_cols(env, which)
        dg[pl.ds(env.z, 1), pl.ds(env.q, 1), :, cols] = left[:, quarter(env.z)][None, None]
        self.left_waits[which] = env.line_send(
            lambda other: left.at[:, quarter(other)],
            lambda step: dg.at[env.z, env.q, :, cols],
            dg.at[pl.ds(0, 3), env.q, :, cols],
        )

    def core_cols(self, env, which):
        return pl.ds(pl.multiple_of(256 * which + 128 * env.c, 128), 128)

    def spread_left_on(self, env, which):
        self.left_waits[which]()
        dg = self.b.dg
        cols = self.core_cols(env, which)
        mine = dg.at[:, env.q, :, cols]
        self.left_waits[which] = env.plane_send(
            lambda other: mine, mine, dg.at[:, pl.ds(0, 3), :, cols]
        )

    def spread_left_core(self, env, which):
        self.left_waits[which]()
        mine = self.b.dg.at[:, :, :, self.core_cols(env, which)]
        copy = env.remote(mine, mine, env.sem(), env.sem(), env.s, 1 - env.c)
        copy.start()
        env.sends.append(copy)
        self.left_waits[which] = copy.wait_recv

    def spread_multiply(self, env, which):
        self.hops[which][2]()
        self.left_waits[which]()
        fg, dg, sb, rb = self.b.fg, self.b.dg, self.b.sb, self.b.rb
        width = WIDTHS[which]
        cols = pl.ds(BEGINS[which], width)
        rows = 16 * self.rows
        product = dot_l(
            dg[:, :, :, 256 * which : 256 * which + 256].reshape(rows, 256),
            fg[:, :, :, cols].reshape(rows, width),
        ).astype(BF)
        for number in range(4):
            sb[number, :, cols] = product[64 * number : 64 * number + 64]
        rb[pl.ds(env.q, 1), :, cols] = sb[pl.ds(env.q, 1), :, cols]
        self.line_waits[which] = env.plane_send(
            lambda other: sb.at[other, :, cols],
            rb.at[env.q, :, cols],
            rb.at[pl.ds(0, 3), :, cols],
        )

    def spread_collect(self, env, which):
        self.line_waits[which]()
        rb, begin, width = self.b.rb, BEGINS[which], WIDTHS[which]
        for at in range(0, SIZES[which], 512):

            def fill(stage):
                for inner in range(0, 512, 128):
                    source, offset = divmod(at + inner, width)
                    stage[:, inner : inner + 128] = rb[
                        source, :, begin + offset : begin + offset + 128
                    ].astype(F32)

            env.store(self.results[which], which, at, fill)


def pick_rows(env, dense, routed):
    hot, labs, first = routed.b.hot, routed.b.labs, env.b.first
    group, slots = dense.per, routed.per
    base = env.s * group
    for seq in range(2):
        listed = env.b.routed[seq : seq + 1, :]
        places = listed.shape[1]
        place = lax.broadcasted_iota(jnp.int32, (group, places), 0) + base
        here = (place == listed).astype(F32).astype(BF)
        before = jnp.sum((listed < base).astype(F32), axis=1, keepdims=True).astype(jnp.int32)
        number = lax.broadcasted_iota(jnp.int32, (slots, places), 1) - before
        slot = lax.broadcasted_iota(jnp.int32, (slots, places), 0)
        mine = (number == slot).astype(F32).astype(BF)
        table = dot_t(mine, here).astype(BF)
        hot[seq] = table
        segments = env.b.segments[seq : seq + 1, :]
        row = (lax.broadcasted_iota(jnp.int32, (group, 1), 0) + base).astype(F32)
        label = jnp.zeros((group, 1), F32)
        for number in range(1, 4):
            edge = jnp.sum((segments < number).astype(F32), axis=1, keepdims=True)
            label = label + (row >= edge).astype(F32)
        lane = lax.broadcasted_iota(jnp.int32, (group, 128), 1)
        one_hot = (lane == label.astype(jnp.int32) + 64).astype(F32).astype(BF)
        labs[seq * slots : (seq + 1) * slots, :] = dot(table, one_hot)
        rows = first[seq * group : (seq + 1) * group, :].astype(BF)
        routed.b.x[seq * slots : (seq + 1) * slots, :] = dot(table, rows).astype(BF)


def restore(env, dense, routed, sent, seq):
    slots = routed.per
    return dot_l(routed.b.hot[seq], sent[seq * slots : (seq + 1) * slots])


def gate_rows(env, dense, routed):
    group, slots = dense.per, routed.per
    sent = routed.b.acc[...].astype(BF)
    router = env.vector(4)
    grad_router = jnp.zeros((1, 1024), F32)
    for seq in range(2):
        rows = slice(seq * group, (seq + 1) * group)
        first = env.b.first[rows, :]
        returned = restore(env, dense, routed, sent, seq)
        gate = jax.nn.sigmoid(jnp.sum(first * router, axis=1, keepdims=True))
        env.b.output[rows, :] = first + gate * returned
        grad = env.b.cotangent[:, seq, :].astype(F32)
        low = (gate * grad).astype(BF)
        routed.b.e[seq * slots : (seq + 1) * slots, :] = dot(routed.b.hot[seq], low)
        logit = jnp.sum(grad * returned, axis=1, keepdims=True) * gate * (1.0 - gate)
        grad_router = grad_router + jnp.sum(logit * first, axis=0, keepdims=True)
        dense.b.e[rows, :] = grad + logit * router
    env.b.vg[4:5, :] = grad_router


def share_vectors(env):
    vg, sv, rv = env.b.vg, env.b.sv, env.b.rv
    for number in range(env.n):
        tile = vg[:, 128 * (number // 2) : 128 * (number // 2) + 128]
        sv[number] = swap_halves(tile) if number % 2 else tile
    return env.exchange(sv, rv)


def sum_vectors(env, wait):
    wait()
    total = env.b.rv[0]
    for number in range(1, env.n):
        total = total + env.b.rv[number]
    env.b.gvec[...] = total


QKV, OUT, UP, DOWN = range(4)
SHAPES = ((3, 1024, 512), (512, 1024), (1024, 2048), (2048, 1024))
GRADS = ((3, 64, 512), (64, 512), (64, 2048), (64, 2048))


def whole_step(env, dense, routed):
    env.greet()
    b = env.b
    copies = [
        pltpu.make_async_copy(source, target, env.sem())
        for source, target in ((b.tokens_hbm, b.tokens), (b.cotangent_hbm, b.cotangent))
    ]
    for copy in copies:
        copy.start()
    dense.load(env, QKV)
    copies[0].wait()
    for seq in range(2):
        dense.b.x[seq * dense.per : (seq + 1) * dense.per, :] = env.b.tokens[:, seq, :]
    env.b.vg[...] = jnp.zeros_like(env.b.vg)
    dense.project(env)
    for number in (OUT, UP, DOWN):
        dense.load(env, number)
    dense.attend(env)
    dense.gather_line(env)
    for number in range(4):
        routed.load(env, number)
    mid_d, first = dense.b.mid, env.b.first
    def finish_dense(number, value):
        cols = slice(256 * number, 256 * number + 256)
        first[:, cols] = mid_d[:, cols] + value
    dense.feed(env, finish_dense)
    pick_rows(env, dense, routed)
    routed.project(env)
    dense.share_left(env, UP)
    routed.attend(env)
    dense.gather_plane(env)
    mid_r, x_r, sent = routed.b.mid, routed.b.x, routed.b.acc
    def finish_routed(number, value):
        cols = slice(256 * number, 256 * number + 256)
        sent[:, cols] = mid_r[:, cols] - x_r[:, cols].astype(F32) + value
    def spread_early():
        routed.spread_right(env, DOWN)
        routed.spread_right(env, OUT)
    routed.feed(env, finish_routed, spread_early)
    dense.quarter_right(env)
    routed.spread_left(env, QKV)
    routed.spread_left(env, UP)
    copies[1].wait()
    gate_rows(env, dense, routed)
    out_copy = pltpu.make_async_copy(b.output, b.output_hbm, env.sem())
    out_copy.start()
    routed.round_incoming()
    routed.back_feed(env)
    dense.gather_core(env)
    routed.spread_right_on(env, DOWN)
    routed.spread_right_on(env, OUT)
    routed.spread_right(env, UP)
    routed.spread_left(env, DOWN)
    routed.spread_left(env, OUT)
    routed.back_attend(env)
    routed.spread_hop(env, DOWN, 0)
    routed.spread_hop(env, OUT, 0)
    dense.share_right(env, OUT)
    routed.spread_right_on(env, UP)
    def finish_back(branch):
        low = branch.astype(BF)
        for seq in range(2):
            rows = slice(seq * dense.per, (seq + 1) * dense.per)
            dense.b.e[rows, :] += restore(env, dense, routed, low, seq)
    routed.back_project(env, finish_back, lambda: routed.spread_right(env, QKV))
    dense.round_incoming()
    dense.quarter_left(env)
    dense.back_feed(env)
    routed.spread_hop(env, DOWN, 1)
    routed.spread_hop(env, OUT, 1)
    routed.spread_hop(env, UP, 0)
    routed.spread_right_on(env, QKV)
    dense.share_left(env, OUT)
    dense.share_right(env, UP, 0, 1024)
    dense.back_attend(env)
    routed.spread_hop(env, UP, 1)
    routed.spread_hop(env, QKV, 0)
    dense.quarter_core(env)
    dense.quarter_multiply(env)
    dense.head_gradient(env)
    dense.multiply(env, OUT)
    dense.share_right(env, UP, 1024, 1024)
    dense.multiply(env, UP, 0, 1024)
    routed.spread_left_on(env, DOWN)
    routed.spread_left_on(env, OUT)
    routed.spread_left_on(env, UP)
    routed.spread_left_on(env, QKV)
    def finish_tokens(branch):
        env.b.grad_tokens[...] = dense.b.e[...] + branch
    dense.back_project(env, finish_tokens)
    grad_copy = pltpu.make_async_copy(b.grad_tokens, b.grad_tokens_hbm, env.sem())
    grad_copy.start()
    routed.spread_hop(env, QKV, 1)
    wait = share_vectors(env)
    dense.quarter_relay(env)
    dense.relay(env, OUT)
    dense.multiply(env, UP, 1024, 2048)
    routed.spread_left_core(env, DOWN)
    routed.spread_left_core(env, OUT)
    routed.spread_left_core(env, UP)
    routed.spread_left_core(env, QKV)
    routed.spread_multiply(env, DOWN)
    routed.spread_multiply(env, QKV)
    routed.spread_multiply(env, OUT)
    routed.spread_multiply(env, UP)
    dense.relay(env, UP)
    dense.quarter_share(env)
    routed.spread_collect(env, DOWN)
    dense.head_collect(env)
    routed.spread_collect(env, OUT)
    routed.spread_collect(env, UP)
    routed.spread_collect(env, QKV)
    dense.collect(env, OUT)
    dense.collect(env, UP)
    sum_vectors(env, wait)
    dense.quarter_collect(env)
    out_copy.wait()
    grad_copy.wait()
    env.drain()


def fused(group, tokens, cotangent, segments, routed_places, vectors, weights):
    n = lax.axis_size("seq")
    rows = 2 * group
    dense, routed = Layer(True, group, n), Layer(False, group // 4, n)
    wide = ((rows, 1024), F32)
    common = dict(
        stage=((4, 64, 512), F32),
        first=wide,
        output=wide,
        grad_tokens=wide,
        tokens=((group, 2, 1024), BF),
        cotangent=((group, 2, 1024), BF),
        vg=((8, 1024), F32),
        sv=((n, 8, 128), F32),
        rv=((n, 8, 128), F32),
    )
    groups = (dense.buffers(), routed.buffers(), common)
    scratch = [spec for table in groups for spec in table.values()]

    def kernel(*refs):
        refs = list(refs)

        def take(count):
            taken = refs[:count]
            del refs[:count]
            return taken

        inputs = take(4)
        vector_refs = take(5)
        sources = take(8)
        outputs = take(3)
        results = take(8)
        held = take(8)
        dense_refs, routed_refs, common_refs = (
            types.SimpleNamespace(**dict(zip(table, take(len(table)), strict=True))) for table in groups
        )
        b = common_refs
        b.tokens_hbm, b.cotangent_hbm, b.segments, b.routed = inputs
        b.output_hbm, b.grad_tokens_hbm, b.gvec = outputs
        b.vectors = vector_refs
        env = Env(b, refs[0], n)
        dense.attach(env, dense_refs, sources[:4], held[:4], results[:4])
        routed.attach(env, routed_refs, sources[4:], held[4:], results[4:])
        whole_step(env, dense, routed)

    vmem = pl.BlockSpec(memory_space=pltpu.VMEM)
    hbm = pl.BlockSpec(memory_space=pl.ANY)
    outs = [wide, wide, ((8, 128), F32)] + [(shape, F32) for shape in GRADS * 2]
    return pl.pallas_call(
        kernel,
        out_shape=[jax.ShapeDtypeStruct(*spec) for spec in outs],
        in_specs=[hbm] * 2 + [vmem] * 7 + [hbm] * 8,
        out_specs=[hbm] * 2 + [vmem] + [hbm] * 8,
        scratch_shapes=[pltpu.VMEM(shape, BF) for shape in SHAPES * 2]
        + [pltpu.VMEM(*spec) for spec in scratch]
        + [pltpu.SemaphoreType.DMA((384,))],
        compiler_params=pltpu.CompilerParams(
            collective_id=0, has_side_effects=True, vmem_limit_bytes=LIMIT
        ),
    )(tokens, cotangent, segments, routed_places, *vectors, *weights)


def place_results(group, parts):
    def kernel(*refs):
        sources, outs, held, sems = refs[:11], refs[11:26], refs[26:38], refs[38]
        gvec = sources[2]
        grads = list(zip(sources[3:], held[:8], outs[7:], strict=True))
        wides = list(zip(sources[:2], held[8:10], held[10:], outs[:2], strict=True))
        loads = [
            pltpu.make_async_copy(item[0], item[1], sems.at[0, number])
            for number, item in enumerate(wides + grads)
        ]
        for copy in loads:
            copy.start()
        for number in range(5):
            outs[2 + number][...] = gvec[number, 0:64]
        stores = []

        def store(source, target):
            stores.append(pltpu.make_async_copy(source, target, sems.at[1, len(stores)]))
            stores[-1].start()

        for number, (_, rows, turned, target) in enumerate(wides):
            loads[number].wait()
            for seq in range(2):
                turned[:, seq, :] = rows[seq * group : (seq + 1) * group, :]
            store(turned, target)
        for number, (_, block, target) in enumerate(grads):
            loads[2 + number].wait()
            store(block, target)
        for copy in stores:
            copy.wait()

    vmem = pl.BlockSpec(memory_space=pltpu.VMEM)
    hbm = pl.BlockSpec(memory_space=pl.ANY)
    wide, turned = (2 * group, 1024), (group, 2, 1024)
    shapes = [turned] * 2 + [(64,)] * 5 + list(GRADS * 2)
    held = list(GRADS * 2) + [wide] * 2 + [turned] * 2
    return pl.pallas_call(
        kernel,
        out_shape=[jax.ShapeDtypeStruct(shape, F32) for shape in shapes],
        in_specs=[hbm] * 2 + [vmem] + [hbm] * 8,
        out_specs=[hbm] * 2 + [vmem] * 5 + [hbm] * 8,
        scratch_shapes=[pltpu.VMEM(shape, F32) for shape in held]
        + [pltpu.SemaphoreType.DMA((2, 10))],
        compiler_params=pltpu.CompilerParams(vmem_limit_bytes=LIMIT),
    )(*parts)


def on_device_fused(
    tokens,
    segments,
    routed,
    router,
    dense_attn_gain,
    dense_qkv,
    dense_out,
    dense_mlp_gain,
    dense_up,
    dense_down,
    routed_attn_gain,
    routed_qkv,
    routed_out,
    routed_mlp_gain,
    routed_up,
    routed_down,
    cotangent,
):
    group = tokens.shape[0]
    parts = fused(
        group,
        tokens,
        cotangent,
        segments,
        routed,
        (dense_attn_gain, dense_mlp_gain, routed_attn_gain, routed_mlp_gain, router),
        (
            jnp.transpose(dense_qkv, (1, 0, 2)),
            dense_out,
            dense_up,
            dense_down,
            jnp.transpose(routed_qkv, (1, 0, 2)),
            routed_out,
            routed_up,
            routed_down,
        ),
    )
    placed = place_results(group, parts)
    vectors = placed[2:7]

    def weights_of(grads, first, second):
        return (
            vectors[first],
            jnp.transpose(grads[QKV], (1, 0, 2)),
            jnp.transpose(grads[OUT]),
            vectors[second],
            grads[UP],
            jnp.transpose(grads[DOWN]),
        )

    return (
        tuple(placed[:2])
        + weights_of(placed[7:11], 0, 1)
        + weights_of(placed[11:], 2, 3)
        + (vectors[4],)
    )


def solution(mesh):
    in_specs = (
        P("seq", None, None),
        P(),
        P(),
        P(),
        P(),
        P(None, None, "mp"),
        P("mp", None),
        P(),
        P(None, "mp"),
        P("mp", None),
        P(),
        P(None, None, "mp"),
        P("mp", None),
        P(),
        P(None, "mp"),
        P("mp", None),
        P("seq", None, None),
    )
    out_specs = (
        P("seq", None, None),
        P("seq", None, None),
        P("seq"),
        P("seq", None, "mp"),
        P("mp", "seq"),
        P("seq"),
        P("seq", "mp"),
        P("mp", "seq"),
        P("seq"),
        P("seq", None, "mp"),
        P("mp", "seq"),
        P("seq"),
        P("seq", "mp"),
        P("mp", "seq"),
        P("seq"),
    )
    seq_size = mesh.shape["seq"]
    pairs = 2 * (16 // mesh.shape["mp"])
    body = on_device_fused if seq_size == pairs else on_device

    return jax.shard_map(
        body, mesh=mesh, in_specs=in_specs, out_specs=out_specs, check_vma=False
    )
```

```python
import math
import types

import jax
import jax.numpy as jnp
from jax import lax
from jax.experimental import pallas as pl
from jax.experimental.pallas import tpu as pltpu
from jax.sharding import PartitionSpec as P

HEAD_DIM = 64


EPSILON = 1e-06
NEGATIVE = -1e30
PRECISE = lax.Precision.HIGHEST


def rms_norm(hidden, gain):
    return hidden * lax.rsqrt(jnp.mean(hidden * hidden, axis=-1, keepdims=True) + EPSILON) * gain


def gelu_tanh(operand):
    return jax.nn.gelu(operand, approximate=True)


def model_sum(operand):
    return lax.psum(operand, "mp")


def block_loop(row_total, advance, carried):
    block_size = math.gcd(row_total, 512)
    return lax.fori_loop(
        0,
        row_total // block_size,
        lambda number, current: advance(current, number * block_size, block_size),
        carried,
    )


def key_mask(query_places, query_live, key_places, key_live, label_rows):
    query_labels = jnp.take_along_axis(label_rows, query_places, axis=0)
    key_labels = jnp.take_along_axis(label_rows, key_places, axis=0)
    allowed = jnp.transpose(key_places)[:, None, :] <= jnp.transpose(query_places)[:, :, None]
    allowed = allowed & (
        jnp.transpose(key_labels)[:, None, :] == jnp.transpose(query_labels)[:, :, None]
    )
    allowed = allowed & jnp.transpose(key_live)[:, None, :] & jnp.transpose(query_live)[:, :, None]
    return allowed[:, None]


def attend_forward(queries, key_rows, value_rows, own_places, own_live, row_info, label_rows):
    row_count, seq_count, head_count, head_size = queries.shape
    score_scale = head_size ** (-0.5)
    shape_rows = (seq_count, head_count, row_count)
    initial = (
        jnp.full(shape_rows, NEGATIVE, jnp.float32),
        jnp.zeros(shape_rows, jnp.float32),
        jnp.zeros(shape_rows + (head_size,), jnp.float32),
    )
    key_piece = lax.all_gather(key_rows, "seq", axis=0, tiled=True)
    value_piece = lax.all_gather(value_rows, "seq", axis=0, tiled=True)

    def advance(current, offset, block_size):
        highest, totals, summed = current
        key_block = lax.dynamic_slice_in_dim(key_piece, offset, block_size, 0).reshape(
            block_size, seq_count, head_count, head_size
        )
        value_block = lax.dynamic_slice_in_dim(value_piece, offset, block_size, 0).reshape(
            block_size, seq_count, head_count, head_size
        )
        key_places, key_live = row_info(offset, block_size)
        allowed = key_mask(own_places, own_live, key_places, key_live, label_rows)
        scores = (
            jnp.einsum("qshe,kshe->shqk", queries, key_block, preferred_element_type=jnp.float32)
            * score_scale
        )
        scores = jnp.where(allowed, scores, NEGATIVE)
        newest = jnp.maximum(highest, jnp.max(scores, axis=-1))
        weights = jnp.exp(scores - newest[..., None])
        factor = jnp.exp(highest - newest)
        totals = totals * factor + jnp.sum(weights, axis=-1)
        summed = summed * factor[..., None] + jnp.einsum(
            "shqk,kshe->shqe",
            weights.astype(jnp.bfloat16),
            value_block,
            preferred_element_type=jnp.float32,
        )
        return (newest, totals, summed)

    highest, totals, summed = block_loop(key_piece.shape[0], advance, initial)
    mixed_rows = jnp.transpose(summed / totals[..., None], (2, 0, 1, 3)).reshape(
        row_count, seq_count, head_count * head_size
    )
    return (mixed_rows, highest + jnp.log(totals), None)


def attend_backward(
    queries,
    key_rows,
    value_rows,
    grad_mixed,
    mixed_rows,
    log_sum,
    own_places,
    own_live,
    row_info,
    label_rows,
):
    row_count, seq_count, head_count, head_size = queries.shape
    score_scale = head_size ** (-0.5)
    grad_heads = grad_mixed.reshape(row_count, seq_count, head_count, head_size)
    offsets = jnp.sum(
        grad_heads.astype(jnp.float32)
        * mixed_rows.reshape(row_count, seq_count, head_count, head_size),
        axis=-1,
    )
    offsets_rows = jnp.transpose(offsets, (1, 2, 0))
    key_piece = lax.all_gather(key_rows, "seq", axis=0, tiled=True)
    value_piece = lax.all_gather(value_rows, "seq", axis=0, tiled=True)

    def advance(current, offset, block_size):
        key_block = lax.dynamic_slice_in_dim(key_piece, offset, block_size, 0).reshape(
            block_size, seq_count, head_count, head_size
        )
        value_block = lax.dynamic_slice_in_dim(value_piece, offset, block_size, 0).reshape(
            block_size, seq_count, head_count, head_size
        )
        key_places, key_live = row_info(offset, block_size)
        allowed = key_mask(own_places, own_live, key_places, key_live, label_rows)
        scores = (
            jnp.einsum("qshe,kshe->shqk", queries, key_block, preferred_element_type=jnp.float32)
            * score_scale
        )
        scores = jnp.where(allowed, scores, NEGATIVE)
        chances = jnp.exp(scores - log_sum[..., None])
        pushes = jnp.einsum(
            "qshe,kshe->shqk", grad_heads, value_block, preferred_element_type=jnp.float32
        )
        slopes = (chances * (pushes - offsets_rows[..., None])).astype(jnp.bfloat16)
        return current + jnp.einsum(
            "shqk,kshe->qshe", slopes, key_block, preferred_element_type=jnp.float32
        )

    grad_queries = block_loop(key_piece.shape[0], advance, jnp.zeros(queries.shape, jnp.float32))
    log_all, offsets_all = (
        lax.all_gather(jnp.transpose(log_sum, (2, 0, 1)), "seq", axis=0, tiled=True),
        lax.all_gather(offsets, "seq", axis=0, tiled=True),
    )
    own_keys = key_rows.reshape(row_count, seq_count, head_count, head_size)
    own_values = value_rows.reshape(row_count, seq_count, head_count, head_size)
    zero_rows = jnp.zeros(queries.shape, jnp.float32)
    query_flat = queries.reshape(row_count, seq_count, head_count * head_size)
    query_piece = lax.all_gather(query_flat, "seq", axis=0, tiled=True)
    grad_piece = lax.all_gather(grad_mixed, "seq", axis=0, tiled=True)

    def advance(current, offset, block_size):
        key_sum, value_sum = current
        query_block = lax.dynamic_slice_in_dim(query_piece, offset, block_size, 0).reshape(
            block_size, seq_count, head_count, head_size
        )
        grad_block = lax.dynamic_slice_in_dim(grad_piece, offset, block_size, 0).reshape(
            block_size, seq_count, head_count, head_size
        )
        block_log = jnp.transpose(
            lax.dynamic_slice_in_dim(log_all, offset, block_size, 0), (1, 2, 0)
        )
        block_offsets = jnp.transpose(
            lax.dynamic_slice_in_dim(offsets_all, offset, block_size, 0), (1, 2, 0)
        )
        query_places, query_live = row_info(offset, block_size)
        allowed = key_mask(query_places, query_live, own_places, own_live, label_rows)
        scores = (
            jnp.einsum("qshe,kshe->shqk", query_block, own_keys, preferred_element_type=jnp.float32)
            * score_scale
        )
        scores = jnp.where(allowed, scores, NEGATIVE)
        chances = jnp.exp(scores - block_log[..., None])
        pushes = jnp.einsum(
            "qshe,kshe->shqk", grad_block, own_values, preferred_element_type=jnp.float32
        )
        slopes = (chances * (pushes - block_offsets[..., None])).astype(jnp.bfloat16)
        key_sum = key_sum + jnp.einsum(
            "shqk,qshe->kshe", slopes, query_block, preferred_element_type=jnp.float32
        )
        value_sum = value_sum + jnp.einsum(
            "shqk,qshe->kshe",
            chances.astype(jnp.bfloat16),
            grad_block,
            preferred_element_type=jnp.float32,
        )
        return (key_sum, value_sum)

    key_sum, value_sum = block_loop(query_piece.shape[0], advance, (zero_rows, zero_rows))
    flat_shape = (row_count, seq_count, head_count * head_size)
    return (
        (grad_queries * score_scale).reshape(flat_shape),
        (key_sum * score_scale).reshape(flat_shape),
        value_sum.reshape(flat_shape),
    )


def block_forward(hidden, params, row_info, label_rows):
    attn_gain, qkv_weight, out_weight, mlp_gain, up_weight, down_weight = params
    row_count, seq_count, _ = hidden.shape
    head_width = qkv_weight.shape[2]
    head_count = head_width // HEAD_DIM
    own_places, own_live = row_info(lax.axis_index("seq") * row_count, row_count)
    normed = rms_norm(hidden, attn_gain.astype(jnp.float32)).astype(jnp.bfloat16)
    projected = jnp.einsum(
        "rsd,dce->rsce", normed, qkv_weight, preferred_element_type=jnp.float32
    ).astype(jnp.bfloat16)
    queries = projected[:, :, 0].reshape(row_count, seq_count, head_count, HEAD_DIM)
    key_rows = projected[:, :, 1]
    value_rows = projected[:, :, 2]
    mixed_rows, log_sum, kept_rows = attend_forward(
        queries, key_rows, value_rows, own_places, own_live, row_info, label_rows
    )
    mixed_low = mixed_rows.astype(jnp.bfloat16)
    attention = model_sum(
        jnp.einsum("rsh,hd->rsd", mixed_low, out_weight, preferred_element_type=jnp.float32)
    )
    middle = hidden + attention
    normed_mlp = rms_norm(middle, mlp_gain.astype(jnp.float32)).astype(jnp.bfloat16)
    before = jnp.einsum("rsd,df->rsf", normed_mlp, up_weight, preferred_element_type=jnp.float32)
    active = gelu_tanh(before).astype(jnp.bfloat16)
    feed_out = model_sum(
        jnp.einsum("rsf,fd->rsd", active, down_weight, preferred_element_type=jnp.float32)
    )
    stored = (
        hidden,
        normed,
        queries,
        key_rows,
        value_rows,
        mixed_rows,
        log_sum,
        mixed_low,
        middle,
        normed_mlp,
        before,
        active,
        own_places,
        own_live,
        kept_rows,
    )
    return (attention, middle, feed_out, stored)


def block_backward(incoming, stored, params, row_info, label_rows):
    attn_gain, qkv_weight, out_weight, mlp_gain, up_weight, down_weight = params
    (
        hidden,
        normed,
        queries,
        key_rows,
        value_rows,
        mixed_rows,
        log_sum,
        mixed_low,
        middle,
        normed_mlp,
        before,
        active,
        own_places,
        own_live,
        kept_rows,
    ) = stored
    incoming_low = incoming.astype(jnp.bfloat16)
    grad_down = jnp.einsum("rsf,rsd->fd", active, incoming_low, preferred_element_type=jnp.float32)
    grad_active = jnp.einsum(
        "rsd,fd->rsf", incoming_low, down_weight, preferred_element_type=jnp.float32
    )
    _, gelu_pull = jax.vjp(gelu_tanh, before)
    grad_before = gelu_pull(grad_active)[0].astype(jnp.bfloat16)
    grad_up = jnp.einsum("rsd,rsf->df", normed_mlp, grad_before, preferred_element_type=jnp.float32)
    grad_normed_mlp = model_sum(
        jnp.einsum("rsf,df->rsd", grad_before, up_weight, preferred_element_type=jnp.float32)
    )
    _, mlp_pull = jax.vjp(rms_norm, middle, mlp_gain.astype(jnp.float32))
    grad_middle, grad_mlp_gain = mlp_pull(grad_normed_mlp)
    along_low = (incoming + grad_middle).astype(jnp.bfloat16)
    grad_out = jnp.einsum("rsh,rsd->hd", mixed_low, along_low, preferred_element_type=jnp.float32)
    grad_mixed = jnp.einsum(
        "rsd,hd->rsh", along_low, out_weight, preferred_element_type=jnp.float32
    ).astype(jnp.bfloat16)
    grad_queries, grad_keys, grad_values = attend_backward(
        queries,
        key_rows,
        value_rows,
        grad_mixed,
        mixed_rows,
        log_sum,
        own_places,
        own_live,
        row_info,
        label_rows,
    )
    grad_projected = jnp.stack((grad_queries, grad_keys, grad_values), axis=2).astype(jnp.bfloat16)
    grad_qkv = jnp.einsum(
        "rsd,rsce->dce", normed, grad_projected, preferred_element_type=jnp.float32
    )
    grad_normed = model_sum(
        jnp.einsum("rsce,dce->rsd", grad_projected, qkv_weight, preferred_element_type=jnp.float32)
    )
    _, attn_pull = jax.vjp(rms_norm, hidden, attn_gain.astype(jnp.float32))
    grad_hidden, grad_attn_gain = attn_pull(grad_normed)
    return (
        grad_middle + grad_hidden,
        (grad_attn_gain, grad_qkv, grad_out, grad_mlp_gain, grad_up, grad_down),
    )


def on_device(
    tokens,
    segments,
    routed,
    router,
    dense_attn_gain,
    dense_qkv,
    dense_out,
    dense_mlp_gain,
    dense_up,
    dense_down,
    routed_attn_gain,
    routed_qkv,
    routed_out,
    routed_mlp_gain,
    routed_up,
    routed_down,
    cotangent,
):
    group_rows, seq_count, _ = tokens.shape
    devices = lax.axis_size("seq")
    my_index = lax.axis_index("seq")
    capacity = routed.shape[1]
    most_rows = group_rows // 4
    label_rows = jnp.transpose(segments)
    route_rows = jnp.transpose(routed)
    local_ids = jnp.arange(group_rows, dtype=jnp.int32)
    bounds = jnp.arange(devices + 1, dtype=jnp.int32) * group_rows
    starts = jnp.sum((routed[None, :, :] < bounds[:, None, None]).astype(jnp.int32), axis=2)
    first_rank = starts[my_index]
    routed_here = starts[my_index + 1] - first_rank
    dense_params = (dense_attn_gain, dense_qkv, dense_out, dense_mlp_gain, dense_up, dense_down)
    routed_params = (
        routed_attn_gain,
        routed_qkv,
        routed_out,
        routed_mlp_gain,
        routed_up,
        routed_down,
    )

    def dense_info(first_row, row_total):
        places = first_row + jnp.broadcast_to(
            jnp.arange(row_total, dtype=jnp.int32)[:, None], (row_total, seq_count)
        )
        return (places, jnp.ones((row_total, seq_count), jnp.bool_))

    slot_rows = jnp.arange(most_rows, dtype=jnp.int32)
    is_live = slot_rows[:, None] < routed_here[None, :]
    hold_places = (
        jnp.take_along_axis(
            route_rows, jnp.clip(first_rank[None, :] + slot_rows[:, None], 0, capacity - 1), axis=0
        )
        - my_index * group_rows
    )
    hold_table = (
        (jnp.transpose(hold_places)[:, :, None] == local_ids[None, None, :])
        & jnp.transpose(is_live)[:, :, None]
    ).astype(jnp.bfloat16)

    def select_rows(rows_in):
        return jnp.einsum(
            "smc,csd->msd", hold_table, rows_in, preferred_element_type=jnp.float32
        ).astype(jnp.bfloat16)

    def restore_rows(rows_in):
        return jnp.einsum("smc,msd->csd", hold_table, rows_in, preferred_element_type=jnp.float32)

    def routed_info(first_row, row_total):
        number = first_row + jnp.arange(row_total, dtype=jnp.int32)
        source = number // most_rows
        within = number % most_rows
        base = jnp.take(starts, source, axis=0)
        filled = jnp.take(starts, source + 1, axis=0) - base
        rank_rows = jnp.clip(base + within[:, None], 0, capacity - 1)
        return (jnp.take_along_axis(route_rows, rank_rows, axis=0), within[:, None] < filled)

    hidden = tokens.astype(jnp.float32)
    _, middle, feed_out, dense_stored = block_forward(hidden, dense_params, dense_info, label_rows)
    first_out = middle + feed_out
    lifted = select_rows(first_out.astype(jnp.bfloat16))
    routed_attention, _, routed_feed, routed_stored = block_forward(
        lifted.astype(jnp.float32), routed_params, routed_info, label_rows
    )
    sent_rows = (routed_attention + routed_feed).astype(jnp.bfloat16)
    returned = restore_rows(sent_rows)
    router_float = router.astype(jnp.float32)
    gate_value = jax.nn.sigmoid(jnp.einsum("csd,d->cs", first_out, router_float, precision=PRECISE))
    output = first_out + gate_value[:, :, None] * returned
    grad_output = cotangent.astype(jnp.float32)
    grad_sent = select_rows((gate_value[:, :, None] * grad_output).astype(jnp.bfloat16))
    grad_logit = jnp.sum(grad_output * returned, axis=-1) * gate_value * (1.0 - gate_value)
    grad_router = jnp.einsum("cs,csd->d", grad_logit, first_out, precision=PRECISE)
    grad_first = grad_output + grad_logit[:, :, None] * router_float
    routed_branch, routed_grads = block_backward(
        grad_sent.astype(jnp.float32), routed_stored, routed_params, routed_info, label_rows
    )
    grad_first = grad_first + restore_rows(routed_branch.astype(jnp.bfloat16))
    dense_branch, dense_grads = block_backward(
        grad_first, dense_stored, dense_params, dense_info, label_rows
    )
    grad_tokens = grad_first + dense_branch
    summed_all = (
        lax.psum_scatter(dense_grads[0], "seq", scatter_dimension=0, tiled=True),
        lax.psum_scatter(dense_grads[1], "seq", scatter_dimension=0, tiled=True),
        lax.psum_scatter(dense_grads[2], "seq", scatter_dimension=1, tiled=True),
        lax.psum_scatter(dense_grads[3], "seq", scatter_dimension=0, tiled=True),
        lax.psum_scatter(dense_grads[4], "seq", scatter_dimension=0, tiled=True),
        lax.psum_scatter(dense_grads[5], "seq", scatter_dimension=1, tiled=True),
        lax.psum_scatter(routed_grads[0], "seq", scatter_dimension=0, tiled=True),
        lax.psum_scatter(routed_grads[1], "seq", scatter_dimension=0, tiled=True),
        lax.psum_scatter(routed_grads[2], "seq", scatter_dimension=1, tiled=True),
        lax.psum_scatter(routed_grads[3], "seq", scatter_dimension=0, tiled=True),
        lax.psum_scatter(routed_grads[4], "seq", scatter_dimension=0, tiled=True),
        lax.psum_scatter(routed_grads[5], "seq", scatter_dimension=1, tiled=True),
        lax.psum_scatter(grad_router, "seq", scatter_dimension=0, tiled=True),
    )
    dense_sums = tuple(summed_all[0:6])
    routed_sums = tuple(summed_all[6:13])
    return (output, grad_tokens) + tuple(dense_sums) + tuple(routed_sums)


BF = jnp.bfloat16
LIMIT = 63 * 1024 * 1024
F32 = jnp.float32
MESH = pl.DeviceIdType.MESH
PIECE = 1024
WIDTHS = (384, 128, 512, 512)
BEGINS = (0, 384, 512, 1024)
SIZES = (1536, 512, 2048, 2048)
COLS = (None, (0, 512), (512, 2048), None)


def dot(a, b):
    return lax.dot_general(a, b, (((1,), (0,)), ((), ())), preferred_element_type=F32)


def dot_t(a, b):
    return lax.dot_general(a, b, (((1,), (1,)), ((), ())), preferred_element_type=F32)


def dot_l(a, b):
    return lax.dot_general(a, b, (((0,), (0,)), ((), ())), preferred_element_type=F32)


def swap_halves(tile):
    return pltpu.roll(tile, 64, 1)


def low_lanes(rows):
    return lax.broadcasted_iota(jnp.int32, (rows, 128), 1) < 64


def inverse_rms(rows):
    return lax.rsqrt(jnp.mean(rows * rows, axis=1, keepdims=True) + EPSILON)


def norm_back(grad, rows, gain):
    inverse = inverse_rms(rows)
    unit = rows * inverse
    pulled = grad * gain
    grad_rows = inverse * (pulled - unit * jnp.mean(pulled * unit, axis=1, keepdims=True))
    return grad_rows, jnp.sum(grad * unit, axis=0, keepdims=True)


class Env:
    def __init__(self, refs, sems, seq_size):
        self.b = refs
        self.sems = sems
        self.count = 0
        self.sends = []
        self.middle_sends = []
        self.flying = {}
        self.stores = {}
        self.stored = 0
        self.barrier_done = False
        self.n = seq_size
        self.s = lax.axis_index("seq")
        self.c = lax.axis_index("mp")
        self.q = lax.rem(self.s, 4)
        self.z = lax.div(self.s, 4)
        high = lax.div(self.z, 2)
        self.near = self.z + 1 - 2 * lax.rem(self.z, 2)
        self.across = 2 - high
        self.far = 3 - 3 * high
        self.middle = lax.rem(self.z + high, 2) == 1

    def sem(self):
        self.count += 1
        return self.sems.at[self.count - 1]

    def vector(self, number):
        return self.b.vectors[number][...].astype(F32).reshape(1, 1024)

    def greet(self):
        barrier = pltpu.get_barrier_semaphore()

        def signal(step, _):
            other = lax.rem(self.s + step, self.n)
            pl.semaphore_signal(barrier, inc=1, device_id=(other, self.c), device_id_type=MESH)
            return 0

        lax.fori_loop(1, self.n, signal, 0)
        pl.semaphore_signal(barrier, inc=1, device_id=(self.s, 1 - self.c), device_id_type=MESH)

    def meet(self):
        if not self.barrier_done:
            pl.semaphore_wait(pltpu.get_barrier_semaphore(), self.n)
            self.barrier_done = True

    def remote(self, src, dst, send, recv, seq, core):
        return pltpu.make_async_remote_copy(
            src_ref=src,
            dst_ref=dst,
            send_sem=send,
            recv_sem=recv,
            device_id=(seq, core),
            device_id_type=MESH,
        )

    def exchange(self, send_ref, recv_ref):
        self.meet()
        send, recv = self.sem(), self.sem()
        n = self.n

        def start(step, _):
            other = lax.rem(self.s + step, n)
            self.remote(
                send_ref.at[other], recv_ref.at[self.s], send, recv, other, self.c
            ).start()
            return 0

        lax.fori_loop(1, n, start, 0)
        recv_ref[pl.ds(self.s, 1)] = send_ref[pl.ds(self.s, 1)]
        whole = self.remote(
            send_ref.at[pl.ds(0, n - 1)],
            recv_ref.at[pl.ds(0, n - 1)],
            send,
            recv,
            lax.rem(self.s + 1, n),
            self.c,
        )
        self.sends.append(whole)
        return whole.wait_recv

    def core_sum(self, layer, half, chunk, sink):
        self.meet()
        send_ref, recv_ref = layer.b.ps.at[half], layer.b.pr.at[half]
        copies = []
        for number in range(4):
            earlier = self.flying.pop((layer.packed, half, number), None)
            if earlier is not None:
                earlier.wait_send()
            send_ref[number] = chunk(number).astype(BF)
            copy = self.remote(
                send_ref.at[number], recv_ref.at[number], self.sem(), self.sem(), self.s, 1 - self.c
            )
            copy.start()
            copies.append(copy)
            self.flying[(layer.packed, half, number)] = copy
        for number, copy in enumerate(copies):
            copy.wait_recv()
            sink(number, send_ref[number].astype(F32) + recv_ref[number].astype(F32))

    def plane_send(self, pieces, recv_piece, wait_piece):
        self.meet()
        send, recv = self.sem(), self.sem()
        for step in range(1, 4):
            other = lax.rem(self.q + step, 4)
            self.remote(
                pieces(other), recv_piece, send, recv, self.z * 4 + other, self.c
            ).start()
        whole = self.remote(wait_piece, wait_piece, send, recv, self.z * 4 + lax.rem(self.q + 1, 4), self.c)
        self.sends.append(whole)
        return whole.wait_recv

    def line_send(self, pieces, recv_piece, wait_piece):
        self.meet()
        send, recv = self.sem(), self.sem()
        for step in range(1, 4):
            other = lax.rem(self.z + step, 4)
            self.remote(
                pieces(other), recv_piece(step), send, recv, other * 4 + self.q, self.c
            ).start()
        whole = self.remote(wait_piece, wait_piece, send, recv, lax.rem(self.z + 1, 4) * 4 + self.q, self.c)
        self.sends.append(whole)
        return whole.wait_recv

    def line_reduce(self, blocks, slots):
        self.meet()
        receive = [self.sem() for _ in range(4)]
        send = [self.sem() for _ in range(3)]

        def copy(block, slot, way, z):
            return self.remote(
                blocks.at[block], slots.at[slot], send[way], receive[slot], z * 4 + self.q, self.c
            )

        @pl.when(jnp.logical_not(self.middle))
        def _():
            copy(self.far, 3, 2, self.near).start()
            copy(self.across, 2, 1, self.near).start()

        copy(self.near, 0, 0, self.near).start()

        self.sends += [copy(0, 0, way, self.near) for way in range(3)]

        def arrived(slot):
            copy(0, slot, 0, self.near).wait_recv()

        def pass_on(slot):
            block = (self.across, self.far)[slot - 2]
            copy(block, 1, slot - 1, block).start()

        def finish():
            for slot in range(2):
                copy(0, slot, 0, self.near).wait_recv()

        return arrived, pass_on, finish

    def line_gather(self, ref):
        self.meet()
        receive = [self.sem() for _ in range(3)]
        send = [self.sem() for _ in range(5)]

        def copy(piece, way, slot, z):
            return self.remote(
                ref.at[piece], ref.at[piece], send[way], receive[slot], z * 4 + self.q, self.c
            )

        copy(self.z, 0, 0, self.near).start()

        @pl.when(self.middle)
        def _():
            copy(self.z, 1, 1, self.across).start()

        def second():
            @pl.when(self.middle)
            def _():
                copy(0, 0, 0, self.near).wait_recv()
                copy(self.near, 2, 2, self.across).start()
                copy(0, 0, 1, self.near).wait_recv()
                copy(self.across, 3, 1, self.near).start()

        def third():
            @pl.when(self.middle)
            def _():
                copy(0, 0, 2, self.near).wait_recv()
                copy(self.far, 4, 2, self.near).start()

        self.sends.append(copy(0, 0, 0, self.near))
        self.middle_sends += [copy(0, way, 0, self.near) for way in range(1, 5)]

        def finish():
            @pl.when(jnp.logical_not(self.middle))
            def _():
                for slot in range(3):
                    copy(0, 0, slot, self.near).wait_recv()

        return second, third, finish

    def store(self, result, which, at, fill):
        slot = self.stored % 4
        self.stored += 1
        if slot in self.stores:
            self.stores.pop(slot).wait()
        stage = self.b.stage.at[slot]
        fill(stage)
        target = result.at[at // 512] if which == 0 else result.at[:, pl.ds(at, 512)]
        copy = pltpu.make_async_copy(stage, target, self.sem())
        copy.start()
        self.stores[slot] = copy

    def drain(self):
        for copy in self.sends + list(self.flying.values()):
            copy.wait_send()
        for copy in self.stores.values():
            copy.wait()

        @pl.when(self.middle)
        def _():
            for copy in self.middle_sends:
                copy.wait_send()


class Layer:
    def __init__(self, packed, per, n):
        self.per = per
        self.n = n
        self.rows = 2 * per
        self.packed = packed
        self.value_rows = per // 2 if self.packed else per
        self.message = per + self.value_rows
        self.total = n * per
        self.block = 256
        self.gains = (0, 1) if packed else (2, 3)

    def attach(self, env, refs, sources, weights, results):
        self.b = refs
        self.sources = sources
        self.held = weights
        self.results = results
        self.right_waits, self.left_waits, self.line_waits, self.hops = {}, {}, {}, {}
        self.loads = {}

    def load(self, env, number):
        copy = pltpu.make_async_copy(self.sources[number], self.held[number], env.sem())
        copy.start()
        self.loads[number] = copy

    def weight(self, number):
        if number in self.loads:
            self.loads.pop(number).wait()
        return self.held[number]

    def buffers(self):
        r, t, n = self.rows, self.total, self.n
        vr, m = self.value_rows, self.message
        table = dict(
            x=((r, 1024), BF),
            normed=((r, 1024), BF),
            s1=((n, m, 128), BF),
            r1=((n, m, 128), BF),
            qa=((t, 128), BF),
            kb=((t, 128), BF),
            va=((t, 128), BF),
            mixp=((t, 128), F32),
            lse=((t, 128), F32),
            s2=((n, vr, 128), BF),
            r2=((n, vr, 128), BF),
            mixl=((r, 512), BF),
            mid=((r, 1024), F32),
            nm=((r, 1024), BF),
            gp=((r, 2048), BF),
            act=((r, 2048), BF),
            e=((r, 1024), F32),
            el=((r, 1024), BF),
            gb=((r, 2048), BF),
            gm=((r, 1024), F32),
            al=((r, 1024), BF),
            s6=((n, vr, 128), BF),
            r6=((n, vr, 128), BF),
            gx=((t, 128), BF),
            dk=((t, 128), F32),
            dv=((t, 128), F32),
            s7=((n, m, 128), BF),
            r7=((n, m, 128), BF),
            dp=((r, 1536), BF),
            acc=((r, 1024), F32),
            ps=((2, 4, r, 256), BF),
            pr=((2, 4, r, 256), BF),
        )
        if self.packed:
            table.update(
                ng=((4, 4, self.per, 1024), BF),
                x7=((t, 256), BF),
                s9=((n, m, 128), BF),
                r9=((n, m, 128), BF),
                fg=((4, r, 2560), BF),
                ds=((4, r, 512), BF),
                dg=((4, r, 512), BF),
                sb=((4, 64, 2560), BF),
                rb=((4, 64, 2560), BF),
                ul=((4, r, 1024), BF),
                ur=((4, r, 512), BF),
                us=((4, 256, 512), BF),
                ub=((4, 256, 512), BF),
                ux=((4, 64, 512), BF),
                uy=((4, 64, 512), BF),
            )
        else:
            table.update(
                fg=((4, 4, r, 1536), BF),
                dg=((4, 4, r, 1024), BF),
                sb=((4, 64, 1536), BF),
                rb=((4, 64, 1536), BF),
                same=((t, t), F32),
                lab=((t, 128), BF),
                hot=((2, self.per, 64), BF),
                labs=((r, 128), F32),
            )
        return table

    def gain(self, env, which):
        return env.vector(self.gains[which])

    def pack(self, tile):
        if not self.packed:
            return tile
        half = self.per // 2
        return jnp.where(low_lanes(half), tile[:half], swap_halves(tile[half:]))

    def send_pairs(self, store, tile_of):
        for seq in range(2):
            for j in range(4):
                tile = tile_of(seq, j)
                store(8 * seq + 2 * j, self.pack(tile))
                store(8 * seq + 2 * j + 1, self.pack(swap_halves(tile)))

    def join_pairs(self, tile_a, tile_b):
        vr = self.value_rows
        low = low_lanes(vr)
        first = jnp.where(low, tile_a, swap_halves(tile_b))
        if not self.packed:
            return [first]
        return [first, jnp.where(low, swap_halves(tile_a), tile_b)]

    def project(self, env, then=None):
        hidden = self.b.x[...].astype(F32)
        normed = (hidden * inverse_rms(hidden) * self.gain(env, 0)).astype(BF)
        self.b.normed[...] = normed
        weight = self.weight(QKV)
        if then is not None:
            then()
        queries, keys, values = (dot(normed, weight[part]) for part in range(3))
        send = self.b.s1
        per = self.per
        low = low_lanes(per)
        for seq in range(2):
            rows = slice(seq * per, (seq + 1) * per)
            for j in range(4):
                cols = slice(128 * j, 128 * j + 128)
                qt, kt, vt = queries[rows, cols], keys[rows, cols], values[rows, cols]
                pair = 8 * seq + 2 * j
                send[pair, 0:per] = jnp.where(low, qt, swap_halves(kt)).astype(BF)
                send[pair + 1, 0:per] = jnp.where(low, swap_halves(qt), kt).astype(BF)
                va, vb = vt, swap_halves(vt)
                if self.packed:
                    va, vb = self.pack(va), self.pack(vb)
                else:
                    labels = self.b.labs[rows, :]
                    va, vb = jnp.where(low, va, labels), jnp.where(low, vb, labels)
                send[pair, per:] = va.astype(BF)
                send[pair + 1, per:] = vb.astype(BF)
        self.wait1 = env.exchange(send, self.b.r1)

    def unpack(self, env):
        recv = self.b.r1
        qa, kb, va = self.b.qa, self.b.kb, self.b.va
        per, vr = self.per, self.value_rows
        low, low_v = low_lanes(per), low_lanes(vr)
        zero = jnp.zeros((per, 128), F32)
        zero_v = jnp.zeros((vr, 128), F32)
        for i in range(self.n):
            both = recv[i, 0:per].astype(F32)
            qa[i * per : (i + 1) * per] = jnp.where(low, both * 0.125, zero).astype(BF)
            kb[i * per : (i + 1) * per] = swap_halves(both).astype(BF)
            tile = recv[i, per:].astype(F32)
            va[i * per : i * per + vr] = jnp.where(low_v, tile, zero_v).astype(BF)
            if self.packed:
                va[i * per + vr : (i + 1) * per] = jnp.where(low_v, swap_halves(tile), zero_v).astype(BF)
            else:
                self.b.lab[i * per : (i + 1) * per] = jnp.where(low_v, zero_v, tile).astype(BF)
        if not self.packed:
            labels = self.b.lab[...]
            self.b.same[...] = dot_t(labels, labels)

    def allowed(self, env, start, stop):
        size = stop - start
        rows = lax.broadcasted_iota(jnp.int32, (size, stop), 0) + start
        keys = lax.broadcasted_iota(jnp.int32, (size, stop), 1)
        ok = keys <= rows
        if self.packed:
            segments = env.b.segments[pl.ds(lax.div(env.s, 8), 1), :]
            row = (lax.broadcasted_iota(jnp.int32, (size, 1), 0) + start).astype(F32)
            opening = jnp.zeros((size, 1), F32)
            for label in range(1, 4):
                edge = jnp.sum((segments < label).astype(F32), axis=1, keepdims=True)
                opening = jnp.where(row >= edge, jnp.maximum(opening, edge), opening)
            return ok & (keys >= opening.astype(jnp.int32))
        return ok & (self.b.same[start:stop, 0:stop] > 0.5)

    def attend(self, env):
        self.wait1()
        self.unpack(env)
        qa, kb, va = self.b.qa, self.b.kb, self.b.va
        mixp, lse = self.b.mixp, self.b.lse
        for start in range(0, self.total, self.block):
            stop = start + self.block
            scores = dot_t(qa[start:stop], kb[0:stop])
            scores = jnp.where(self.allowed(env, start, stop), scores, NEGATIVE)
            highest = jnp.max(scores, axis=1, keepdims=True)
            weights = jnp.exp(scores - highest)
            totals = jnp.sum(weights, axis=1, keepdims=True)
            mixp[start:stop] = dot(weights.astype(BF), va[0:stop]) / totals
            lse[start:stop] = jnp.broadcast_to(highest + jnp.log(totals), (self.block, 128))
        send = self.b.s2
        for i in range(self.n):
            send[i] = self.pack(mixp[i * self.per : (i + 1) * self.per]).astype(BF)
        self.wait2 = env.exchange(send, self.b.r2)

    def gather_heads(self, recv, row0, put):
        per, vr = self.per, self.value_rows
        for seq in range(2):
            for j in range(4):
                pair = 8 * seq + 2 * j
                tiles = self.join_pairs(
                    recv[pair, row0:].astype(F32), recv[pair + 1, row0:].astype(F32)
                )
                for number, tile in enumerate(tiles):
                    begin = seq * per + number * vr
                    put(slice(begin, begin + vr), slice(128 * j, 128 * j + 128), tile)

    def feed(self, env, finish, then=None):
        self.wait2()
        mixl = self.b.mixl

        def put(rows, cols, tile):
            mixl[rows, cols] = tile.astype(BF)

        self.gather_heads(self.b.r2, 0, put)
        out = self.weight(OUT)
        mid = self.b.mid
        hidden = self.b.x
        mixed = mixl[...]

        def sink(number, value):
            cols = slice(256 * number, 256 * number + 256)
            mid[:, cols] = value + hidden[:, cols].astype(F32)

        env.core_sum(
            self,
            0,
            lambda number: dot(mixed, out[:, 256 * number : 256 * number + 256]),
            sink,
        )
        middle = mid[...]
        normed = (middle * inverse_rms(middle) * self.gain(env, 1)).astype(BF)
        self.b.nm[...] = normed
        up = self.weight(UP)
        act, slope = self.b.act, self.b.gp
        for number in range(4):
            cols = slice(512 * number, 512 * number + 512)
            before = dot(normed, up[:, cols])
            square = before * before
            bent = jnp.tanh(0.7978845608028654 * before * (1.0 + 0.044715 * square))
            half = 0.5 * (1.0 + bent)
            act[:, cols] = (before * half).astype(BF)
            slope[:, cols] = (
                half
                + 0.5 * before * (1.0 - bent * bent) * (0.7978845608028654 + 0.1070322243 * square)
            ).astype(BF)
        if then is not None:
            then()
        down = self.weight(DOWN)
        env.core_sum(
            self,
            1,
            lambda number: dot(act[...], down[:, 256 * number : 256 * number + 256]),
            finish,
        )

    def round_incoming(self):
        self.b.el[...] = self.b.e[...].astype(BF)

    def back_feed(self, env):
        grad_low = self.b.el[...]
        down, up, out = self.weight(DOWN), self.weight(UP), self.weight(OUT)
        gb, slope = self.b.gb, self.b.gp
        for number in range(4):
            cols = slice(512 * number, 512 * number + 512)
            grad = dot_t(grad_low, down[cols, :])
            gb[:, cols] = (grad * slope[:, cols].astype(F32)).astype(BF)
        acc = self.b.acc

        def sink(number, value):
            acc[:, 256 * number : 256 * number + 256] = value

        env.core_sum(
            self,
            0,
            lambda number: dot_t(gb[...], up[256 * number : 256 * number + 256, :]),
            sink,
        )
        grad_mid, grad_gain = norm_back(acc[...], self.b.mid[...], self.gain(env, 1))
        row = self.gains[1]
        env.b.vg[row : row + 1, :] = grad_gain
        self.b.gm[...] = grad_mid
        along = (self.b.e[...] + grad_mid).astype(BF)
        self.b.al[...] = along
        grad_mixed = dot_t(along, out[...])
        send = self.b.s6
        per = self.per

        def store(pair, tile):
            send[pair] = tile.astype(BF)

        self.send_pairs(
            store,
            lambda seq, j: grad_mixed[seq * per : (seq + 1) * per, 128 * j : 128 * j + 128],
        )
        self.wait6 = env.exchange(send, self.b.r6)

    def back_attend(self, env):
        self.wait6()
        recv, gx = self.b.r6, self.b.gx
        per, vr = self.per, self.value_rows
        low_v = low_lanes(vr)
        zero_v = jnp.zeros((vr, 128), F32)
        for i in range(self.n):
            tile = recv[i].astype(F32)
            gx[i * per : i * per + vr] = jnp.where(low_v, tile, zero_v).astype(BF)
            if self.packed:
                gx[i * per + vr : (i + 1) * per] = jnp.where(low_v, swap_halves(tile), zero_v).astype(BF)
        qa, kb, va = self.b.qa, self.b.kb, self.b.va
        mixp, lse = self.b.mixp, self.b.lse
        dk, dv = self.b.dk, self.b.dv
        dk[...] = jnp.zeros_like(dk)
        dv[...] = jnp.zeros_like(dv)
        dq = {}
        for start in range(0, self.total, self.block):
            stop = start + self.block
            query, grad = qa[start:stop], gx[start:stop]
            scores = dot_t(query, kb[0:stop])
            scores = jnp.where(self.allowed(env, start, stop), scores, NEGATIVE)
            probs = jnp.exp(scores - lse[start:stop, 0:1])
            offsets = jnp.sum(grad.astype(F32) * mixp[start:stop], axis=1, keepdims=True)
            slopes = (probs * (dot_t(grad, va[0:stop]) - offsets)).astype(BF)
            mixp[start:stop] = dot(slopes, kb[0:stop])
            dk[0:stop] += dot_l(slopes, query)
            dv[0:stop] += dot_l(probs.astype(BF), grad)
        send = self.b.s7
        low = low_lanes(per)
        for i in range(self.n):
            rows = slice(i * per, (i + 1) * per)
            send[i, 0:per] = jnp.where(low, mixp[rows] * 0.125, swap_halves(dk[rows])).astype(BF)
            send[i, per:] = self.pack(dv[rows]).astype(BF)
            if self.packed:
                self.b.x7[rows, 0:128] = send[i, 0:per]
                self.b.x7[rows, 128:256] = dv[rows].astype(BF)
        self.wait7 = env.exchange(send, self.b.r7)

    def back_project(self, env, finish, then=None):
        self.wait7()
        recv, dp = self.b.r7, self.b.dp
        per = self.per
        low = low_lanes(per)
        for seq in range(2):
            rows = slice(seq * per, (seq + 1) * per)
            for j in range(4):
                pair = 8 * seq + 2 * j
                one, two = recv[pair, 0:per].astype(F32), recv[pair + 1, 0:per].astype(F32)
                dp[rows, 128 * j : 128 * j + 128] = jnp.where(low, one, swap_halves(two)).astype(BF)
                dp[rows, 512 + 128 * j : 640 + 128 * j] = jnp.where(low, swap_halves(one), two).astype(BF)

        def put(rows, cols, tile):
            dp[rows, 1024 + cols.start : 1024 + cols.stop] = tile.astype(BF)

        self.gather_heads(recv, per, put)
        if then is not None:
            then()
        weight = self.weight(QKV)
        acc = self.b.acc

        def chunk(number):
            rows = slice(256 * number, 256 * number + 256)
            total = dot_t(dp[:, 0:512], weight[0, rows, :])
            total += dot_t(dp[:, 512:1024], weight[1, rows, :])
            return total + dot_t(dp[:, 1024:1536], weight[2, rows, :])

        def sink(number, value):
            acc[:, 256 * number : 256 * number + 256] = value

        env.core_sum(self, 1, chunk, sink)
        grad_hidden, grad_gain = norm_back(
            acc[...], self.b.x[...].astype(F32), self.gain(env, 0)
        )
        row = self.gains[0]
        env.b.vg[row : row + 1, :] = grad_gain
        finish(self.b.gm[...] + grad_hidden)

    def parts(self, env, which):
        b = self.b
        left = (b.normed, b.al, b.nm, b.el)[which]
        right = (b.dp, b.mixl, b.gb, b.act)[which]
        return left, right

    def share_right(self, env, which, begin=0, size=None):
        at, full = COLS[which]
        size = full if size is None else size
        _, right = self.parts(env, which)
        fg = self.b.fg
        cols = pl.ds(at + begin, size)
        fg[pl.ds(env.q, 1), :, cols] = right[:, begin : begin + size][None]
        mine = fg.at[env.q, :, cols]
        self.right_waits.setdefault(which, []).append(
            env.plane_send(lambda other: mine, mine, fg.at[pl.ds(0, 3), :, cols])
        )

    def share_left(self, env, which):
        left, _ = self.parts(env, which)
        ds, dg = self.b.ds, self.b.dg
        low = low_lanes(self.rows)
        begin = 256 * (which - 1)
        for a in range(2):
            tiles = [
                left[:, 128 * (2 * z + a) : 128 * (2 * z + a) + 128].astype(F32) for z in range(4)
            ]
            for two in range(2):
                even, odd = tiles[2 * two], tiles[2 * two + 1]
                at = begin + 128 * two
                ds[2 * a, :, at : at + 128] = jnp.where(low, even, swap_halves(odd)).astype(BF)
                ds[2 * a + 1, :, at : at + 128] = jnp.where(low, swap_halves(even), odd).astype(BF)
        cols = pl.ds(begin, 256)
        dg[pl.ds(env.q, 1), :, begin : begin + 256] = ds[pl.ds(env.q, 1), :, begin : begin + 256]
        self.left_waits[which] = env.plane_send(
            lambda other: ds.at[other, :, cols],
            dg.at[env.q, :, cols],
            dg.at[pl.ds(0, 3), :, cols],
        )

    def multiply(self, env, which, first=0, last=None):
        if first == 0:
            self.left_waits[which]()
        self.right_waits[which].pop(0)()
        if last is None:
            for wait in self.right_waits.pop(which):
                wait()
        begin, size = COLS[which]
        last = size if last is None else last
        fg, dg, sb, rb = self.b.fg, self.b.dg, self.b.sb, self.b.rb
        rows = 4 * self.rows
        left = dg[:, :, 256 * (which - 1) : 256 * which].reshape(rows, 256)
        for at in range(begin + first, begin + last, 512):
            right = fg[:, :, at : at + 512].reshape(rows, 512)
            product = dot_l(left, right)
            for z in range(4):
                sb[z, :, at : at + 512] = product[64 * z : 64 * z + 64].astype(BF)
            if (at + 512 - begin) % PIECE == 0 or at + 512 == begin + last:
                low = begin + (at - begin) // PIECE * PIECE
                cols = pl.ds(low, at + 512 - low)
                steps = env.line_reduce(sb.at[:, :, cols], rb.at[:, :, cols])
                self.line_waits.setdefault(which, []).append((low, at + 512, steps))

    def relay(self, env, which, pieces=None):
        sb, rb = self.b.sb, self.b.rb
        for low, high, (arrived, pass_on, _) in self.line_waits[which][pieces or slice(None)]:

            @pl.when(env.middle)
            def _():
                for slot, block in ((3, env.far), (2, env.across)):
                    arrived(slot)
                    for at in range(low, high, 512):
                        cols = slice(at, at + 512)
                        total = sb[pl.ds(block, 1), :, cols].astype(F32)
                        total = total + rb[slot : slot + 1, :, cols].astype(F32)
                        sb[pl.ds(block, 1), :, cols] = total.astype(BF)
                    pass_on(slot)

    def collect(self, env, which):
        begin, _ = COLS[which]
        sb, rb = self.b.sb, self.b.rb
        for low, high, (_, _, finish) in self.line_waits[which]:
            finish()
            for at in range(low, high, 512):
                cols = slice(at, at + 512)

                def fill(stage):
                    total = sb[pl.ds(env.z, 1), :, cols].astype(F32)
                    for slot in range(2):
                        total = total + rb[slot : slot + 1, :, cols].astype(F32)
                    stage[...] = total[0]

                env.store(self.results[which], which, at - begin, fill)

    def quarter_left(self, env):
        ul, left = self.b.ul, self.b.el
        cols = pl.ds(pl.multiple_of(512 * env.c, 512), 512)
        ul[pl.ds(env.q, 1), :, cols] = left[:, cols][None]
        self.quarter_wait = env.plane_send(
            lambda other: left.at[:, cols], ul.at[env.q, :, cols], ul.at[pl.ds(0, 3), :, cols]
        )

    def quarter_core(self, env):
        self.quarter_wait()
        mine = self.b.ul.at[:, :, pl.ds(pl.multiple_of(512 * env.c, 512), 512)]
        copy = env.remote(mine, mine, env.sem(), env.sem(), env.s, 1 - env.c)
        copy.start()
        env.sends.append(copy)
        self.quarter_wait = copy.wait_recv

    def quarter_right(self, env):
        right, ur = self.b.act, self.b.ur

        def quarter(number):
            return pl.ds(pl.multiple_of(number * 512, 512), 512)

        ur[pl.ds(env.q, 1)] = right[:, quarter(env.q)][None]
        self.quarter_columns = env.plane_send(
            lambda other: right.at[:, quarter(other)], ur.at[env.q], ur.at[pl.ds(0, 3)]
        )

    def quarter_multiply(self, env):
        self.quarter_wait()
        self.quarter_columns()
        ul, ur, us, ub = self.b.ul, self.b.ur, self.b.us, self.b.ub
        rows = 4 * self.rows
        left = ul[...].reshape(rows, 1024)
        self.quarter_steps = []
        for at in range(0, 512, 256):
            product = dot_l(left, ur[:, :, at : at + 256].reshape(rows, 256))
            for z in range(4):
                us[z, :, at : at + 256] = product[256 * z : 256 * z + 256].astype(BF)
            cols = pl.ds(at, 256)
            self.quarter_steps.append(env.line_reduce(us.at[:, :, cols], ub.at[:, :, cols]))

    def quarter_relay(self, env):
        us, ub = self.b.us, self.b.ub
        for number, (arrived, pass_on, _) in enumerate(self.quarter_steps):
            cols = slice(256 * number, 256 * number + 256)

            @pl.when(env.middle)
            def _():
                for slot, block in ((3, env.far), (2, env.across)):
                    arrived(slot)
                    total = us[pl.ds(block, 1), :, cols].astype(F32)
                    total = total + ub[slot : slot + 1, :, cols].astype(F32)
                    us[pl.ds(block, 1), :, cols] = total.astype(BF)
                    pass_on(slot)

    def quarter_share(self, env):
        us, ub, ux, uy = self.b.us, self.b.ub, self.b.ux, self.b.uy
        for number, (_, _, finish) in enumerate(self.quarter_steps):
            finish()
            cols = slice(256 * number, 256 * number + 256)
            total = us[pl.ds(env.z, 1), :, cols].astype(F32)
            for slot in range(2):
                total = total + ub[slot : slot + 1, :, cols].astype(F32)
            for q in range(4):
                ux[q, :, cols] = total[0, 64 * q : 64 * q + 64].astype(BF)
        uy[pl.ds(env.q, 1)] = ux[pl.ds(env.q, 1)]
        self.quarter_back = env.plane_send(
            lambda other: ux.at[other], uy.at[env.q], uy.at[pl.ds(0, 3)]
        )

    def quarter_collect(self, env):
        self.quarter_back()
        for q in range(4):

            def fill(stage):
                stage[...] = self.b.uy[q].astype(F32)

            env.store(self.results[DOWN], DOWN, 512 * q, fill)

    def gather_line(self, env):
        normed, ng, per = self.b.normed, self.b.ng, self.per
        cols = pl.ds(pl.multiple_of(512 * env.c, 512), 512)

        def rows(z):
            return pl.ds(pl.multiple_of(lax.div(z, 2) * per, per), per)

        ng[pl.ds(env.z, 1), pl.ds(env.q, 1), :, cols] = normed[rows(env.z), cols][None, None]
        self.gather_wait = env.line_send(
            lambda other: normed.at[rows(other), cols],
            lambda step: ng.at[env.z, env.q, :, cols],
            ng.at[pl.ds(0, 3), 0, :, cols],
        )

    def gather_plane(self, env):
        self.gather_wait()
        ng = self.b.ng
        cols = pl.ds(pl.multiple_of(512 * env.c, 512), 512)
        mine = ng.at[:, env.q, :, cols]
        self.gather_wait = env.plane_send(lambda other: mine, mine, ng.at[:, pl.ds(0, 3), :, cols])

    def gather_core(self, env):
        self.gather_wait()
        cols = pl.ds(pl.multiple_of(512 * env.c, 512), 512)
        mine = self.b.ng.at[:, :, :, cols]
        copy = env.remote(mine, mine, env.sem(), env.sem(), env.s, 1 - env.c)
        copy.start()
        env.sends.append(copy)
        self.gather_wait = copy.wait_recv

    def head_gradient(self, env):
        self.gather_wait()
        per, total = self.per, self.total
        product = dot_l(self.b.x7[...], self.b.ng[...].reshape(total, 1024))
        turned = jnp.transpose(product)
        send = self.b.s9
        for i in range(self.n):
            rows = slice(i * 64, i * 64 + 64)
            send[i, 0:per] = turned[rows, 0:128].astype(BF)
            send[i, per:] = self.pack(turned[rows, 128:256]).astype(BF)
        self.wait9 = env.exchange(send, self.b.r9)

    def head_collect(self, env):
        self.wait9()
        recv, per, vr = self.b.r9, self.per, self.value_rows
        low = low_lanes(per)

        def both(pair, rows):
            return recv[pair, rows].astype(F32) + recv[pair + 8, rows].astype(F32)

        for part in range(3):

            def fill(stage):
                for j in range(4):
                    cols = slice(128 * j, 128 * j + 128)
                    rows = slice(0, per) if part < 2 else slice(per, per + vr)
                    one, two = both(2 * j, rows), both(2 * j + 1, rows)
                    if part == 0:
                        stage[:, cols] = jnp.where(low, one, swap_halves(two))
                    elif part == 1:
                        stage[:, cols] = jnp.where(low, swap_halves(one), two)
                    else:
                        first, second = self.join_pairs(one, two)
                        stage[0:vr, cols] = first
                        stage[vr:, cols] = second

            env.store(self.results[QKV], QKV, 512 * part, fill)

    def spread_right(self, env, which):
        _, right = self.parts(env, which)
        fg, width = self.b.fg, WIDTHS[which]
        cols = pl.ds(BEGINS[which], width)

        def quarter(number):
            return pl.ds(pl.multiple_of(number * width, 128), width)

        fg[pl.ds(env.z, 1), pl.ds(env.q, 1), :, cols] = right[:, quarter(env.q)][None, None]
        self.right_waits[which] = env.plane_send(
            lambda other: right.at[:, quarter(other)],
            fg.at[env.z, env.q, :, cols],
            fg.at[env.z, pl.ds(0, 3), :, cols],
        )

    def spread_right_on(self, env, which):
        self.right_waits[which]()
        fg = self.b.fg
        cols = pl.ds(BEGINS[which], WIDTHS[which])
        self.hops[which] = env.line_gather(fg.at[:, :, :, cols])

    def spread_hop(self, env, which, number):
        self.hops[which][number]()

    def spread_left(self, env, which):
        left, _ = self.parts(env, which)
        dg = self.b.dg

        def quarter(number):
            return pl.ds(pl.multiple_of(number * 256 + 128 * env.c, 128), 128)

        cols = self.core_cols(env, which)
        dg[pl.ds(env.z, 1), pl.ds(env.q, 1), :, cols] = left[:, quarter(env.z)][None, None]
        self.left_waits[which] = env.line_send(
            lambda other: left.at[:, quarter(other)],
            lambda step: dg.at[env.z, env.q, :, cols],
            dg.at[pl.ds(0, 3), env.q, :, cols],
        )

    def core_cols(self, env, which):
        return pl.ds(pl.multiple_of(256 * which + 128 * env.c, 128), 128)

    def spread_left_on(self, env, which):
        self.left_waits[which]()
        dg = self.b.dg
        cols = self.core_cols(env, which)
        mine = dg.at[:, env.q, :, cols]
        self.left_waits[which] = env.plane_send(
            lambda other: mine, mine, dg.at[:, pl.ds(0, 3), :, cols]
        )

    def spread_left_core(self, env, which):
        self.left_waits[which]()
        mine = self.b.dg.at[:, :, :, self.core_cols(env, which)]
        copy = env.remote(mine, mine, env.sem(), env.sem(), env.s, 1 - env.c)
        copy.start()
        env.sends.append(copy)
        self.left_waits[which] = copy.wait_recv

    def spread_multiply(self, env, which):
        self.hops[which][2]()
        self.left_waits[which]()
        fg, dg, sb, rb = self.b.fg, self.b.dg, self.b.sb, self.b.rb
        width = WIDTHS[which]
        cols = pl.ds(BEGINS[which], width)
        rows = 16 * self.rows
        product = dot_l(
            dg[:, :, :, 256 * which : 256 * which + 256].reshape(rows, 256),
            fg[:, :, :, cols].reshape(rows, width),
        ).astype(BF)
        for number in range(4):
            sb[number, :, cols] = product[64 * number : 64 * number + 64]
        rb[pl.ds(env.q, 1), :, cols] = sb[pl.ds(env.q, 1), :, cols]
        self.line_waits[which] = env.plane_send(
            lambda other: sb.at[other, :, cols],
            rb.at[env.q, :, cols],
            rb.at[pl.ds(0, 3), :, cols],
        )

    def spread_collect(self, env, which):
        self.line_waits[which]()
        rb, begin, width = self.b.rb, BEGINS[which], WIDTHS[which]
        for at in range(0, SIZES[which], 512):

            def fill(stage):
                for inner in range(0, 512, 128):
                    source, offset = divmod(at + inner, width)
                    stage[:, inner : inner + 128] = rb[
                        source, :, begin + offset : begin + offset + 128
                    ].astype(F32)

            env.store(self.results[which], which, at, fill)


def pick_rows(env, dense, routed):
    hot, labs, first = routed.b.hot, routed.b.labs, env.b.first
    group, slots = dense.per, routed.per
    base = env.s * group
    for seq in range(2):
        listed = env.b.routed[seq : seq + 1, :]
        places = listed.shape[1]
        place = lax.broadcasted_iota(jnp.int32, (group, places), 0) + base
        here = (place == listed).astype(F32).astype(BF)
        before = jnp.sum((listed < base).astype(F32), axis=1, keepdims=True).astype(jnp.int32)
        number = lax.broadcasted_iota(jnp.int32, (slots, places), 1) - before
        slot = lax.broadcasted_iota(jnp.int32, (slots, places), 0)
        mine = (number == slot).astype(F32).astype(BF)
        table = dot_t(mine, here).astype(BF)
        hot[seq] = table
        segments = env.b.segments[seq : seq + 1, :]
        row = (lax.broadcasted_iota(jnp.int32, (group, 1), 0) + base).astype(F32)
        label = jnp.zeros((group, 1), F32)
        for number in range(1, 4):
            edge = jnp.sum((segments < number).astype(F32), axis=1, keepdims=True)
            label = label + (row >= edge).astype(F32)
        lane = lax.broadcasted_iota(jnp.int32, (group, 128), 1)
        one_hot = (lane == label.astype(jnp.int32) + 64).astype(F32).astype(BF)
        labs[seq * slots : (seq + 1) * slots, :] = dot(table, one_hot)
        rows = first[seq * group : (seq + 1) * group, :].astype(BF)
        routed.b.x[seq * slots : (seq + 1) * slots, :] = dot(table, rows).astype(BF)


def restore(env, dense, routed, sent, seq):
    slots = routed.per
    return dot_l(routed.b.hot[seq], sent[seq * slots : (seq + 1) * slots])


def gate_rows(env, dense, routed):
    group, slots = dense.per, routed.per
    sent = routed.b.acc[...].astype(BF)
    router = env.vector(4)
    grad_router = jnp.zeros((1, 1024), F32)
    for seq in range(2):
        rows = slice(seq * group, (seq + 1) * group)
        first = env.b.first[rows, :]
        returned = restore(env, dense, routed, sent, seq)
        gate = jax.nn.sigmoid(jnp.sum(first * router, axis=1, keepdims=True))
        env.b.output[rows, :] = first + gate * returned
        grad = env.b.cotangent[:, seq, :].astype(F32)
        low = (gate * grad).astype(BF)
        routed.b.e[seq * slots : (seq + 1) * slots, :] = dot(routed.b.hot[seq], low)
        logit = jnp.sum(grad * returned, axis=1, keepdims=True) * gate * (1.0 - gate)
        grad_router = grad_router + jnp.sum(logit * first, axis=0, keepdims=True)
        dense.b.e[rows, :] = grad + logit * router
    env.b.vg[4:5, :] = grad_router


def share_vectors(env):
    vg, sv, rv = env.b.vg, env.b.sv, env.b.rv
    for number in range(env.n):
        tile = vg[:, 128 * (number // 2) : 128 * (number // 2) + 128]
        sv[number] = swap_halves(tile) if number % 2 else tile
    return env.exchange(sv, rv)


def sum_vectors(env, wait):
    wait()
    total = env.b.rv[0]
    for number in range(1, env.n):
        total = total + env.b.rv[number]
    env.b.gvec[...] = total


QKV, OUT, UP, DOWN = range(4)
SHAPES = ((3, 1024, 512), (512, 1024), (1024, 2048), (2048, 1024))
GRADS = ((3, 64, 512), (64, 512), (64, 2048), (64, 2048))


def whole_step(env, dense, routed):
    env.greet()
    b = env.b
    copies = [
        pltpu.make_async_copy(source, target, env.sem())
        for source, target in ((b.tokens_hbm, b.tokens), (b.cotangent_hbm, b.cotangent))
    ]
    for copy in copies:
        copy.start()
    dense.load(env, QKV)
    copies[0].wait()
    for seq in range(2):
        dense.b.x[seq * dense.per : (seq + 1) * dense.per, :] = env.b.tokens[:, seq, :]
    env.b.vg[...] = jnp.zeros_like(env.b.vg)
    dense.project(env)
    for number in (OUT, UP, DOWN):
        dense.load(env, number)
    dense.attend(env)
    dense.gather_line(env)
    for number in range(4):
        routed.load(env, number)
    mid_d, first = dense.b.mid, env.b.first
    def finish_dense(number, value):
        cols = slice(256 * number, 256 * number + 256)
        first[:, cols] = mid_d[:, cols] + value
    dense.feed(env, finish_dense)
    pick_rows(env, dense, routed)
    routed.project(env)
    routed.attend(env)
    dense.gather_plane(env)
    mid_r, x_r, sent = routed.b.mid, routed.b.x, routed.b.acc
    def finish_routed(number, value):
        cols = slice(256 * number, 256 * number + 256)
        sent[:, cols] = mid_r[:, cols] - x_r[:, cols].astype(F32) + value
    def spread_early():
        routed.spread_right(env, DOWN)
        routed.spread_right(env, OUT)
    routed.feed(env, finish_routed, spread_early)
    dense.quarter_right(env)
    routed.spread_left(env, QKV)
    routed.spread_left(env, UP)
    copies[1].wait()
    gate_rows(env, dense, routed)
    out_copy = pltpu.make_async_copy(b.output, b.output_hbm, env.sem())
    out_copy.start()
    routed.round_incoming()
    routed.back_feed(env)
    dense.gather_core(env)
    routed.spread_right_on(env, DOWN)
    routed.spread_right_on(env, OUT)
    routed.spread_right(env, UP)
    routed.spread_left(env, DOWN)
    routed.spread_left(env, OUT)
    routed.back_attend(env)
    routed.spread_hop(env, DOWN, 0)
    routed.spread_hop(env, OUT, 0)
    dense.share_right(env, OUT)
    routed.spread_right_on(env, UP)
    def finish_back(branch):
        low = branch.astype(BF)
        for seq in range(2):
            rows = slice(seq * dense.per, (seq + 1) * dense.per)
            dense.b.e[rows, :] += restore(env, dense, routed, low, seq)
    routed.back_project(env, finish_back, lambda: routed.spread_right(env, QKV))
    dense.round_incoming()
    dense.quarter_left(env)
    dense.back_feed(env)
    routed.spread_hop(env, DOWN, 1)
    routed.spread_hop(env, OUT, 1)
    routed.spread_hop(env, UP, 0)
    routed.spread_right_on(env, QKV)
    dense.share_left(env, UP)
    dense.share_left(env, OUT)
    dense.share_right(env, UP, 0, 1024)
    dense.back_attend(env)
    dense.quarter_core(env)
    dense.quarter_multiply(env)
    dense.head_gradient(env)
    routed.spread_hop(env, UP, 1)
    routed.spread_hop(env, QKV, 0)
    dense.multiply(env, OUT)
    dense.share_right(env, UP, 1024, 1024)
    dense.multiply(env, UP, 0, 1024)
    routed.spread_left_on(env, DOWN)
    routed.spread_left_on(env, OUT)
    routed.spread_left_on(env, UP)
    routed.spread_left_on(env, QKV)
    def finish_tokens(branch):
        env.b.grad_tokens[...] = dense.b.e[...] + branch
    dense.back_project(env, finish_tokens)
    grad_copy = pltpu.make_async_copy(b.grad_tokens, b.grad_tokens_hbm, env.sem())
    grad_copy.start()
    routed.spread_hop(env, QKV, 1)
    wait = share_vectors(env)
    dense.quarter_relay(env)
    dense.relay(env, OUT)
    dense.multiply(env, UP, 1024, 2048)
    routed.spread_left_core(env, DOWN)
    routed.spread_left_core(env, OUT)
    routed.spread_left_core(env, UP)
    routed.spread_left_core(env, QKV)
    routed.spread_multiply(env, DOWN)
    routed.spread_multiply(env, QKV)
    routed.spread_multiply(env, OUT)
    routed.spread_multiply(env, UP)
    dense.relay(env, UP)
    dense.quarter_share(env)
    routed.spread_collect(env, DOWN)
    dense.head_collect(env)
    routed.spread_collect(env, OUT)
    routed.spread_collect(env, UP)
    routed.spread_collect(env, QKV)
    dense.collect(env, OUT)
    dense.collect(env, UP)
    sum_vectors(env, wait)
    dense.quarter_collect(env)
    out_copy.wait()
    grad_copy.wait()
    env.drain()


def fused(group, tokens, cotangent, segments, routed_places, vectors, weights):
    n = lax.axis_size("seq")
    rows = 2 * group
    dense, routed = Layer(True, group, n), Layer(False, group // 4, n)
    wide = ((rows, 1024), F32)
    common = dict(
        stage=((4, 64, 512), F32),
        first=wide,
        output=wide,
        grad_tokens=wide,
        tokens=((group, 2, 1024), BF),
        cotangent=((group, 2, 1024), BF),
        vg=((8, 1024), F32),
        sv=((n, 8, 128), F32),
        rv=((n, 8, 128), F32),
    )
    groups = (dense.buffers(), routed.buffers(), common)
    scratch = [spec for table in groups for spec in table.values()]

    def kernel(*refs):
        refs = list(refs)

        def take(count):
            taken = refs[:count]
            del refs[:count]
            return taken

        inputs = take(4)
        vector_refs = take(5)
        sources = take(8)
        outputs = take(3)
        results = take(8)
        held = take(8)
        dense_refs, routed_refs, common_refs = (
            types.SimpleNamespace(**dict(zip(table, take(len(table)), strict=True))) for table in groups
        )
        b = common_refs
        b.tokens_hbm, b.cotangent_hbm, b.segments, b.routed = inputs
        b.output_hbm, b.grad_tokens_hbm, b.gvec = outputs
        b.vectors = vector_refs
        env = Env(b, refs[0], n)
        dense.attach(env, dense_refs, sources[:4], held[:4], results[:4])
        routed.attach(env, routed_refs, sources[4:], held[4:], results[4:])
        whole_step(env, dense, routed)

    vmem = pl.BlockSpec(memory_space=pltpu.VMEM)
    hbm = pl.BlockSpec(memory_space=pl.ANY)
    outs = [wide, wide, ((8, 128), F32)] + [(shape, F32) for shape in GRADS * 2]
    return pl.pallas_call(
        kernel,
        out_shape=[jax.ShapeDtypeStruct(*spec) for spec in outs],
        in_specs=[hbm] * 2 + [vmem] * 7 + [hbm] * 8,
        out_specs=[hbm] * 2 + [vmem] + [hbm] * 8,
        scratch_shapes=[pltpu.VMEM(shape, BF) for shape in SHAPES * 2]
        + [pltpu.VMEM(*spec) for spec in scratch]
        + [pltpu.SemaphoreType.DMA((384,))],
        compiler_params=pltpu.CompilerParams(
            collective_id=0, has_side_effects=True, vmem_limit_bytes=LIMIT
        ),
    )(tokens, cotangent, segments, routed_places, *vectors, *weights)


def place_results(group, parts):
    def kernel(*refs):
        sources, outs, held, sems = refs[:11], refs[11:26], refs[26:38], refs[38]
        gvec = sources[2]
        grads = list(zip(sources[3:], held[:8], outs[7:], strict=True))
        wides = list(zip(sources[:2], held[8:10], held[10:], outs[:2], strict=True))
        loads = [
            pltpu.make_async_copy(item[0], item[1], sems.at[0, number])
            for number, item in enumerate(wides + grads)
        ]
        for copy in loads:
            copy.start()
        for number in range(5):
            outs[2 + number][...] = gvec[number, 0:64]
        stores = []

        def store(source, target):
            stores.append(pltpu.make_async_copy(source, target, sems.at[1, len(stores)]))
            stores[-1].start()

        for number, (_, rows, turned, target) in enumerate(wides):
            loads[number].wait()
            for seq in range(2):
                turned[:, seq, :] = rows[seq * group : (seq + 1) * group, :]
            store(turned, target)
        for number, (_, block, target) in enumerate(grads):
            loads[2 + number].wait()
            store(block, target)
        for copy in stores:
            copy.wait()

    vmem = pl.BlockSpec(memory_space=pltpu.VMEM)
    hbm = pl.BlockSpec(memory_space=pl.ANY)
    wide, turned = (2 * group, 1024), (group, 2, 1024)
    shapes = [turned] * 2 + [(64,)] * 5 + list(GRADS * 2)
    held = list(GRADS * 2) + [wide] * 2 + [turned] * 2
    return pl.pallas_call(
        kernel,
        out_shape=[jax.ShapeDtypeStruct(shape, F32) for shape in shapes],
        in_specs=[hbm] * 2 + [vmem] + [hbm] * 8,
        out_specs=[hbm] * 2 + [vmem] * 5 + [hbm] * 8,
        scratch_shapes=[pltpu.VMEM(shape, F32) for shape in held]
        + [pltpu.SemaphoreType.DMA((2, 10))],
        compiler_params=pltpu.CompilerParams(vmem_limit_bytes=LIMIT),
    )(*parts)


def on_device_fused(
    tokens,
    segments,
    routed,
    router,
    dense_attn_gain,
    dense_qkv,
    dense_out,
    dense_mlp_gain,
    dense_up,
    dense_down,
    routed_attn_gain,
    routed_qkv,
    routed_out,
    routed_mlp_gain,
    routed_up,
    routed_down,
    cotangent,
):
    group = tokens.shape[0]
    parts = fused(
        group,
        tokens,
        cotangent,
        segments,
        routed,
        (dense_attn_gain, dense_mlp_gain, routed_attn_gain, routed_mlp_gain, router),
        (
            jnp.transpose(dense_qkv, (1, 0, 2)),
            dense_out,
            dense_up,
            dense_down,
            jnp.transpose(routed_qkv, (1, 0, 2)),
            routed_out,
            routed_up,
            routed_down,
        ),
    )
    placed = place_results(group, parts)
    vectors = placed[2:7]

    def weights_of(grads, first, second):
        return (
            vectors[first],
            jnp.transpose(grads[QKV], (1, 0, 2)),
            jnp.transpose(grads[OUT]),
            vectors[second],
            grads[UP],
            jnp.transpose(grads[DOWN]),
        )

    return (
        tuple(placed[:2])
        + weights_of(placed[7:11], 0, 1)
        + weights_of(placed[11:], 2, 3)
        + (vectors[4],)
    )


def solution(mesh):
    in_specs = (
        P("seq", None, None),
        P(),
        P(),
        P(),
        P(),
        P(None, None, "mp"),
        P("mp", None),
        P(),
        P(None, "mp"),
        P("mp", None),
        P(),
        P(None, None, "mp"),
        P("mp", None),
        P(),
        P(None, "mp"),
        P("mp", None),
        P("seq", None, None),
    )
    out_specs = (
        P("seq", None, None),
        P("seq", None, None),
        P("seq"),
        P("seq", None, "mp"),
        P("mp", "seq"),
        P("seq"),
        P("seq", "mp"),
        P("mp", "seq"),
        P("seq"),
        P("seq", None, "mp"),
        P("mp", "seq"),
        P("seq"),
        P("seq", "mp"),
        P("mp", "seq"),
        P("seq"),
    )
    seq_size = mesh.shape["seq"]
    pairs = 2 * (16 // mesh.shape["mp"])
    body = on_device_fused if seq_size == pairs else on_device

    return jax.shard_map(
        body, mesh=mesh, in_specs=in_specs, out_specs=out_specs, check_vma=False
    )
```

```python
import math
import types

import jax
import jax.numpy as jnp
from jax import lax
from jax.experimental import pallas as pl
from jax.experimental.pallas import tpu as pltpu
from jax.sharding import PartitionSpec as P

HEAD_DIM = 64


EPSILON = 1e-06
NEGATIVE = -1e30
PRECISE = lax.Precision.HIGHEST


def rms_norm(hidden, gain):
    return hidden * lax.rsqrt(jnp.mean(hidden * hidden, axis=-1, keepdims=True) + EPSILON) * gain


def gelu_tanh(operand):
    return jax.nn.gelu(operand, approximate=True)


def model_sum(operand):
    return lax.psum(operand, "mp")


def block_loop(row_total, advance, carried):
    block_size = math.gcd(row_total, 512)
    return lax.fori_loop(
        0,
        row_total // block_size,
        lambda number, current: advance(current, number * block_size, block_size),
        carried,
    )


def key_mask(query_places, query_live, key_places, key_live, label_rows):
    query_labels = jnp.take_along_axis(label_rows, query_places, axis=0)
    key_labels = jnp.take_along_axis(label_rows, key_places, axis=0)
    allowed = jnp.transpose(key_places)[:, None, :] <= jnp.transpose(query_places)[:, :, None]
    allowed = allowed & (
        jnp.transpose(key_labels)[:, None, :] == jnp.transpose(query_labels)[:, :, None]
    )
    allowed = allowed & jnp.transpose(key_live)[:, None, :] & jnp.transpose(query_live)[:, :, None]
    return allowed[:, None]


def attend_forward(queries, key_rows, value_rows, own_places, own_live, row_info, label_rows):
    row_count, seq_count, head_count, head_size = queries.shape
    score_scale = head_size ** (-0.5)
    shape_rows = (seq_count, head_count, row_count)
    initial = (
        jnp.full(shape_rows, NEGATIVE, jnp.float32),
        jnp.zeros(shape_rows, jnp.float32),
        jnp.zeros(shape_rows + (head_size,), jnp.float32),
    )
    key_piece = lax.all_gather(key_rows, "seq", axis=0, tiled=True)
    value_piece = lax.all_gather(value_rows, "seq", axis=0, tiled=True)

    def advance(current, offset, block_size):
        highest, totals, summed = current
        key_block = lax.dynamic_slice_in_dim(key_piece, offset, block_size, 0).reshape(
            block_size, seq_count, head_count, head_size
        )
        value_block = lax.dynamic_slice_in_dim(value_piece, offset, block_size, 0).reshape(
            block_size, seq_count, head_count, head_size
        )
        key_places, key_live = row_info(offset, block_size)
        allowed = key_mask(own_places, own_live, key_places, key_live, label_rows)
        scores = (
            jnp.einsum("qshe,kshe->shqk", queries, key_block, preferred_element_type=jnp.float32)
            * score_scale
        )
        scores = jnp.where(allowed, scores, NEGATIVE)
        newest = jnp.maximum(highest, jnp.max(scores, axis=-1))
        weights = jnp.exp(scores - newest[..., None])
        factor = jnp.exp(highest - newest)
        totals = totals * factor + jnp.sum(weights, axis=-1)
        summed = summed * factor[..., None] + jnp.einsum(
            "shqk,kshe->shqe",
            weights.astype(jnp.bfloat16),
            value_block,
            preferred_element_type=jnp.float32,
        )
        return (newest, totals, summed)

    highest, totals, summed = block_loop(key_piece.shape[0], advance, initial)
    mixed_rows = jnp.transpose(summed / totals[..., None], (2, 0, 1, 3)).reshape(
        row_count, seq_count, head_count * head_size
    )
    return (mixed_rows, highest + jnp.log(totals), None)


def attend_backward(
    queries,
    key_rows,
    value_rows,
    grad_mixed,
    mixed_rows,
    log_sum,
    own_places,
    own_live,
    row_info,
    label_rows,
):
    row_count, seq_count, head_count, head_size = queries.shape
    score_scale = head_size ** (-0.5)
    grad_heads = grad_mixed.reshape(row_count, seq_count, head_count, head_size)
    offsets = jnp.sum(
        grad_heads.astype(jnp.float32)
        * mixed_rows.reshape(row_count, seq_count, head_count, head_size),
        axis=-1,
    )
    offsets_rows = jnp.transpose(offsets, (1, 2, 0))
    key_piece = lax.all_gather(key_rows, "seq", axis=0, tiled=True)
    value_piece = lax.all_gather(value_rows, "seq", axis=0, tiled=True)

    def advance(current, offset, block_size):
        key_block = lax.dynamic_slice_in_dim(key_piece, offset, block_size, 0).reshape(
            block_size, seq_count, head_count, head_size
        )
        value_block = lax.dynamic_slice_in_dim(value_piece, offset, block_size, 0).reshape(
            block_size, seq_count, head_count, head_size
        )
        key_places, key_live = row_info(offset, block_size)
        allowed = key_mask(own_places, own_live, key_places, key_live, label_rows)
        scores = (
            jnp.einsum("qshe,kshe->shqk", queries, key_block, preferred_element_type=jnp.float32)
            * score_scale
        )
        scores = jnp.where(allowed, scores, NEGATIVE)
        chances = jnp.exp(scores - log_sum[..., None])
        pushes = jnp.einsum(
            "qshe,kshe->shqk", grad_heads, value_block, preferred_element_type=jnp.float32
        )
        slopes = (chances * (pushes - offsets_rows[..., None])).astype(jnp.bfloat16)
        return current + jnp.einsum(
            "shqk,kshe->qshe", slopes, key_block, preferred_element_type=jnp.float32
        )

    grad_queries = block_loop(key_piece.shape[0], advance, jnp.zeros(queries.shape, jnp.float32))
    log_all, offsets_all = (
        lax.all_gather(jnp.transpose(log_sum, (2, 0, 1)), "seq", axis=0, tiled=True),
        lax.all_gather(offsets, "seq", axis=0, tiled=True),
    )
    own_keys = key_rows.reshape(row_count, seq_count, head_count, head_size)
    own_values = value_rows.reshape(row_count, seq_count, head_count, head_size)
    zero_rows = jnp.zeros(queries.shape, jnp.float32)
    query_flat = queries.reshape(row_count, seq_count, head_count * head_size)
    query_piece = lax.all_gather(query_flat, "seq", axis=0, tiled=True)
    grad_piece = lax.all_gather(grad_mixed, "seq", axis=0, tiled=True)

    def advance(current, offset, block_size):
        key_sum, value_sum = current
        query_block = lax.dynamic_slice_in_dim(query_piece, offset, block_size, 0).reshape(
            block_size, seq_count, head_count, head_size
        )
        grad_block = lax.dynamic_slice_in_dim(grad_piece, offset, block_size, 0).reshape(
            block_size, seq_count, head_count, head_size
        )
        block_log = jnp.transpose(
            lax.dynamic_slice_in_dim(log_all, offset, block_size, 0), (1, 2, 0)
        )
        block_offsets = jnp.transpose(
            lax.dynamic_slice_in_dim(offsets_all, offset, block_size, 0), (1, 2, 0)
        )
        query_places, query_live = row_info(offset, block_size)
        allowed = key_mask(query_places, query_live, own_places, own_live, label_rows)
        scores = (
            jnp.einsum("qshe,kshe->shqk", query_block, own_keys, preferred_element_type=jnp.float32)
            * score_scale
        )
        scores = jnp.where(allowed, scores, NEGATIVE)
        chances = jnp.exp(scores - block_log[..., None])
        pushes = jnp.einsum(
            "qshe,kshe->shqk", grad_block, own_values, preferred_element_type=jnp.float32
        )
        slopes = (chances * (pushes - block_offsets[..., None])).astype(jnp.bfloat16)
        key_sum = key_sum + jnp.einsum(
            "shqk,qshe->kshe", slopes, query_block, preferred_element_type=jnp.float32
        )
        value_sum = value_sum + jnp.einsum(
            "shqk,qshe->kshe",
            chances.astype(jnp.bfloat16),
            grad_block,
            preferred_element_type=jnp.float32,
        )
        return (key_sum, value_sum)

    key_sum, value_sum = block_loop(query_piece.shape[0], advance, (zero_rows, zero_rows))
    flat_shape = (row_count, seq_count, head_count * head_size)
    return (
        (grad_queries * score_scale).reshape(flat_shape),
        (key_sum * score_scale).reshape(flat_shape),
        value_sum.reshape(flat_shape),
    )


def block_forward(hidden, params, row_info, label_rows):
    attn_gain, qkv_weight, out_weight, mlp_gain, up_weight, down_weight = params
    row_count, seq_count, _ = hidden.shape
    head_width = qkv_weight.shape[2]
    head_count = head_width // HEAD_DIM
    own_places, own_live = row_info(lax.axis_index("seq") * row_count, row_count)
    normed = rms_norm(hidden, attn_gain.astype(jnp.float32)).astype(jnp.bfloat16)
    projected = jnp.einsum(
        "rsd,dce->rsce", normed, qkv_weight, preferred_element_type=jnp.float32
    ).astype(jnp.bfloat16)
    queries = projected[:, :, 0].reshape(row_count, seq_count, head_count, HEAD_DIM)
    key_rows = projected[:, :, 1]
    value_rows = projected[:, :, 2]
    mixed_rows, log_sum, kept_rows = attend_forward(
        queries, key_rows, value_rows, own_places, own_live, row_info, label_rows
    )
    mixed_low = mixed_rows.astype(jnp.bfloat16)
    attention = model_sum(
        jnp.einsum("rsh,hd->rsd", mixed_low, out_weight, preferred_element_type=jnp.float32)
    )
    middle = hidden + attention
    normed_mlp = rms_norm(middle, mlp_gain.astype(jnp.float32)).astype(jnp.bfloat16)
    before = jnp.einsum("rsd,df->rsf", normed_mlp, up_weight, preferred_element_type=jnp.float32)
    active = gelu_tanh(before).astype(jnp.bfloat16)
    feed_out = model_sum(
        jnp.einsum("rsf,fd->rsd", active, down_weight, preferred_element_type=jnp.float32)
    )
    stored = (
        hidden,
        normed,
        queries,
        key_rows,
        value_rows,
        mixed_rows,
        log_sum,
        mixed_low,
        middle,
        normed_mlp,
        before,
        active,
        own_places,
        own_live,
        kept_rows,
    )
    return (attention, middle, feed_out, stored)


def block_backward(incoming, stored, params, row_info, label_rows):
    attn_gain, qkv_weight, out_weight, mlp_gain, up_weight, down_weight = params
    (
        hidden,
        normed,
        queries,
        key_rows,
        value_rows,
        mixed_rows,
        log_sum,
        mixed_low,
        middle,
        normed_mlp,
        before,
        active,
        own_places,
        own_live,
        kept_rows,
    ) = stored
    incoming_low = incoming.astype(jnp.bfloat16)
    grad_down = jnp.einsum("rsf,rsd->fd", active, incoming_low, preferred_element_type=jnp.float32)
    grad_active = jnp.einsum(
        "rsd,fd->rsf", incoming_low, down_weight, preferred_element_type=jnp.float32
    )
    _, gelu_pull = jax.vjp(gelu_tanh, before)
    grad_before = gelu_pull(grad_active)[0].astype(jnp.bfloat16)
    grad_up = jnp.einsum("rsd,rsf->df", normed_mlp, grad_before, preferred_element_type=jnp.float32)
    grad_normed_mlp = model_sum(
        jnp.einsum("rsf,df->rsd", grad_before, up_weight, preferred_element_type=jnp.float32)
    )
    _, mlp_pull = jax.vjp(rms_norm, middle, mlp_gain.astype(jnp.float32))
    grad_middle, grad_mlp_gain = mlp_pull(grad_normed_mlp)
    along_low = (incoming + grad_middle).astype(jnp.bfloat16)
    grad_out = jnp.einsum("rsh,rsd->hd", mixed_low, along_low, preferred_element_type=jnp.float32)
    grad_mixed = jnp.einsum(
        "rsd,hd->rsh", along_low, out_weight, preferred_element_type=jnp.float32
    ).astype(jnp.bfloat16)
    grad_queries, grad_keys, grad_values = attend_backward(
        queries,
        key_rows,
        value_rows,
        grad_mixed,
        mixed_rows,
        log_sum,
        own_places,
        own_live,
        row_info,
        label_rows,
    )
    grad_projected = jnp.stack((grad_queries, grad_keys, grad_values), axis=2).astype(jnp.bfloat16)
    grad_qkv = jnp.einsum(
        "rsd,rsce->dce", normed, grad_projected, preferred_element_type=jnp.float32
    )
    grad_normed = model_sum(
        jnp.einsum("rsce,dce->rsd", grad_projected, qkv_weight, preferred_element_type=jnp.float32)
    )
    _, attn_pull = jax.vjp(rms_norm, hidden, attn_gain.astype(jnp.float32))
    grad_hidden, grad_attn_gain = attn_pull(grad_normed)
    return (
        grad_middle + grad_hidden,
        (grad_attn_gain, grad_qkv, grad_out, grad_mlp_gain, grad_up, grad_down),
    )


def on_device(
    tokens,
    segments,
    routed,
    router,
    dense_attn_gain,
    dense_qkv,
    dense_out,
    dense_mlp_gain,
    dense_up,
    dense_down,
    routed_attn_gain,
    routed_qkv,
    routed_out,
    routed_mlp_gain,
    routed_up,
    routed_down,
    cotangent,
):
    group_rows, seq_count, _ = tokens.shape
    devices = lax.axis_size("seq")
    my_index = lax.axis_index("seq")
    capacity = routed.shape[1]
    most_rows = group_rows // 4
    label_rows = jnp.transpose(segments)
    route_rows = jnp.transpose(routed)
    local_ids = jnp.arange(group_rows, dtype=jnp.int32)
    bounds = jnp.arange(devices + 1, dtype=jnp.int32) * group_rows
    starts = jnp.sum((routed[None, :, :] < bounds[:, None, None]).astype(jnp.int32), axis=2)
    first_rank = starts[my_index]
    routed_here = starts[my_index + 1] - first_rank
    dense_params = (dense_attn_gain, dense_qkv, dense_out, dense_mlp_gain, dense_up, dense_down)
    routed_params = (
        routed_attn_gain,
        routed_qkv,
        routed_out,
        routed_mlp_gain,
        routed_up,
        routed_down,
    )

    def dense_info(first_row, row_total):
        places = first_row + jnp.broadcast_to(
            jnp.arange(row_total, dtype=jnp.int32)[:, None], (row_total, seq_count)
        )
        return (places, jnp.ones((row_total, seq_count), jnp.bool_))

    slot_rows = jnp.arange(most_rows, dtype=jnp.int32)
    is_live = slot_rows[:, None] < routed_here[None, :]
    hold_places = (
        jnp.take_along_axis(
            route_rows, jnp.clip(first_rank[None, :] + slot_rows[:, None], 0, capacity - 1), axis=0
        )
        - my_index * group_rows
    )
    hold_table = (
        (jnp.transpose(hold_places)[:, :, None] == local_ids[None, None, :])
        & jnp.transpose(is_live)[:, :, None]
    ).astype(jnp.bfloat16)

    def select_rows(rows_in):
        return jnp.einsum(
            "smc,csd->msd", hold_table, rows_in, preferred_element_type=jnp.float32
        ).astype(jnp.bfloat16)

    def restore_rows(rows_in):
        return jnp.einsum("smc,msd->csd", hold_table, rows_in, preferred_element_type=jnp.float32)

    def routed_info(first_row, row_total):
        number = first_row + jnp.arange(row_total, dtype=jnp.int32)
        source = number // most_rows
        within = number % most_rows
        base = jnp.take(starts, source, axis=0)
        filled = jnp.take(starts, source + 1, axis=0) - base
        rank_rows = jnp.clip(base + within[:, None], 0, capacity - 1)
        return (jnp.take_along_axis(route_rows, rank_rows, axis=0), within[:, None] < filled)

    hidden = tokens.astype(jnp.float32)
    _, middle, feed_out, dense_stored = block_forward(hidden, dense_params, dense_info, label_rows)
    first_out = middle + feed_out
    lifted = select_rows(first_out.astype(jnp.bfloat16))
    routed_attention, _, routed_feed, routed_stored = block_forward(
        lifted.astype(jnp.float32), routed_params, routed_info, label_rows
    )
    sent_rows = (routed_attention + routed_feed).astype(jnp.bfloat16)
    returned = restore_rows(sent_rows)
    router_float = router.astype(jnp.float32)
    gate_value = jax.nn.sigmoid(jnp.einsum("csd,d->cs", first_out, router_float, precision=PRECISE))
    output = first_out + gate_value[:, :, None] * returned
    grad_output = cotangent.astype(jnp.float32)
    grad_sent = select_rows((gate_value[:, :, None] * grad_output).astype(jnp.bfloat16))
    grad_logit = jnp.sum(grad_output * returned, axis=-1) * gate_value * (1.0 - gate_value)
    grad_router = jnp.einsum("cs,csd->d", grad_logit, first_out, precision=PRECISE)
    grad_first = grad_output + grad_logit[:, :, None] * router_float
    routed_branch, routed_grads = block_backward(
        grad_sent.astype(jnp.float32), routed_stored, routed_params, routed_info, label_rows
    )
    grad_first = grad_first + restore_rows(routed_branch.astype(jnp.bfloat16))
    dense_branch, dense_grads = block_backward(
        grad_first, dense_stored, dense_params, dense_info, label_rows
    )
    grad_tokens = grad_first + dense_branch
    summed_all = (
        lax.psum_scatter(dense_grads[0], "seq", scatter_dimension=0, tiled=True),
        lax.psum_scatter(dense_grads[1], "seq", scatter_dimension=0, tiled=True),
        lax.psum_scatter(dense_grads[2], "seq", scatter_dimension=1, tiled=True),
        lax.psum_scatter(dense_grads[3], "seq", scatter_dimension=0, tiled=True),
        lax.psum_scatter(dense_grads[4], "seq", scatter_dimension=0, tiled=True),
        lax.psum_scatter(dense_grads[5], "seq", scatter_dimension=1, tiled=True),
        lax.psum_scatter(routed_grads[0], "seq", scatter_dimension=0, tiled=True),
        lax.psum_scatter(routed_grads[1], "seq", scatter_dimension=0, tiled=True),
        lax.psum_scatter(routed_grads[2], "seq", scatter_dimension=1, tiled=True),
        lax.psum_scatter(routed_grads[3], "seq", scatter_dimension=0, tiled=True),
        lax.psum_scatter(routed_grads[4], "seq", scatter_dimension=0, tiled=True),
        lax.psum_scatter(routed_grads[5], "seq", scatter_dimension=1, tiled=True),
        lax.psum_scatter(grad_router, "seq", scatter_dimension=0, tiled=True),
    )
    dense_sums = tuple(summed_all[0:6])
    routed_sums = tuple(summed_all[6:13])
    return (output, grad_tokens) + tuple(dense_sums) + tuple(routed_sums)


BF = jnp.bfloat16
LIMIT = 63 * 1024 * 1024
F32 = jnp.float32
MESH = pl.DeviceIdType.MESH
PIECE = 1024
WIDTHS = (384, 128, 512, 512)
BEGINS = (0, 384, 512, 1024)
SIZES = (1536, 512, 2048, 2048)
COLS = (None, (0, 512), (512, 2048), None)


def dot(a, b):
    return lax.dot_general(a, b, (((1,), (0,)), ((), ())), preferred_element_type=F32)


def dot_t(a, b):
    return lax.dot_general(a, b, (((1,), (1,)), ((), ())), preferred_element_type=F32)


def dot_l(a, b):
    return lax.dot_general(a, b, (((0,), (0,)), ((), ())), preferred_element_type=F32)


def swap_halves(tile):
    return pltpu.roll(tile, 64, 1)


def low_lanes(rows):
    return lax.broadcasted_iota(jnp.int32, (rows, 128), 1) < 64


def inverse_rms(rows):
    return lax.rsqrt(jnp.mean(rows * rows, axis=1, keepdims=True) + EPSILON)


def norm_back(grad, rows, gain):
    inverse = inverse_rms(rows)
    unit = rows * inverse
    pulled = grad * gain
    grad_rows = inverse * (pulled - unit * jnp.mean(pulled * unit, axis=1, keepdims=True))
    return grad_rows, jnp.sum(grad * unit, axis=0, keepdims=True)


class Env:
    def __init__(self, refs, sems, seq_size):
        self.b = refs
        self.sems = sems
        self.count = 0
        self.sends = []
        self.middle_sends = []
        self.flying = {}
        self.stores = {}
        self.stored = 0
        self.barrier_done = False
        self.n = seq_size
        self.s = lax.axis_index("seq")
        self.c = lax.axis_index("mp")
        self.q = lax.rem(self.s, 4)
        self.z = lax.div(self.s, 4)
        high = lax.div(self.z, 2)
        self.near = self.z + 1 - 2 * lax.rem(self.z, 2)
        self.across = 2 - high
        self.far = 3 - 3 * high
        self.middle = lax.rem(self.z + high, 2) == 1

    def sem(self):
        self.count += 1
        return self.sems.at[self.count - 1]

    def vector(self, number):
        return self.b.vectors[number][...].astype(F32).reshape(1, 1024)

    def greet(self):
        barrier = pltpu.get_barrier_semaphore()

        def signal(step, _):
            other = lax.rem(self.s + step, self.n)
            pl.semaphore_signal(barrier, inc=1, device_id=(other, self.c), device_id_type=MESH)
            return 0

        lax.fori_loop(1, self.n, signal, 0)
        pl.semaphore_signal(barrier, inc=1, device_id=(self.s, 1 - self.c), device_id_type=MESH)

    def meet(self):
        if not self.barrier_done:
            pl.semaphore_wait(pltpu.get_barrier_semaphore(), self.n)
            self.barrier_done = True

    def remote(self, src, dst, send, recv, seq, core):
        return pltpu.make_async_remote_copy(
            src_ref=src,
            dst_ref=dst,
            send_sem=send,
            recv_sem=recv,
            device_id=(seq, core),
            device_id_type=MESH,
        )

    def exchange(self, send_ref, recv_ref):
        self.meet()
        send, recv = self.sem(), self.sem()
        n = self.n

        def start(step, _):
            other = lax.rem(self.s + step, n)
            self.remote(
                send_ref.at[other], recv_ref.at[self.s], send, recv, other, self.c
            ).start()
            return 0

        lax.fori_loop(1, n, start, 0)
        recv_ref[pl.ds(self.s, 1)] = send_ref[pl.ds(self.s, 1)]
        whole = self.remote(
            send_ref.at[pl.ds(0, n - 1)],
            recv_ref.at[pl.ds(0, n - 1)],
            send,
            recv,
            lax.rem(self.s + 1, n),
            self.c,
        )
        self.sends.append(whole)
        return whole.wait_recv

    def core_sum(self, layer, half, chunk, sink):
        self.meet()
        send_ref, recv_ref = layer.b.ps.at[half], layer.b.pr.at[half]
        copies = []
        for number in range(4):
            earlier = self.flying.pop((layer.packed, half, number), None)
            if earlier is not None:
                earlier.wait_send()
            send_ref[number] = chunk(number).astype(BF)
            copy = self.remote(
                send_ref.at[number], recv_ref.at[number], self.sem(), self.sem(), self.s, 1 - self.c
            )
            copy.start()
            copies.append(copy)
            self.flying[(layer.packed, half, number)] = copy
        for number, copy in enumerate(copies):
            copy.wait_recv()
            sink(number, send_ref[number].astype(F32) + recv_ref[number].astype(F32))

    def plane_send(self, pieces, recv_piece, wait_piece):
        self.meet()
        send, recv = self.sem(), self.sem()
        for step in range(1, 4):
            other = lax.rem(self.q + step, 4)
            self.remote(
                pieces(other), recv_piece, send, recv, self.z * 4 + other, self.c
            ).start()
        whole = self.remote(wait_piece, wait_piece, send, recv, self.z * 4 + lax.rem(self.q + 1, 4), self.c)
        self.sends.append(whole)
        return whole.wait_recv

    def line_send(self, pieces, recv_piece, wait_piece):
        self.meet()
        send, recv = self.sem(), self.sem()
        for step in range(1, 4):
            other = lax.rem(self.z + step, 4)
            self.remote(
                pieces(other), recv_piece(step), send, recv, other * 4 + self.q, self.c
            ).start()
        whole = self.remote(wait_piece, wait_piece, send, recv, lax.rem(self.z + 1, 4) * 4 + self.q, self.c)
        self.sends.append(whole)
        return whole.wait_recv

    def line_reduce(self, blocks, slots):
        self.meet()
        receive = [self.sem() for _ in range(4)]
        send = [self.sem() for _ in range(3)]

        def copy(block, slot, way, z):
            return self.remote(
                blocks.at[block], slots.at[slot], send[way], receive[slot], z * 4 + self.q, self.c
            )

        @pl.when(jnp.logical_not(self.middle))
        def _():
            copy(self.far, 3, 2, self.near).start()
            copy(self.across, 2, 1, self.near).start()

        copy(self.near, 0, 0, self.near).start()

        self.sends += [copy(0, 0, way, self.near) for way in range(3)]

        def arrived(slot):
            copy(0, slot, 0, self.near).wait_recv()

        def pass_on(slot):
            block = (self.across, self.far)[slot - 2]
            copy(block, 1, slot - 1, block).start()

        def finish():
            for slot in range(2):
                copy(0, slot, 0, self.near).wait_recv()

        return arrived, pass_on, finish

    def line_gather(self, ref):
        self.meet()
        receive = [self.sem() for _ in range(3)]
        send = [self.sem() for _ in range(5)]

        def copy(piece, way, slot, z):
            return self.remote(
                ref.at[piece], ref.at[piece], send[way], receive[slot], z * 4 + self.q, self.c
            )

        copy(self.z, 0, 0, self.near).start()

        @pl.when(self.middle)
        def _():
            copy(self.z, 1, 1, self.across).start()

        def second():
            @pl.when(self.middle)
            def _():
                copy(0, 0, 0, self.near).wait_recv()
                copy(self.near, 2, 2, self.across).start()
                copy(0, 0, 1, self.near).wait_recv()
                copy(self.across, 3, 1, self.near).start()

        def third():
            @pl.when(self.middle)
            def _():
                copy(0, 0, 2, self.near).wait_recv()
                copy(self.far, 4, 2, self.near).start()

        self.sends.append(copy(0, 0, 0, self.near))
        self.middle_sends += [copy(0, way, 0, self.near) for way in range(1, 5)]

        def finish():
            @pl.when(jnp.logical_not(self.middle))
            def _():
                for slot in range(3):
                    copy(0, 0, slot, self.near).wait_recv()

        return second, third, finish

    def store(self, result, which, at, fill):
        slot = self.stored % 8
        self.stored += 1
        if slot in self.stores:
            self.stores.pop(slot).wait()
        stage = self.b.stage.at[slot]
        fill(stage)
        target = result.at[at // 512] if which == 0 else result.at[:, pl.ds(at, 512)]
        copy = pltpu.make_async_copy(stage, target, self.sem())
        copy.start()
        self.stores[slot] = copy

    def drain(self):
        for copy in self.sends + list(self.flying.values()):
            copy.wait_send()
        for copy in self.stores.values():
            copy.wait()

        @pl.when(self.middle)
        def _():
            for copy in self.middle_sends:
                copy.wait_send()


class Layer:
    def __init__(self, packed, per, n):
        self.per = per
        self.n = n
        self.rows = 2 * per
        self.packed = packed
        self.value_rows = per // 2 if self.packed else per
        self.message = per + self.value_rows
        self.total = n * per
        self.block = 256
        self.gains = (0, 1) if packed else (2, 3)

    def attach(self, env, refs, sources, weights, results):
        self.b = refs
        self.sources = sources
        self.held = weights
        self.results = results
        self.right_waits, self.left_waits, self.line_waits, self.hops = {}, {}, {}, {}
        self.loads = {}

    def load(self, env, number):
        copy = pltpu.make_async_copy(self.sources[number], self.held[number], env.sem())
        copy.start()
        self.loads[number] = copy

    def weight(self, number):
        if number in self.loads:
            self.loads.pop(number).wait()
        return self.held[number]

    def buffers(self):
        r, t, n = self.rows, self.total, self.n
        vr, m = self.value_rows, self.message
        table = dict(
            x=((r, 1024), BF),
            normed=((r, 1024), BF),
            s1=((n, m, 128), BF),
            r1=((n, m, 128), BF),
            qa=((t, 128), BF),
            kb=((t, 128), BF),
            va=((t, 128), BF),
            mixp=((t, 128), F32),
            lse=((t, 128), F32),
            s2=((n, vr, 128), BF),
            r2=((n, vr, 128), BF),
            mixl=((r, 512), BF),
            mid=((r, 1024), F32),
            nm=((r, 1024), BF),
            gp=((r, 2048), BF),
            act=((r, 2048), BF),
            e=((r, 1024), F32),
            el=((r, 1024), BF),
            gb=((r, 2048), BF),
            gm=((r, 1024), F32),
            al=((r, 1024), BF),
            s6=((n, vr, 128), BF),
            r6=((n, vr, 128), BF),
            gx=((t, 128), BF),
            dk=((t, 128), F32),
            dv=((t, 128), F32),
            s7=((n, m, 128), BF),
            r7=((n, m, 128), BF),
            dp=((r, 1536), BF),
            acc=((r, 1024), F32),
            ps=((2, 4, r, 256), BF),
            pr=((2, 4, r, 256), BF),
        )
        if self.packed:
            table.update(
                ng=((4, 4, self.per, 1024), BF),
                x7=((t, 256), BF),
                s9=((n, m, 128), BF),
                r9=((n, m, 128), BF),
                fg=((4, r, 2560), BF),
                ds=((4, r, 512), BF),
                dg=((4, r, 512), BF),
                sb=((4, 64, 2560), BF),
                rb=((4, 64, 2560), BF),
                ul=((4, r, 1024), BF),
                ur=((4, r, 512), BF),
                us=((4, 256, 512), BF),
                ub=((4, 256, 512), BF),
                ux=((4, 64, 512), BF),
                uy=((4, 64, 512), BF),
            )
        else:
            table.update(
                fg=((4, 4, r, 1536), BF),
                dg=((4, 4, r, 1024), BF),
                sb=((4, 64, 1536), BF),
                rb=((4, 64, 1536), BF),
                same=((t, t), F32),
                lab=((t, 128), BF),
                hot=((2, self.per, 64), BF),
                labs=((r, 128), F32),
            )
        return table

    def gain(self, env, which):
        return env.vector(self.gains[which])

    def pack(self, tile):
        if not self.packed:
            return tile
        half = self.per // 2
        return jnp.where(low_lanes(half), tile[:half], swap_halves(tile[half:]))

    def send_pairs(self, store, tile_of):
        for seq in range(2):
            for j in range(4):
                tile = tile_of(seq, j)
                store(8 * seq + 2 * j, self.pack(tile))
                store(8 * seq + 2 * j + 1, self.pack(swap_halves(tile)))

    def join_pairs(self, tile_a, tile_b):
        vr = self.value_rows
        low = low_lanes(vr)
        first = jnp.where(low, tile_a, swap_halves(tile_b))
        if not self.packed:
            return [first]
        return [first, jnp.where(low, swap_halves(tile_a), tile_b)]

    def project(self, env, then=None):
        hidden = self.b.x[...].astype(F32)
        normed = (hidden * inverse_rms(hidden) * self.gain(env, 0)).astype(BF)
        self.b.normed[...] = normed
        weight = self.weight(QKV)
        if then is not None:
            then()
        queries, keys, values = (dot(normed, weight[part]) for part in range(3))
        send = self.b.s1
        per = self.per
        low = low_lanes(per)
        for seq in range(2):
            rows = slice(seq * per, (seq + 1) * per)
            for j in range(4):
                cols = slice(128 * j, 128 * j + 128)
                qt, kt, vt = queries[rows, cols], keys[rows, cols], values[rows, cols]
                pair = 8 * seq + 2 * j
                send[pair, 0:per] = jnp.where(low, qt, swap_halves(kt)).astype(BF)
                send[pair + 1, 0:per] = jnp.where(low, swap_halves(qt), kt).astype(BF)
                va, vb = vt, swap_halves(vt)
                if self.packed:
                    va, vb = self.pack(va), self.pack(vb)
                else:
                    labels = self.b.labs[rows, :]
                    va, vb = jnp.where(low, va, labels), jnp.where(low, vb, labels)
                send[pair, per:] = va.astype(BF)
                send[pair + 1, per:] = vb.astype(BF)
        self.wait1 = env.exchange(send, self.b.r1)

    def unpack(self, env):
        recv = self.b.r1
        qa, kb, va = self.b.qa, self.b.kb, self.b.va
        per, vr = self.per, self.value_rows
        low, low_v = low_lanes(per), low_lanes(vr)
        zero = jnp.zeros((per, 128), F32)
        zero_v = jnp.zeros((vr, 128), F32)
        for i in range(self.n):
            both = recv[i, 0:per].astype(F32)
            qa[i * per : (i + 1) * per] = jnp.where(low, both * 0.125, zero).astype(BF)
            kb[i * per : (i + 1) * per] = swap_halves(both).astype(BF)
            tile = recv[i, per:].astype(F32)
            va[i * per : i * per + vr] = jnp.where(low_v, tile, zero_v).astype(BF)
            if self.packed:
                va[i * per + vr : (i + 1) * per] = jnp.where(low_v, swap_halves(tile), zero_v).astype(BF)
            else:
                self.b.lab[i * per : (i + 1) * per] = jnp.where(low_v, zero_v, tile).astype(BF)
        if not self.packed:
            labels = self.b.lab[...]
            self.b.same[...] = dot_t(labels, labels)

    def allowed(self, env, start, stop):
        size = stop - start
        rows = lax.broadcasted_iota(jnp.int32, (size, stop), 0) + start
        keys = lax.broadcasted_iota(jnp.int32, (size, stop), 1)
        ok = keys <= rows
        if self.packed:
            segments = env.b.segments[pl.ds(lax.div(env.s, 8), 1), :]
            row = (lax.broadcasted_iota(jnp.int32, (size, 1), 0) + start).astype(F32)
            opening = jnp.zeros((size, 1), F32)
            for label in range(1, 4):
                edge = jnp.sum((segments < label).astype(F32), axis=1, keepdims=True)
                opening = jnp.where(row >= edge, jnp.maximum(opening, edge), opening)
            return ok & (keys >= opening.astype(jnp.int32))
        return ok & (self.b.same[start:stop, 0:stop] > 0.5)

    def attend(self, env):
        self.wait1()
        self.unpack(env)
        qa, kb, va = self.b.qa, self.b.kb, self.b.va
        mixp, lse = self.b.mixp, self.b.lse
        for start in range(0, self.total, self.block):
            stop = start + self.block
            scores = dot_t(qa[start:stop], kb[0:stop])
            scores = jnp.where(self.allowed(env, start, stop), scores, NEGATIVE)
            highest = jnp.max(scores, axis=1, keepdims=True)
            weights = jnp.exp(scores - highest)
            totals = jnp.sum(weights, axis=1, keepdims=True)
            mixp[start:stop] = dot(weights.astype(BF), va[0:stop]) / totals
            lse[start:stop] = jnp.broadcast_to(highest + jnp.log(totals), (self.block, 128))
        send = self.b.s2
        for i in range(self.n):
            send[i] = self.pack(mixp[i * self.per : (i + 1) * self.per]).astype(BF)
        self.wait2 = env.exchange(send, self.b.r2)

    def gather_heads(self, recv, row0, put):
        per, vr = self.per, self.value_rows
        for seq in range(2):
            for j in range(4):
                pair = 8 * seq + 2 * j
                tiles = self.join_pairs(
                    recv[pair, row0:].astype(F32), recv[pair + 1, row0:].astype(F32)
                )
                for number, tile in enumerate(tiles):
                    begin = seq * per + number * vr
                    put(slice(begin, begin + vr), slice(128 * j, 128 * j + 128), tile)

    def feed(self, env, finish, then=None):
        self.wait2()
        mixl = self.b.mixl

        def put(rows, cols, tile):
            mixl[rows, cols] = tile.astype(BF)

        self.gather_heads(self.b.r2, 0, put)
        out = self.weight(OUT)
        mid = self.b.mid
        hidden = self.b.x
        mixed = mixl[...]

        def sink(number, value):
            cols = slice(256 * number, 256 * number + 256)
            mid[:, cols] = value + hidden[:, cols].astype(F32)

        env.core_sum(
            self,
            0,
            lambda number: dot(mixed, out[:, 256 * number : 256 * number + 256]),
            sink,
        )
        middle = mid[...]
        normed = (middle * inverse_rms(middle) * self.gain(env, 1)).astype(BF)
        self.b.nm[...] = normed
        up = self.weight(UP)
        act, slope = self.b.act, self.b.gp
        for number in range(4):
            cols = slice(512 * number, 512 * number + 512)
            before = dot(normed, up[:, cols])
            square = before * before
            bent = jnp.tanh(0.7978845608028654 * before * (1.0 + 0.044715 * square))
            half = 0.5 * (1.0 + bent)
            act[:, cols] = (before * half).astype(BF)
            slope[:, cols] = (
                half
                + 0.5 * before * (1.0 - bent * bent) * (0.7978845608028654 + 0.1070322243 * square)
            ).astype(BF)
        if then is not None:
            then()
        down = self.weight(DOWN)
        env.core_sum(
            self,
            1,
            lambda number: dot(act[...], down[:, 256 * number : 256 * number + 256]),
            finish,
        )

    def round_incoming(self):
        self.b.el[...] = self.b.e[...].astype(BF)

    def back_feed(self, env):
        grad_low = self.b.el[...]
        down, up, out = self.weight(DOWN), self.weight(UP), self.weight(OUT)
        gb, slope = self.b.gb, self.b.gp
        for number in range(4):
            cols = slice(512 * number, 512 * number + 512)
            grad = dot_t(grad_low, down[cols, :])
            gb[:, cols] = (grad * slope[:, cols].astype(F32)).astype(BF)
        acc = self.b.acc

        def sink(number, value):
            acc[:, 256 * number : 256 * number + 256] = value

        env.core_sum(
            self,
            0,
            lambda number: dot_t(gb[...], up[256 * number : 256 * number + 256, :]),
            sink,
        )
        grad_mid, grad_gain = norm_back(acc[...], self.b.mid[...], self.gain(env, 1))
        row = self.gains[1]
        env.b.vg[row : row + 1, :] = grad_gain
        self.b.gm[...] = grad_mid
        along = (self.b.e[...] + grad_mid).astype(BF)
        self.b.al[...] = along
        grad_mixed = dot_t(along, out[...])
        send = self.b.s6
        per = self.per

        def store(pair, tile):
            send[pair] = tile.astype(BF)

        self.send_pairs(
            store,
            lambda seq, j: grad_mixed[seq * per : (seq + 1) * per, 128 * j : 128 * j + 128],
        )
        self.wait6 = env.exchange(send, self.b.r6)

    def back_attend(self, env):
        self.wait6()
        recv, gx = self.b.r6, self.b.gx
        per, vr = self.per, self.value_rows
        low_v = low_lanes(vr)
        zero_v = jnp.zeros((vr, 128), F32)
        for i in range(self.n):
            tile = recv[i].astype(F32)
            gx[i * per : i * per + vr] = jnp.where(low_v, tile, zero_v).astype(BF)
            if self.packed:
                gx[i * per + vr : (i + 1) * per] = jnp.where(low_v, swap_halves(tile), zero_v).astype(BF)
        qa, kb, va = self.b.qa, self.b.kb, self.b.va
        mixp, lse = self.b.mixp, self.b.lse
        dk, dv = self.b.dk, self.b.dv
        dk[...] = jnp.zeros_like(dk)
        dv[...] = jnp.zeros_like(dv)
        dq = {}
        for start in range(0, self.total, self.block):
            stop = start + self.block
            query, grad = qa[start:stop], gx[start:stop]
            scores = dot_t(query, kb[0:stop])
            scores = jnp.where(self.allowed(env, start, stop), scores, NEGATIVE)
            probs = jnp.exp(scores - lse[start:stop, 0:1])
            offsets = jnp.sum(grad.astype(F32) * mixp[start:stop], axis=1, keepdims=True)
            slopes = (probs * (dot_t(grad, va[0:stop]) - offsets)).astype(BF)
            mixp[start:stop] = dot(slopes, kb[0:stop])
            dk[0:stop] += dot_l(slopes, query)
            dv[0:stop] += dot_l(probs.astype(BF), grad)
        send = self.b.s7
        low = low_lanes(per)
        for i in range(self.n):
            rows = slice(i * per, (i + 1) * per)
            send[i, 0:per] = jnp.where(low, mixp[rows] * 0.125, swap_halves(dk[rows])).astype(BF)
            send[i, per:] = self.pack(dv[rows]).astype(BF)
            if self.packed:
                self.b.x7[rows, 0:128] = send[i, 0:per]
                self.b.x7[rows, 128:256] = dv[rows].astype(BF)
        self.wait7 = env.exchange(send, self.b.r7)

    def back_project(self, env, finish, then=None):
        self.wait7()
        recv, dp = self.b.r7, self.b.dp
        per = self.per
        low = low_lanes(per)
        for seq in range(2):
            rows = slice(seq * per, (seq + 1) * per)
            for j in range(4):
                pair = 8 * seq + 2 * j
                one, two = recv[pair, 0:per].astype(F32), recv[pair + 1, 0:per].astype(F32)
                dp[rows, 128 * j : 128 * j + 128] = jnp.where(low, one, swap_halves(two)).astype(BF)
                dp[rows, 512 + 128 * j : 640 + 128 * j] = jnp.where(low, swap_halves(one), two).astype(BF)

        def put(rows, cols, tile):
            dp[rows, 1024 + cols.start : 1024 + cols.stop] = tile.astype(BF)

        self.gather_heads(recv, per, put)
        if then is not None:
            then()
        weight = self.weight(QKV)
        acc = self.b.acc

        def chunk(number):
            rows = slice(256 * number, 256 * number + 256)
            total = dot_t(dp[:, 0:512], weight[0, rows, :])
            total += dot_t(dp[:, 512:1024], weight[1, rows, :])
            return total + dot_t(dp[:, 1024:1536], weight[2, rows, :])

        def sink(number, value):
            acc[:, 256 * number : 256 * number + 256] = value

        env.core_sum(self, 1, chunk, sink)
        grad_hidden, grad_gain = norm_back(
            acc[...], self.b.x[...].astype(F32), self.gain(env, 0)
        )
        row = self.gains[0]
        env.b.vg[row : row + 1, :] = grad_gain
        finish(self.b.gm[...] + grad_hidden)

    def parts(self, env, which):
        b = self.b
        left = (b.normed, b.al, b.nm, b.el)[which]
        right = (b.dp, b.mixl, b.gb, b.act)[which]
        return left, right

    def share_right(self, env, which, begin=0, size=None):
        at, full = COLS[which]
        size = full if size is None else size
        _, right = self.parts(env, which)
        fg = self.b.fg
        cols = pl.ds(at + begin, size)
        fg[pl.ds(env.q, 1), :, cols] = right[:, begin : begin + size][None]
        mine = fg.at[env.q, :, cols]
        self.right_waits.setdefault(which, []).append(
            env.plane_send(lambda other: mine, mine, fg.at[pl.ds(0, 3), :, cols])
        )

    def share_left(self, env, which):
        left, _ = self.parts(env, which)
        ds, dg = self.b.ds, self.b.dg
        low = low_lanes(self.rows)
        begin = 256 * (which - 1)
        for a in range(2):
            tiles = [
                left[:, 128 * (2 * z + a) : 128 * (2 * z + a) + 128].astype(F32) for z in range(4)
            ]
            for two in range(2):
                even, odd = tiles[2 * two], tiles[2 * two + 1]
                at = begin + 128 * two
                ds[2 * a, :, at : at + 128] = jnp.where(low, even, swap_halves(odd)).astype(BF)
                ds[2 * a + 1, :, at : at + 128] = jnp.where(low, swap_halves(even), odd).astype(BF)
        cols = pl.ds(begin, 256)
        dg[pl.ds(env.q, 1), :, begin : begin + 256] = ds[pl.ds(env.q, 1), :, begin : begin + 256]
        self.left_waits[which] = env.plane_send(
            lambda other: ds.at[other, :, cols],
            dg.at[env.q, :, cols],
            dg.at[pl.ds(0, 3), :, cols],
        )

    def multiply(self, env, which, first=0, last=None):
        if first == 0:
            self.left_waits[which]()
        self.right_waits[which].pop(0)()
        if last is None:
            for wait in self.right_waits.pop(which):
                wait()
        begin, size = COLS[which]
        last = size if last is None else last
        fg, dg, sb, rb = self.b.fg, self.b.dg, self.b.sb, self.b.rb
        rows = 4 * self.rows
        left = dg[:, :, 256 * (which - 1) : 256 * which].reshape(rows, 256)
        for at in range(begin + first, begin + last, 512):
            right = fg[:, :, at : at + 512].reshape(rows, 512)
            product = dot_l(left, right)
            for z in range(4):
                sb[z, :, at : at + 512] = product[64 * z : 64 * z + 64].astype(BF)
            if (at + 512 - begin) % PIECE == 0 or at + 512 == begin + last:
                low = begin + (at - begin) // PIECE * PIECE
                cols = pl.ds(low, at + 512 - low)
                steps = env.line_reduce(sb.at[:, :, cols], rb.at[:, :, cols])
                self.line_waits.setdefault(which, []).append((low, at + 512, steps))

    def relay(self, env, which, pieces=None):
        sb, rb = self.b.sb, self.b.rb
        for low, high, (arrived, pass_on, _) in self.line_waits[which][pieces or slice(None)]:

            @pl.when(env.middle)
            def _():
                for slot, block in ((3, env.far), (2, env.across)):
                    arrived(slot)
                    for at in range(low, high, 512):
                        cols = slice(at, at + 512)
                        total = sb[pl.ds(block, 1), :, cols].astype(F32)
                        total = total + rb[slot : slot + 1, :, cols].astype(F32)
                        sb[pl.ds(block, 1), :, cols] = total.astype(BF)
                    pass_on(slot)

    def collect(self, env, which):
        begin, _ = COLS[which]
        sb, rb = self.b.sb, self.b.rb
        for low, high, (_, _, finish) in self.line_waits[which]:
            finish()
            for at in range(low, high, 512):
                cols = slice(at, at + 512)

                def fill(stage):
                    total = sb[pl.ds(env.z, 1), :, cols].astype(F32)
                    for slot in range(2):
                        total = total + rb[slot : slot + 1, :, cols].astype(F32)
                    stage[...] = total[0]

                env.store(self.results[which], which, at - begin, fill)

    def quarter_left(self, env):
        ul, left = self.b.ul, self.b.el
        cols = pl.ds(pl.multiple_of(512 * env.c, 512), 512)
        ul[pl.ds(env.q, 1), :, cols] = left[:, cols][None]
        self.quarter_wait = env.plane_send(
            lambda other: left.at[:, cols], ul.at[env.q, :, cols], ul.at[pl.ds(0, 3), :, cols]
        )

    def quarter_core(self, env):
        self.quarter_wait()
        mine = self.b.ul.at[:, :, pl.ds(pl.multiple_of(512 * env.c, 512), 512)]
        copy = env.remote(mine, mine, env.sem(), env.sem(), env.s, 1 - env.c)
        copy.start()
        env.sends.append(copy)
        self.quarter_wait = copy.wait_recv

    def quarter_right(self, env):
        right, ur = self.b.act, self.b.ur

        def quarter(number):
            return pl.ds(pl.multiple_of(number * 512, 512), 512)

        ur[pl.ds(env.q, 1)] = right[:, quarter(env.q)][None]
        self.quarter_columns = env.plane_send(
            lambda other: right.at[:, quarter(other)], ur.at[env.q], ur.at[pl.ds(0, 3)]
        )

    def quarter_multiply(self, env):
        self.quarter_wait()
        self.quarter_columns()
        ul, ur, us, ub = self.b.ul, self.b.ur, self.b.us, self.b.ub
        rows = 4 * self.rows
        left = ul[...].reshape(rows, 1024)
        self.quarter_steps = []
        for at in range(0, 512, 256):
            product = dot_l(left, ur[:, :, at : at + 256].reshape(rows, 256))
            for z in range(4):
                us[z, :, at : at + 256] = product[256 * z : 256 * z + 256].astype(BF)
            cols = pl.ds(at, 256)
            self.quarter_steps.append(env.line_reduce(us.at[:, :, cols], ub.at[:, :, cols]))

    def quarter_relay(self, env):
        us, ub = self.b.us, self.b.ub
        for number, (arrived, pass_on, _) in enumerate(self.quarter_steps):
            cols = slice(256 * number, 256 * number + 256)

            @pl.when(env.middle)
            def _():
                for slot, block in ((3, env.far), (2, env.across)):
                    arrived(slot)
                    total = us[pl.ds(block, 1), :, cols].astype(F32)
                    total = total + ub[slot : slot + 1, :, cols].astype(F32)
                    us[pl.ds(block, 1), :, cols] = total.astype(BF)
                    pass_on(slot)

    def quarter_share(self, env):
        us, ub, ux, uy = self.b.us, self.b.ub, self.b.ux, self.b.uy
        for number, (_, _, finish) in enumerate(self.quarter_steps):
            finish()
            cols = slice(256 * number, 256 * number + 256)
            total = us[pl.ds(env.z, 1), :, cols].astype(F32)
            for slot in range(2):
                total = total + ub[slot : slot + 1, :, cols].astype(F32)
            for q in range(4):
                ux[q, :, cols] = total[0, 64 * q : 64 * q + 64].astype(BF)
        uy[pl.ds(env.q, 1)] = ux[pl.ds(env.q, 1)]
        self.quarter_back = env.plane_send(
            lambda other: ux.at[other], uy.at[env.q], uy.at[pl.ds(0, 3)]
        )

    def quarter_collect(self, env):
        self.quarter_back()
        for q in range(4):

            def fill(stage):
                stage[...] = self.b.uy[q].astype(F32)

            env.store(self.results[DOWN], DOWN, 512 * q, fill)

    def gather_line(self, env):
        normed, ng, per = self.b.normed, self.b.ng, self.per
        cols = pl.ds(pl.multiple_of(512 * env.c, 512), 512)

        def rows(z):
            return pl.ds(pl.multiple_of(lax.div(z, 2) * per, per), per)

        ng[pl.ds(env.z, 1), pl.ds(env.q, 1), :, cols] = normed[rows(env.z), cols][None, None]
        self.gather_wait = env.line_send(
            lambda other: normed.at[rows(other), cols],
            lambda step: ng.at[env.z, env.q, :, cols],
            ng.at[pl.ds(0, 3), 0, :, cols],
        )

    def gather_plane(self, env):
        self.gather_wait()
        ng = self.b.ng
        cols = pl.ds(pl.multiple_of(512 * env.c, 512), 512)
        mine = ng.at[:, env.q, :, cols]
        self.gather_wait = env.plane_send(lambda other: mine, mine, ng.at[:, pl.ds(0, 3), :, cols])

    def gather_core(self, env):
        self.gather_wait()
        cols = pl.ds(pl.multiple_of(512 * env.c, 512), 512)
        mine = self.b.ng.at[:, :, :, cols]
        copy = env.remote(mine, mine, env.sem(), env.sem(), env.s, 1 - env.c)
        copy.start()
        env.sends.append(copy)
        self.gather_wait = copy.wait_recv

    def head_gradient(self, env):
        self.gather_wait()
        per, total = self.per, self.total
        product = dot_l(self.b.x7[...], self.b.ng[...].reshape(total, 1024))
        turned = jnp.transpose(product)
        send = self.b.s9
        for i in range(self.n):
            rows = slice(i * 64, i * 64 + 64)
            send[i, 0:per] = turned[rows, 0:128].astype(BF)
            send[i, per:] = self.pack(turned[rows, 128:256]).astype(BF)
        self.wait9 = env.exchange(send, self.b.r9)

    def head_collect(self, env):
        self.wait9()
        recv, per, vr = self.b.r9, self.per, self.value_rows
        low = low_lanes(per)

        def both(pair, rows):
            return recv[pair, rows].astype(F32) + recv[pair + 8, rows].astype(F32)

        for part in range(3):

            def fill(stage):
                for j in range(4):
                    cols = slice(128 * j, 128 * j + 128)
                    rows = slice(0, per) if part < 2 else slice(per, per + vr)
                    one, two = both(2 * j, rows), both(2 * j + 1, rows)
                    if part == 0:
                        stage[:, cols] = jnp.where(low, one, swap_halves(two))
                    elif part == 1:
                        stage[:, cols] = jnp.where(low, swap_halves(one), two)
                    else:
                        first, second = self.join_pairs(one, two)
                        stage[0:vr, cols] = first
                        stage[vr:, cols] = second

            env.store(self.results[QKV], QKV, 512 * part, fill)

    def spread_right(self, env, which):
        _, right = self.parts(env, which)
        fg, width = self.b.fg, WIDTHS[which]
        cols = pl.ds(BEGINS[which], width)

        def quarter(number):
            return pl.ds(pl.multiple_of(number * width, 128), width)

        fg[pl.ds(env.z, 1), pl.ds(env.q, 1), :, cols] = right[:, quarter(env.q)][None, None]
        self.right_waits[which] = env.plane_send(
            lambda other: right.at[:, quarter(other)],
            fg.at[env.z, env.q, :, cols],
            fg.at[env.z, pl.ds(0, 3), :, cols],
        )

    def spread_right_on(self, env, which):
        self.right_waits[which]()
        fg = self.b.fg
        cols = pl.ds(BEGINS[which], WIDTHS[which])
        self.hops[which] = env.line_gather(fg.at[:, :, :, cols])

    def spread_hop(self, env, which, number):
        self.hops[which][number]()

    def spread_left(self, env, which):
        left, _ = self.parts(env, which)
        dg = self.b.dg

        def quarter(number):
            return pl.ds(pl.multiple_of(number * 256 + 128 * env.c, 128), 128)

        cols = self.core_cols(env, which)
        dg[pl.ds(env.z, 1), pl.ds(env.q, 1), :, cols] = left[:, quarter(env.z)][None, None]
        self.left_waits[which] = env.line_send(
            lambda other: left.at[:, quarter(other)],
            lambda step: dg.at[env.z, env.q, :, cols],
            dg.at[pl.ds(0, 3), env.q, :, cols],
        )

    def core_cols(self, env, which):
        return pl.ds(pl.multiple_of(256 * which + 128 * env.c, 128), 128)

    def spread_left_on(self, env, which):
        self.left_waits[which]()
        dg = self.b.dg
        cols = self.core_cols(env, which)
        mine = dg.at[:, env.q, :, cols]
        self.left_waits[which] = env.plane_send(
            lambda other: mine, mine, dg.at[:, pl.ds(0, 3), :, cols]
        )

    def spread_left_core(self, env, which):
        self.left_waits[which]()
        mine = self.b.dg.at[:, :, :, self.core_cols(env, which)]
        copy = env.remote(mine, mine, env.sem(), env.sem(), env.s, 1 - env.c)
        copy.start()
        env.sends.append(copy)
        self.left_waits[which] = copy.wait_recv

    def spread_multiply(self, env, which):
        self.hops[which][2]()
        self.left_waits[which]()
        fg, dg, sb, rb = self.b.fg, self.b.dg, self.b.sb, self.b.rb
        width = WIDTHS[which]
        cols = pl.ds(BEGINS[which], width)
        rows = 16 * self.rows
        product = dot_l(
            dg[:, :, :, 256 * which : 256 * which + 256].reshape(rows, 256),
            fg[:, :, :, cols].reshape(rows, width),
        ).astype(BF)
        for number in range(4):
            sb[number, :, cols] = product[64 * number : 64 * number + 64]
        rb[pl.ds(env.q, 1), :, cols] = sb[pl.ds(env.q, 1), :, cols]
        self.line_waits[which] = env.plane_send(
            lambda other: sb.at[other, :, cols],
            rb.at[env.q, :, cols],
            rb.at[pl.ds(0, 3), :, cols],
        )

    def spread_collect(self, env, which):
        self.line_waits[which]()
        rb, begin, width = self.b.rb, BEGINS[which], WIDTHS[which]
        for at in range(0, SIZES[which], 512):

            def fill(stage):
                for inner in range(0, 512, 128):
                    source, offset = divmod(at + inner, width)
                    stage[:, inner : inner + 128] = rb[
                        source, :, begin + offset : begin + offset + 128
                    ].astype(F32)

            env.store(self.results[which], which, at, fill)


def pick_rows(env, dense, routed):
    hot, labs, first = routed.b.hot, routed.b.labs, env.b.first
    group, slots = dense.per, routed.per
    base = env.s * group
    for seq in range(2):
        listed = env.b.routed[seq : seq + 1, :]
        places = listed.shape[1]
        place = lax.broadcasted_iota(jnp.int32, (group, places), 0) + base
        here = (place == listed).astype(F32).astype(BF)
        before = jnp.sum((listed < base).astype(F32), axis=1, keepdims=True).astype(jnp.int32)
        number = lax.broadcasted_iota(jnp.int32, (slots, places), 1) - before
        slot = lax.broadcasted_iota(jnp.int32, (slots, places), 0)
        mine = (number == slot).astype(F32).astype(BF)
        table = dot_t(mine, here).astype(BF)
        hot[seq] = table
        segments = env.b.segments[seq : seq + 1, :]
        row = (lax.broadcasted_iota(jnp.int32, (group, 1), 0) + base).astype(F32)
        label = jnp.zeros((group, 1), F32)
        for number in range(1, 4):
            edge = jnp.sum((segments < number).astype(F32), axis=1, keepdims=True)
            label = label + (row >= edge).astype(F32)
        lane = lax.broadcasted_iota(jnp.int32, (group, 128), 1)
        one_hot = (lane == label.astype(jnp.int32) + 64).astype(F32).astype(BF)
        labs[seq * slots : (seq + 1) * slots, :] = dot(table, one_hot)
        rows = first[seq * group : (seq + 1) * group, :].astype(BF)
        routed.b.x[seq * slots : (seq + 1) * slots, :] = dot(table, rows).astype(BF)


def restore(env, dense, routed, sent, seq):
    slots = routed.per
    return dot_l(routed.b.hot[seq], sent[seq * slots : (seq + 1) * slots])


def gate_rows(env, dense, routed):
    group, slots = dense.per, routed.per
    sent = routed.b.acc[...].astype(BF)
    router = env.vector(4)
    grad_router = jnp.zeros((1, 1024), F32)
    for seq in range(2):
        rows = slice(seq * group, (seq + 1) * group)
        first = env.b.first[rows, :]
        returned = restore(env, dense, routed, sent, seq)
        gate = jax.nn.sigmoid(jnp.sum(first * router, axis=1, keepdims=True))
        env.b.output[rows, :] = first + gate * returned
        grad = env.b.cotangent[:, seq, :].astype(F32)
        low = (gate * grad).astype(BF)
        routed.b.e[seq * slots : (seq + 1) * slots, :] = dot(routed.b.hot[seq], low)
        logit = jnp.sum(grad * returned, axis=1, keepdims=True) * gate * (1.0 - gate)
        grad_router = grad_router + jnp.sum(logit * first, axis=0, keepdims=True)
        dense.b.e[rows, :] = grad + logit * router
    env.b.vg[4:5, :] = grad_router


def share_vectors(env):
    vg, sv, rv = env.b.vg, env.b.sv, env.b.rv
    for number in range(env.n):
        tile = vg[:, 128 * (number // 2) : 128 * (number // 2) + 128]
        sv[number] = swap_halves(tile) if number % 2 else tile
    return env.exchange(sv, rv)


def sum_vectors(env, wait):
    wait()
    total = env.b.rv[0]
    for number in range(1, env.n):
        total = total + env.b.rv[number]
    env.b.gvec[...] = total


QKV, OUT, UP, DOWN = range(4)
SHAPES = ((3, 1024, 512), (512, 1024), (1024, 2048), (2048, 1024))
GRADS = ((3, 64, 512), (64, 512), (64, 2048), (64, 2048))


def whole_step(env, dense, routed):
    env.greet()
    b = env.b
    copies = [
        pltpu.make_async_copy(source, target, env.sem())
        for source, target in ((b.tokens_hbm, b.tokens), (b.cotangent_hbm, b.cotangent))
    ]
    for copy in copies:
        copy.start()
    dense.load(env, QKV)
    copies[0].wait()
    for seq in range(2):
        dense.b.x[seq * dense.per : (seq + 1) * dense.per, :] = env.b.tokens[:, seq, :]
    env.b.vg[...] = jnp.zeros_like(env.b.vg)
    dense.project(env)
    for number in (OUT, UP, DOWN):
        dense.load(env, number)
    dense.attend(env)
    dense.gather_line(env)
    for number in range(4):
        routed.load(env, number)
    mid_d, first = dense.b.mid, env.b.first
    def finish_dense(number, value):
        cols = slice(256 * number, 256 * number + 256)
        first[:, cols] = mid_d[:, cols] + value
    dense.feed(env, finish_dense)
    pick_rows(env, dense, routed)
    routed.project(env)
    dense.share_left(env, UP)
    routed.attend(env)
    dense.gather_plane(env)
    mid_r, x_r, sent = routed.b.mid, routed.b.x, routed.b.acc
    def finish_routed(number, value):
        cols = slice(256 * number, 256 * number + 256)
        sent[:, cols] = mid_r[:, cols] - x_r[:, cols].astype(F32) + value
    def spread_early():
        routed.spread_right(env, DOWN)
        routed.spread_right(env, OUT)
    routed.feed(env, finish_routed, spread_early)
    dense.quarter_right(env)
    routed.spread_left(env, QKV)
    routed.spread_left(env, UP)
    copies[1].wait()
    gate_rows(env, dense, routed)
    out_copy = pltpu.make_async_copy(b.output, b.output_hbm, env.sem())
    out_copy.start()
    routed.round_incoming()
    routed.back_feed(env)
    dense.gather_core(env)
    routed.spread_right_on(env, DOWN)
    routed.spread_right_on(env, OUT)
    routed.spread_right(env, UP)
    routed.spread_left(env, DOWN)
    routed.spread_left(env, OUT)
    routed.back_attend(env)
    routed.spread_hop(env, DOWN, 0)
    routed.spread_hop(env, OUT, 0)
    dense.share_right(env, OUT)
    routed.spread_right_on(env, UP)
    def finish_back(branch):
        low = branch.astype(BF)
        for seq in range(2):
            rows = slice(seq * dense.per, (seq + 1) * dense.per)
            dense.b.e[rows, :] += restore(env, dense, routed, low, seq)
    routed.back_project(env, finish_back, lambda: routed.spread_right(env, QKV))
    dense.round_incoming()
    dense.quarter_left(env)
    dense.back_feed(env)
    routed.spread_hop(env, DOWN, 1)
    routed.spread_hop(env, OUT, 1)
    routed.spread_hop(env, UP, 0)
    routed.spread_right_on(env, QKV)
    dense.share_left(env, OUT)
    dense.share_right(env, UP, 0, 1024)
    dense.back_attend(env)
    routed.spread_hop(env, UP, 1)
    routed.spread_hop(env, QKV, 0)
    dense.quarter_core(env)
    dense.quarter_multiply(env)
    dense.head_gradient(env)
    dense.multiply(env, OUT)
    dense.share_right(env, UP, 1024, 1024)
    dense.multiply(env, UP, 0, 1024)
    routed.spread_left_on(env, DOWN)
    routed.spread_left_on(env, OUT)
    routed.spread_left_on(env, UP)
    routed.spread_left_on(env, QKV)
    def finish_tokens(branch):
        env.b.grad_tokens[...] = dense.b.e[...] + branch
    dense.back_project(env, finish_tokens)
    grad_copy = pltpu.make_async_copy(b.grad_tokens, b.grad_tokens_hbm, env.sem())
    grad_copy.start()
    routed.spread_hop(env, QKV, 1)
    wait = share_vectors(env)
    dense.quarter_relay(env)
    dense.relay(env, OUT)
    dense.multiply(env, UP, 1024, 2048)
    routed.spread_left_core(env, DOWN)
    routed.spread_left_core(env, OUT)
    routed.spread_left_core(env, UP)
    routed.spread_left_core(env, QKV)
    routed.spread_multiply(env, DOWN)
    routed.spread_multiply(env, QKV)
    routed.spread_multiply(env, OUT)
    routed.spread_multiply(env, UP)
    dense.relay(env, UP)
    dense.quarter_share(env)
    routed.spread_collect(env, DOWN)
    dense.head_collect(env)
    routed.spread_collect(env, OUT)
    routed.spread_collect(env, UP)
    routed.spread_collect(env, QKV)
    dense.collect(env, OUT)
    dense.collect(env, UP)
    sum_vectors(env, wait)
    dense.quarter_collect(env)
    out_copy.wait()
    grad_copy.wait()
    env.drain()


def fused(group, tokens, cotangent, segments, routed_places, vectors, weights):
    n = lax.axis_size("seq")
    rows = 2 * group
    dense, routed = Layer(True, group, n), Layer(False, group // 4, n)
    wide = ((rows, 1024), F32)
    common = dict(
        stage=((8, 64, 512), F32),
        first=wide,
        output=wide,
        grad_tokens=wide,
        tokens=((group, 2, 1024), BF),
        cotangent=((group, 2, 1024), BF),
        vg=((8, 1024), F32),
        sv=((n, 8, 128), F32),
        rv=((n, 8, 128), F32),
    )
    groups = (dense.buffers(), routed.buffers(), common)
    scratch = [spec for table in groups for spec in table.values()]

    def kernel(*refs):
        refs = list(refs)

        def take(count):
            taken = refs[:count]
            del refs[:count]
            return taken

        inputs = take(4)
        vector_refs = take(5)
        sources = take(8)
        outputs = take(3)
        results = take(8)
        held = take(8)
        dense_refs, routed_refs, common_refs = (
            types.SimpleNamespace(**dict(zip(table, take(len(table)), strict=True))) for table in groups
        )
        b = common_refs
        b.tokens_hbm, b.cotangent_hbm, b.segments, b.routed = inputs
        b.output_hbm, b.grad_tokens_hbm, b.gvec = outputs
        b.vectors = vector_refs
        env = Env(b, refs[0], n)
        dense.attach(env, dense_refs, sources[:4], held[:4], results[:4])
        routed.attach(env, routed_refs, sources[4:], held[4:], results[4:])
        whole_step(env, dense, routed)

    vmem = pl.BlockSpec(memory_space=pltpu.VMEM)
    hbm = pl.BlockSpec(memory_space=pl.ANY)
    outs = [wide, wide, ((8, 128), F32)] + [(shape, F32) for shape in GRADS * 2]
    return pl.pallas_call(
        kernel,
        out_shape=[jax.ShapeDtypeStruct(*spec) for spec in outs],
        in_specs=[hbm] * 2 + [vmem] * 7 + [hbm] * 8,
        out_specs=[hbm] * 2 + [vmem] + [hbm] * 8,
        scratch_shapes=[pltpu.VMEM(shape, BF) for shape in SHAPES * 2]
        + [pltpu.VMEM(*spec) for spec in scratch]
        + [pltpu.SemaphoreType.DMA((384,))],
        compiler_params=pltpu.CompilerParams(
            collective_id=0, has_side_effects=True, vmem_limit_bytes=LIMIT
        ),
    )(tokens, cotangent, segments, routed_places, *vectors, *weights)


def place_results(group, parts):
    def kernel(*refs):
        sources, outs, held, sems = refs[:11], refs[11:26], refs[26:38], refs[38]
        gvec = sources[2]
        grads = list(zip(sources[3:], held[:8], outs[7:], strict=True))
        wides = list(zip(sources[:2], held[8:10], held[10:], outs[:2], strict=True))
        loads = [
            pltpu.make_async_copy(item[0], item[1], sems.at[0, number])
            for number, item in enumerate(wides + grads)
        ]
        for copy in loads:
            copy.start()
        for number in range(5):
            outs[2 + number][...] = gvec[number, 0:64]
        stores = []

        def store(source, target):
            stores.append(pltpu.make_async_copy(source, target, sems.at[1, len(stores)]))
            stores[-1].start()

        for number, (_, rows, turned, target) in enumerate(wides):
            loads[number].wait()
            for seq in range(2):
                turned[:, seq, :] = rows[seq * group : (seq + 1) * group, :]
            store(turned, target)
        for number, (_, block, target) in enumerate(grads):
            loads[2 + number].wait()
            store(block, target)
        for copy in stores:
            copy.wait()

    vmem = pl.BlockSpec(memory_space=pltpu.VMEM)
    hbm = pl.BlockSpec(memory_space=pl.ANY)
    wide, turned = (2 * group, 1024), (group, 2, 1024)
    shapes = [turned] * 2 + [(64,)] * 5 + list(GRADS * 2)
    held = list(GRADS * 2) + [wide] * 2 + [turned] * 2
    return pl.pallas_call(
        kernel,
        out_shape=[jax.ShapeDtypeStruct(shape, F32) for shape in shapes],
        in_specs=[hbm] * 2 + [vmem] + [hbm] * 8,
        out_specs=[hbm] * 2 + [vmem] * 5 + [hbm] * 8,
        scratch_shapes=[pltpu.VMEM(shape, F32) for shape in held]
        + [pltpu.SemaphoreType.DMA((2, 10))],
        compiler_params=pltpu.CompilerParams(vmem_limit_bytes=LIMIT),
    )(*parts)


def on_device_fused(
    tokens,
    segments,
    routed,
    router,
    dense_attn_gain,
    dense_qkv,
    dense_out,
    dense_mlp_gain,
    dense_up,
    dense_down,
    routed_attn_gain,
    routed_qkv,
    routed_out,
    routed_mlp_gain,
    routed_up,
    routed_down,
    cotangent,
):
    group = tokens.shape[0]
    parts = fused(
        group,
        tokens,
        cotangent,
        segments,
        routed,
        (dense_attn_gain, dense_mlp_gain, routed_attn_gain, routed_mlp_gain, router),
        (
            jnp.transpose(dense_qkv, (1, 0, 2)),
            dense_out,
            dense_up,
            dense_down,
            jnp.transpose(routed_qkv, (1, 0, 2)),
            routed_out,
            routed_up,
            routed_down,
        ),
    )
    placed = place_results(group, parts)
    vectors = placed[2:7]

    def weights_of(grads, first, second):
        return (
            vectors[first],
            jnp.transpose(grads[QKV], (1, 0, 2)),
            jnp.transpose(grads[OUT]),
            vectors[second],
            grads[UP],
            jnp.transpose(grads[DOWN]),
        )

    return (
        tuple(placed[:2])
        + weights_of(placed[7:11], 0, 1)
        + weights_of(placed[11:], 2, 3)
        + (vectors[4],)
    )


def solution(mesh):
    in_specs = (
        P("seq", None, None),
        P(),
        P(),
        P(),
        P(),
        P(None, None, "mp"),
        P("mp", None),
        P(),
        P(None, "mp"),
        P("mp", None),
        P(),
        P(None, None, "mp"),
        P("mp", None),
        P(),
        P(None, "mp"),
        P("mp", None),
        P("seq", None, None),
    )
    out_specs = (
        P("seq", None, None),
        P("seq", None, None),
        P("seq"),
        P("seq", None, "mp"),
        P("mp", "seq"),
        P("seq"),
        P("seq", "mp"),
        P("mp", "seq"),
        P("seq"),
        P("seq", None, "mp"),
        P("mp", "seq"),
        P("seq"),
        P("seq", "mp"),
        P("mp", "seq"),
        P("seq"),
    )
    seq_size = mesh.shape["seq"]
    pairs = 2 * (16 // mesh.shape["mp"])
    body = on_device_fused if seq_size == pairs else on_device

    return jax.shard_map(
        body, mesh=mesh, in_specs=in_specs, out_specs=out_specs, check_vma=False
    )
```
